32 devices in a mesh: section: 2 (over x), rows: 16 (over z, y, core).
Axes of the slice: x: 2, y: 2, z: 4, core: 2. Of those that a mesh axis runs over, the one named last changes fastest.
Arguments:
- block_input: bfloat16 [2, 2, 2048, 1472], P('section', None, 'rows'), may hold values from -6 to 6
- lengths: int32 [2, 2, 16], P(None, None, 'rows'), may hold values from 1 to 128
- targets: int32 [2, 2048], P(None, 'rows'), may hold values from 0 to 383
- attention_weight: float32 [2, 384, 4, 1472], P('section', 'rows')
- attention_first: float32 [2, 384, 4, 1472], P('section', 'rows'), may hold values from -1 to 1
- attention_second: float32 [2, 384, 4, 1472], P('section', 'rows'), may hold values from 0.0004096 to 0.0016384
- feed_weight: float32 [2, 3584, 3, 1472], P('section', 'rows'), may hold values from -0.15625 to 0.15625
- feed_first: float32 [2, 3584, 3, 1472], P('section', 'rows'), may hold values from -1 to 1
- feed_second: float32 [2, 3584, 3, 1472], P('section', 'rows'), may hold values from 0.0004096 to 0.0016384
- norm_gain: float32 [2, 3, 1472], P('section'), may hold values from 0.5 to 1.5
- gain_first: float32 [2, 3, 1472], P('section'), may hold values from -5 to 5
- gain_second: float32 [2, 3, 1472], P('section'), may hold values from 0.01024 to 0.04096
- cross_weight: float32 [384, 4, 1472], P('rows', None, 'section')
- cross_first: float32 [384, 4, 1472], P('rows', None, 'section'), may hold values from -1 to 1
- cross_second: float32 [384, 4, 1472], P('rows', None, 'section'), may hold values from 0.012288 to 0.049152
- head_weight: float32 [384, 1472], P('rows', 'section'), may hold values from -0.3125 to 0.3125
- head_first: float32 [384, 1472], P('rows', 'section'), may hold values from -5 to 5
- head_second: float32 [384, 1472], P('rows', 'section'), may hold values from 0.010666667 to 0.042666666
- cross_gain: float32 [1472], replicated, may hold values from 0.5 to 1.5
- cross_gain_first: float32 [1472], replicated, may hold values from -5 to 5
- cross_gain_second: float32 [1472], replicated, may hold values from 0.0016384 to 0.0065536
Outputs:
- input_gradient: float32 [2, 2, 2048, 1472], P('section', None, 'rows')
- total_loss: float32 [], replicated
- attention_first_new: float32 [2, 384, 4, 1472], P('section', 'rows')
- attention_second_new: float32 [2, 384, 4, 1472], P('section', 'rows')
- attention_weight_new: float32 [2, 384, 4, 1472], P('section', 'rows')
- feed_first_new: float32 [2, 3584, 3, 1472], P('section', 'rows')
- feed_second_new: float32 [2, 3584, 3, 1472], P('section', 'rows')
- feed_weight_new: float32 [2, 3584, 3, 1472], P('section', 'rows')
- gain_first_new: float32 [2, 3, 1472], P('section')
- gain_second_new: float32 [2, 3, 1472], P('section')
- norm_gain_new: float32 [2, 3, 1472], P('section')
- cross_first_new: float32 [384, 4, 1472], P('rows', None, 'section')
- cross_second_new: float32 [384, 4, 1472], P('rows', None, 'section')
- cross_weight_new: float32 [384, 4, 1472], P('rows', None, 'section')
- head_first_new: float32 [384, 1472], P('rows', 'section')
- head_second_new: float32 [384, 1472], P('rows', 'section')
- head_weight_new: float32 [384, 1472], P('rows', 'section')
- cross_gain_first_new: float32 [1472], replicated
- cross_gain_second_new: float32 [1472], replicated
- cross_gain_new: float32 [1472], replicated
The draws below stay inside these ranges and needn't reach their ends.
All inputs are finite; a program needn't handle non-finite values.
Results may differ from the reference program's by a relative error of at most 0.028.
Values may be sent and summed in bfloat16 or wider, within the bound.
A program may use at most 384 MiB of HBM per device.

```python
import math
import jax
import jax.numpy as jnp
import numpy as np
from jax import lax

D = 1472
HD = 64
FF = 3584
VOCAB = 384
INNER = 384
SEQ = 128
MICRO = 2
STEP = 10
TOKENS = 2048
N_ROWS = 16


def projection_rows(key, shape):
    normals = jax.random.truncated_normal(key, -4.0, 4.0, shape, jnp.float32)
    kind_scale = jnp.array([D ** (-0.5), D ** (-0.5), D ** (-0.5), 2.5 * INNER ** (-0.5)], jnp.float32)
    return normals * kind_scale[:, None]


def draw_attention_weight(key, part):
    key = jax.random.fold_in(key, 11)
    return projection_rows(key, (2, INNER, 4, D))


def draw_cross_weight(key, part):
    key = jax.random.fold_in(key, 12)
    return projection_rows(key, (INNER, 4, D))


def draw_lengths(key, part):
    key = jax.random.fold_in(key, 13)
    row_total = TOKENS // SEQ
    low_end = SEQ // 3
    row_ids = jnp.arange(row_total, dtype=jnp.int32)
    rising = low_end + (SEQ - low_end) * row_ids // max(row_total - 1, 1)
    jitter = jax.random.randint(key, (2, MICRO, row_total), 0, SEQ // 8 + 1)
    micro_ids = jnp.arange(MICRO, dtype=jnp.int32)
    keep_full = (row_ids[None, None, :] == row_total - 1) & (micro_ids[None, :, None] == 0)
    jitter = jnp.where(keep_full, 0, jitter)
    return (rising[None, None, :] - jitter).astype(jnp.int32)


def with_ends(values, stream_key, least, high):
    index_at = [jax.random.randint(jax.random.fold_in(stream_key, axis), (), 0, length) for axis, length in enumerate(values.shape)]
    widest = values.shape.index(max(values.shape))
    beside = index_at[:widest] + [(index_at[widest] + 1) % values.shape[widest]] + index_at[widest + 1:]
    return values.at[tuple(index_at)].set(least).at[tuple(beside)].set(high)


def steps_of(stream_key, shape, split, least, largest):
    factor_of, own = 1.0, jax.random.fold_in(stream_key, 6)
    for position, parts in split:
        draws = jnp.exp(jax.random.uniform(jax.random.fold_in(own, position), (parts,), jnp.float32, least / len(split), largest / len(split)))
        factor_of = factor_of * jnp.repeat(draws, shape[position] // parts).reshape([-1 if axis == position else 1 for axis in range(len(shape))])
    return factor_of


def rank_bounds(amount, skew):
    weights = [(1 << 20) // math.isqrt(rank ** skew) + 1 for rank in range(1, amount + 1)]
    scale = 1 + sum(weights) // (1 << 30)
    return np.cumsum(np.array([max(1, weight // scale) for weight in weights]))


def ranked_ids(rng, extent, count, lean):
    table = rank_bounds(count, lean)
    pick = jax.random.randint(jax.random.fold_in(rng, 1), extent, 0, int(table[count - 1]))
    standing = jnp.searchsorted(jnp.asarray(table, jnp.int32), pick, side="right")
    return jax.random.permutation(jax.random.fold_in(rng, 2), count)[standing].astype(jnp.int32)


def normal_values(key, shape, width, limit, split=(), held_as=jnp.bfloat16):
    loudness = steps_of(key, shape, split, -0.22, 0.18) if split else 1.0
    values = jax.random.normal(key, shape, jnp.float32) * width * loudness
    return jnp.minimum(jnp.maximum(values, -limit), limit).astype(held_as)


def setup_inputs(seed: int = 0) -> dict:
    streams_of = jax.random.split(jax.random.key(seed), 22)
    return {
        "block_input": normal_values(streams_of[0], (2, MICRO, TOKENS, D), 1.0, 6.0, ((0, 2), (2, 16))),
        "lengths": draw_lengths(jax.random.fold_in(streams_of[21], 71), 0),
        "targets": with_ends(ranked_ids(streams_of[2], (MICRO, TOKENS), VOCAB, 0), jax.random.fold_in(streams_of[2], 3), 0, VOCAB - 1).astype(jnp.int32),
        "attention_weight": draw_attention_weight(jax.random.fold_in(streams_of[21], 71), 0),
        "attention_first": normal_values(streams_of[4], (2, INNER, 4, D), (0.001 * (MICRO * TOKENS) ** 0.5), 1.0, ((0, 2), (1, 16)), jnp.float32),
        "attention_second": jnp.clip(jnp.exp(math.log(0.0016384) - 1.3862944 * jax.random.uniform(streams_of[5], (2, INNER, 4, D), jnp.float32) ** steps_of(streams_of[5], (2, INNER, 4, D), ((0, 2), (1, 16)), -0.2, 0.2)), 0.0004096, 0.0016384),
        "feed_weight": normal_values(streams_of[6], (2, FF, 3, D), D ** -0.5, 0.15625, ((0, 2), (1, 16)), jnp.float32),
        "feed_first": normal_values(streams_of[7], (2, FF, 3, D), (0.001 * (MICRO * TOKENS) ** 0.5), 1.0, ((0, 2), (1, 16)), jnp.float32),
        "feed_second": jnp.clip(jnp.exp(math.log(0.0016384) - 1.3862944 * jax.random.uniform(streams_of[8], (2, FF, 3, D), jnp.float32) ** steps_of(streams_of[8], (2, FF, 3, D), ((0, 2), (1, 16)), -0.2, 0.2)), 0.0004096, 0.0016384),
        "norm_gain": jnp.clip(1.0 + 0.1 * jax.random.normal(streams_of[9], (2, 3, D), jnp.float32), 0.5, 1.5),
        "gain_first": normal_values(streams_of[10], (2, 3, D), (0.005 * (MICRO * TOKENS) ** 0.5), 5.0, ((0, 2),), jnp.float32),
        "gain_second": jnp.clip(jnp.exp(math.log(0.04096) - 1.3862944 * jax.random.uniform(streams_of[11], (2, 3, D), jnp.float32) ** steps_of(streams_of[11], (2, 3, D), ((0, 2),), -0.2, 0.2)), 0.01024, 0.04096),
        "cross_weight": draw_cross_weight(jax.random.fold_in(streams_of[21], 71), 0),
        "cross_first": normal_values(streams_of[13], (INNER, 4, D), (0.001 * (MICRO * TOKENS) ** 0.5), 1.0, ((0, 16), (2, 2)), jnp.float32),
        "cross_second": jnp.clip(jnp.exp(math.log(0.049152) - 1.3862944 * jax.random.uniform(streams_of[14], (INNER, 4, D), jnp.float32) ** steps_of(streams_of[14], (INNER, 4, D), ((0, 16), (2, 2)), -0.2, 0.2)), 0.012288, 0.049152),
        "head_weight": normal_values(streams_of[15], (VOCAB, D), (D // 4) ** -0.5, 0.3125, ((0, 16), (1, 2)), jnp.float32),
        "head_first": normal_values(streams_of[16], (VOCAB, D), (0.1 * (MICRO * TOKENS * VOCAB ** -1.0) ** 0.5), 5.0, ((0, 16), (1, 2)), jnp.float32),
        "head_second": jnp.clip(jnp.exp(math.log(0.042666666) - 1.3862944 * jax.random.uniform(streams_of[17], (VOCAB, D), jnp.float32) ** steps_of(streams_of[17], (VOCAB, D), ((0, 16), (1, 2)), -0.2, 0.2)), 0.010666667, 0.042666666),
        "cross_gain": jnp.clip(1.0 + 0.1 * jax.random.normal(streams_of[18], (D,), jnp.float32), 0.5, 1.5),
        "cross_gain_first": normal_values(streams_of[19], (D,), (0.005 * (MICRO * TOKENS) ** 0.5), 5.0, (), jnp.float32),
        "cross_gain_second": jnp.clip(jnp.exp(jax.random.uniform(streams_of[20], (D,), jnp.float32, math.log(0.0016384), math.log(0.0065536))), 0.0016384, 0.0065536),
    }


@jax.custom_vjp
def low(v):
    return lax.optimization_barrier(v.astype(jnp.bfloat16)).astype(jnp.float32)

@jax.custom_vjp
def low_back(v):
    return v

def low_keep(v):
    return (low(v), None)

def low_pass(kept, grad):
    return (grad,)

def back_keep(v):
    return (v, None)

def back_low(kept, grad):
    return (low(grad),)
low.defvjp(low_keep, low_pass)
low_back.defvjp(back_keep, back_low)
masked_value = -1000000000.0
highest = lax.Precision.HIGHEST

def rounded_both(values):
    return low_back(low(values))

def norm_rows(states, scale_gain):
    return states * lax.rsqrt(lax.optimization_barrier(jnp.mean(states * states, axis=-1, keepdims=True)) + 1e-06) * scale_gain

def attend(query_in, source_in, weights, allowed):
    batch_size = query_in.shape[0]
    length = query_in.shape[1]
    inner_width = weights.shape[0]
    head_count = inner_width // HD
    queries = rounded_both(jnp.einsum('bsd,jd->bsj', query_in, weights[:, 0, :], precision=highest))
    key_rows = rounded_both(jnp.einsum('bsd,jd->bsj', source_in, weights[:, 1, :], precision=highest))
    value_rows = rounded_both(jnp.einsum('bsd,jd->bsj', source_in, weights[:, 2, :], precision=highest))
    scores = jnp.einsum('bqhd,bkhd->bhqk', queries.reshape(batch_size, length, head_count, HD), key_rows.reshape(batch_size, length, head_count, HD), precision=highest)
    scores = low_back(scores * HD ** (-0.5))
    scores = jnp.where(allowed[:, None], scores, masked_value)
    shifted = jnp.exp(scores - lax.optimization_barrier(jnp.max(scores, axis=-1, keepdims=True)))
    soft_weights = low(shifted / lax.optimization_barrier(jnp.sum(shifted, axis=-1, keepdims=True)))
    mixed_heads = jnp.einsum('bhqk,bkhd->bqhd', soft_weights, value_rows.reshape(batch_size, length, head_count, HD), precision=highest)
    mixed_heads = rounded_both(mixed_heads.reshape(batch_size, length, inner_width))
    return low_back(jnp.einsum('bsj,jd->bsd', mixed_heads, weights[:, 3, :], precision=highest))

def feed_block(normed, weights):
    gate_part = low_back(jnp.einsum('bsd,jd->bsj', normed, weights[:, 0, :], precision=highest))
    up_part = low_back(jnp.einsum('bsd,jd->bsj', normed, weights[:, 1, :], precision=highest))
    hidden = low(jax.nn.gelu(gate_part, approximate=True) * up_part)
    return low_back(jnp.einsum('bsj,jd->bsd', hidden, weights[:, 2, :], precision=highest))

def encoder_block(inputs, gains, attention, feed, enc_count):
    length = inputs.shape[1]
    allowed = lax.broadcasted_iota(jnp.int32, (length, length), 1)[None] < enc_count[:, None, None]
    normed_attn = low(norm_rows(inputs, gains[0]))
    middle = inputs + attend(normed_attn, normed_attn, attention, allowed)
    normed_feed = low(norm_rows(middle, gains[1]))
    last_state = middle + feed_block(normed_feed, feed)
    return rounded_both(norm_rows(last_state, gains[2]))

def decoder_block(inputs, encoded, gains, cross_scale, attention, cross, feed, head, dec_count, enc_count, target_rows):
    length = inputs.shape[1]
    row_ids = lax.broadcasted_iota(jnp.int32, (length, length), 0)
    col_ids = lax.broadcasted_iota(jnp.int32, (length, length), 1)
    causal = (col_ids <= row_ids)[None]
    cross_allowed = col_ids[None] < enc_count[:, None, None]
    normed_attn = low(norm_rows(inputs, gains[0]))
    middle = inputs + attend(normed_attn, normed_attn, attention, causal)
    normed_cross = low(norm_rows(middle, cross_scale))
    second_state = middle + attend(normed_cross, encoded, cross, cross_allowed)
    normed_feed = low(norm_rows(second_state, gains[1]))
    last_state = second_state + feed_block(normed_feed, feed)
    final_rows = low(norm_rows(last_state, gains[2]))
    logits = low_back(jnp.einsum('bsd,vd->bsv', final_rows, head, precision=highest))
    top_logit = lax.optimization_barrier(jnp.max(logits, axis=-1, keepdims=True))
    log_total = top_logit[..., 0] + jnp.log(lax.optimization_barrier(jnp.sum(jnp.exp(logits - top_logit), axis=-1)))
    vocab_ids = lax.broadcasted_iota(jnp.int32, logits.shape, 2)
    picked = lax.optimization_barrier(jnp.sum(jnp.where(vocab_ids == target_rows[..., None], logits, 0.0), axis=-1))
    valid_rows = lax.broadcasted_iota(jnp.int32, (length,), 0)[None] < dec_count[:, None]
    return jnp.sum(jnp.where(valid_rows, log_total - picked, 0.0))

def adam_step(weight, first_moment, second_moment, gradient, step_rate, weight_decay):
    first_new = 0.9 * first_moment + 0.1 * gradient
    second_new = 0.999 * second_moment + 0.001 * gradient * gradient
    first_fix = 1.0 - 0.9 ** STEP
    second_fix = 1.0 - 0.999 ** STEP
    update = first_new / first_fix / (jnp.sqrt(second_new / second_fix) + 1e-08)
    return (first_new, second_new, weight - step_rate * (update + weight_decay * weight))

def reference(block_input, lengths, targets, attention_weight, attention_first, attention_second, feed_weight, feed_first, feed_second, norm_gain, gain_first, gain_second, cross_weight, cross_first, cross_second, head_weight, head_first, head_second, cross_gain, cross_gain_first, cross_gain_second):
    sequence_count = MICRO * N_ROWS
    group_size = math.gcd(sequence_count, max(1, 4096 // SEQ))
    group_count = sequence_count // group_size
    enc_counts = lengths[0].reshape(group_count, group_size)
    dec_counts = lengths[1].reshape(group_count, group_size)
    target_ids = targets.reshape(group_count, group_size, SEQ)

    def total(inputs, attention, feed, gains, cross, head, cross_scale):
        attention_low = low(attention)
        feed_low = low(feed)
        cross_low = low(cross)
        head_low = low(head)
        enc_inputs = inputs[0].reshape(group_count, group_size, SEQ, D)
        dec_inputs = inputs[1].reshape(group_count, group_size, SEQ, D)

        def pair_loss(sequence_pack):
            enc_rows, dec_rows, enc_count, dec_count, target_rows = sequence_pack
            encoded = encoder_block(enc_rows, gains[0], attention_low[0], feed_low[0], enc_count)
            return decoder_block(dec_rows, encoded, gains[1], cross_scale, attention_low[1], cross_low, feed_low[1], head_low, dec_count, enc_count, target_rows)
        losses = lax.map(jax.checkpoint(pair_loss), (enc_inputs, dec_inputs, enc_counts, dec_counts, target_ids))
        return jnp.sum(losses)
    total_loss, pullback = jax.vjp(total, block_input.astype(jnp.float32), attention_weight, feed_weight, norm_gain, cross_weight, head_weight, cross_gain)
    gradients = pullback(jnp.ones_like(total_loss))
    attention_new = adam_step(attention_weight, attention_first, attention_second, gradients[1], 0.05, 0.1)
    feed_new = adam_step(feed_weight, feed_first, feed_second, gradients[2], 0.05, 0.1)
    gain_new = adam_step(norm_gain, gain_first, gain_second, gradients[3], 0.5, 0.0)
    cross_new = adam_step(cross_weight, cross_first, cross_second, gradients[4], 0.05, 0.1)
    head_new = adam_step(head_weight, head_first, head_second, gradients[5], 0.05, 0.1)
    cross_gain_update = adam_step(cross_gain, cross_gain_first, cross_gain_second, gradients[6], 0.5, 0.0)
    return (gradients[0], total_loss, attention_new[0], attention_new[1], attention_new[2], feed_new[0], feed_new[1], feed_new[2], gain_new[0], gain_new[1], gain_new[2], cross_new[0], cross_new[1], cross_new[2], head_new[0], head_new[1], head_new[2], cross_gain_update[0], cross_gain_update[1], cross_gain_update[2])
```

```python
import functools

import jax
import jax.numpy as jnp
from jax import lax
from jax.experimental import pallas as pl
from jax.experimental.pallas import tpu as pltpu
from jax.sharding import PartitionSpec as P

HD = 64
STEP = 10
PAIR = 2 * HD
BLOCKS = 16
VMEM_BYTES = 52 * 1024 * 1024

bf16 = jnp.bfloat16
f32 = jnp.float32
masked_value = -1000000000.0
scale = HD ** (-0.5)


def dot(a, b):
    return lax.dot_general(a, b, (((1,), (0,)), ((), ())), preferred_element_type=f32)


def dot_last(a, b):
    return lax.dot_general(a, b, (((1,), (1,)), ((), ())), preferred_element_type=f32)


def dot_rows(a, b):
    return lax.dot_general(a, b, (((0,), (0,)), ((), ())), preferred_element_type=f32)


def unit_rows(v):
    r = lax.rsqrt(jnp.mean(v * v, axis=-1, keepdims=True) + 1e-06)
    return r, v * r


def norm_back(v, gain, up):
    r, n = unit_rows(v)
    g = up * gain
    back = r * (g - n * jnp.mean(g * n, axis=-1, keepdims=True))
    return back, jnp.sum(up * n, axis=0, keepdims=True)


def gelu_parts(x):
    c = 0.7978845608028654
    t = jnp.tanh(c * (x + 0.044715 * (x * x * x)))
    act = 0.5 * x * (1.0 + t)
    slope = 0.5 * (1.0 + t) + 0.5 * x * (1.0 - t * t) * (c * (1.0 + 3.0 * 0.044715 * (x * x)))
    return act, slope


def low_half(length):
    return lax.broadcasted_iota(jnp.int32, (length, PAIR), 1) < HD


def stack_pair(m, low):
    zero = jnp.zeros_like(m)
    return jnp.concatenate([jnp.where(low, m, zero), jnp.where(low, zero, m)], axis=0)


def allowed_twice(cnt_ref, s, length):
    row = lax.broadcasted_iota(jnp.int32, (length, length), 0)
    col = lax.broadcasted_iota(jnp.int32, (length, length), 1)
    limit = jnp.where(cnt_ref[0] == 1, row + 1, cnt_ref[1 + s])
    one = jnp.where(col < limit, 1, 0)
    return jnp.concatenate([one, one], axis=0) == 1


def soft_pair(q2, k, allowed):
    s = dot_last(q2, k) * scale
    s = jnp.where(allowed, s, masked_value)
    e = jnp.exp(s - jnp.max(s, axis=-1, keepdims=True))
    return e / jnp.sum(e, axis=-1, keepdims=True)


def attend_fwd_kernel(cross, length, cnt_ref, x_ref, gain_ref, *refs):
    if cross:
        src_ref, w_ref, n_ref, qkv_ref, o_ref, y_ref = refs
    else:
        w_ref, n_ref, qkv_ref, o_ref, y_ref = refs
    inner = w_ref.shape[0] // 4
    x = x_ref[...].astype(f32)
    n = (unit_rows(x)[1] * gain_ref[...]).astype(bf16)
    n_ref[...] = n
    if cross:
        qkv_ref[:, :inner] = dot_last(n, w_ref[:inner, :]).astype(bf16)
        qkv_ref[:, inner:] = dot_last(src_ref[...], w_ref[inner : 3 * inner, :]).astype(bf16)
    else:
        qkv_ref[...] = dot_last(n, w_ref[: 3 * inner, :]).astype(bf16)
    low = low_half(length)
    for s in range(x.shape[0] // length):
        allowed = allowed_twice(cnt_ref, s, length)
        rows = slice(s * length, (s + 1) * length)
        for h in range(inner // PAIR):
            cols = [slice(j * inner + h * PAIR, j * inner + (h + 1) * PAIR) for j in range(3)]
            q2 = stack_pair(qkv_ref[rows, cols[0]], low)
            p = soft_pair(q2, qkv_ref[rows, cols[1]], allowed).astype(bf16)
            wide = jnp.concatenate([p[:length], p[length:]], axis=1)
            o_ref[rows, cols[0]] = dot(wide, stack_pair(qkv_ref[rows, cols[2]], low)).astype(bf16)
    y_ref[...] = x + dot(o_ref[...], w_ref[3 * inner :, :])


def attend_fwd(counts, x, gain, w, length, source=None):
    t, d = x.shape
    inner = w.shape[0] // 4
    ins = [counts, x, gain] + ([] if source is None else [source]) + [w]
    vm = pl.BlockSpec(memory_space=pltpu.VMEM)
    return pl.pallas_call(
        functools.partial(attend_fwd_kernel, source is not None, length),
        out_shape=(
            jax.ShapeDtypeStruct((t, d), bf16),
            jax.ShapeDtypeStruct((t, 3 * inner), bf16),
            jax.ShapeDtypeStruct((t, inner), bf16),
            jax.ShapeDtypeStruct((t, d), f32),
        ),
        in_specs=[pl.BlockSpec(memory_space=pltpu.SMEM)] + [vm] * (len(ins) - 1),
        out_specs=(vm,) * 4,
        compiler_params=pltpu.CompilerParams(vmem_limit_bytes=VMEM_BYTES),
        cost_estimate=pl.CostEstimate(
            flops=2 * t * d * inner * 4 + 8 * t * length * inner,
            bytes_accessed=w.size * 2 + t * d * 10,
            transcendentals=t * length * 6,
        ),
    )(*ins)


def attend_bwd_kernel(cross, length, cnt_ref, x_ref, gain_ref, gy_ref, qkv_ref, w_ref, *refs):
    if cross:
        ga_ref, dqkv_ref, gx_ref, gg_ref, gs_ref, do_ref = refs
    else:
        ga_ref, dqkv_ref, gx_ref, gg_ref, do_ref = refs
    inner = w_ref.shape[0] // 4
    ga = gy_ref[...].astype(bf16)
    ga_ref[...] = ga
    do_ref[...] = dot_last(ga, w_ref[3 * inner :, :]).astype(bf16)
    low = low_half(length)
    for s in range(ga.shape[0] // length):
        allowed = allowed_twice(cnt_ref, s, length)
        rows = slice(s * length, (s + 1) * length)
        for h in range(inner // PAIR):
            cols = [slice(j * inner + h * PAIR, j * inner + (h + 1) * PAIR) for j in range(3)]
            q2 = stack_pair(qkv_ref[rows, cols[0]], low)
            k = qkv_ref[rows, cols[1]]
            p = soft_pair(q2, k, allowed)
            do2 = stack_pair(do_ref[rows, cols[0]], low)
            dp = dot_last(do2, qkv_ref[rows, cols[2]])
            ds = p * (dp - jnp.sum(dp * p, axis=-1, keepdims=True))
            ds = jnp.where(allowed, ds, 0.0).astype(bf16)
            wide = jnp.concatenate([ds[:length], ds[length:]], axis=1)
            dqkv_ref[rows, cols[0]] = (dot(wide, stack_pair(k, low)) * scale).astype(bf16)
            dqkv_ref[rows, cols[1]] = (dot_rows(ds, q2) * scale).astype(bf16)
            dqkv_ref[rows, cols[2]] = dot_rows(p.astype(bf16), do2).astype(bf16)
    if cross:
        up = dot(dqkv_ref[:, :inner], w_ref[:inner, :])
        gs_ref[...] = dot(dqkv_ref[:, inner:], w_ref[inner : 3 * inner, :]).astype(bf16)
    else:
        up = dot(dqkv_ref[...], w_ref[: 3 * inner, :])
    back, gg_ref[...] = norm_back(x_ref[...].astype(f32), gain_ref[...], up)
    gx_ref[...] = gy_ref[...] + back


def attend_bwd(counts, x, gain, gy, qkv, w, length, cross=False):
    t, d = x.shape
    inner = w.shape[0] // 4
    vm = pl.BlockSpec(memory_space=pltpu.VMEM)
    outs = [
        jax.ShapeDtypeStruct((t, d), bf16),
        jax.ShapeDtypeStruct((t, 3 * inner), bf16),
        jax.ShapeDtypeStruct((t, d), f32),
        jax.ShapeDtypeStruct((1, d), f32),
    ]
    if cross:
        outs.append(jax.ShapeDtypeStruct((t, d), bf16))
    return pl.pallas_call(
        functools.partial(attend_bwd_kernel, cross, length),
        out_shape=tuple(outs),
        in_specs=[pl.BlockSpec(memory_space=pltpu.SMEM)] + [vm] * 5,
        out_specs=(vm,) * len(outs),
        scratch_shapes=[pltpu.VMEM((t, inner), bf16)],
        compiler_params=pltpu.CompilerParams(vmem_limit_bytes=VMEM_BYTES),
        cost_estimate=pl.CostEstimate(
            flops=2 * t * d * inner * 4 + 20 * t * length * inner,
            bytes_accessed=w.size * 2 + t * d * 16,
            transcendentals=t * length * 6,
        ),
    )(counts, x, gain, gy, qkv, w)


def feed_fwd_kernel(y_ref, g_in_ref, g_out_ref, w_ref, n_ref, gu_ref, y2_ref, f_ref):
    i = pl.program_id(0)
    f = w_ref.shape[1] // 3

    @pl.when(i == 0)
    def _():
        y = y_ref[...]
        n_ref[...] = (unit_rows(y)[1] * g_in_ref[...]).astype(bf16)
        y2_ref[...] = y

    gu = dot_last(n_ref[...], w_ref[0, : 2 * f, :])
    gu_ref[0] = gu
    hidden = (gelu_parts(gu[:, :f])[0] * gu[:, f:]).astype(bf16)
    y2_ref[...] += dot(hidden, w_ref[0, 2 * f :, :])

    @pl.when(i == pl.num_programs(0) - 1)
    def _():
        f_ref[...] = (unit_rows(y2_ref[...])[1] * g_out_ref[...]).astype(bf16)


def feed_fwd(y, gain_in, gain_out, w):
    t, d = y.shape
    nb, rows, _ = w.shape
    f = rows // 3
    whole = lambda *shape: pl.BlockSpec(shape, lambda i: (0,) * len(shape))
    part = lambda *shape: pl.BlockSpec((1,) + shape, lambda i: (i, 0, 0))
    return pl.pallas_call(
        feed_fwd_kernel,
        grid=(nb,),
        out_shape=(
            jax.ShapeDtypeStruct((t, d), bf16),
            jax.ShapeDtypeStruct((nb, t, 2 * f), f32),
            jax.ShapeDtypeStruct((t, d), f32),
            jax.ShapeDtypeStruct((t, d), bf16),
        ),
        in_specs=[whole(t, d), whole(1, d), whole(1, d), part(rows, d)],
        out_specs=(whole(t, d), part(t, 2 * f), whole(t, d), whole(t, d)),
        compiler_params=pltpu.CompilerParams(vmem_limit_bytes=VMEM_BYTES),
        cost_estimate=pl.CostEstimate(
            flops=2 * t * d * rows * nb,
            bytes_accessed=w.size * 2 + t * d * 12 + nb * t * f * 8,
            transcendentals=nb * t * f,
        ),
    )(y, gain_in, gain_out, w)


def feed_bwd_kernel(emit, up_ref, y_ref, y2_ref, g_in_ref, g_out_ref, gu_ref, w_ref, *refs):
    if emit:
        gf_ref, gy_ref, gg_ref, dgu_ref, hid_ref, last_ref = refs
    else:
        gf_ref, gy_ref, gg_ref, last_ref = refs
    i = pl.program_id(0)
    f = w_ref.shape[1] // 3

    @pl.when(i == 0)
    def _():
        back, gain_grad = norm_back(y2_ref[...], g_out_ref[...], up_ref[...].astype(f32))
        gg_ref[1:2, :] = gain_grad
        last_ref[...] = back
        gf_ref[...] = back.astype(bf16)
        gy_ref[...] = jnp.zeros_like(gy_ref)

    gh = dot_last(gf_ref[...], w_ref[0, 2 * f :, :])
    act, slope = gelu_parts(gu_ref[0, :, :f])
    u = gu_ref[0, :, f:]
    dg = (gh * u * slope).astype(bf16)
    du = (gh * act).astype(bf16)
    if emit:
        dgu_ref[0, :, :f] = dg
        dgu_ref[0, :, f:] = du
        hid_ref[0] = (act * u).astype(bf16)
    gy_ref[...] += dot(dg, w_ref[0, :f, :]) + dot(du, w_ref[0, f : 2 * f, :])

    @pl.when(i == pl.num_programs(0) - 1)
    def _():
        back, gain_grad = norm_back(y_ref[...], g_in_ref[...], gy_ref[...])
        gg_ref[0:1, :] = gain_grad
        gy_ref[...] = last_ref[...] + back


def feed_bwd(up, y, y2, gain_in, gain_out, gu, w, emit):
    t, d = y.shape
    nb, rows, _ = w.shape
    f = rows // 3
    whole = lambda *shape: pl.BlockSpec(shape, lambda i: (0,) * len(shape))
    part = lambda *shape: pl.BlockSpec((1,) + shape, lambda i: (i, 0, 0))
    outs = [
        jax.ShapeDtypeStruct((t, d), bf16),
        jax.ShapeDtypeStruct((t, d), f32),
        jax.ShapeDtypeStruct((2, d), f32),
    ]
    specs = [whole(t, d), whole(t, d), whole(2, d)]
    if emit:
        outs += [
            jax.ShapeDtypeStruct((nb, t, 2 * f), bf16),
            jax.ShapeDtypeStruct((nb, t, f), bf16),
        ]
        specs += [part(t, 2 * f), part(t, f)]
    return pl.pallas_call(
        functools.partial(feed_bwd_kernel, emit),
        grid=(nb,),
        out_shape=tuple(outs),
        in_specs=[whole(t, d)] * 3 + [whole(1, d)] * 2 + [part(t, 2 * f), part(rows, d)],
        out_specs=tuple(specs),
        scratch_shapes=[pltpu.VMEM((t, d), f32)],
        compiler_params=pltpu.CompilerParams(vmem_limit_bytes=VMEM_BYTES),
        cost_estimate=pl.CostEstimate(
            flops=2 * t * d * rows * nb,
            bytes_accessed=w.size * 2 + t * d * 18 + nb * t * f * 8,
            transcendentals=nb * t * f,
        ),
    )(up, y, y2, gain_in, gain_out, gu, w)


def head_kernel(length, cnt_ref, f_ref, w_ref, target_ref, gl_ref, up_ref, loss_ref):
    logits = dot_last(f_ref[...], w_ref[...])
    top = jnp.max(logits, axis=-1, keepdims=True)
    log_total = top + jnp.log(jnp.sum(jnp.exp(logits - top), axis=-1, keepdims=True))
    hit = lax.broadcasted_iota(jnp.int32, logits.shape, 1) == target_ref[...]
    picked = jnp.sum(jnp.where(hit, logits, 0.0), axis=-1, keepdims=True)
    probs = jnp.exp(logits - log_total) - jnp.where(hit, 1.0, 0.0)
    total = jnp.zeros((1, 1), f32)
    for s in range(logits.shape[0] // length):
        rows = slice(s * length, (s + 1) * length)
        count = cnt_ref[s]
        valid = lax.broadcasted_iota(jnp.int32, (length, 1), 0) < count
        total += jnp.sum(
            jnp.where(valid, log_total[rows] - picked[rows], 0.0), axis=0, keepdims=True
        )
        gl_ref[rows, :] = jnp.where(valid, probs[rows], 0.0).astype(bf16)
    loss_ref[...] = total
    up_ref[...] = dot(gl_ref[...], w_ref[...])


def head_loss(counts, final, w, target, length):
    t, d = final.shape
    v = w.shape[0]
    vm = pl.BlockSpec(memory_space=pltpu.VMEM)
    return pl.pallas_call(
        functools.partial(head_kernel, length),
        out_shape=(
            jax.ShapeDtypeStruct((t, v), bf16),
            jax.ShapeDtypeStruct((t, d), f32),
            jax.ShapeDtypeStruct((1, 1), f32),
        ),
        in_specs=[pl.BlockSpec(memory_space=pltpu.SMEM), vm, vm, vm],
        out_specs=(vm,) * 3,
        compiler_params=pltpu.CompilerParams(vmem_limit_bytes=VMEM_BYTES),
        cost_estimate=pl.CostEstimate(
            flops=4 * t * d * v, bytes_accessed=w.size * 2 + t * d * 6, transcendentals=t * v * 2
        ),
    )(counts, final, w, target)


def adam_step(weight, first_moment, second_moment, gradient, step_rate, weight_decay):
    first_new = 0.9 * first_moment + 0.1 * gradient
    second_new = 0.999 * second_moment + 0.001 * gradient * gradient
    first_fix = 1.0 - 0.9**STEP
    second_fix = 1.0 - 0.999**STEP
    update = first_new / first_fix / (jnp.sqrt(second_new / second_fix) + 1e-08)
    return (first_new, second_new, weight - step_rate * (update + weight_decay * weight))


def kinds_first(gathered, n, kinds, per):
    d = gathered.shape[-1]
    return gathered.reshape(n, kinds, per, d).transpose(1, 0, 2, 3).reshape(kinds * n * per, d)


def owners_first(left, right, n):
    t, k, units = left.shape
    grad = jnp.einsum("tku,td->kud", left, right, preferred_element_type=f32)
    return grad.reshape(k, n, units // n, -1).transpose(1, 0, 2, 3)


def own_feed_grads(n_all, gf_all, w_own):
    f = w_own.shape[1]
    gate, up = dot_last(n_all, w_own[0]), dot_last(n_all, w_own[1])
    gh = dot_last(gf_all, w_own[2])
    act, slope = gelu_parts(gate)
    dg = (gh * up * slope).astype(bf16)
    du = (gh * act).astype(bf16)
    hid = (act * up).astype(bf16)
    return jnp.stack([dot_rows(dg, n_all), dot_rows(du, n_all), dot_rows(hid, gf_all)])


def local(
    block_input,
    lengths,
    targets,
    attention_weight,
    attention_first,
    attention_second,
    feed_weight,
    feed_first,
    feed_second,
    norm_gain,
    gain_first,
    gain_second,
    cross_weight,
    cross_first,
    cross_second,
    head_weight,
    head_first,
    head_second,
    cross_gain,
    cross_gain_first,
    cross_gain_second,
):
    n = lax.axis_size("rows")
    is_encoder = lax.axis_index("section") == 0
    micro, length, d = block_input.shape[1:]
    t = micro * length
    per = attention_weight.shape[1]
    f = feed_weight.shape[1]
    inner = per * n

    attn_own = attention_weight[0].astype(bf16).transpose(1, 0, 2).reshape(4 * per, d)
    feed_own = feed_weight[0].astype(bf16).transpose(1, 0, 2)
    half_rows = jnp.concatenate(
        [cross_weight.astype(bf16).transpose(1, 0, 2), head_weight.astype(bf16)[None]], axis=0
    )
    other_half = lax.ppermute(half_rows, "section", [(0, 1)])
    extra_own = jnp.concatenate([other_half, half_rows], axis=-1).reshape(5 * per, d)

    attn_all = lax.all_gather(attn_own, "rows", axis=0, tiled=True)
    attn_w = kinds_first(attn_all, n, 4, per)
    feed_all = lax.all_gather(feed_own.reshape(3 * f, d), "rows", axis=0, tiled=True)
    feed_w = feed_all.reshape(n, 3 * f, d)
    if n != BLOCKS:
        feed_w = kinds_first(feed_all, n, 3, f).reshape(3, BLOCKS, -1, d)
        feed_w = feed_w.transpose(1, 0, 2, 3).reshape(BLOCKS, -1, d)
    extra_all = lax.all_gather(extra_own, "rows", axis=0, tiled=True)
    extra_w = kinds_first(extra_all, n, 5, per)
    cross_w, head_w = extra_w[: 4 * inner], extra_w[4 * inner :]

    gains = norm_gain[0]
    gain_attn, gain_feed, gain_final = gains[0:1], gains[1:2], gains[2:3]
    gain_cross = cross_gain[None]
    x = block_input[0].reshape(t, d)
    enc_counts = lengths[0, :, 0]
    dec_counts = lengths[1, :, 0]
    zero_one = jnp.zeros((1,), jnp.int32)
    self_counts = jnp.concatenate([jnp.where(is_encoder, 0, 1).astype(jnp.int32)[None], enc_counts])
    cross_counts = jnp.concatenate([zero_one, enc_counts])
    target_column = targets.reshape(t, 1)

    n1, qkv, mixed, y1 = attend_fwd(self_counts, x, gain_attn, attn_w, length)

    def enc_feed():
        return feed_fwd(y1, gain_feed, gain_final, feed_w)

    def blank(maker):
        return jax.tree.map(lambda a: jnp.zeros(a.shape, a.dtype), jax.eval_shape(maker))

    enc_state = lax.cond(is_encoder, enc_feed, lambda: blank(enc_feed))
    encoded = lax.ppermute(enc_state[3], "section", [(0, 1)])

    def dec_front():
        mc, cqkv, cmixed, z2 = attend_fwd(cross_counts, y1, gain_cross, cross_w, length, encoded)
        return feed_fwd(z2, gain_feed, gain_final, feed_w) + (mc, cqkv, cmixed, z2)

    def enc_pass():
        rest = jax.eval_shape(dec_front)[4:7]
        return tuple(enc_state) + tuple(jnp.zeros(a.shape, a.dtype) for a in rest) + (y1,)

    n2, gu, y2, final, mc, cqkv, cmixed, mid = lax.cond(is_encoder, enc_pass, dec_front)
    emit = n != BLOCKS
    if not emit:
        n2_all = lax.all_gather(n2, "rows", axis=0, tiled=True)

    def dec_back():
        gl, up, loss = head_loss(dec_counts, final, head_w, target_column, length)
        feed_out = feed_bwd(up, mid, y2, gain_feed, gain_final, gu, feed_w, emit)
        ga_c, dqkv_c, gy1, gg_c, ge = attend_bwd(
            cross_counts, y1, gain_cross, feed_out[1], cqkv, cross_w, length, True
        )
        return (ge, gy1, feed_out[2], feed_out[0], *feed_out[3:], gl, ga_c, dqkv_c, gg_c, loss)

    back = lax.cond(is_encoder, lambda: blank(dec_back), dec_back)
    returned = lax.ppermute(back[0], "section", [(1, 0)])
    at = 6 if emit else 4
    gl, ga_c, dqkv_c, gg_c, loss = back[at:]

    def enc_back():
        feed_out = feed_bwd(returned, mid, y2, gain_feed, gain_final, gu, feed_w, emit)
        return (feed_out[1], feed_out[2], feed_out[0], *feed_out[3:])

    backs = lax.cond(is_encoder, enc_back, lambda: tuple(back[1:at]))
    gy1, gg_feed, gf = backs[:3]
    if not emit:
        gf_all = lax.all_gather(gf, "rows", axis=0, tiled=True)

    ga, dqkv, gx, gg_attn = attend_bwd(self_counts, x, gain_attn, gy1, qkv, attn_w, length)

    extra_part = jnp.concatenate(
        [
            owners_first(dqkv_c[:, None, :inner], mc, n),
            owners_first(dqkv_c[:, inner:].reshape(t, 2, inner), encoded, n),
            owners_first(cmixed[:, None], ga_c, n),
            owners_first(gl[:, None], final, n),
        ],
        axis=1,
    ).astype(bf16)
    extra_sum = lax.psum_scatter(
        extra_part.reshape(n * 5 * per, d), "rows", scatter_dimension=0, tiled=True
    )
    half = d // 2
    extra_first = lax.ppermute(extra_sum[:, :half], "section", [(1, 0)])
    extra_grad = jnp.where(is_encoder, extra_first, extra_sum[:, half:]).astype(f32)
    extra_grad = extra_grad.reshape(5, per, half)

    attn_part = jnp.concatenate(
        [
            owners_first(dqkv.reshape(t, 3, inner), n1, n),
            owners_first(mixed[:, None], ga, n),
        ],
        axis=1,
    ).astype(bf16)
    attn_sum = lax.psum_scatter(
        attn_part.reshape(n * 4 * per, d), "rows", scatter_dimension=0, tiled=True
    )
    attn_grad = attn_sum.astype(f32).reshape(4, per, d).transpose(1, 0, 2)

    if emit:
        dgu, hid = backs[3], backs[4]
        nb, _, fb = hid.shape
        left = dgu.reshape(nb, t, 2, fb).transpose(1, 2, 0, 3).reshape(t, 2, nb * fb)
        hid = hid.transpose(1, 0, 2).reshape(t, 1, nb * fb)
        feed_part = jnp.concatenate(
            [owners_first(left, n2, n), owners_first(hid, gf, n)], axis=1
        ).astype(bf16)
        feed_grad = lax.psum_scatter(
            feed_part.reshape(n * 3 * f, d), "rows", scatter_dimension=0, tiled=True
        )
        feed_grad = feed_grad.astype(f32).reshape(3, f, d)
    else:
        feed_grad = own_feed_grads(n2_all, gf_all, feed_own)
    feed_grad = feed_grad.transpose(1, 0, 2)

    tiny = jnp.concatenate(
        [
            gg_attn,
            gg_feed,
            gg_c,
            jnp.broadcast_to(loss, (1, d)),
            jnp.zeros((3, d), f32),
        ],
        axis=0,
    )
    tiny_sum = jnp.sum(lax.all_gather(tiny, "rows", axis=0), axis=0)
    tiny_dec = lax.ppermute(tiny_sum[3:5], "section", [(1, 0)])
    tiny_dec = jnp.where(is_encoder, tiny_dec, tiny_sum[3:5])
    cross_gain_total = tiny_dec[0]
    loss_total = tiny_dec[1, 0]

    attention_new = adam_step(
        attention_weight, attention_first, attention_second, attn_grad[None], 0.05, 0.1
    )
    feed_new = adam_step(feed_weight, feed_first, feed_second, feed_grad[None], 0.05, 0.1)
    gain_new = adam_step(norm_gain, gain_first, gain_second, tiny_sum[None, 0:3], 0.5, 0.0)
    cross_new = adam_step(
        cross_weight, cross_first, cross_second, extra_grad[:4].transpose(1, 0, 2), 0.05, 0.1
    )
    head_new = adam_step(head_weight, head_first, head_second, extra_grad[4], 0.05, 0.1)
    cross_gain_new = adam_step(
        cross_gain, cross_gain_first, cross_gain_second, cross_gain_total, 0.5, 0.0
    )
    return (
        gx.reshape(1, micro, length, d),
        loss_total,
        *attention_new,
        *feed_new,
        *gain_new,
        *cross_new,
        *head_new,
        *cross_gain_new,
    )


def solution(mesh):
    by_row = P("section", "rows", None, None)
    gain = P("section", None, None)
    cross = P("rows", None, "section")
    head = P("rows", "section")
    weights = (by_row,) * 6 + (gain,) * 3 + (cross,) * 3 + (head,) * 3 + (P(),) * 3
    tokens = P("section", None, "rows", None)
    return jax.shard_map(
        local,
        mesh=mesh,
        in_specs=(tokens, P(None, None, "rows"), P(None, "rows")) + weights,
        out_specs=(tokens, P()) + weights,
        check_vma=False,
    )
```

```python
import functools

import jax
import jax.numpy as jnp
from jax import lax
from jax.experimental import pallas as pl
from jax.experimental.pallas import tpu as pltpu
from jax.sharding import PartitionSpec as P

HD = 64
STEP = 10
PAIR = 2 * HD
BLOCKS = 16
VMEM_BYTES = 52 * 1024 * 1024

bf16 = jnp.bfloat16
f32 = jnp.float32
masked_value = -1000000000.0
scale = HD ** (-0.5)


def dot(a, b):
    return lax.dot_general(a, b, (((1,), (0,)), ((), ())), preferred_element_type=f32)


def dot_last(a, b):
    return lax.dot_general(a, b, (((1,), (1,)), ((), ())), preferred_element_type=f32)


def dot_rows(a, b):
    return lax.dot_general(a, b, (((0,), (0,)), ((), ())), preferred_element_type=f32)


def unit_rows(v):
    r = lax.rsqrt(jnp.mean(v * v, axis=-1, keepdims=True) + 1e-06)
    return r, v * r


def norm_back(v, gain, up):
    r, n = unit_rows(v)
    g = up * gain
    back = r * (g - n * jnp.mean(g * n, axis=-1, keepdims=True))
    return back, jnp.sum(up * n, axis=0, keepdims=True)


def gelu_parts(x):
    c = 0.7978845608028654
    t = jnp.tanh(c * (x + 0.044715 * (x * x * x)))
    act = 0.5 * x * (1.0 + t)
    slope = 0.5 * (1.0 + t) + 0.5 * x * (1.0 - t * t) * (c * (1.0 + 3.0 * 0.044715 * (x * x)))
    return act, slope


def low_half(length):
    return lax.broadcasted_iota(jnp.int32, (length, PAIR), 1) < HD


def stack_pair(m, low):
    zero = jnp.zeros_like(m)
    return jnp.concatenate([jnp.where(low, m, zero), jnp.where(low, zero, m)], axis=0)


def allowed_twice(cnt_ref, s, length):
    row = lax.broadcasted_iota(jnp.int32, (length, length), 0)
    col = lax.broadcasted_iota(jnp.int32, (length, length), 1)
    limit = jnp.where(cnt_ref[0] == 1, row + 1, cnt_ref[1 + s])
    one = jnp.where(col < limit, 1, 0)
    return jnp.concatenate([one, one], axis=0) == 1


def soft_pair(q2, k, allowed):
    s = dot_last(q2, k) * scale
    s = jnp.where(allowed, s, masked_value)
    e = jnp.exp(s - jnp.max(s, axis=-1, keepdims=True))
    return e / jnp.sum(e, axis=-1, keepdims=True)


def attend_fwd_kernel(cross, length, cnt_ref, x_ref, gain_ref, *refs):
    if cross:
        src_ref, w_ref, n_ref, qkv_ref, o_ref, y_ref = refs
    else:
        w_ref, n_ref, qkv_ref, o_ref, y_ref = refs
    inner = w_ref.shape[0] // 4
    x = x_ref[...].astype(f32)
    n = (unit_rows(x)[1] * gain_ref[...]).astype(bf16)
    n_ref[...] = n
    if cross:
        qkv_ref[:, :inner] = dot_last(n, w_ref[:inner, :]).astype(bf16)
        qkv_ref[:, inner:] = dot_last(src_ref[...], w_ref[inner : 3 * inner, :]).astype(bf16)
    else:
        qkv_ref[...] = dot_last(n, w_ref[: 3 * inner, :]).astype(bf16)
    low = low_half(length)
    for s in range(x.shape[0] // length):
        allowed = allowed_twice(cnt_ref, s, length)
        rows = slice(s * length, (s + 1) * length)
        for h in range(inner // PAIR):
            cols = [slice(j * inner + h * PAIR, j * inner + (h + 1) * PAIR) for j in range(3)]
            q2 = stack_pair(qkv_ref[rows, cols[0]], low)
            p = soft_pair(q2, qkv_ref[rows, cols[1]], allowed).astype(bf16)
            wide = jnp.concatenate([p[:length], p[length:]], axis=1)
            o_ref[rows, cols[0]] = dot(wide, stack_pair(qkv_ref[rows, cols[2]], low)).astype(bf16)
    y_ref[...] = x + dot(o_ref[...], w_ref[3 * inner :, :])


def attend_fwd(counts, x, gain, w, length, source=None):
    t, d = x.shape
    inner = w.shape[0] // 4
    ins = [counts, x, gain] + ([] if source is None else [source]) + [w]
    vm = pl.BlockSpec(memory_space=pltpu.VMEM)
    return pl.pallas_call(
        functools.partial(attend_fwd_kernel, source is not None, length),
        out_shape=(
            jax.ShapeDtypeStruct((t, d), bf16),
            jax.ShapeDtypeStruct((t, 3 * inner), bf16),
            jax.ShapeDtypeStruct((t, inner), bf16),
            jax.ShapeDtypeStruct((t, d), f32),
        ),
        in_specs=[pl.BlockSpec(memory_space=pltpu.SMEM)] + [vm] * (len(ins) - 1),
        out_specs=(vm,) * 4,
        compiler_params=pltpu.CompilerParams(vmem_limit_bytes=VMEM_BYTES),
        cost_estimate=pl.CostEstimate(
            flops=2 * t * d * inner * 4 + 8 * t * length * inner,
            bytes_accessed=w.size * 2 + t * d * 10,
            transcendentals=t * length * 6,
        ),
    )(*ins)


def attend_bwd_kernel(cross, length, cnt_ref, x_ref, gain_ref, gy_ref, qkv_ref, w_ref, *refs):
    if cross:
        ga_ref, dqkv_ref, gx_ref, gg_ref, gs_ref, do_ref = refs
    else:
        ga_ref, dqkv_ref, gx_ref, gg_ref, do_ref = refs
    inner = w_ref.shape[0] // 4
    ga = gy_ref[...].astype(bf16)
    ga_ref[...] = ga
    do_ref[...] = dot_last(ga, w_ref[3 * inner :, :]).astype(bf16)
    low = low_half(length)
    for s in range(ga.shape[0] // length):
        allowed = allowed_twice(cnt_ref, s, length)
        rows = slice(s * length, (s + 1) * length)
        for h in range(inner // PAIR):
            cols = [slice(j * inner + h * PAIR, j * inner + (h + 1) * PAIR) for j in range(3)]
            q2 = stack_pair(qkv_ref[rows, cols[0]], low)
            k = qkv_ref[rows, cols[1]]
            p = soft_pair(q2, k, allowed)
            do2 = stack_pair(do_ref[rows, cols[0]], low)
            dp = dot_last(do2, qkv_ref[rows, cols[2]])
            ds = p * (dp - jnp.sum(dp * p, axis=-1, keepdims=True))
            ds = jnp.where(allowed, ds, 0.0).astype(bf16)
            wide = jnp.concatenate([ds[:length], ds[length:]], axis=1)
            dqkv_ref[rows, cols[0]] = (dot(wide, stack_pair(k, low)) * scale).astype(bf16)
            dqkv_ref[rows, cols[1]] = (dot_rows(ds, q2) * scale).astype(bf16)
            dqkv_ref[rows, cols[2]] = dot_rows(p.astype(bf16), do2).astype(bf16)
    if cross:
        up = dot(dqkv_ref[:, :inner], w_ref[:inner, :])
        gs_ref[...] = dot(dqkv_ref[:, inner:], w_ref[inner : 3 * inner, :]).astype(bf16)
    else:
        up = dot(dqkv_ref[...], w_ref[: 3 * inner, :])
    back, gg_ref[...] = norm_back(x_ref[...].astype(f32), gain_ref[...], up)
    gx_ref[...] = gy_ref[...] + back


def attend_bwd(counts, x, gain, gy, qkv, w, length, cross=False):
    t, d = x.shape
    inner = w.shape[0] // 4
    vm = pl.BlockSpec(memory_space=pltpu.VMEM)
    outs = [
        jax.ShapeDtypeStruct((t, d), bf16),
        jax.ShapeDtypeStruct((t, 3 * inner), bf16),
        jax.ShapeDtypeStruct((t, d), f32),
        jax.ShapeDtypeStruct((1, d), f32),
    ]
    if cross:
        outs.append(jax.ShapeDtypeStruct((t, d), bf16))
    return pl.pallas_call(
        functools.partial(attend_bwd_kernel, cross, length),
        out_shape=tuple(outs),
        in_specs=[pl.BlockSpec(memory_space=pltpu.SMEM)] + [vm] * 5,
        out_specs=(vm,) * len(outs),
        scratch_shapes=[pltpu.VMEM((t, inner), bf16)],
        compiler_params=pltpu.CompilerParams(vmem_limit_bytes=VMEM_BYTES),
        cost_estimate=pl.CostEstimate(
            flops=2 * t * d * inner * 4 + 20 * t * length * inner,
            bytes_accessed=w.size * 2 + t * d * 16,
            transcendentals=t * length * 6,
        ),
    )(counts, x, gain, gy, qkv, w)


def feed_fwd_kernel(y_ref, g_in_ref, g_out_ref, w_ref, n_ref, gu_ref, y2_ref, f_ref):
    i = pl.program_id(0)
    f = w_ref.shape[1] // 3

    @pl.when(i == 0)
    def _():
        y = y_ref[...]
        n_ref[...] = (unit_rows(y)[1] * g_in_ref[...]).astype(bf16)
        y2_ref[...] = y

    gu = dot_last(n_ref[...], w_ref[0, : 2 * f, :])
    gu_ref[0] = gu
    hidden = (gelu_parts(gu[:, :f])[0] * gu[:, f:]).astype(bf16)
    y2_ref[...] += dot(hidden, w_ref[0, 2 * f :, :])

    @pl.when(i == pl.num_programs(0) - 1)
    def _():
        f_ref[...] = (unit_rows(y2_ref[...])[1] * g_out_ref[...]).astype(bf16)


def feed_fwd(y, gain_in, gain_out, w):
    t, d = y.shape
    nb, rows, _ = w.shape
    f = rows // 3
    whole = lambda *shape: pl.BlockSpec(shape, lambda i: (0,) * len(shape))
    part = lambda *shape: pl.BlockSpec((1,) + shape, lambda i: (i, 0, 0))
    return pl.pallas_call(
        feed_fwd_kernel,
        grid=(nb,),
        out_shape=(
            jax.ShapeDtypeStruct((t, d), bf16),
            jax.ShapeDtypeStruct((nb, t, 2 * f), f32),
            jax.ShapeDtypeStruct((t, d), f32),
            jax.ShapeDtypeStruct((t, d), bf16),
        ),
        in_specs=[whole(t, d), whole(1, d), whole(1, d), part(rows, d)],
        out_specs=(whole(t, d), part(t, 2 * f), whole(t, d), whole(t, d)),
        compiler_params=pltpu.CompilerParams(vmem_limit_bytes=VMEM_BYTES),
        cost_estimate=pl.CostEstimate(
            flops=2 * t * d * rows * nb,
            bytes_accessed=w.size * 2 + t * d * 12 + nb * t * f * 8,
            transcendentals=nb * t * f,
        ),
    )(y, gain_in, gain_out, w)


def feed_bwd_kernel(emit, up_ref, y_ref, y2_ref, g_in_ref, g_out_ref, gu_ref, w_ref, *refs):
    if emit:
        gf_ref, gy_ref, gg_ref, dgu_ref, hid_ref, last_ref = refs
    else:
        gf_ref, gy_ref, gg_ref, last_ref = refs
    i = pl.program_id(0)
    f = w_ref.shape[1] // 3

    @pl.when(i == 0)
    def _():
        back, gain_grad = norm_back(y2_ref[...], g_out_ref[...], up_ref[...].astype(f32))
        gg_ref[1:2, :] = gain_grad
        last_ref[...] = back
        gf_ref[...] = back.astype(bf16)
        gy_ref[...] = jnp.zeros_like(gy_ref)

    gh = dot_last(gf_ref[...], w_ref[0, 2 * f :, :])
    act, slope = gelu_parts(gu_ref[0, :, :f])
    u = gu_ref[0, :, f:]
    dg = (gh * u * slope).astype(bf16)
    du = (gh * act).astype(bf16)
    if emit:
        dgu_ref[0, :, :f] = dg
        dgu_ref[0, :, f:] = du
        hid_ref[0] = (act * u).astype(bf16)
    gy_ref[...] += dot(dg, w_ref[0, :f, :]) + dot(du, w_ref[0, f : 2 * f, :])

    @pl.when(i == pl.num_programs(0) - 1)
    def _():
        back, gain_grad = norm_back(y_ref[...], g_in_ref[...], gy_ref[...])
        gg_ref[0:1, :] = gain_grad
        gy_ref[...] = last_ref[...] + back


def feed_bwd(up, y, y2, gain_in, gain_out, gu, w, emit):
    t, d = y.shape
    nb, rows, _ = w.shape
    f = rows // 3
    whole = lambda *shape: pl.BlockSpec(shape, lambda i: (0,) * len(shape))
    part = lambda *shape: pl.BlockSpec((1,) + shape, lambda i: (i, 0, 0))
    outs = [
        jax.ShapeDtypeStruct((t, d), bf16),
        jax.ShapeDtypeStruct((t, d), f32),
        jax.ShapeDtypeStruct((2, d), f32),
    ]
    specs = [whole(t, d), whole(t, d), whole(2, d)]
    if emit:
        outs += [
            jax.ShapeDtypeStruct((nb, t, 2 * f), bf16),
            jax.ShapeDtypeStruct((nb, t, f), bf16),
        ]
        specs += [part(t, 2 * f), part(t, f)]
    return pl.pallas_call(
        functools.partial(feed_bwd_kernel, emit),
        grid=(nb,),
        out_shape=tuple(outs),
        in_specs=[whole(t, d)] * 3 + [whole(1, d)] * 2 + [part(t, 2 * f), part(rows, d)],
        out_specs=tuple(specs),
        scratch_shapes=[pltpu.VMEM((t, d), f32)],
        compiler_params=pltpu.CompilerParams(vmem_limit_bytes=VMEM_BYTES),
        cost_estimate=pl.CostEstimate(
            flops=2 * t * d * rows * nb,
            bytes_accessed=w.size * 2 + t * d * 18 + nb * t * f * 8,
            transcendentals=nb * t * f,
        ),
    )(up, y, y2, gain_in, gain_out, gu, w)


def head_kernel(length, cnt_ref, f_ref, w_ref, target_ref, gl_ref, up_ref, loss_ref):
    logits = dot_last(f_ref[...], w_ref[...])
    top = jnp.max(logits, axis=-1, keepdims=True)
    log_total = top + jnp.log(jnp.sum(jnp.exp(logits - top), axis=-1, keepdims=True))
    hit = lax.broadcasted_iota(jnp.int32, logits.shape, 1) == target_ref[...]
    picked = jnp.sum(jnp.where(hit, logits, 0.0), axis=-1, keepdims=True)
    probs = jnp.exp(logits - log_total) - jnp.where(hit, 1.0, 0.0)
    total = jnp.zeros((1, 1), f32)
    for s in range(logits.shape[0] // length):
        rows = slice(s * length, (s + 1) * length)
        count = cnt_ref[s]
        valid = lax.broadcasted_iota(jnp.int32, (length, 1), 0) < count
        total += jnp.sum(
            jnp.where(valid, log_total[rows] - picked[rows], 0.0), axis=0, keepdims=True
        )
        gl_ref[rows, :] = jnp.where(valid, probs[rows], 0.0).astype(bf16)
    loss_ref[...] = total
    up_ref[...] = dot(gl_ref[...], w_ref[...])


def head_loss(counts, final, w, target, length):
    t, d = final.shape
    v = w.shape[0]
    vm = pl.BlockSpec(memory_space=pltpu.VMEM)
    return pl.pallas_call(
        functools.partial(head_kernel, length),
        out_shape=(
            jax.ShapeDtypeStruct((t, v), bf16),
            jax.ShapeDtypeStruct((t, d), f32),
            jax.ShapeDtypeStruct((1, 1), f32),
        ),
        in_specs=[pl.BlockSpec(memory_space=pltpu.SMEM), vm, vm, vm],
        out_specs=(vm,) * 3,
        compiler_params=pltpu.CompilerParams(vmem_limit_bytes=VMEM_BYTES),
        cost_estimate=pl.CostEstimate(
            flops=4 * t * d * v, bytes_accessed=w.size * 2 + t * d * 6, transcendentals=t * v * 2
        ),
    )(counts, final, w, target)


def tail_kernel(
    tiny_ref, gf_ref, lefts_ref, n1_ref, ga_ref, w_ref, n_all_ref,
    feed_ref, attn_ref, total_ref,
    shards, n_buf, part, from_core, four, from_y, from_far, from_near, from_cross, from_out, cross_out,
    ag_send, ag_recv, rs_send, rs_recv, n_sem,
):
    me = lax.axis_index("rows")
    z, y, c = me // 4, (me // 2) % 2, me % 2
    high = z // 2
    inner = (z + high) % 2
    t = gf_ref.shape[0]
    f = w_ref.shape[0] // 3
    core_peer, y_peer = me + 1 - 2 * c, me + 2 - 4 * y
    toward = me + 4 - 8 * high
    across = me + 4 - 8 * high
    outward = me - 4 + 8 * high

    def remote(src, dst, send, recv, device):
        return pltpu.make_async_remote_copy(
            src_ref=src, dst_ref=dst, send_sem=send, recv_sem=recv,
            device_id={"rows": device}, device_id_type=pl.DeviceIdType.MESH,
        )

    barrier = pltpu.get_barrier_semaphore()

    def greet(device):
        pl.semaphore_signal(
            barrier, inc=1, device_id={"rows": device}, device_id_type=pl.DeviceIdType.MESH
        )

    greet(core_peer)
    greet(y_peer)
    greet(toward)

    @pl.when(inner == 1)
    def _():
        greet(outward)

    pl.semaphore_wait(barrier, 3 + inner)

    def piece(p):
        odd = p % 2
        j = jnp.where(p == 0, 0, jnp.where(p == 7, 3, jnp.where(odd == 1, (p + 1) // 2, p // 2 - 1)))
        other = jnp.where(p == 0, 0, jnp.where(p == 7, 1, 1 - odd))
        first, second, third = z + 1 - 2 * (z % 2), 2 - high, 3 - 3 * high
        zz = jnp.where(j == 0, z, jnp.where(j == 1, first, jnp.where(j == 2, second, third)))
        yy = y + other - 2 * other * y
        return zz, yy, other

    def shard_copy(kind, p, s, device):
        return remote(shards.at[s], shards.at[s], ag_send.at[kind, p], ag_recv.at[s], device)

    def each_send(p, zz, yy, other, act):
        s = 4 * zz + 2 * yy + c

        @pl.when((other == 0) & (zz <= z) & (z < 3))
        def _():
            act(shard_copy(0, p, s, me + 4))

        @pl.when((other == 0) & (zz >= z) & (z > 0))
        def _():
            act(shard_copy(1, p, s, me - 4))

        @pl.when(other == 0)
        def _():
            act(shard_copy(2, p, s, y_peer))

        act(shard_copy(3, p, s, core_peer))

    def n_copy(p):
        zz, yy, _ = piece(p)
        rows = pl.ds((2 * zz + yy) * (2 * t), 2 * t)
        slot = p % 2
        return pltpu.make_async_copy(n_all_ref.at[rows], n_buf.at[slot], n_sem.at[slot])

    n_copy(0).start()
    shards[me, :t, :] = gf_ref[...]
    tiny = tiny_ref[...]
    tiny_high = tiny.astype(bf16)
    tiny_low = (tiny - tiny_high.astype(f32)).astype(bf16)
    shards[me, t:, :] = jnp.concatenate([tiny_high, tiny_low], axis=0)
    each_send(0, z, y, 0, lambda copy: copy.start())

    blocks, per = part.shape[1:3]
    row = lax.broadcasted_iota(jnp.int32, (blocks * per, n1_ref.shape[1]), 0)
    from_mixed = row % per >= per // 4 * 3

    def half_sums(half):
        left = lefts_ref[half]
        both = jnp.where(from_mixed, dot(left, ga_ref[...]), dot(left, n1_ref[...]))
        return both.reshape(blocks, per, -1)

    part[0] = half_sums(1 - c).astype(bf16)
    to_core = remote(part.at[0], from_core, rs_send.at[0], rs_recv.at[0], core_peer)
    to_core.start()
    own_half = half_sums(c)
    to_core.wait_recv()
    part[1] = (own_half + from_core[...].astype(f32)).astype(bf16)
    quarter = blocks // 2
    to_y = remote(
        part.at[1, pl.ds((1 - y) * quarter, quarter)], from_y, rs_send.at[1], rs_recv.at[1], y_peer
    )
    to_y.start()

    far = 2 - 2 * high
    far_copy = remote(four.at[pl.ds(far, 2)], from_far, rs_send.at[2], rs_recv.at[2], toward)
    near_copy = remote(four.at[1 + high], from_near, rs_send.at[3], rs_recv.at[3], toward)
    cross_copy = remote(four.at[pl.ds(far, 2)], from_cross, rs_send.at[4], rs_recv.at[4], across)
    out_copy = remote(cross_out, from_out, rs_send.at[5], rs_recv.at[5], outward)

    def stage_y():
        to_y.wait_recv()
        mine = part[1, pl.ds(y * quarter, quarter)].astype(f32)
        four[...] = (mine + from_y[...].astype(f32)).astype(bf16)

        @pl.when(inner == 0)
        def _():
            far_copy.start()
            near_copy.start()

    def stage_cross():
        @pl.when(inner == 1)
        def _():
            far_copy.wait_recv()
            both = four[pl.ds(far, 2)].astype(f32) + from_far[...].astype(f32)
            four[pl.ds(far, 2)] = both.astype(bf16)
            cross_copy.start()

    def stage_out():
        @pl.when(inner == 1)
        def _():
            near_copy.wait_recv()
            cross_copy.wait_recv()
            attn_ref[...] = (
                four[z].astype(f32) + from_near[...].astype(f32) + from_cross[1 - high].astype(f32)
            )
            out = four[3 * high].astype(f32) + from_cross[high].astype(f32)
            cross_out[...] = out.astype(bf16)
            out_copy.start()

    def stage_end():
        @pl.when(inner == 0)
        def _():
            out_copy.wait_recv()
            attn_ref[...] = four[z].astype(f32) + from_out[...].astype(f32)

    feed_ref[...] = jnp.zeros_like(feed_ref)

    def visit(p, carry):
        zz, yy, other = piece(p)
        pair = 4 * zz + 2 * yy

        @pl.when(p > 0)
        def _():
            shard_copy(0, p, pair + c, me).wait_recv()
            each_send(p, zz, yy, other, lambda copy: copy.start())

        shard_copy(0, p, pair + 1 - c, me).wait_recv()

        @pl.when(p < 7)
        def _():
            n_copy(p + 1).start()

        n_copy(p).wait()
        n_rows = n_buf[p % 2]
        g_rows = jnp.concatenate([shards[pair, :t, :], shards[pair + 1, :t, :]], axis=0)
        gu = dot_last(n_rows, w_ref[: 2 * f, :])
        gh = dot_last(g_rows, w_ref[2 * f :, :])
        act, slope = gelu_parts(gu[:, :f])
        up = gu[:, f:]
        dg = (gh * up * slope).astype(bf16)
        du = (gh * act).astype(bf16)
        hid = (act * up).astype(bf16)
        feed_ref[:f, :] += dot_rows(dg, n_rows)
        feed_ref[f : 2 * f, :] += dot_rows(du, n_rows)
        feed_ref[2 * f :, :] += dot_rows(hid, g_rows)
        pl.when(p == 3)(stage_y)
        pl.when(p == 4)(stage_cross)
        pl.when(p == 5)(stage_out)
        pl.when(p == 6)(stage_end)
        return carry

    lax.fori_loop(0, 8, visit, 0)

    def add_tiny(s, total):
        both = shards[s, t:, :].astype(f32)
        return total + both[:8] + both[8:]

    total_ref[...] = lax.fori_loop(0, 16, add_tiny, jnp.zeros(total_ref.shape, f32))

    def settle(p, carry):
        zz, yy, other = piece(p)
        each_send(p, zz, yy, other, lambda copy: copy.wait_send())
        return carry

    lax.fori_loop(0, 8, settle, 0)
    to_core.wait_send()
    to_y.wait_send()

    @pl.when(inner == 0)
    def _():
        far_copy.wait_send()
        near_copy.wait_send()

    @pl.when(inner == 1)
    def _():
        cross_copy.wait_send()
        out_copy.wait_send()


def tail(tiny, gf, lefts, n1, ga, w_own, n_all):
    t, d = gf.shape
    rows = w_own.shape[0]
    blocks = 8
    per = lefts.shape[1] // blocks
    vm = pl.BlockSpec(memory_space=pltpu.VMEM)
    return pl.pallas_call(
        tail_kernel,
        out_shape=(
            jax.ShapeDtypeStruct((rows, d), f32),
            jax.ShapeDtypeStruct((per, d), f32),
            jax.ShapeDtypeStruct(tiny.shape, f32),
        ),
        in_specs=[vm] * 6 + [pl.BlockSpec(memory_space=pl.ANY)],
        out_specs=(vm,) * 3,
        scratch_shapes=[
            pltpu.VMEM((16, t + 16, d), bf16),
            pltpu.VMEM((2, 2 * t, d), bf16),
            pltpu.VMEM((2, blocks, per, d), bf16),
            pltpu.VMEM((blocks, per, d), bf16),
            pltpu.VMEM((4, per, d), bf16),
            pltpu.VMEM((4, per, d), bf16),
            pltpu.VMEM((2, per, d), bf16),
            pltpu.VMEM((per, d), bf16),
            pltpu.VMEM((2, per, d), bf16),
            pltpu.VMEM((per, d), bf16),
            pltpu.VMEM((per, d), bf16),
            pltpu.SemaphoreType.DMA((4, 8)),
            pltpu.SemaphoreType.DMA((16,)),
            pltpu.SemaphoreType.DMA((6,)),
            pltpu.SemaphoreType.DMA((6,)),
            pltpu.SemaphoreType.DMA((2,)),
        ],
        compiler_params=pltpu.CompilerParams(
            vmem_limit_bytes=VMEM_BYTES, collective_id=0, has_side_effects=True
        ),
        cost_estimate=pl.CostEstimate(
            flops=2 * t * 16 * d * rows * 2, bytes_accessed=16 * t * d * 4, transcendentals=16 * t * rows
        ),
    )(tiny, gf, lefts, n1, ga, w_own, n_all)


def adam_step(weight, first_moment, second_moment, gradient, step_rate, weight_decay):
    first_new = 0.9 * first_moment + 0.1 * gradient
    second_new = 0.999 * second_moment + 0.001 * gradient * gradient
    first_fix = 1.0 - 0.9**STEP
    second_fix = 1.0 - 0.999**STEP
    update = first_new / first_fix / (jnp.sqrt(second_new / second_fix) + 1e-08)
    return (first_new, second_new, weight - step_rate * (update + weight_decay * weight))


def kinds_first(gathered, n, kinds, per):
    d = gathered.shape[-1]
    return gathered.reshape(n, kinds, per, d).transpose(1, 0, 2, 3).reshape(kinds * n * per, d)


def owners_first(left, right, n):
    t, k, units = left.shape
    grad = jnp.einsum("tku,td->kud", left, right, preferred_element_type=f32)
    return grad.reshape(k, n, units // n, -1).transpose(1, 0, 2, 3)


def local(
    block_input,
    lengths,
    targets,
    attention_weight,
    attention_first,
    attention_second,
    feed_weight,
    feed_first,
    feed_second,
    norm_gain,
    gain_first,
    gain_second,
    cross_weight,
    cross_first,
    cross_second,
    head_weight,
    head_first,
    head_second,
    cross_gain,
    cross_gain_first,
    cross_gain_second,
):
    n = lax.axis_size("rows")
    is_encoder = lax.axis_index("section") == 0
    micro, length, d = block_input.shape[1:]
    t = micro * length
    per = attention_weight.shape[1]
    f = feed_weight.shape[1]
    inner = per * n

    attn_own = attention_weight[0].astype(bf16).transpose(1, 0, 2).reshape(4 * per, d)
    feed_own = feed_weight[0].astype(bf16).transpose(1, 0, 2)
    half_rows = jnp.concatenate(
        [cross_weight.astype(bf16).transpose(1, 0, 2), head_weight.astype(bf16)[None]], axis=0
    )
    other_half = lax.ppermute(half_rows, "section", [(0, 1)])
    extra_own = jnp.concatenate([other_half, half_rows], axis=-1).reshape(5 * per, d)

    attn_all = lax.all_gather(attn_own, "rows", axis=0, tiled=True)
    attn_w = kinds_first(attn_all, n, 4, per)
    feed_all = lax.all_gather(feed_own.reshape(3 * f, d), "rows", axis=0, tiled=True)
    feed_w = feed_all.reshape(n, 3 * f, d)
    if n != BLOCKS:
        feed_w = kinds_first(feed_all, n, 3, f).reshape(3, BLOCKS, -1, d)
        feed_w = feed_w.transpose(1, 0, 2, 3).reshape(BLOCKS, -1, d)
    extra_all = lax.all_gather(extra_own, "rows", axis=0, tiled=True)
    extra_w = kinds_first(extra_all, n, 5, per)
    cross_w, head_w = extra_w[: 4 * inner], extra_w[4 * inner :]

    gains = norm_gain[0]
    gain_attn, gain_feed, gain_final = gains[0:1], gains[1:2], gains[2:3]
    gain_cross = cross_gain[None]
    x = block_input[0].reshape(t, d)
    enc_counts = lengths[0, :, 0]
    dec_counts = lengths[1, :, 0]
    zero_one = jnp.zeros((1,), jnp.int32)
    self_counts = jnp.concatenate([jnp.where(is_encoder, 0, 1).astype(jnp.int32)[None], enc_counts])
    cross_counts = jnp.concatenate([zero_one, enc_counts])
    target_column = targets.reshape(t, 1)

    n1, qkv, mixed, y1 = attend_fwd(self_counts, x, gain_attn, attn_w, length)

    def enc_feed():
        return feed_fwd(y1, gain_feed, gain_final, feed_w)

    def blank(maker):
        return jax.tree.map(lambda a: jnp.zeros(a.shape, a.dtype), jax.eval_shape(maker))

    enc_state = lax.cond(is_encoder, enc_feed, lambda: blank(enc_feed))
    encoded = lax.ppermute(enc_state[3], "section", [(0, 1)])

    def dec_front():
        mc, cqkv, cmixed, z2 = attend_fwd(cross_counts, y1, gain_cross, cross_w, length, encoded)
        return feed_fwd(z2, gain_feed, gain_final, feed_w) + (mc, cqkv, cmixed, z2)

    def enc_pass():
        rest = jax.eval_shape(dec_front)[4:7]
        return tuple(enc_state) + tuple(jnp.zeros(a.shape, a.dtype) for a in rest) + (y1,)

    n2, gu, y2, final, mc, cqkv, cmixed, mid = lax.cond(is_encoder, enc_pass, dec_front)
    emit = n != BLOCKS
    if not emit:
        n2_all = lax.all_gather(n2, "rows", axis=0, tiled=True)

    def dec_back():
        gl, up, loss = head_loss(dec_counts, final, head_w, target_column, length)
        feed_out = feed_bwd(up, mid, y2, gain_feed, gain_final, gu, feed_w, emit)
        ga_c, dqkv_c, gy1, gg_c, ge = attend_bwd(
            cross_counts, y1, gain_cross, feed_out[1], cqkv, cross_w, length, True
        )
        return (ge, gy1, feed_out[2], feed_out[0], *feed_out[3:], gl, ga_c, dqkv_c, gg_c, loss)

    back = lax.cond(is_encoder, lambda: blank(dec_back), dec_back)
    returned = lax.ppermute(back[0], "section", [(1, 0)])
    at = 6 if emit else 4
    gl, ga_c, dqkv_c, gg_c, loss = back[at:]

    if not emit:
        returned, n2_all = lax.optimization_barrier((returned, n2_all))

    def enc_back():
        feed_out = feed_bwd(returned, mid, y2, gain_feed, gain_final, gu, feed_w, emit)
        return (feed_out[1], feed_out[2], feed_out[0], *feed_out[3:])

    backs = lax.cond(is_encoder, enc_back, lambda: tuple(back[1:at]))
    gy1, gg_feed, gf = backs[:3]

    ga, dqkv, gx, gg_attn = attend_bwd(self_counts, x, gain_attn, gy1, qkv, attn_w, length)

    extra_part = jnp.concatenate(
        [
            owners_first(dqkv_c[:, None, :inner], mc, n),
            owners_first(dqkv_c[:, inner:].reshape(t, 2, inner), encoded, n),
            owners_first(cmixed[:, None], ga_c, n),
            owners_first(gl[:, None], final, n),
        ],
        axis=1,
    ).astype(bf16)
    extra_sum = lax.psum_scatter(
        extra_part.reshape(n * 5 * per, d), "rows", scatter_dimension=0, tiled=True
    )
    half = d // 2
    extra_first = lax.ppermute(extra_sum[:, :half], "section", [(1, 0)])
    extra_grad = jnp.where(is_encoder, extra_first, extra_sum[:, half:]).astype(f32)
    extra_grad = extra_grad.reshape(5, per, half)

    tiny = jnp.concatenate(
        [
            gg_attn,
            gg_feed,
            gg_c,
            jnp.broadcast_to(loss, (1, d)),
            jnp.zeros((3, d), f32),
        ],
        axis=0,
    )

    if emit:
        attn_part = jnp.concatenate(
            [
                owners_first(dqkv.reshape(t, 3, inner), n1, n),
                owners_first(mixed[:, None], ga, n),
            ],
            axis=1,
        ).astype(bf16)
        attn_sum = lax.psum_scatter(
            attn_part.reshape(n * 4 * per, d), "rows", scatter_dimension=0, tiled=True
        ).astype(f32)
        dgu, hid = backs[3], backs[4]
        nb, _, fb = hid.shape
        left = dgu.reshape(nb, t, 2, fb).transpose(1, 2, 0, 3).reshape(t, 2, nb * fb)
        hid = hid.transpose(1, 0, 2).reshape(t, 1, nb * fb)
        feed_part = jnp.concatenate(
            [owners_first(left, n2, n), owners_first(hid, gf, n)], axis=1
        ).astype(bf16)
        feed_grad = lax.psum_scatter(
            feed_part.reshape(n * 3 * f, d), "rows", scatter_dimension=0, tiled=True
        ).astype(f32)
        tiny_sum = jnp.sum(lax.all_gather(tiny, "rows", axis=0), axis=0)
    else:
        lefts = jnp.concatenate([dqkv, mixed], axis=1).reshape(t, 4, 4, 2, 2, per)
        lefts = lefts.transpose(4, 3, 2, 1, 5, 0).reshape(2, 8 * 4 * per, t)
        feed_grad, attn_sum, tiny_sum = tail(
            tiny, gf, lefts, n1, ga, feed_own.reshape(3 * f, d), n2_all
        )
    attn_grad = attn_sum.reshape(4, per, d).transpose(1, 0, 2)
    feed_grad = feed_grad.reshape(3, f, d).transpose(1, 0, 2)
    tiny_dec = lax.ppermute(tiny_sum[3:5], "section", [(1, 0)])
    tiny_dec = jnp.where(is_encoder, tiny_dec, tiny_sum[3:5])
    cross_gain_total = tiny_dec[0]
    loss_total = tiny_dec[1, 0]

    attention_new = adam_step(
        attention_weight, attention_first, attention_second, attn_grad[None], 0.05, 0.1
    )
    feed_new = adam_step(feed_weight, feed_first, feed_second, feed_grad[None], 0.05, 0.1)
    gain_new = adam_step(norm_gain, gain_first, gain_second, tiny_sum[None, 0:3], 0.5, 0.0)
    cross_new = adam_step(
        cross_weight, cross_first, cross_second, extra_grad[:4].transpose(1, 0, 2), 0.05, 0.1
    )
    head_new = adam_step(head_weight, head_first, head_second, extra_grad[4], 0.05, 0.1)
    cross_gain_new = adam_step(
        cross_gain, cross_gain_first, cross_gain_second, cross_gain_total, 0.5, 0.0
    )
    return (
        gx.reshape(1, micro, length, d),
        loss_total,
        *attention_new,
        *feed_new,
        *gain_new,
        *cross_new,
        *head_new,
        *cross_gain_new,
    )


def solution(mesh):
    by_row = P("section", "rows", None, None)
    gain = P("section", None, None)
    cross = P("rows", None, "section")
    head = P("rows", "section")
    weights = (by_row,) * 6 + (gain,) * 3 + (cross,) * 3 + (head,) * 3 + (P(),) * 3
    tokens = P("section", None, "rows", None)
    return jax.shard_map(
        local,
        mesh=mesh,
        in_specs=(tokens, P(None, None, "rows"), P(None, "rows")) + weights,
        out_specs=(tokens, P()) + weights,
        check_vma=False,
    )
```

```python
import functools

import jax
import jax.numpy as jnp
from jax import lax
from jax.experimental import pallas as pl
from jax.experimental.pallas import tpu as pltpu
from jax.sharding import PartitionSpec as P

HD = 64
STEP = 10
PAIR = 2 * HD
BLOCKS = 16
VMEM_BYTES = 52 * 1024 * 1024

bf16 = jnp.bfloat16
f32 = jnp.float32
masked_value = -1000000000.0
scale = HD ** (-0.5)


def dot(a, b):
    return lax.dot_general(a, b, (((1,), (0,)), ((), ())), preferred_element_type=f32)


def dot_last(a, b):
    return lax.dot_general(a, b, (((1,), (1,)), ((), ())), preferred_element_type=f32)


def dot_rows(a, b):
    return lax.dot_general(a, b, (((0,), (0,)), ((), ())), preferred_element_type=f32)


def unit_rows(v):
    r = lax.rsqrt(jnp.mean(v * v, axis=-1, keepdims=True) + 1e-06)
    return r, v * r


def norm_back(v, gain, up):
    r, n = unit_rows(v)
    g = up * gain
    back = r * (g - n * jnp.mean(g * n, axis=-1, keepdims=True))
    return back, jnp.sum(up * n, axis=0, keepdims=True)


def gelu_parts(x):
    c = 0.7978845608028654
    t = jnp.tanh(c * (x + 0.044715 * (x * x * x)))
    act = 0.5 * x * (1.0 + t)
    slope = 0.5 * (1.0 + t) + 0.5 * x * (1.0 - t * t) * (c * (1.0 + 3.0 * 0.044715 * (x * x)))
    return act, slope


def low_half(length):
    return lax.broadcasted_iota(jnp.int32, (length, PAIR), 1) < HD


def stack_pair(m, low):
    zero = jnp.zeros_like(m)
    return jnp.concatenate([jnp.where(low, m, zero), jnp.where(low, zero, m)], axis=0)


def allowed_twice(cnt_ref, s, length):
    row = lax.broadcasted_iota(jnp.int32, (length, length), 0)
    col = lax.broadcasted_iota(jnp.int32, (length, length), 1)
    limit = jnp.where(cnt_ref[0] == 1, row + 1, cnt_ref[1 + s])
    one = jnp.where(col < limit, 1, 0)
    return jnp.concatenate([one, one], axis=0) == 1


def soft_pair(q2, k, allowed):
    s = dot_last(q2, k) * scale
    s = jnp.where(allowed, s, masked_value)
    e = jnp.exp(s - jnp.max(s, axis=-1, keepdims=True))
    return e / jnp.sum(e, axis=-1, keepdims=True)


def attend_fwd_kernel(cross, length, cnt_ref, x_ref, gain_ref, *refs):
    if cross:
        src_ref, w_ref, n_ref, qkv_ref, o_ref, y_ref = refs
    else:
        w_ref, n_ref, qkv_ref, o_ref, y_ref = refs
    inner = w_ref.shape[0] // 4
    x = x_ref[...].astype(f32)
    n = (unit_rows(x)[1] * gain_ref[...]).astype(bf16)
    n_ref[...] = n
    if cross:
        qkv_ref[:, :inner] = dot_last(n, w_ref[:inner, :]).astype(bf16)
        qkv_ref[:, inner:] = dot_last(src_ref[...], w_ref[inner : 3 * inner, :]).astype(bf16)
    else:
        qkv_ref[...] = dot_last(n, w_ref[: 3 * inner, :]).astype(bf16)
    low = low_half(length)
    for s in range(x.shape[0] // length):
        allowed = allowed_twice(cnt_ref, s, length)
        rows = slice(s * length, (s + 1) * length)
        for h in range(inner // PAIR):
            cols = [slice(j * inner + h * PAIR, j * inner + (h + 1) * PAIR) for j in range(3)]
            q2 = stack_pair(qkv_ref[rows, cols[0]], low)
            p = soft_pair(q2, qkv_ref[rows, cols[1]], allowed).astype(bf16)
            wide = jnp.concatenate([p[:length], p[length:]], axis=1)
            o_ref[rows, cols[0]] = dot(wide, stack_pair(qkv_ref[rows, cols[2]], low)).astype(bf16)
    y_ref[...] = x + dot(o_ref[...], w_ref[3 * inner :, :])


def attend_fwd(counts, x, gain, w, length, source=None):
    t, d = x.shape
    inner = w.shape[0] // 4
    ins = [counts, x, gain] + ([] if source is None else [source]) + [w]
    vm = pl.BlockSpec(memory_space=pltpu.VMEM)
    return pl.pallas_call(
        functools.partial(attend_fwd_kernel, source is not None, length),
        out_shape=(
            jax.ShapeDtypeStruct((t, d), bf16),
            jax.ShapeDtypeStruct((t, 3 * inner), bf16),
            jax.ShapeDtypeStruct((t, inner), bf16),
            jax.ShapeDtypeStruct((t, d), f32),
        ),
        in_specs=[pl.BlockSpec(memory_space=pltpu.SMEM)] + [vm] * (len(ins) - 1),
        out_specs=(vm,) * 4,
        compiler_params=pltpu.CompilerParams(vmem_limit_bytes=VMEM_BYTES),
        cost_estimate=pl.CostEstimate(
            flops=2 * t * d * inner * 4 + 8 * t * length * inner,
            bytes_accessed=w.size * 2 + t * d * 10,
            transcendentals=t * length * 6,
        ),
    )(*ins)


def attend_bwd_kernel(cross, length, cnt_ref, x_ref, gain_ref, gy_ref, qkv_ref, w_ref, *refs):
    if cross:
        ga_ref, dqkv_ref, gx_ref, gg_ref, gs_ref, do_ref = refs
    else:
        ga_ref, dqkv_ref, gx_ref, gg_ref, do_ref = refs
    inner = w_ref.shape[0] // 4
    ga = gy_ref[...].astype(bf16)
    ga_ref[...] = ga
    do_ref[...] = dot_last(ga, w_ref[3 * inner :, :]).astype(bf16)
    low = low_half(length)
    for s in range(ga.shape[0] // length):
        allowed = allowed_twice(cnt_ref, s, length)
        rows = slice(s * length, (s + 1) * length)
        for h in range(inner // PAIR):
            cols = [slice(j * inner + h * PAIR, j * inner + (h + 1) * PAIR) for j in range(3)]
            q2 = stack_pair(qkv_ref[rows, cols[0]], low)
            k = qkv_ref[rows, cols[1]]
            p = soft_pair(q2, k, allowed)
            do2 = stack_pair(do_ref[rows, cols[0]], low)
            dp = dot_last(do2, qkv_ref[rows, cols[2]])
            ds = p * (dp - jnp.sum(dp * p, axis=-1, keepdims=True))
            ds = jnp.where(allowed, ds, 0.0).astype(bf16)
            wide = jnp.concatenate([ds[:length], ds[length:]], axis=1)
            dqkv_ref[rows, cols[0]] = (dot(wide, stack_pair(k, low)) * scale).astype(bf16)
            dqkv_ref[rows, cols[1]] = (dot_rows(ds, q2) * scale).astype(bf16)
            dqkv_ref[rows, cols[2]] = dot_rows(p.astype(bf16), do2).astype(bf16)
    if cross:
        up = dot(dqkv_ref[:, :inner], w_ref[:inner, :])
        gs_ref[...] = dot(dqkv_ref[:, inner:], w_ref[inner : 3 * inner, :]).astype(bf16)
    else:
        up = dot(dqkv_ref[...], w_ref[: 3 * inner, :])
    back, gg_ref[...] = norm_back(x_ref[...].astype(f32), gain_ref[...], up)
    gx_ref[...] = gy_ref[...] + back


def attend_bwd(counts, x, gain, gy, qkv, w, length, cross=False):
    t, d = x.shape
    inner = w.shape[0] // 4
    vm = pl.BlockSpec(memory_space=pltpu.VMEM)
    outs = [
        jax.ShapeDtypeStruct((t, d), bf16),
        jax.ShapeDtypeStruct((t, 3 * inner), bf16),
        jax.ShapeDtypeStruct((t, d), f32),
        jax.ShapeDtypeStruct((1, d), f32),
    ]
    if cross:
        outs.append(jax.ShapeDtypeStruct((t, d), bf16))
    return pl.pallas_call(
        functools.partial(attend_bwd_kernel, cross, length),
        out_shape=tuple(outs),
        in_specs=[pl.BlockSpec(memory_space=pltpu.SMEM)] + [vm] * 5,
        out_specs=(vm,) * len(outs),
        scratch_shapes=[pltpu.VMEM((t, inner), bf16)],
        compiler_params=pltpu.CompilerParams(vmem_limit_bytes=VMEM_BYTES),
        cost_estimate=pl.CostEstimate(
            flops=2 * t * d * inner * 4 + 20 * t * length * inner,
            bytes_accessed=w.size * 2 + t * d * 16,
            transcendentals=t * length * 6,
        ),
    )(counts, x, gain, gy, qkv, w)


def feed_fwd_kernel(y_ref, g_in_ref, g_out_ref, w_ref, n_ref, gu_ref, y2_ref, f_ref):
    i = pl.program_id(0)
    f = w_ref.shape[1] // 3

    @pl.when(i == 0)
    def _():
        y = y_ref[...]
        n_ref[...] = (unit_rows(y)[1] * g_in_ref[...]).astype(bf16)
        y2_ref[...] = y

    gu = dot_last(n_ref[...], w_ref[0, : 2 * f, :])
    gu_ref[0] = gu
    hidden = (gelu_parts(gu[:, :f])[0] * gu[:, f:]).astype(bf16)
    y2_ref[...] += dot(hidden, w_ref[0, 2 * f :, :])

    @pl.when(i == pl.num_programs(0) - 1)
    def _():
        f_ref[...] = (unit_rows(y2_ref[...])[1] * g_out_ref[...]).astype(bf16)


def feed_fwd(y, gain_in, gain_out, w):
    t, d = y.shape
    nb, rows, _ = w.shape
    f = rows // 3
    whole = lambda *shape: pl.BlockSpec(shape, lambda i: (0,) * len(shape))
    part = lambda *shape: pl.BlockSpec((1,) + shape, lambda i: (i, 0, 0))
    return pl.pallas_call(
        feed_fwd_kernel,
        grid=(nb,),
        out_shape=(
            jax.ShapeDtypeStruct((t, d), bf16),
            jax.ShapeDtypeStruct((nb, t, 2 * f), f32),
            jax.ShapeDtypeStruct((t, d), f32),
            jax.ShapeDtypeStruct((t, d), bf16),
        ),
        in_specs=[whole(t, d), whole(1, d), whole(1, d), part(rows, d)],
        out_specs=(whole(t, d), part(t, 2 * f), whole(t, d), whole(t, d)),
        compiler_params=pltpu.CompilerParams(vmem_limit_bytes=VMEM_BYTES),
        cost_estimate=pl.CostEstimate(
            flops=2 * t * d * rows * nb,
            bytes_accessed=w.size * 2 + t * d * 12 + nb * t * f * 8,
            transcendentals=nb * t * f,
        ),
    )(y, gain_in, gain_out, w)


def feed_bwd_kernel(emit, up_ref, y_ref, y2_ref, g_in_ref, g_out_ref, gu_ref, w_ref, *refs):
    if emit:
        gf_ref, gy_ref, gg_ref, dgu_ref, hid_ref, last_ref = refs
    else:
        gf_ref, gy_ref, gg_ref, last_ref = refs
    i = pl.program_id(0)
    f = w_ref.shape[1] // 3

    @pl.when(i == 0)
    def _():
        back, gain_grad = norm_back(y2_ref[...], g_out_ref[...], up_ref[...].astype(f32))
        gg_ref[1:2, :] = gain_grad
        last_ref[...] = back
        gf_ref[...] = back.astype(bf16)
        gy_ref[...] = jnp.zeros_like(gy_ref)

    gh = dot_last(gf_ref[...], w_ref[0, 2 * f :, :])
    act, slope = gelu_parts(gu_ref[0, :, :f])
    u = gu_ref[0, :, f:]
    dg = (gh * u * slope).astype(bf16)
    du = (gh * act).astype(bf16)
    if emit:
        dgu_ref[0, :, :f] = dg
        dgu_ref[0, :, f:] = du
        hid_ref[0] = (act * u).astype(bf16)
    gy_ref[...] += dot(dg, w_ref[0, :f, :]) + dot(du, w_ref[0, f : 2 * f, :])

    @pl.when(i == pl.num_programs(0) - 1)
    def _():
        back, gain_grad = norm_back(y_ref[...], g_in_ref[...], gy_ref[...])
        gg_ref[0:1, :] = gain_grad
        gy_ref[...] = last_ref[...] + back


def feed_bwd(up, y, y2, gain_in, gain_out, gu, w, emit):
    t, d = y.shape
    nb, rows, _ = w.shape
    f = rows // 3
    whole = lambda *shape: pl.BlockSpec(shape, lambda i: (0,) * len(shape))
    part = lambda *shape: pl.BlockSpec((1,) + shape, lambda i: (i, 0, 0))
    outs = [
        jax.ShapeDtypeStruct((t, d), bf16),
        jax.ShapeDtypeStruct((t, d), f32),
        jax.ShapeDtypeStruct((2, d), f32),
    ]
    specs = [whole(t, d), whole(t, d), whole(2, d)]
    if emit:
        outs += [
            jax.ShapeDtypeStruct((nb, t, 2 * f), bf16),
            jax.ShapeDtypeStruct((nb, t, f), bf16),
        ]
        specs += [part(t, 2 * f), part(t, f)]
    return pl.pallas_call(
        functools.partial(feed_bwd_kernel, emit),
        grid=(nb,),
        out_shape=tuple(outs),
        in_specs=[whole(t, d)] * 3 + [whole(1, d)] * 2 + [part(t, 2 * f), part(rows, d)],
        out_specs=tuple(specs),
        scratch_shapes=[pltpu.VMEM((t, d), f32)],
        compiler_params=pltpu.CompilerParams(vmem_limit_bytes=VMEM_BYTES),
        cost_estimate=pl.CostEstimate(
            flops=2 * t * d * rows * nb,
            bytes_accessed=w.size * 2 + t * d * 18 + nb * t * f * 8,
            transcendentals=nb * t * f,
        ),
    )(up, y, y2, gain_in, gain_out, gu, w)


def head_kernel(length, cnt_ref, f_ref, w_ref, target_ref, gl_ref, up_ref, loss_ref):
    logits = dot_last(f_ref[...], w_ref[...])
    top = jnp.max(logits, axis=-1, keepdims=True)
    log_total = top + jnp.log(jnp.sum(jnp.exp(logits - top), axis=-1, keepdims=True))
    hit = lax.broadcasted_iota(jnp.int32, logits.shape, 1) == target_ref[...]
    picked = jnp.sum(jnp.where(hit, logits, 0.0), axis=-1, keepdims=True)
    probs = jnp.exp(logits - log_total) - jnp.where(hit, 1.0, 0.0)
    total = jnp.zeros((1, 1), f32)
    for s in range(logits.shape[0] // length):
        rows = slice(s * length, (s + 1) * length)
        count = cnt_ref[s]
        valid = lax.broadcasted_iota(jnp.int32, (length, 1), 0) < count
        total += jnp.sum(
            jnp.where(valid, log_total[rows] - picked[rows], 0.0), axis=0, keepdims=True
        )
        gl_ref[rows, :] = jnp.where(valid, probs[rows], 0.0).astype(bf16)
    loss_ref[...] = total
    up_ref[...] = dot(gl_ref[...], w_ref[...])


def head_loss(counts, final, w, target, length):
    t, d = final.shape
    v = w.shape[0]
    vm = pl.BlockSpec(memory_space=pltpu.VMEM)
    return pl.pallas_call(
        functools.partial(head_kernel, length),
        out_shape=(
            jax.ShapeDtypeStruct((t, v), bf16),
            jax.ShapeDtypeStruct((t, d), f32),
            jax.ShapeDtypeStruct((1, 1), f32),
        ),
        in_specs=[pl.BlockSpec(memory_space=pltpu.SMEM), vm, vm, vm],
        out_specs=(vm,) * 3,
        compiler_params=pltpu.CompilerParams(vmem_limit_bytes=VMEM_BYTES),
        cost_estimate=pl.CostEstimate(
            flops=4 * t * d * v, bytes_accessed=w.size * 2 + t * d * 6, transcendentals=t * v * 2
        ),
    )(counts, final, w, target)


def tail_kernel(
    tiny_ref, gf_ref, lefts_ref, n1_ref, ga_ref, w_ref, n_all_ref,
    feed_ref, attn_ref, total_ref,
    shards, n_buf, part, from_core, four, from_y, from_far, from_near, from_cross, from_out, cross_out,
    ag_send, ag_recv, rs_send, rs_recv, n_sem,
):
    me = lax.axis_index("rows")
    z, y, c = me // 4, (me // 2) % 2, me % 2
    high = z // 2
    inner = (z + high) % 2
    t = gf_ref.shape[0]
    f = w_ref.shape[0] // 3
    core_peer, y_peer = me + 1 - 2 * c, me + 2 - 4 * y
    toward = me + 4 - 8 * high
    across = me + 4 - 8 * high
    outward = me - 4 + 8 * high

    def remote(src, dst, send, recv, device):
        return pltpu.make_async_remote_copy(
            src_ref=src, dst_ref=dst, send_sem=send, recv_sem=recv,
            device_id={"rows": device}, device_id_type=pl.DeviceIdType.MESH,
        )

    barrier = pltpu.get_barrier_semaphore()

    def greet(device):
        pl.semaphore_signal(
            barrier, inc=1, device_id={"rows": device}, device_id_type=pl.DeviceIdType.MESH
        )

    greet(core_peer)
    greet(y_peer)
    greet(toward)

    @pl.when(inner == 1)
    def _():
        greet(outward)

    pl.semaphore_wait(barrier, 3 + inner)

    def piece(p):
        odd = p % 2
        j = jnp.where(p == 0, 0, jnp.where(p == 7, 3, jnp.where(odd == 1, (p + 1) // 2, p // 2 - 1)))
        other = jnp.where(p == 0, 0, jnp.where(p == 7, 1, 1 - odd))
        first, second, third = z + 1 - 2 * (z % 2), 2 - high, 3 - 3 * high
        zz = jnp.where(j == 0, z, jnp.where(j == 1, first, jnp.where(j == 2, second, third)))
        yy = y + other - 2 * other * y
        return zz, yy, other

    def shard_copy(kind, p, s, device):
        return remote(shards.at[s], shards.at[s], ag_send.at[kind, p], ag_recv.at[s], device)

    def each_send(p, zz, yy, other, act):
        s = 4 * zz + 2 * yy + c

        @pl.when((other == 0) & (zz <= z) & (z < 3))
        def _():
            act(shard_copy(0, p, s, me + 4))

        @pl.when((other == 0) & (zz >= z) & (z > 0))
        def _():
            act(shard_copy(1, p, s, me - 4))

        @pl.when(other == 0)
        def _():
            act(shard_copy(2, p, s, y_peer))

        act(shard_copy(3, p, s, core_peer))

    def n_copy(p):
        zz, yy, _ = piece(p)
        rows = pl.ds((2 * zz + yy) * (2 * t), 2 * t)
        slot = p % 2
        return pltpu.make_async_copy(n_all_ref.at[rows], n_buf.at[slot], n_sem.at[slot])

    n_copy(0).start()
    shards[me, :t, :] = gf_ref[...]
    tiny = tiny_ref[...]
    tiny_high = tiny.astype(bf16)
    tiny_low = (tiny - tiny_high.astype(f32)).astype(bf16)
    shards[me, t:, :] = jnp.concatenate([tiny_high, tiny_low], axis=0)
    each_send(0, z, y, 0, lambda copy: copy.start())

    blocks, per = part.shape[1:3]
    row = lax.broadcasted_iota(jnp.int32, (blocks * per, n1_ref.shape[1]), 0)
    from_mixed = row % per >= per // 4 * 3

    def half_sums(half):
        left = lefts_ref[half]
        both = jnp.where(from_mixed, dot(left, ga_ref[...]), dot(left, n1_ref[...]))
        return both.reshape(blocks, per, -1)

    part[0] = half_sums(1 - c).astype(bf16)
    to_core = remote(part.at[0], from_core, rs_send.at[0], rs_recv.at[0], core_peer)
    to_core.start()
    own_half = half_sums(c)
    to_core.wait_recv()
    part[1] = (own_half + from_core[...].astype(f32)).astype(bf16)
    quarter = blocks // 2
    to_y = remote(
        part.at[1, pl.ds((1 - y) * quarter, quarter)], from_y, rs_send.at[1], rs_recv.at[1], y_peer
    )
    to_y.start()

    far = 2 - 2 * high
    far_copy = remote(four.at[pl.ds(far, 2)], from_far, rs_send.at[2], rs_recv.at[2], toward)
    near_copy = remote(four.at[1 + high], from_near, rs_send.at[3], rs_recv.at[3], toward)
    cross_copy = remote(four.at[pl.ds(far, 2)], from_cross, rs_send.at[4], rs_recv.at[4], across)
    out_copy = remote(cross_out, from_out, rs_send.at[5], rs_recv.at[5], outward)

    def stage_y():
        to_y.wait_recv()
        mine = part[1, pl.ds(y * quarter, quarter)].astype(f32)
        four[...] = (mine + from_y[...].astype(f32)).astype(bf16)

        @pl.when(inner == 0)
        def _():
            far_copy.start()
            near_copy.start()

    def stage_cross():
        @pl.when(inner == 1)
        def _():
            far_copy.wait_recv()
            both = four[pl.ds(far, 2)].astype(f32) + from_far[...].astype(f32)
            four[pl.ds(far, 2)] = both.astype(bf16)
            cross_copy.start()

    def stage_out():
        @pl.when(inner == 1)
        def _():
            near_copy.wait_recv()
            cross_copy.wait_recv()
            attn_ref[...] = (
                four[z].astype(f32) + from_near[...].astype(f32) + from_cross[1 - high].astype(f32)
            )
            out = four[3 * high].astype(f32) + from_cross[high].astype(f32)
            cross_out[...] = out.astype(bf16)
            out_copy.start()

    def stage_end():
        @pl.when(inner == 0)
        def _():
            out_copy.wait_recv()
            attn_ref[...] = four[z].astype(f32) + from_out[...].astype(f32)

    feed_ref[...] = jnp.zeros_like(feed_ref)

    def visit(p, carry):
        zz, yy, other = piece(p)
        pair = 4 * zz + 2 * yy

        @pl.when(p > 0)
        def _():
            shard_copy(0, p, pair + c, me).wait_recv()
            each_send(p, zz, yy, other, lambda copy: copy.start())

        shard_copy(0, p, pair + 1 - c, me).wait_recv()

        @pl.when(p < 7)
        def _():
            n_copy(p + 1).start()

        n_copy(p).wait()
        n_rows = n_buf[p % 2]
        g_rows = jnp.concatenate([shards[pair, :t, :], shards[pair + 1, :t, :]], axis=0)
        gu = dot_last(n_rows, w_ref[: 2 * f, :])
        gh = dot_last(g_rows, w_ref[2 * f :, :])
        act, slope = gelu_parts(gu[:, :f])
        up = gu[:, f:]
        dg = (gh * up * slope).astype(bf16)
        du = (gh * act).astype(bf16)
        hid = (act * up).astype(bf16)
        feed_ref[:f, :] += dot_rows(dg, n_rows)
        feed_ref[f : 2 * f, :] += dot_rows(du, n_rows)
        feed_ref[2 * f :, :] += dot_rows(hid, g_rows)
        pl.when(p == 3)(stage_y)
        pl.when(p == 4)(stage_cross)
        pl.when(p == 5)(stage_out)
        pl.when(p == 6)(stage_end)
        return carry

    lax.fori_loop(0, 8, visit, 0)

    def add_tiny(s, total):
        both = shards[s, t:, :].astype(f32)
        return total + both[:8] + both[8:]

    total_ref[...] = lax.fori_loop(0, 16, add_tiny, jnp.zeros(total_ref.shape, f32))

    def settle(p, carry):
        zz, yy, other = piece(p)
        each_send(p, zz, yy, other, lambda copy: copy.wait_send())
        return carry

    lax.fori_loop(0, 8, settle, 0)
    to_core.wait_send()
    to_y.wait_send()

    @pl.when(inner == 0)
    def _():
        far_copy.wait_send()
        near_copy.wait_send()

    @pl.when(inner == 1)
    def _():
        cross_copy.wait_send()
        out_copy.wait_send()


def tail(tiny, gf, lefts, n1, ga, w_own, n_all):
    t, d = gf.shape
    rows = w_own.shape[0]
    blocks = 8
    per = lefts.shape[1] // blocks
    vm = pl.BlockSpec(memory_space=pltpu.VMEM)
    return pl.pallas_call(
        tail_kernel,
        out_shape=(
            jax.ShapeDtypeStruct((rows, d), f32),
            jax.ShapeDtypeStruct((per, d), f32),
            jax.ShapeDtypeStruct(tiny.shape, f32),
        ),
        in_specs=[vm] * 6 + [pl.BlockSpec(memory_space=pl.ANY)],
        out_specs=(vm,) * 3,
        scratch_shapes=[
            pltpu.VMEM((16, t + 16, d), bf16),
            pltpu.VMEM((2, 2 * t, d), bf16),
            pltpu.VMEM((2, blocks, per, d), bf16),
            pltpu.VMEM((blocks, per, d), bf16),
            pltpu.VMEM((4, per, d), bf16),
            pltpu.VMEM((4, per, d), bf16),
            pltpu.VMEM((2, per, d), bf16),
            pltpu.VMEM((per, d), bf16),
            pltpu.VMEM((2, per, d), bf16),
            pltpu.VMEM((per, d), bf16),
            pltpu.VMEM((per, d), bf16),
            pltpu.SemaphoreType.DMA((4, 8)),
            pltpu.SemaphoreType.DMA((16,)),
            pltpu.SemaphoreType.DMA((6,)),
            pltpu.SemaphoreType.DMA((6,)),
            pltpu.SemaphoreType.DMA((2,)),
        ],
        compiler_params=pltpu.CompilerParams(
            vmem_limit_bytes=VMEM_BYTES, collective_id=0, has_side_effects=True
        ),
        cost_estimate=pl.CostEstimate(
            flops=2 * t * 16 * d * rows * 2, bytes_accessed=16 * t * d * 4, transcendentals=16 * t * rows
        ),
    )(tiny, gf, lefts, n1, ga, w_own, n_all)


def adam_step(weight, first_moment, second_moment, gradient, step_rate, weight_decay):
    first_new = 0.9 * first_moment + 0.1 * gradient
    second_new = 0.999 * second_moment + 0.001 * gradient * gradient
    first_fix = 1.0 - 0.9**STEP
    second_fix = 1.0 - 0.999**STEP
    update = first_new / first_fix / (jnp.sqrt(second_new / second_fix) + 1e-08)
    return (first_new, second_new, weight - step_rate * (update + weight_decay * weight))


def kinds_first(gathered, n, kinds, per):
    d = gathered.shape[-1]
    return gathered.reshape(n, kinds, per, d).transpose(1, 0, 2, 3).reshape(kinds * n * per, d)


def owners_first(left, right, n):
    t, k, units = left.shape
    grad = jnp.einsum("tku,td->kud", left, right, preferred_element_type=f32)
    return grad.reshape(k, n, units // n, -1).transpose(1, 0, 2, 3)


def local(
    block_input,
    lengths,
    targets,
    attention_weight,
    attention_first,
    attention_second,
    feed_weight,
    feed_first,
    feed_second,
    norm_gain,
    gain_first,
    gain_second,
    cross_weight,
    cross_first,
    cross_second,
    head_weight,
    head_first,
    head_second,
    cross_gain,
    cross_gain_first,
    cross_gain_second,
):
    n = lax.axis_size("rows")
    is_encoder = lax.axis_index("section") == 0
    micro, length, d = block_input.shape[1:]
    t = micro * length
    per = attention_weight.shape[1]
    f = feed_weight.shape[1]
    inner = per * n

    attn_own = attention_weight[0].astype(bf16).transpose(1, 0, 2).reshape(4 * per, d)
    feed_own = feed_weight[0].astype(bf16).transpose(1, 0, 2)
    half_rows = jnp.concatenate(
        [cross_weight.astype(bf16).transpose(1, 0, 2), head_weight.astype(bf16)[None]], axis=0
    )
    other_half = lax.ppermute(half_rows, "section", [(0, 1)])
    extra_own = jnp.concatenate([other_half, half_rows], axis=-1).reshape(5 * per, d)

    attn_all = lax.all_gather(attn_own, "rows", axis=0, tiled=True)
    attn_w = kinds_first(attn_all, n, 4, per)
    feed_all = lax.all_gather(feed_own.reshape(3 * f, d), "rows", axis=0, tiled=True)
    feed_w = feed_all.reshape(n, 3 * f, d)
    if n != BLOCKS:
        feed_w = kinds_first(feed_all, n, 3, f).reshape(3, BLOCKS, -1, d)
        feed_w = feed_w.transpose(1, 0, 2, 3).reshape(BLOCKS, -1, d)
    extra_all = lax.all_gather(extra_own, "rows", axis=0, tiled=True)
    extra_w = kinds_first(extra_all, n, 5, per)
    cross_w, head_w = extra_w[: 4 * inner], extra_w[4 * inner :]

    gains = norm_gain[0]
    gain_attn, gain_feed, gain_final = gains[0:1], gains[1:2], gains[2:3]
    gain_cross = cross_gain[None]
    x = block_input[0].reshape(t, d)
    enc_counts = lengths[0, :, 0]
    dec_counts = lengths[1, :, 0]
    zero_one = jnp.zeros((1,), jnp.int32)
    self_counts = jnp.concatenate([jnp.where(is_encoder, 0, 1).astype(jnp.int32)[None], enc_counts])
    cross_counts = jnp.concatenate([zero_one, enc_counts])
    target_column = targets.reshape(t, 1)

    n1, qkv, mixed, y1 = attend_fwd(self_counts, x, gain_attn, attn_w, length)

    def enc_feed():
        return feed_fwd(y1, gain_feed, gain_final, feed_w)

    def blank(maker):
        return jax.tree.map(lambda a: jnp.zeros(a.shape, a.dtype), jax.eval_shape(maker))

    enc_state = lax.cond(is_encoder, enc_feed, lambda: blank(enc_feed))
    encoded = lax.ppermute(enc_state[3], "section", [(0, 1)])

    def dec_front():
        mc, cqkv, cmixed, z2 = attend_fwd(cross_counts, y1, gain_cross, cross_w, length, encoded)
        return feed_fwd(z2, gain_feed, gain_final, feed_w) + (mc, cqkv, cmixed, z2)

    def enc_pass():
        rest = jax.eval_shape(dec_front)[4:7]
        return tuple(enc_state) + tuple(jnp.zeros(a.shape, a.dtype) for a in rest) + (y1,)

    n2, gu, y2, final, mc, cqkv, cmixed, mid = lax.cond(is_encoder, enc_pass, dec_front)
    emit = n != BLOCKS
    if not emit:
        n2_all = lax.all_gather(n2, "rows", axis=0, tiled=True)

    def dec_back():
        gl, up, loss = head_loss(dec_counts, final, head_w, target_column, length)
        feed_out = feed_bwd(up, mid, y2, gain_feed, gain_final, gu, feed_w, emit)
        ga_c, dqkv_c, gy1, gg_c, ge = attend_bwd(
            cross_counts, y1, gain_cross, feed_out[1], cqkv, cross_w, length, True
        )
        return (ge, gy1, feed_out[2], feed_out[0], *feed_out[3:], gl, ga_c, dqkv_c, gg_c, loss)

    back = lax.cond(is_encoder, lambda: blank(dec_back), dec_back)
    returned = lax.ppermute(back[0], "section", [(1, 0)])
    at = 6 if emit else 4
    gl, ga_c, dqkv_c, gg_c, loss = back[at:]

    if not emit:
        returned, n2_all = lax.optimization_barrier((returned, n2_all))

    def enc_back():
        feed_out = feed_bwd(returned, mid, y2, gain_feed, gain_final, gu, feed_w, emit)
        return (feed_out[1], feed_out[2], feed_out[0], *feed_out[3:])

    backs = lax.cond(is_encoder, enc_back, lambda: tuple(back[1:at]))
    gy1, gg_feed, gf = backs[:3]

    ga, dqkv, gx, gg_attn = attend_bwd(self_counts, x, gain_attn, gy1, qkv, attn_w, length)

    extra_part = jnp.concatenate(
        [
            owners_first(dqkv_c[:, None, :inner], mc, n),
            owners_first(dqkv_c[:, inner:].reshape(t, 2, inner), encoded, n),
            owners_first(cmixed[:, None], ga_c, n),
            owners_first(gl[:, None], final, n),
        ],
        axis=1,
    ).astype(bf16)
    if not emit:
        extra_part, gx = lax.optimization_barrier((extra_part, gx))
    extra_sum = lax.psum_scatter(
        extra_part.reshape(n * 5 * per, d), "rows", scatter_dimension=0, tiled=True
    )
    half = d // 2
    extra_first = lax.ppermute(extra_sum[:, :half], "section", [(1, 0)])
    extra_grad = jnp.where(is_encoder, extra_first, extra_sum[:, half:]).astype(f32)
    extra_grad = extra_grad.reshape(5, per, half)

    tiny = jnp.concatenate(
        [
            gg_attn,
            gg_feed,
            gg_c,
            jnp.broadcast_to(loss, (1, d)),
            jnp.zeros((3, d), f32),
        ],
        axis=0,
    )

    if emit:
        attn_part = jnp.concatenate(
            [
                owners_first(dqkv.reshape(t, 3, inner), n1, n),
                owners_first(mixed[:, None], ga, n),
            ],
            axis=1,
        ).astype(bf16)
        attn_sum = lax.psum_scatter(
            attn_part.reshape(n * 4 * per, d), "rows", scatter_dimension=0, tiled=True
        ).astype(f32)
        dgu, hid = backs[3], backs[4]
        nb, _, fb = hid.shape
        left = dgu.reshape(nb, t, 2, fb).transpose(1, 2, 0, 3).reshape(t, 2, nb * fb)
        hid = hid.transpose(1, 0, 2).reshape(t, 1, nb * fb)
        feed_part = jnp.concatenate(
            [owners_first(left, n2, n), owners_first(hid, gf, n)], axis=1
        ).astype(bf16)
        feed_grad = lax.psum_scatter(
            feed_part.reshape(n * 3 * f, d), "rows", scatter_dimension=0, tiled=True
        ).astype(f32)
        tiny_sum = jnp.sum(lax.all_gather(tiny, "rows", axis=0), axis=0)
    else:
        lefts = jnp.concatenate([dqkv, mixed], axis=1).reshape(t, 4, 4, 2, 2, per)
        lefts = lefts.transpose(4, 3, 2, 1, 5, 0).reshape(2, 8 * 4 * per, t)
        feed_grad, attn_sum, tiny_sum = tail(
            tiny, gf, lefts, n1, ga, feed_own.reshape(3 * f, d), n2_all
        )
    attn_grad = attn_sum.reshape(4, per, d).transpose(1, 0, 2)
    feed_grad = feed_grad.reshape(3, f, d).transpose(1, 0, 2)
    tiny_dec = lax.ppermute(tiny_sum[3:5], "section", [(1, 0)])
    tiny_dec = jnp.where(is_encoder, tiny_dec, tiny_sum[3:5])
    cross_gain_total = tiny_dec[0]
    loss_total = tiny_dec[1, 0]

    attention_new = adam_step(
        attention_weight, attention_first, attention_second, attn_grad[None], 0.05, 0.1
    )
    feed_new = adam_step(feed_weight, feed_first, feed_second, feed_grad[None], 0.05, 0.1)
    gain_new = adam_step(norm_gain, gain_first, gain_second, tiny_sum[None, 0:3], 0.5, 0.0)
    cross_new = adam_step(
        cross_weight, cross_first, cross_second, extra_grad[:4].transpose(1, 0, 2), 0.05, 0.1
    )
    head_new = adam_step(head_weight, head_first, head_second, extra_grad[4], 0.05, 0.1)
    cross_gain_new = adam_step(
        cross_gain, cross_gain_first, cross_gain_second, cross_gain_total, 0.5, 0.0
    )
    return (
        gx.reshape(1, micro, length, d),
        loss_total,
        *attention_new,
        *feed_new,
        *gain_new,
        *cross_new,
        *head_new,
        *cross_gain_new,
    )


def solution(mesh):
    by_row = P("section", "rows", None, None)
    gain = P("section", None, None)
    cross = P("rows", None, "section")
    head = P("rows", "section")
    weights = (by_row,) * 6 + (gain,) * 3 + (cross,) * 3 + (head,) * 3 + (P(),) * 3
    tokens = P("section", None, "rows", None)
    return jax.shard_map(
        local,
        mesh=mesh,
        in_specs=(tokens, P(None, None, "rows"), P(None, "rows")) + weights,
        out_specs=(tokens, P()) + weights,
        check_vma=False,
    )
```

```python
import functools

import jax
import jax.numpy as jnp
from jax import lax
from jax.experimental import pallas as pl
from jax.experimental.pallas import tpu as pltpu
from jax.sharding import PartitionSpec as P

HD = 64
STEP = 10
PAIR = 2 * HD
BLOCKS = 16
VMEM_BYTES = 52 * 1024 * 1024

bf16 = jnp.bfloat16
f32 = jnp.float32
masked_value = -1000000000.0
scale = HD ** (-0.5)


def dot(a, b):
    return lax.dot_general(a, b, (((1,), (0,)), ((), ())), preferred_element_type=f32)


def dot_last(a, b):
    return lax.dot_general(a, b, (((1,), (1,)), ((), ())), preferred_element_type=f32)


def dot_rows(a, b):
    return lax.dot_general(a, b, (((0,), (0,)), ((), ())), preferred_element_type=f32)


def unit_rows(v):
    r = lax.rsqrt(jnp.mean(v * v, axis=-1, keepdims=True) + 1e-06)
    return r, v * r


def norm_back(v, gain, up):
    r, n = unit_rows(v)
    g = up * gain
    back = r * (g - n * jnp.mean(g * n, axis=-1, keepdims=True))
    return back, jnp.sum(up * n, axis=0, keepdims=True)


def gelu_parts(x):
    c = 0.7978845608028654
    t = jnp.tanh(c * (x + 0.044715 * (x * x * x)))
    act = 0.5 * x * (1.0 + t)
    slope = 0.5 * (1.0 + t) + 0.5 * x * (1.0 - t * t) * (c * (1.0 + 3.0 * 0.044715 * (x * x)))
    return act, slope


def low_half(length):
    return lax.broadcasted_iota(jnp.int32, (length, PAIR), 1) < HD


def stack_pair(m, low):
    zero = jnp.zeros_like(m)
    return jnp.concatenate([jnp.where(low, m, zero), jnp.where(low, zero, m)], axis=0)


def allowed_twice(cnt_ref, s, length):
    row = lax.broadcasted_iota(jnp.int32, (length, length), 0)
    col = lax.broadcasted_iota(jnp.int32, (length, length), 1)
    limit = jnp.where(cnt_ref[0] == 1, row + 1, cnt_ref[1 + s])
    one = jnp.where(col < limit, 1, 0)
    return jnp.concatenate([one, one], axis=0) == 1


def soft_pair(q2, k, allowed):
    s = dot_last(q2, k) * scale
    s = jnp.where(allowed, s, masked_value)
    e = jnp.exp(s - jnp.max(s, axis=-1, keepdims=True))
    return e / jnp.sum(e, axis=-1, keepdims=True)


def attend_fwd_kernel(cross, length, cnt_ref, x_ref, gain_ref, *refs):
    if cross:
        src_ref, w_ref, n_ref, qkv_ref, o_ref, y_ref = refs
    else:
        w_ref, n_ref, qkv_ref, o_ref, y_ref = refs
    inner = w_ref.shape[0] // 4
    x = x_ref[...].astype(f32)
    n = (unit_rows(x)[1] * gain_ref[...]).astype(bf16)
    n_ref[...] = n
    if cross:
        qkv_ref[:, :inner] = dot_last(n, w_ref[:inner, :]).astype(bf16)
        qkv_ref[:, inner:] = dot_last(src_ref[...], w_ref[inner : 3 * inner, :]).astype(bf16)
    else:
        qkv_ref[...] = dot_last(n, w_ref[: 3 * inner, :]).astype(bf16)
    low = low_half(length)
    for s in range(x.shape[0] // length):
        allowed = allowed_twice(cnt_ref, s, length)
        rows = slice(s * length, (s + 1) * length)
        for h in range(inner // PAIR):
            cols = [slice(j * inner + h * PAIR, j * inner + (h + 1) * PAIR) for j in range(3)]
            q2 = stack_pair(qkv_ref[rows, cols[0]], low)
            p = soft_pair(q2, qkv_ref[rows, cols[1]], allowed).astype(bf16)
            wide = jnp.concatenate([p[:length], p[length:]], axis=1)
            o_ref[rows, cols[0]] = dot(wide, stack_pair(qkv_ref[rows, cols[2]], low)).astype(bf16)
    y_ref[...] = x + dot(o_ref[...], w_ref[3 * inner :, :])


def attend_fwd(counts, x, gain, w, length, source=None):
    t, d = x.shape
    inner = w.shape[0] // 4
    ins = [counts, x, gain] + ([] if source is None else [source]) + [w]
    vm = pl.BlockSpec(memory_space=pltpu.VMEM)
    return pl.pallas_call(
        functools.partial(attend_fwd_kernel, source is not None, length),
        out_shape=(
            jax.ShapeDtypeStruct((t, d), bf16),
            jax.ShapeDtypeStruct((t, 3 * inner), bf16),
            jax.ShapeDtypeStruct((t, inner), bf16),
            jax.ShapeDtypeStruct((t, d), f32),
        ),
        in_specs=[pl.BlockSpec(memory_space=pltpu.SMEM)] + [vm] * (len(ins) - 1),
        out_specs=(vm,) * 4,
        compiler_params=pltpu.CompilerParams(vmem_limit_bytes=VMEM_BYTES),
        cost_estimate=pl.CostEstimate(
            flops=2 * t * d * inner * 4 + 8 * t * length * inner,
            bytes_accessed=w.size * 2 + t * d * 10,
            transcendentals=t * length * 6,
        ),
    )(*ins)


def attend_bwd_kernel(cross, length, cnt_ref, x_ref, gain_ref, gy_ref, qkv_ref, w_ref, *refs):
    if cross:
        ga_ref, dqkv_ref, gx_ref, gg_ref, gs_ref, do_ref = refs
    else:
        ga_ref, dqkv_ref, gx_ref, gg_ref, do_ref = refs
    inner = w_ref.shape[0] // 4
    ga = gy_ref[...].astype(bf16)
    ga_ref[...] = ga
    do_ref[...] = dot_last(ga, w_ref[3 * inner :, :]).astype(bf16)
    low = low_half(length)
    for s in range(ga.shape[0] // length):
        allowed = allowed_twice(cnt_ref, s, length)
        rows = slice(s * length, (s + 1) * length)
        for h in range(inner // PAIR):
            cols = [slice(j * inner + h * PAIR, j * inner + (h + 1) * PAIR) for j in range(3)]
            q2 = stack_pair(qkv_ref[rows, cols[0]], low)
            k = qkv_ref[rows, cols[1]]
            p = soft_pair(q2, k, allowed)
            do2 = stack_pair(do_ref[rows, cols[0]], low)
            dp = dot_last(do2, qkv_ref[rows, cols[2]])
            ds = p * (dp - jnp.sum(dp * p, axis=-1, keepdims=True))
            ds = jnp.where(allowed, ds, 0.0).astype(bf16)
            wide = jnp.concatenate([ds[:length], ds[length:]], axis=1)
            dqkv_ref[rows, cols[0]] = (dot(wide, stack_pair(k, low)) * scale).astype(bf16)
            dqkv_ref[rows, cols[1]] = (dot_rows(ds, q2) * scale).astype(bf16)
            dqkv_ref[rows, cols[2]] = dot_rows(p.astype(bf16), do2).astype(bf16)
    if cross:
        up = dot(dqkv_ref[:, :inner], w_ref[:inner, :])
        gs_ref[...] = dot(dqkv_ref[:, inner:], w_ref[inner : 3 * inner, :]).astype(bf16)
    else:
        up = dot(dqkv_ref[...], w_ref[: 3 * inner, :])
    back, gg_ref[...] = norm_back(x_ref[...].astype(f32), gain_ref[...], up)
    gx_ref[...] = gy_ref[...] + back


def attend_bwd(counts, x, gain, gy, qkv, w, length, cross=False):
    t, d = x.shape
    inner = w.shape[0] // 4
    vm = pl.BlockSpec(memory_space=pltpu.VMEM)
    outs = [
        jax.ShapeDtypeStruct((t, d), bf16),
        jax.ShapeDtypeStruct((t, 3 * inner), bf16),
        jax.ShapeDtypeStruct((t, d), f32),
        jax.ShapeDtypeStruct((1, d), f32),
    ]
    if cross:
        outs.append(jax.ShapeDtypeStruct((t, d), bf16))
    return pl.pallas_call(
        functools.partial(attend_bwd_kernel, cross, length),
        out_shape=tuple(outs),
        in_specs=[pl.BlockSpec(memory_space=pltpu.SMEM)] + [vm] * 5,
        out_specs=(vm,) * len(outs),
        scratch_shapes=[pltpu.VMEM((t, inner), bf16)],
        compiler_params=pltpu.CompilerParams(vmem_limit_bytes=VMEM_BYTES),
        cost_estimate=pl.CostEstimate(
            flops=2 * t * d * inner * 4 + 20 * t * length * inner,
            bytes_accessed=w.size * 2 + t * d * 16,
            transcendentals=t * length * 6,
        ),
    )(counts, x, gain, gy, qkv, w)


def feed_fwd_kernel(y_ref, g_in_ref, g_out_ref, w_ref, n_ref, gu_ref, y2_ref, f_ref):
    i = pl.program_id(0)
    f = w_ref.shape[1] // 3

    @pl.when(i == 0)
    def _():
        y = y_ref[...]
        n_ref[...] = (unit_rows(y)[1] * g_in_ref[...]).astype(bf16)
        y2_ref[...] = y

    gu = dot_last(n_ref[...], w_ref[0, : 2 * f, :])
    gu_ref[0] = gu
    hidden = (gelu_parts(gu[:, :f])[0] * gu[:, f:]).astype(bf16)
    y2_ref[...] += dot(hidden, w_ref[0, 2 * f :, :])

    @pl.when(i == pl.num_programs(0) - 1)
    def _():
        f_ref[...] = (unit_rows(y2_ref[...])[1] * g_out_ref[...]).astype(bf16)


def feed_fwd(y, gain_in, gain_out, w):
    t, d = y.shape
    nb, rows, _ = w.shape
    f = rows // 3
    whole = lambda *shape: pl.BlockSpec(shape, lambda i: (0,) * len(shape))
    part = lambda *shape: pl.BlockSpec((1,) + shape, lambda i: (i, 0, 0))
    return pl.pallas_call(
        feed_fwd_kernel,
        grid=(nb,),
        out_shape=(
            jax.ShapeDtypeStruct((t, d), bf16),
            jax.ShapeDtypeStruct((nb, t, 2 * f), f32),
            jax.ShapeDtypeStruct((t, d), f32),
            jax.ShapeDtypeStruct((t, d), bf16),
        ),
        in_specs=[whole(t, d), whole(1, d), whole(1, d), part(rows, d)],
        out_specs=(whole(t, d), part(t, 2 * f), whole(t, d), whole(t, d)),
        compiler_params=pltpu.CompilerParams(vmem_limit_bytes=VMEM_BYTES),
        cost_estimate=pl.CostEstimate(
            flops=2 * t * d * rows * nb,
            bytes_accessed=w.size * 2 + t * d * 12 + nb * t * f * 8,
            transcendentals=nb * t * f,
        ),
    )(y, gain_in, gain_out, w)


def feed_bwd_kernel(emit, up_ref, y_ref, y2_ref, g_in_ref, g_out_ref, gu_ref, w_ref, *refs):
    if emit:
        gf_ref, gy_ref, gg_ref, dgu_ref, hid_ref, last_ref = refs
    else:
        gf_ref, gy_ref, gg_ref, last_ref = refs
    i = pl.program_id(0)
    f = w_ref.shape[1] // 3

    @pl.when(i == 0)
    def _():
        back, gain_grad = norm_back(y2_ref[...], g_out_ref[...], up_ref[...].astype(f32))
        gg_ref[1:2, :] = gain_grad
        last_ref[...] = back
        gf_ref[...] = back.astype(bf16)
        gy_ref[...] = jnp.zeros_like(gy_ref)

    gh = dot_last(gf_ref[...], w_ref[0, 2 * f :, :])
    act, slope = gelu_parts(gu_ref[0, :, :f])
    u = gu_ref[0, :, f:]
    dg = (gh * u * slope).astype(bf16)
    du = (gh * act).astype(bf16)
    if emit:
        dgu_ref[0, :, :f] = dg
        dgu_ref[0, :, f:] = du
        hid_ref[0] = (act * u).astype(bf16)
    gy_ref[...] += dot(dg, w_ref[0, :f, :]) + dot(du, w_ref[0, f : 2 * f, :])

    @pl.when(i == pl.num_programs(0) - 1)
    def _():
        back, gain_grad = norm_back(y_ref[...], g_in_ref[...], gy_ref[...])
        gg_ref[0:1, :] = gain_grad
        gy_ref[...] = last_ref[...] + back


def feed_bwd(up, y, y2, gain_in, gain_out, gu, w, emit):
    t, d = y.shape
    nb, rows, _ = w.shape
    f = rows // 3
    whole = lambda *shape: pl.BlockSpec(shape, lambda i: (0,) * len(shape))
    part = lambda *shape: pl.BlockSpec((1,) + shape, lambda i: (i, 0, 0))
    outs = [
        jax.ShapeDtypeStruct((t, d), bf16),
        jax.ShapeDtypeStruct((t, d), f32),
        jax.ShapeDtypeStruct((2, d), f32),
    ]
    specs = [whole(t, d), whole(t, d), whole(2, d)]
    if emit:
        outs += [
            jax.ShapeDtypeStruct((nb, t, 2 * f), bf16),
            jax.ShapeDtypeStruct((nb, t, f), bf16),
        ]
        specs += [part(t, 2 * f), part(t, f)]
    return pl.pallas_call(
        functools.partial(feed_bwd_kernel, emit),
        grid=(nb,),
        out_shape=tuple(outs),
        in_specs=[whole(t, d)] * 3 + [whole(1, d)] * 2 + [part(t, 2 * f), part(rows, d)],
        out_specs=tuple(specs),
        scratch_shapes=[pltpu.VMEM((t, d), f32)],
        compiler_params=pltpu.CompilerParams(vmem_limit_bytes=VMEM_BYTES),
        cost_estimate=pl.CostEstimate(
            flops=2 * t * d * rows * nb,
            bytes_accessed=w.size * 2 + t * d * 18 + nb * t * f * 8,
            transcendentals=nb * t * f,
        ),
    )(up, y, y2, gain_in, gain_out, gu, w)


def head_kernel(length, cnt_ref, f_ref, w_ref, target_ref, gl_ref, up_ref, loss_ref):
    logits = dot_last(f_ref[...], w_ref[...])
    top = jnp.max(logits, axis=-1, keepdims=True)
    log_total = top + jnp.log(jnp.sum(jnp.exp(logits - top), axis=-1, keepdims=True))
    hit = lax.broadcasted_iota(jnp.int32, logits.shape, 1) == target_ref[...]
    picked = jnp.sum(jnp.where(hit, logits, 0.0), axis=-1, keepdims=True)
    probs = jnp.exp(logits - log_total) - jnp.where(hit, 1.0, 0.0)
    total = jnp.zeros((1, 1), f32)
    for s in range(logits.shape[0] // length):
        rows = slice(s * length, (s + 1) * length)
        count = cnt_ref[s]
        valid = lax.broadcasted_iota(jnp.int32, (length, 1), 0) < count
        total += jnp.sum(
            jnp.where(valid, log_total[rows] - picked[rows], 0.0), axis=0, keepdims=True
        )
        gl_ref[rows, :] = jnp.where(valid, probs[rows], 0.0).astype(bf16)
    loss_ref[...] = total
    up_ref[...] = dot(gl_ref[...], w_ref[...])


def head_loss(counts, final, w, target, length):
    t, d = final.shape
    v = w.shape[0]
    vm = pl.BlockSpec(memory_space=pltpu.VMEM)
    return pl.pallas_call(
        functools.partial(head_kernel, length),
        out_shape=(
            jax.ShapeDtypeStruct((t, v), bf16),
            jax.ShapeDtypeStruct((t, d), f32),
            jax.ShapeDtypeStruct((1, 1), f32),
        ),
        in_specs=[pl.BlockSpec(memory_space=pltpu.SMEM), vm, vm, vm],
        out_specs=(vm,) * 3,
        compiler_params=pltpu.CompilerParams(vmem_limit_bytes=VMEM_BYTES),
        cost_estimate=pl.CostEstimate(
            flops=4 * t * d * v, bytes_accessed=w.size * 2 + t * d * 6, transcendentals=t * v * 2
        ),
    )(counts, final, w, target)


def tail_kernel(
    tiny_ref, gf_ref, lefts_ref, n1_ref, ga_ref, w_ref, n_all_ref,
    feed_ref, attn_ref, total_ref,
    shards, n_buf, part, from_core, four, from_y, from_far, from_near, from_cross, from_out, cross_out,
    ag_send, ag_recv, rs_send, rs_recv, n_sem,
):
    me = lax.axis_index("rows")
    z, y, c = me // 4, (me // 2) % 2, me % 2
    high = z // 2
    inner = (z + high) % 2
    t = gf_ref.shape[0]
    f = w_ref.shape[0] // 3
    core_peer, y_peer = me + 1 - 2 * c, me + 2 - 4 * y
    toward = me + 4 - 8 * high
    across = me + 4 - 8 * high
    outward = me - 4 + 8 * high

    def remote(src, dst, send, recv, device):
        return pltpu.make_async_remote_copy(
            src_ref=src, dst_ref=dst, send_sem=send, recv_sem=recv,
            device_id={"rows": device}, device_id_type=pl.DeviceIdType.MESH,
        )

    barrier = pltpu.get_barrier_semaphore()

    def greet(device):
        pl.semaphore_signal(
            barrier, inc=1, device_id={"rows": device}, device_id_type=pl.DeviceIdType.MESH
        )

    greet(core_peer)
    greet(y_peer)
    greet(toward)

    @pl.when(inner == 1)
    def _():
        greet(outward)

    pl.semaphore_wait(barrier, 3 + inner)

    def piece(p):
        odd = p % 2
        j = jnp.where(p == 0, 0, jnp.where(p == 7, 3, jnp.where(odd == 1, (p + 1) // 2, p // 2 - 1)))
        other = jnp.where(p == 0, 0, jnp.where(p == 7, 1, 1 - odd))
        first, second, third = z + 1 - 2 * (z % 2), 2 - high, 3 - 3 * high
        zz = jnp.where(j == 0, z, jnp.where(j == 1, first, jnp.where(j == 2, second, third)))
        yy = y + other - 2 * other * y
        return zz, yy, other

    def shard_copy(kind, p, s, device):
        return remote(shards.at[s], shards.at[s], ag_send.at[kind, p], ag_recv.at[s], device)

    def each_send(p, zz, yy, other, act):
        s = 4 * zz + 2 * yy + c

        @pl.when((other == 0) & (zz <= z) & (z < 3))
        def _():
            act(shard_copy(0, p, s, me + 4))

        @pl.when((other == 0) & (zz >= z) & (z > 0))
        def _():
            act(shard_copy(1, p, s, me - 4))

        @pl.when(other == 0)
        def _():
            act(shard_copy(2, p, s, y_peer))

        act(shard_copy(3, p, s, core_peer))

    def n_copy(p):
        zz, yy, _ = piece(p)
        rows = pl.ds((2 * zz + yy) * (2 * t), 2 * t)
        slot = p % 2
        return pltpu.make_async_copy(n_all_ref.at[rows], n_buf.at[slot], n_sem.at[slot])

    n_copy(0).start()
    shards[me, :t, :] = gf_ref[...]
    tiny = tiny_ref[...]
    tiny_high = tiny.astype(bf16)
    tiny_low = (tiny - tiny_high.astype(f32)).astype(bf16)
    shards[me, t:, :] = jnp.concatenate([tiny_high, tiny_low], axis=0)
    each_send(0, z, y, 0, lambda copy: copy.start())

    blocks, per = part.shape[1:3]
    row = lax.broadcasted_iota(jnp.int32, (blocks * per, n1_ref.shape[1]), 0)
    from_mixed = row % per >= per // 4 * 3

    def half_sums(half):
        left = lefts_ref[half]
        both = jnp.where(from_mixed, dot(left, ga_ref[...]), dot(left, n1_ref[...]))
        return both.reshape(blocks, per, -1)

    part[0] = half_sums(1 - c).astype(bf16)
    to_core = remote(part.at[0], from_core, rs_send.at[0], rs_recv.at[0], core_peer)
    to_core.start()
    own_half = half_sums(c)
    to_core.wait_recv()
    part[1] = (own_half + from_core[...].astype(f32)).astype(bf16)
    quarter = blocks // 2
    to_y = remote(
        part.at[1, pl.ds((1 - y) * quarter, quarter)], from_y, rs_send.at[1], rs_recv.at[1], y_peer
    )
    to_y.start()

    far = 2 - 2 * high
    far_copy = remote(four.at[pl.ds(far, 2)], from_far, rs_send.at[2], rs_recv.at[2], toward)
    near_copy = remote(four.at[1 + high], from_near, rs_send.at[3], rs_recv.at[3], toward)
    cross_copy = remote(four.at[pl.ds(far, 2)], from_cross, rs_send.at[4], rs_recv.at[4], across)
    out_copy = remote(cross_out, from_out, rs_send.at[5], rs_recv.at[5], outward)

    def stage_y():
        to_y.wait_recv()
        mine = part[1, pl.ds(y * quarter, quarter)].astype(f32)
        four[...] = (mine + from_y[...].astype(f32)).astype(bf16)

        @pl.when(inner == 0)
        def _():
            far_copy.start()
            near_copy.start()

    def stage_cross():
        @pl.when(inner == 1)
        def _():
            far_copy.wait_recv()
            both = four[pl.ds(far, 2)].astype(f32) + from_far[...].astype(f32)
            four[pl.ds(far, 2)] = both.astype(bf16)
            cross_copy.start()

    def stage_out():
        @pl.when(inner == 1)
        def _():
            near_copy.wait_recv()
            cross_copy.wait_recv()
            attn_ref[...] = (
                four[z].astype(f32) + from_near[...].astype(f32) + from_cross[1 - high].astype(f32)
            )
            out = four[3 * high].astype(f32) + from_cross[high].astype(f32)
            cross_out[...] = out.astype(bf16)
            out_copy.start()

    def stage_end():
        @pl.when(inner == 0)
        def _():
            out_copy.wait_recv()
            attn_ref[...] = four[z].astype(f32) + from_out[...].astype(f32)

    feed_ref[...] = jnp.zeros_like(feed_ref)

    def visit(p, carry):
        zz, yy, other = piece(p)
        pair = 4 * zz + 2 * yy

        @pl.when(p > 0)
        def _():
            shard_copy(0, p, pair + c, me).wait_recv()
            each_send(p, zz, yy, other, lambda copy: copy.start())

        shard_copy(0, p, pair + 1 - c, me).wait_recv()

        @pl.when(p < 7)
        def _():
            n_copy(p + 1).start()

        n_copy(p).wait()
        n_rows = n_buf[p % 2]
        g_rows = jnp.concatenate([shards[pair, :t, :], shards[pair + 1, :t, :]], axis=0)
        gu = dot_last(n_rows, w_ref[: 2 * f, :])
        gh = dot_last(g_rows, w_ref[2 * f :, :])
        act, slope = gelu_parts(gu[:, :f])
        up = gu[:, f:]
        dg = (gh * up * slope).astype(bf16)
        du = (gh * act).astype(bf16)
        hid = (act * up).astype(bf16)
        feed_ref[:f, :] += dot_rows(dg, n_rows)
        feed_ref[f : 2 * f, :] += dot_rows(du, n_rows)
        feed_ref[2 * f :, :] += dot_rows(hid, g_rows)
        pl.when(p == 3)(stage_y)
        pl.when(p == 4)(stage_cross)
        pl.when(p == 5)(stage_out)
        pl.when(p == 6)(stage_end)
        return carry

    lax.fori_loop(0, 8, visit, 0)

    def add_tiny(s, total):
        both = shards[s, t:, :].astype(f32)
        return total + both[:8] + both[8:]

    total_ref[...] = lax.fori_loop(0, 16, add_tiny, jnp.zeros(total_ref.shape, f32))

    def settle(p, carry):
        zz, yy, other = piece(p)
        each_send(p, zz, yy, other, lambda copy: copy.wait_send())
        return carry

    lax.fori_loop(0, 8, settle, 0)
    to_core.wait_send()
    to_y.wait_send()

    @pl.when(inner == 0)
    def _():
        far_copy.wait_send()
        near_copy.wait_send()

    @pl.when(inner == 1)
    def _():
        cross_copy.wait_send()
        out_copy.wait_send()


def tail(tiny, gf, lefts, n1, ga, w_own, n_all):
    t, d = gf.shape
    rows = w_own.shape[0]
    blocks = 8
    per = lefts.shape[1] // blocks
    vm = pl.BlockSpec(memory_space=pltpu.VMEM)
    return pl.pallas_call(
        tail_kernel,
        out_shape=(
            jax.ShapeDtypeStruct((rows, d), f32),
            jax.ShapeDtypeStruct((per, d), f32),
            jax.ShapeDtypeStruct(tiny.shape, f32),
        ),
        in_specs=[vm] * 6 + [pl.BlockSpec(memory_space=pl.ANY)],
        out_specs=(vm,) * 3,
        scratch_shapes=[
            pltpu.VMEM((16, t + 16, d), bf16),
            pltpu.VMEM((2, 2 * t, d), bf16),
            pltpu.VMEM((2, blocks, per, d), bf16),
            pltpu.VMEM((blocks, per, d), bf16),
            pltpu.VMEM((4, per, d), bf16),
            pltpu.VMEM((4, per, d), bf16),
            pltpu.VMEM((2, per, d), bf16),
            pltpu.VMEM((per, d), bf16),
            pltpu.VMEM((2, per, d), bf16),
            pltpu.VMEM((per, d), bf16),
            pltpu.VMEM((per, d), bf16),
            pltpu.SemaphoreType.DMA((4, 8)),
            pltpu.SemaphoreType.DMA((16,)),
            pltpu.SemaphoreType.DMA((6,)),
            pltpu.SemaphoreType.DMA((6,)),
            pltpu.SemaphoreType.DMA((2,)),
        ],
        compiler_params=pltpu.CompilerParams(
            vmem_limit_bytes=VMEM_BYTES, collective_id=0, has_side_effects=True
        ),
        cost_estimate=pl.CostEstimate(
            flops=2 * t * 16 * d * rows * 2, bytes_accessed=16 * t * d * 4, transcendentals=16 * t * rows
        ),
    )(tiny, gf, lefts, n1, ga, w_own, n_all)


def front_kernel(
    length, cnt_ref, order_ref, x_ref, g_attn_ref, g_feed_ref, g_final_ref,
    attn_own, feed_own, half_own,
    attn_all, feed_all, first_all, second_all,
    n1_ref, qkv_ref, mixed_ref, y1_ref, n2_ref, gu_ref, y2_ref, enc_ref, arrived_ref,
    w_attn, w_feed, place, wide_buf, first_own,
    send_sem, recv_sem, own_sem, load_sem, x_send, x_recv,
):
    section = lax.axis_index("section")
    me = lax.axis_index("rows")
    z, y, c = me // 4, (me // 2) % 2, me % 2
    core_peer, y_peer = me + 1 - 2 * c, me + 2 - 4 * y
    mesh_id = pl.DeviceIdType.MESH
    inner = mixed_ref.shape[1]
    f = feed_own.shape[0] // 3

    barrier = pltpu.get_barrier_semaphore()

    def greet(where):
        pl.semaphore_signal(barrier, inc=1, device_id=where, device_id_type=mesh_id)

    greet({"rows": core_peer})
    greet({"rows": y_peer})
    greet({"section": 1 - section})

    @pl.when(z > 0)
    def _():
        greet({"rows": me - 4})

    @pl.when(z < 3)
    def _():
        greet({"rows": me + 4})

    own_copies = [
        pltpu.make_async_copy(own, whole.at[me], own_sem.at[k])
        for k, (own, whole) in enumerate(
            [(attn_own, attn_all), (feed_own, feed_all), (half_own, second_all)]
        )
    ]
    own_copies[0].start()
    own_copies[1].start()

    @pl.when(section == 1)
    def _():
        own_copies[2].start()

    pl.semaphore_wait(barrier, 4 + (z + z // 2) % 2)

    def remote(src, dst, send, recv, where):
        return pltpu.make_async_remote_copy(
            src_ref=src, dst_ref=dst, send_sem=send, recv_sem=recv,
            device_id=where, device_id_type=mesh_id,
        )

    def piece(route, p):
        odd = p % 2
        if route == 1:
            j = jnp.where(
                p == 0, 0, jnp.where(p == 7, 3, jnp.where(odd == 1, (p + 1) // 2, p // 2 - 1))
            )
            other = jnp.where(p == 0, 0, jnp.where(p == 7, 1, 1 - odd))
        else:
            j, other = p // 2, odd
        first, second, third = z + 1 - 2 * (z % 2), 2 - z // 2, 3 - 3 * (z // 2)
        zz = jnp.where(j == 0, z, jnp.where(j == 1, first, jnp.where(j == 2, second, third)))
        yy = y + other - 2 * other * y
        return zz, yy, other

    def block_copy(k, whole, kind, p, s, where, src=None):
        return remote(
            whole.at[s] if src is None else src,
            whole.at[s], send_sem.at[k, kind, p], recv_sem.at[k, s], where,
        )

    def each_send(k, whole, route, p, act, src=None):
        zz, yy, other = piece(route, p)
        s = 4 * zz + 2 * yy + c
        along_z = (other == 0) if route == 1 else (p >= 0)
        over_y = (other == 0) if route == 1 else (p == 0)

        @pl.when(along_z & (zz <= z) & (z < 3))
        def _():
            act(block_copy(k, whole, 0, p, s, {"rows": me + 4}, src))

        @pl.when(along_z & (zz >= z) & (z > 0))
        def _():
            act(block_copy(k, whole, 1, p, s, {"rows": me - 4}, src))

        @pl.when(over_y)
        def _():
            act(block_copy(k, whole, 2, p, s, {"rows": y_peer}, src))

        act(block_copy(k, whole, 3, p, s, {"rows": core_peer}, src))

    def begin(k, whole, route, own):
        each_send(k, whole, route, 0, lambda copy: copy.start(), own)

    def arrive(k, whole, route, p):
        zz, yy, _ = piece(route, p)
        pair = 4 * zz + 2 * yy

        @pl.when(p > 0)
        def _():
            block_copy(k, whole, 0, p, pair + c, {"rows": me}).wait_recv()
            each_send(k, whole, route, p, lambda copy: copy.start())

        block_copy(k, whole, 0, p, pair + 1 - c, {"rows": me}).wait_recv()
        return pair

    def gather_all(k, whole, route):
        def step(p, carry):
            arrive(k, whole, route, p)
            return carry

        lax.fori_loop(0, 8, step, 0)

    def settle(k, whole, route):
        def step(p, carry):
            each_send(k, whole, route, p, lambda copy: copy.wait_send())
            return carry

        lax.fori_loop(0, 8, step, 0)

    half_copy = remote(half_own, first_own, x_send.at[0], x_recv.at[0], {"section": 1 - section})
    enc_copy = remote(enc_ref, arrived_ref, x_send.at[1], x_recv.at[1], {"section": 1 - section})

    begin(0, attn_all, 2, attn_own)

    @pl.when(section == 0)
    def _():
        half_copy.start()

    @pl.when(section == 1)
    def _():
        begin(3, second_all, 2, half_own)

    begin(1, feed_all, 1, feed_own)

    @pl.when(section == 1)
    def _():
        half_copy.wait_recv()
        begin(2, first_all, 1, first_own)
        own_half = pltpu.make_async_copy(first_own, first_all.at[me], own_sem.at[3])
        own_half.start()
        own_half.wait()

    row = lax.broadcasted_iota(jnp.int32, place.shape, 0)
    place[...] = jnp.where(row == order_ref[...], 1.0, 0.0).astype(bf16)
    x = x_ref[...].astype(f32)
    n1_ref[...] = (unit_rows(x)[1] * g_attn_ref[...]).astype(bf16)

    gather_all(0, attn_all, 2)

    @pl.when(section == 1)
    def _():
        gather_all(3, second_all, 2)
        gather_all(2, first_all, 1)

    own_copies[0].wait()
    load = pltpu.make_async_copy(attn_all, w_attn, load_sem.at[0])
    load.start()
    load.wait()
    w = w_attn[...].reshape(4 * inner, -1)
    wide_buf[...] = dot_last(n1_ref[...], w).astype(bf16)
    qkv_ref[...] = dot(wide_buf[...], place[:, : 3 * inner]).astype(bf16)
    low = low_half(length)
    for s in range(x_ref.shape[0] // length):
        allowed = allowed_twice(cnt_ref, s, length)
        rows = slice(s * length, (s + 1) * length)
        for h in range(inner // PAIR):
            cols = [slice(j * inner + h * PAIR, j * inner + (h + 1) * PAIR) for j in range(3)]
            q2 = stack_pair(qkv_ref[rows, cols[0]], low)
            p = soft_pair(q2, qkv_ref[rows, cols[1]], allowed).astype(bf16)
            wide = jnp.concatenate([p[:length], p[length:]], axis=1)
            mixed_ref[rows, cols[0]] = dot(wide, stack_pair(qkv_ref[rows, cols[2]], low)).astype(bf16)
    wide_buf[...] = dot_last(mixed_ref[...], place[:, 3 * inner :]).astype(bf16)
    y1_ref[...] = x_ref[...].astype(f32) + dot(wide_buf[...], w_attn[...].reshape(4 * inner, -1))
    y2_ref[...] = y1_ref[...]
    n2_ref[...] = (unit_rows(y1_ref[...])[1] * g_feed_ref[...]).astype(bf16)
    own_copies[1].wait()

    def feed_step(p, carry):
        pair = arrive(1, feed_all, 1, p)

        @pl.when(section == 0)
        def _():
            blocks = pltpu.make_async_copy(feed_all.at[pl.ds(pair, 2)], w_feed, load_sem.at[1])
            blocks.start()
            blocks.wait()
            for k in range(2):
                gu = dot_last(n2_ref[...], w_feed[k, : 2 * f, :])
                gu_ref[pair + k] = gu
                hidden = (gelu_parts(gu[:, :f])[0] * gu[:, f:]).astype(bf16)
                y2_ref[...] += dot(hidden, w_feed[k, 2 * f :, :])

        return carry

    lax.fori_loop(0, 8, feed_step, 0)

    @pl.when(section == 0)
    def _():
        enc_ref[...] = (unit_rows(y2_ref[...])[1] * g_final_ref[...]).astype(bf16)
        enc_copy.start()

    settle(0, attn_all, 2)
    settle(1, feed_all, 1)

    @pl.when(section == 1)
    def _():
        settle(2, first_all, 1)
        settle(3, second_all, 2)
        own_copies[2].wait()
        enc_copy.wait_recv()

    @pl.when(section == 0)
    def _():
        half_copy.wait_send()
        enc_copy.wait_send()


def front(counts, order, x, gain_attn, gain_feed, gain_final, attn_own, feed_own, half_own, length):
    t, d = x.shape
    attn_rows, feed_rows = attn_own.shape[0], feed_own.shape[0]
    inner = attn_rows * 4
    half_shape = (16,) + half_own.shape
    vm = pl.BlockSpec(memory_space=pltpu.VMEM)
    anywhere = pl.BlockSpec(memory_space=pl.ANY)
    return pl.pallas_call(
        functools.partial(front_kernel, length),
        out_shape=(
            jax.ShapeDtypeStruct((16, attn_rows, d), bf16),
            jax.ShapeDtypeStruct((16, feed_rows, d), bf16),
            jax.ShapeDtypeStruct(half_shape, bf16),
            jax.ShapeDtypeStruct(half_shape, bf16),
            jax.ShapeDtypeStruct((t, d), bf16),
            jax.ShapeDtypeStruct((t, 3 * inner), bf16),
            jax.ShapeDtypeStruct((t, inner), bf16),
            jax.ShapeDtypeStruct((t, d), f32),
            jax.ShapeDtypeStruct((t, d), bf16),
            jax.ShapeDtypeStruct((16, t, feed_rows // 3 * 2), f32),
            jax.ShapeDtypeStruct((t, d), f32),
            jax.ShapeDtypeStruct((t, d), bf16),
            jax.ShapeDtypeStruct((t, d), bf16),
        ),
        in_specs=[pl.BlockSpec(memory_space=pltpu.SMEM)] + [vm] * 5 + [anywhere] * 3,
        out_specs=(anywhere,) * 4 + (vm,) * 9,
        scratch_shapes=[
            pltpu.VMEM((16, attn_rows, d), bf16),
            pltpu.VMEM((2, feed_rows, d), bf16),
            pltpu.VMEM((4 * inner, 4 * inner), bf16),
            pltpu.VMEM((t, 4 * inner), bf16),
            pltpu.VMEM(half_own.shape, bf16),
            pltpu.SemaphoreType.DMA((4, 4, 8)),
            pltpu.SemaphoreType.DMA((4, 16)),
            pltpu.SemaphoreType.DMA((4,)),
            pltpu.SemaphoreType.DMA((2,)),
            pltpu.SemaphoreType.DMA((2,)),
            pltpu.SemaphoreType.DMA((2,)),
        ],
        compiler_params=pltpu.CompilerParams(
            vmem_limit_bytes=VMEM_BYTES, collective_id=1, has_side_effects=True
        ),
        cost_estimate=pl.CostEstimate(
            flops=2 * t * d * (feed_rows * 16 + 8 * inner),
            bytes_accessed=2 * 16 * (attn_rows + feed_rows) * d * 2,
            transcendentals=t * feed_rows * 6,
        ),
    )(counts, order, x, gain_attn, gain_feed, gain_final, attn_own, feed_own, half_own)


def adam_step(weight, first_moment, second_moment, gradient, step_rate, weight_decay):
    first_new = 0.9 * first_moment + 0.1 * gradient
    second_new = 0.999 * second_moment + 0.001 * gradient * gradient
    first_fix = 1.0 - 0.9**STEP
    second_fix = 1.0 - 0.999**STEP
    update = first_new / first_fix / (jnp.sqrt(second_new / second_fix) + 1e-08)
    return (first_new, second_new, weight - step_rate * (update + weight_decay * weight))


def kinds_first(gathered, n, kinds, per):
    d = gathered.shape[-1]
    return gathered.reshape(n, kinds, per, d).transpose(1, 0, 2, 3).reshape(kinds * n * per, d)


def owners_first(left, right, n):
    t, k, units = left.shape
    grad = jnp.einsum("tku,td->kud", left, right, preferred_element_type=f32)
    return grad.reshape(k, n, units // n, -1).transpose(1, 0, 2, 3)


def local(
    block_input,
    lengths,
    targets,
    attention_weight,
    attention_first,
    attention_second,
    feed_weight,
    feed_first,
    feed_second,
    norm_gain,
    gain_first,
    gain_second,
    cross_weight,
    cross_first,
    cross_second,
    head_weight,
    head_first,
    head_second,
    cross_gain,
    cross_gain_first,
    cross_gain_second,
):
    n = lax.axis_size("rows")
    is_encoder = lax.axis_index("section") == 0
    micro, length, d = block_input.shape[1:]
    t = micro * length
    per = attention_weight.shape[1]
    f = feed_weight.shape[1]
    inner = per * n

    attn_own = attention_weight[0].astype(bf16).transpose(1, 0, 2).reshape(4 * per, d)
    feed_own = feed_weight[0].astype(bf16).transpose(1, 0, 2)
    half_rows = jnp.concatenate(
        [cross_weight.astype(bf16).transpose(1, 0, 2), head_weight.astype(bf16)[None]], axis=0
    )

    gains = norm_gain[0]
    gain_attn, gain_feed, gain_final = gains[0:1], gains[1:2], gains[2:3]
    gain_cross = cross_gain[None]
    x = block_input[0].reshape(t, d)
    enc_counts = lengths[0, :, 0]
    dec_counts = lengths[1, :, 0]
    zero_one = jnp.zeros((1,), jnp.int32)
    self_counts = jnp.concatenate([jnp.where(is_encoder, 0, 1).astype(jnp.int32)[None], enc_counts])
    cross_counts = jnp.concatenate([zero_one, enc_counts])
    target_column = targets.reshape(t, 1)

    def blank(maker):
        return jax.tree.map(lambda a: jnp.zeros(a.shape, a.dtype), jax.eval_shape(maker))

    emit = n != BLOCKS
    if emit:
        attn_all = lax.all_gather(attn_own, "rows", axis=0, tiled=True)
        attn_w = kinds_first(attn_all, n, 4, per)
        feed_all = lax.all_gather(feed_own.reshape(3 * f, d), "rows", axis=0, tiled=True)
        feed_w = kinds_first(feed_all, n, 3, f).reshape(3, BLOCKS, -1, d)
        feed_w = feed_w.transpose(1, 0, 2, 3).reshape(BLOCKS, -1, d)
        other_half = lax.ppermute(half_rows, "section", [(0, 1)])
        extra_own = jnp.concatenate([other_half, half_rows], axis=-1).reshape(5 * per, d)
        extra_all = lax.all_gather(extra_own, "rows", axis=0, tiled=True)
        n1, qkv, mixed, y1 = attend_fwd(self_counts, x, gain_attn, attn_w, length)

        def enc_feed():
            return feed_fwd(y1, gain_feed, gain_final, feed_w)

        enc_state = lax.cond(is_encoder, enc_feed, lambda: blank(enc_feed))
        encoded = lax.ppermute(enc_state[3], "section", [(0, 1)])
    else:
        units = jnp.arange(4 * inner, dtype=jnp.int32).reshape(n, 4, per)
        order = units.transpose(1, 0, 2).reshape(1, 4 * inner)
        pad = -(5 * per) % 16
        half_own = jnp.pad(half_rows.reshape(5 * per, d // 2), ((0, pad), (0, 0)))
        outs = front(
            self_counts, order, x, gain_attn, gain_feed, gain_final,
            attn_own, feed_own.reshape(3 * f, d), half_own, length,
        )
        attn_all, feed_w, first_all, second_all, n1, qkv, mixed, y1 = outs[:8]
        enc_state, encoded = outs[8:12], outs[12]
        attn_w = kinds_first(attn_all, n, 4, per)
        extra_all = jnp.concatenate([first_all, second_all], axis=-1)[:, : 5 * per]
    extra_w = kinds_first(extra_all, n, 5, per)
    cross_w, head_w = extra_w[: 4 * inner], extra_w[4 * inner :]

    def dec_front():
        mc, cqkv, cmixed, z2 = attend_fwd(cross_counts, y1, gain_cross, cross_w, length, encoded)
        return feed_fwd(z2, gain_feed, gain_final, feed_w) + (mc, cqkv, cmixed, z2)

    def enc_pass():
        rest = jax.eval_shape(dec_front)[4:7]
        return tuple(enc_state) + tuple(jnp.zeros(a.shape, a.dtype) for a in rest) + (y1,)

    n2, gu, y2, final, mc, cqkv, cmixed, mid = lax.cond(is_encoder, enc_pass, dec_front)
    if not emit:
        n2_all = lax.all_gather(n2, "rows", axis=0, tiled=True)

    def dec_back():
        gl, up, loss = head_loss(dec_counts, final, head_w, target_column, length)
        feed_out = feed_bwd(up, mid, y2, gain_feed, gain_final, gu, feed_w, emit)
        ga_c, dqkv_c, gy1, gg_c, ge = attend_bwd(
            cross_counts, y1, gain_cross, feed_out[1], cqkv, cross_w, length, True
        )
        return (ge, gy1, feed_out[2], feed_out[0], *feed_out[3:], gl, ga_c, dqkv_c, gg_c, loss)

    back = lax.cond(is_encoder, lambda: blank(dec_back), dec_back)
    returned = lax.ppermute(back[0], "section", [(1, 0)])
    at = 6 if emit else 4
    gl, ga_c, dqkv_c, gg_c, loss = back[at:]

    if not emit:
        returned, n2_all = lax.optimization_barrier((returned, n2_all))

    def enc_back():
        feed_out = feed_bwd(returned, mid, y2, gain_feed, gain_final, gu, feed_w, emit)
        return (feed_out[1], feed_out[2], feed_out[0], *feed_out[3:])

    backs = lax.cond(is_encoder, enc_back, lambda: tuple(back[1:at]))
    gy1, gg_feed, gf = backs[:3]

    ga, dqkv, gx, gg_attn = attend_bwd(self_counts, x, gain_attn, gy1, qkv, attn_w, length)

    extra_part = jnp.concatenate(
        [
            owners_first(dqkv_c[:, None, :inner], mc, n),
            owners_first(dqkv_c[:, inner:].reshape(t, 2, inner), encoded, n),
            owners_first(cmixed[:, None], ga_c, n),
            owners_first(gl[:, None], final, n),
        ],
        axis=1,
    ).astype(bf16)
    if not emit:
        extra_part, gx = lax.optimization_barrier((extra_part, gx))
    extra_sum = lax.psum_scatter(
        extra_part.reshape(n * 5 * per, d), "rows", scatter_dimension=0, tiled=True
    )
    half = d // 2
    extra_first = lax.ppermute(extra_sum[:, :half], "section", [(1, 0)])
    extra_grad = jnp.where(is_encoder, extra_first, extra_sum[:, half:]).astype(f32)
    extra_grad = extra_grad.reshape(5, per, half)

    tiny = jnp.concatenate(
        [
            gg_attn,
            gg_feed,
            gg_c,
            jnp.broadcast_to(loss, (1, d)),
            jnp.zeros((3, d), f32),
        ],
        axis=0,
    )

    if emit:
        attn_part = jnp.concatenate(
            [
                owners_first(dqkv.reshape(t, 3, inner), n1, n),
                owners_first(mixed[:, None], ga, n),
            ],
            axis=1,
        ).astype(bf16)
        attn_sum = lax.psum_scatter(
            attn_part.reshape(n * 4 * per, d), "rows", scatter_dimension=0, tiled=True
        ).astype(f32)
        dgu, hid = backs[3], backs[4]
        nb, _, fb = hid.shape
        left = dgu.reshape(nb, t, 2, fb).transpose(1, 2, 0, 3).reshape(t, 2, nb * fb)
        hid = hid.transpose(1, 0, 2).reshape(t, 1, nb * fb)
        feed_part = jnp.concatenate(
            [owners_first(left, n2, n), owners_first(hid, gf, n)], axis=1
        ).astype(bf16)
        feed_grad = lax.psum_scatter(
            feed_part.reshape(n * 3 * f, d), "rows", scatter_dimension=0, tiled=True
        ).astype(f32)
        tiny_sum = jnp.sum(lax.all_gather(tiny, "rows", axis=0), axis=0)
    else:
        lefts = jnp.concatenate([dqkv, mixed], axis=1).reshape(t, 4, 4, 2, 2, per)
        lefts = lefts.transpose(4, 3, 2, 1, 5, 0).reshape(2, 8 * 4 * per, t)
        feed_grad, attn_sum, tiny_sum = tail(
            tiny, gf, lefts, n1, ga, feed_own.reshape(3 * f, d), n2_all
        )
    attn_grad = attn_sum.reshape(4, per, d).transpose(1, 0, 2)
    feed_grad = feed_grad.reshape(3, f, d).transpose(1, 0, 2)
    tiny_dec = lax.ppermute(tiny_sum[3:5], "section", [(1, 0)])
    tiny_dec = jnp.where(is_encoder, tiny_dec, tiny_sum[3:5])
    cross_gain_total = tiny_dec[0]
    loss_total = tiny_dec[1, 0]

    attention_new = adam_step(
        attention_weight, attention_first, attention_second, attn_grad[None], 0.05, 0.1
    )
    feed_new = adam_step(feed_weight, feed_first, feed_second, feed_grad[None], 0.05, 0.1)
    gain_new = adam_step(norm_gain, gain_first, gain_second, tiny_sum[None, 0:3], 0.5, 0.0)
    cross_new = adam_step(
        cross_weight, cross_first, cross_second, extra_grad[:4].transpose(1, 0, 2), 0.05, 0.1
    )
    head_new = adam_step(head_weight, head_first, head_second, extra_grad[4], 0.05, 0.1)
    cross_gain_new = adam_step(
        cross_gain, cross_gain_first, cross_gain_second, cross_gain_total, 0.5, 0.0
    )
    return (
        gx.reshape(1, micro, length, d),
        loss_total,
        *attention_new,
        *feed_new,
        *gain_new,
        *cross_new,
        *head_new,
        *cross_gain_new,
    )


def solution(mesh):
    by_row = P("section", "rows", None, None)
    gain = P("section", None, None)
    cross = P("rows", None, "section")
    head = P("rows", "section")
    weights = (by_row,) * 6 + (gain,) * 3 + (cross,) * 3 + (head,) * 3 + (P(),) * 3
    tokens = P("section", None, "rows", None)
    return jax.shard_map(
        local,
        mesh=mesh,
        in_specs=(tokens, P(None, None, "rows"), P(None, "rows")) + weights,
        out_specs=(tokens, P()) + weights,
        check_vma=False,
    )
```

```python
import functools

import jax
import jax.numpy as jnp
from jax import lax
from jax.experimental import pallas as pl
from jax.experimental.pallas import tpu as pltpu
from jax.sharding import PartitionSpec as P

HD = 64
STEP = 10
PAIR = 2 * HD
BLOCKS = 16
VMEM_BYTES = 52 * 1024 * 1024

bf16 = jnp.bfloat16
f32 = jnp.float32
masked_value = -1000000000.0
scale = HD ** (-0.5)


def dot(a, b):
    return lax.dot_general(a, b, (((1,), (0,)), ((), ())), preferred_element_type=f32)


def dot_last(a, b):
    return lax.dot_general(a, b, (((1,), (1,)), ((), ())), preferred_element_type=f32)


def dot_rows(a, b):
    return lax.dot_general(a, b, (((0,), (0,)), ((), ())), preferred_element_type=f32)


def unit_rows(v):
    r = lax.rsqrt(jnp.mean(v * v, axis=-1, keepdims=True) + 1e-06)
    return r, v * r


def norm_back(v, gain, up):
    r, n = unit_rows(v)
    g = up * gain
    back = r * (g - n * jnp.mean(g * n, axis=-1, keepdims=True))
    return back, jnp.sum(up * n, axis=0, keepdims=True)


def gelu_parts(x):
    c = 0.7978845608028654
    t = jnp.tanh(c * (x + 0.044715 * (x * x * x)))
    act = 0.5 * x * (1.0 + t)
    slope = 0.5 * (1.0 + t) + 0.5 * x * (1.0 - t * t) * (c * (1.0 + 3.0 * 0.044715 * (x * x)))
    return act, slope


def low_half(length):
    return lax.broadcasted_iota(jnp.int32, (length, PAIR), 1) < HD


def stack_pair(m, low):
    zero = jnp.zeros_like(m)
    return jnp.concatenate([jnp.where(low, m, zero), jnp.where(low, zero, m)], axis=0)


def allowed_twice(cnt_ref, s, length):
    row = lax.broadcasted_iota(jnp.int32, (length, length), 0)
    col = lax.broadcasted_iota(jnp.int32, (length, length), 1)
    limit = jnp.where(cnt_ref[0] == 1, row + 1, cnt_ref[1 + s])
    one = jnp.where(col < limit, 1, 0)
    return jnp.concatenate([one, one], axis=0) == 1


def soft_pair(q2, k, allowed):
    s = dot_last(q2, k) * scale
    s = jnp.where(allowed, s, masked_value)
    e = jnp.exp(s - jnp.max(s, axis=-1, keepdims=True))
    return e / jnp.sum(e, axis=-1, keepdims=True)


def attend_fwd_kernel(cross, length, cnt_ref, x_ref, gain_ref, *refs):
    if cross:
        src_ref, w_ref, n_ref, qkv_ref, o_ref, y_ref = refs
    else:
        w_ref, n_ref, qkv_ref, o_ref, y_ref = refs
    inner = w_ref.shape[0] // 4
    x = x_ref[...].astype(f32)
    n = (unit_rows(x)[1] * gain_ref[...]).astype(bf16)
    n_ref[...] = n
    if cross:
        qkv_ref[:, :inner] = dot_last(n, w_ref[:inner, :]).astype(bf16)
        qkv_ref[:, inner:] = dot_last(src_ref[...], w_ref[inner : 3 * inner, :]).astype(bf16)
    else:
        qkv_ref[...] = dot_last(n, w_ref[: 3 * inner, :]).astype(bf16)
    low = low_half(length)
    for s in range(x.shape[0] // length):
        allowed = allowed_twice(cnt_ref, s, length)
        rows = slice(s * length, (s + 1) * length)
        for h in range(inner // PAIR):
            cols = [slice(j * inner + h * PAIR, j * inner + (h + 1) * PAIR) for j in range(3)]
            q2 = stack_pair(qkv_ref[rows, cols[0]], low)
            p = soft_pair(q2, qkv_ref[rows, cols[1]], allowed).astype(bf16)
            wide = jnp.concatenate([p[:length], p[length:]], axis=1)
            o_ref[rows, cols[0]] = dot(wide, stack_pair(qkv_ref[rows, cols[2]], low)).astype(bf16)
    y_ref[...] = x + dot(o_ref[...], w_ref[3 * inner :, :])


def attend_fwd(counts, x, gain, w, length, source=None):
    t, d = x.shape
    inner = w.shape[0] // 4
    ins = [counts, x, gain] + ([] if source is None else [source]) + [w]
    vm = pl.BlockSpec(memory_space=pltpu.VMEM)
    return pl.pallas_call(
        functools.partial(attend_fwd_kernel, source is not None, length),
        out_shape=(
            jax.ShapeDtypeStruct((t, d), bf16),
            jax.ShapeDtypeStruct((t, 3 * inner), bf16),
            jax.ShapeDtypeStruct((t, inner), bf16),
            jax.ShapeDtypeStruct((t, d), f32),
        ),
        in_specs=[pl.BlockSpec(memory_space=pltpu.SMEM)] + [vm] * (len(ins) - 1),
        out_specs=(vm,) * 4,
        compiler_params=pltpu.CompilerParams(vmem_limit_bytes=VMEM_BYTES),
        cost_estimate=pl.CostEstimate(
            flops=2 * t * d * inner * 4 + 8 * t * length * inner,
            bytes_accessed=w.size * 2 + t * d * 10,
            transcendentals=t * length * 6,
        ),
    )(*ins)


def attend_bwd_kernel(cross, length, cnt_ref, x_ref, gain_ref, gy_ref, qkv_ref, w_ref, *refs):
    if cross:
        ga_ref, dqkv_ref, gx_ref, gg_ref, gs_ref, do_ref = refs
    else:
        ga_ref, dqkv_ref, gx_ref, gg_ref, do_ref = refs
    inner = w_ref.shape[0] // 4
    ga = gy_ref[...].astype(bf16)
    ga_ref[...] = ga
    do_ref[...] = dot_last(ga, w_ref[3 * inner :, :]).astype(bf16)
    low = low_half(length)
    for s in range(ga.shape[0] // length):
        allowed = allowed_twice(cnt_ref, s, length)
        rows = slice(s * length, (s + 1) * length)
        for h in range(inner // PAIR):
            cols = [slice(j * inner + h * PAIR, j * inner + (h + 1) * PAIR) for j in range(3)]
            q2 = stack_pair(qkv_ref[rows, cols[0]], low)
            k = qkv_ref[rows, cols[1]]
            p = soft_pair(q2, k, allowed)
            do2 = stack_pair(do_ref[rows, cols[0]], low)
            dp = dot_last(do2, qkv_ref[rows, cols[2]])
            ds = p * (dp - jnp.sum(dp * p, axis=-1, keepdims=True))
            ds = jnp.where(allowed, ds, 0.0).astype(bf16)
            wide = jnp.concatenate([ds[:length], ds[length:]], axis=1)
            dqkv_ref[rows, cols[0]] = (dot(wide, stack_pair(k, low)) * scale).astype(bf16)
            dqkv_ref[rows, cols[1]] = (dot_rows(ds, q2) * scale).astype(bf16)
            dqkv_ref[rows, cols[2]] = dot_rows(p.astype(bf16), do2).astype(bf16)
    if cross:
        up = dot(dqkv_ref[:, :inner], w_ref[:inner, :])
        gs_ref[...] = dot(dqkv_ref[:, inner:], w_ref[inner : 3 * inner, :]).astype(bf16)
    else:
        up = dot(dqkv_ref[...], w_ref[: 3 * inner, :])
    back, gg_ref[...] = norm_back(x_ref[...].astype(f32), gain_ref[...], up)
    gx_ref[...] = gy_ref[...] + back


def attend_bwd(counts, x, gain, gy, qkv, w, length, cross=False):
    t, d = x.shape
    inner = w.shape[0] // 4
    vm = pl.BlockSpec(memory_space=pltpu.VMEM)
    outs = [
        jax.ShapeDtypeStruct((t, d), bf16),
        jax.ShapeDtypeStruct((t, 3 * inner), bf16),
        jax.ShapeDtypeStruct((t, d), f32),
        jax.ShapeDtypeStruct((1, d), f32),
    ]
    if cross:
        outs.append(jax.ShapeDtypeStruct((t, d), bf16))
    return pl.pallas_call(
        functools.partial(attend_bwd_kernel, cross, length),
        out_shape=tuple(outs),
        in_specs=[pl.BlockSpec(memory_space=pltpu.SMEM)] + [vm] * 5,
        out_specs=(vm,) * len(outs),
        scratch_shapes=[pltpu.VMEM((t, inner), bf16)],
        compiler_params=pltpu.CompilerParams(vmem_limit_bytes=VMEM_BYTES),
        cost_estimate=pl.CostEstimate(
            flops=2 * t * d * inner * 4 + 20 * t * length * inner,
            bytes_accessed=w.size * 2 + t * d * 16,
            transcendentals=t * length * 6,
        ),
    )(counts, x, gain, gy, qkv, w)


def feed_fwd_kernel(y_ref, g_in_ref, g_out_ref, w_ref, n_ref, gu_ref, y2_ref, f_ref):
    i = pl.program_id(0)
    f = w_ref.shape[1] // 3

    @pl.when(i == 0)
    def _():
        y = y_ref[...]
        n_ref[...] = (unit_rows(y)[1] * g_in_ref[...]).astype(bf16)
        y2_ref[...] = y

    gu = dot_last(n_ref[...], w_ref[0, : 2 * f, :])
    gu_ref[0] = gu
    hidden = (gelu_parts(gu[:, :f])[0] * gu[:, f:]).astype(bf16)
    y2_ref[...] += dot(hidden, w_ref[0, 2 * f :, :])

    @pl.when(i == pl.num_programs(0) - 1)
    def _():
        f_ref[...] = (unit_rows(y2_ref[...])[1] * g_out_ref[...]).astype(bf16)


def feed_fwd(y, gain_in, gain_out, w):
    t, d = y.shape
    nb, rows, _ = w.shape
    f = rows // 3
    whole = lambda *shape: pl.BlockSpec(shape, lambda i: (0,) * len(shape))
    part = lambda *shape: pl.BlockSpec((1,) + shape, lambda i: (i, 0, 0))
    return pl.pallas_call(
        feed_fwd_kernel,
        grid=(nb,),
        out_shape=(
            jax.ShapeDtypeStruct((t, d), bf16),
            jax.ShapeDtypeStruct((nb, t, 2 * f), f32),
            jax.ShapeDtypeStruct((t, d), f32),
            jax.ShapeDtypeStruct((t, d), bf16),
        ),
        in_specs=[whole(t, d), whole(1, d), whole(1, d), part(rows, d)],
        out_specs=(whole(t, d), part(t, 2 * f), whole(t, d), whole(t, d)),
        compiler_params=pltpu.CompilerParams(vmem_limit_bytes=VMEM_BYTES),
        cost_estimate=pl.CostEstimate(
            flops=2 * t * d * rows * nb,
            bytes_accessed=w.size * 2 + t * d * 12 + nb * t * f * 8,
            transcendentals=nb * t * f,
        ),
    )(y, gain_in, gain_out, w)


def feed_bwd_kernel(emit, up_ref, y_ref, y2_ref, g_in_ref, g_out_ref, gu_ref, w_ref, *refs):
    if emit:
        gf_ref, gy_ref, gg_ref, dgu_ref, hid_ref, last_ref = refs
    else:
        gf_ref, gy_ref, gg_ref, last_ref = refs
    i = pl.program_id(0)
    f = w_ref.shape[1] // 3

    @pl.when(i == 0)
    def _():
        back, gain_grad = norm_back(y2_ref[...], g_out_ref[...], up_ref[...].astype(f32))
        gg_ref[1:2, :] = gain_grad
        last_ref[...] = back
        gf_ref[...] = back.astype(bf16)
        gy_ref[...] = jnp.zeros_like(gy_ref)

    gh = dot_last(gf_ref[...], w_ref[0, 2 * f :, :])
    act, slope = gelu_parts(gu_ref[0, :, :f])
    u = gu_ref[0, :, f:]
    dg = (gh * u * slope).astype(bf16)
    du = (gh * act).astype(bf16)
    if emit:
        dgu_ref[0, :, :f] = dg
        dgu_ref[0, :, f:] = du
        hid_ref[0] = (act * u).astype(bf16)
    gy_ref[...] += dot(dg, w_ref[0, :f, :]) + dot(du, w_ref[0, f : 2 * f, :])

    @pl.when(i == pl.num_programs(0) - 1)
    def _():
        back, gain_grad = norm_back(y_ref[...], g_in_ref[...], gy_ref[...])
        gg_ref[0:1, :] = gain_grad
        gy_ref[...] = last_ref[...] + back


def feed_bwd(up, y, y2, gain_in, gain_out, gu, w, emit):
    t, d = y.shape
    nb, rows, _ = w.shape
    f = rows // 3
    whole = lambda *shape: pl.BlockSpec(shape, lambda i: (0,) * len(shape))
    part = lambda *shape: pl.BlockSpec((1,) + shape, lambda i: (i, 0, 0))
    outs = [
        jax.ShapeDtypeStruct((t, d), bf16),
        jax.ShapeDtypeStruct((t, d), f32),
        jax.ShapeDtypeStruct((2, d), f32),
    ]
    specs = [whole(t, d), whole(t, d), whole(2, d)]
    if emit:
        outs += [
            jax.ShapeDtypeStruct((nb, t, 2 * f), bf16),
            jax.ShapeDtypeStruct((nb, t, f), bf16),
        ]
        specs += [part(t, 2 * f), part(t, f)]
    return pl.pallas_call(
        functools.partial(feed_bwd_kernel, emit),
        grid=(nb,),
        out_shape=tuple(outs),
        in_specs=[whole(t, d)] * 3 + [whole(1, d)] * 2 + [part(t, 2 * f), part(rows, d)],
        out_specs=tuple(specs),
        scratch_shapes=[pltpu.VMEM((t, d), f32)],
        compiler_params=pltpu.CompilerParams(vmem_limit_bytes=VMEM_BYTES),
        cost_estimate=pl.CostEstimate(
            flops=2 * t * d * rows * nb,
            bytes_accessed=w.size * 2 + t * d * 18 + nb * t * f * 8,
            transcendentals=nb * t * f,
        ),
    )(up, y, y2, gain_in, gain_out, gu, w)


def head_kernel(length, cnt_ref, f_ref, w_ref, target_ref, gl_ref, up_ref, loss_ref):
    logits = dot_last(f_ref[...], w_ref[...])
    top = jnp.max(logits, axis=-1, keepdims=True)
    log_total = top + jnp.log(jnp.sum(jnp.exp(logits - top), axis=-1, keepdims=True))
    hit = lax.broadcasted_iota(jnp.int32, logits.shape, 1) == target_ref[...]
    picked = jnp.sum(jnp.where(hit, logits, 0.0), axis=-1, keepdims=True)
    probs = jnp.exp(logits - log_total) - jnp.where(hit, 1.0, 0.0)
    total = jnp.zeros((1, 1), f32)
    for s in range(logits.shape[0] // length):
        rows = slice(s * length, (s + 1) * length)
        count = cnt_ref[s]
        valid = lax.broadcasted_iota(jnp.int32, (length, 1), 0) < count
        total += jnp.sum(
            jnp.where(valid, log_total[rows] - picked[rows], 0.0), axis=0, keepdims=True
        )
        gl_ref[rows, :] = jnp.where(valid, probs[rows], 0.0).astype(bf16)
    loss_ref[...] = total
    up_ref[...] = dot(gl_ref[...], w_ref[...])


def head_loss(counts, final, w, target, length):
    t, d = final.shape
    v = w.shape[0]
    vm = pl.BlockSpec(memory_space=pltpu.VMEM)
    return pl.pallas_call(
        functools.partial(head_kernel, length),
        out_shape=(
            jax.ShapeDtypeStruct((t, v), bf16),
            jax.ShapeDtypeStruct((t, d), f32),
            jax.ShapeDtypeStruct((1, 1), f32),
        ),
        in_specs=[pl.BlockSpec(memory_space=pltpu.SMEM), vm, vm, vm],
        out_specs=(vm,) * 3,
        compiler_params=pltpu.CompilerParams(vmem_limit_bytes=VMEM_BYTES),
        cost_estimate=pl.CostEstimate(
            flops=4 * t * d * v, bytes_accessed=w.size * 2 + t * d * 6, transcendentals=t * v * 2
        ),
    )(counts, final, w, target)


def tail_kernel(
    tiny_ref, gf_ref, lefts_ref, n1_ref, ga_ref, w_ref, n_all_ref,
    feed_ref, attn_ref, total_ref,
    shards, n_buf, part, from_core, four, from_y, from_far, from_near, from_cross, from_out, cross_out,
    ag_send, ag_recv, rs_send, rs_recv, n_sem,
):
    me = lax.axis_index("rows")
    z, y, c = me // 4, (me // 2) % 2, me % 2
    high = z // 2
    inner = (z + high) % 2
    t = gf_ref.shape[0]
    f = w_ref.shape[0] // 3
    core_peer, y_peer = me + 1 - 2 * c, me + 2 - 4 * y
    toward = me + 4 - 8 * high
    across = me + 4 - 8 * high
    outward = me - 4 + 8 * high

    def remote(src, dst, send, recv, device):
        return pltpu.make_async_remote_copy(
            src_ref=src, dst_ref=dst, send_sem=send, recv_sem=recv,
            device_id={"rows": device}, device_id_type=pl.DeviceIdType.MESH,
        )

    barrier = pltpu.get_barrier_semaphore()

    def greet(device):
        pl.semaphore_signal(
            barrier, inc=1, device_id={"rows": device}, device_id_type=pl.DeviceIdType.MESH
        )

    greet(core_peer)
    greet(y_peer)
    greet(toward)

    @pl.when(inner == 1)
    def _():
        greet(outward)

    pl.semaphore_wait(barrier, 3 + inner)

    def piece(p):
        odd = p % 2
        j = jnp.where(p == 0, 0, jnp.where(p == 7, 3, jnp.where(odd == 1, (p + 1) // 2, p // 2 - 1)))
        other = jnp.where(p == 0, 0, jnp.where(p == 7, 1, 1 - odd))
        first, second, third = z + 1 - 2 * (z % 2), 2 - high, 3 - 3 * high
        zz = jnp.where(j == 0, z, jnp.where(j == 1, first, jnp.where(j == 2, second, third)))
        yy = y + other - 2 * other * y
        return zz, yy, other

    def shard_copy(kind, p, s, device):
        return remote(shards.at[s], shards.at[s], ag_send.at[kind, p], ag_recv.at[s], device)

    def each_send(p, zz, yy, other, act):
        s = 4 * zz + 2 * yy + c

        @pl.when((other == 0) & (zz <= z) & (z < 3))
        def _():
            act(shard_copy(0, p, s, me + 4))

        @pl.when((other == 0) & (zz >= z) & (z > 0))
        def _():
            act(shard_copy(1, p, s, me - 4))

        @pl.when(other == 0)
        def _():
            act(shard_copy(2, p, s, y_peer))

        act(shard_copy(3, p, s, core_peer))

    def n_copy(p):
        zz, yy, _ = piece(p)
        rows = pl.ds((2 * zz + yy) * (2 * t), 2 * t)
        slot = p % 2
        return pltpu.make_async_copy(n_all_ref.at[rows], n_buf.at[slot], n_sem.at[slot])

    n_copy(0).start()
    shards[me, :t, :] = gf_ref[...]
    tiny = tiny_ref[...]
    tiny_high = tiny.astype(bf16)
    tiny_low = (tiny - tiny_high.astype(f32)).astype(bf16)
    shards[me, t:, :] = jnp.concatenate([tiny_high, tiny_low], axis=0)
    each_send(0, z, y, 0, lambda copy: copy.start())

    blocks, per = part.shape[1:3]
    row = lax.broadcasted_iota(jnp.int32, (blocks * per, n1_ref.shape[1]), 0)
    from_mixed = row % per >= per // 4 * 3

    def half_sums(half):
        left = lefts_ref[half]
        both = jnp.where(from_mixed, dot(left, ga_ref[...]), dot(left, n1_ref[...]))
        return both.reshape(blocks, per, -1)

    part[0] = half_sums(1 - c).astype(bf16)
    to_core = remote(part.at[0], from_core, rs_send.at[0], rs_recv.at[0], core_peer)
    to_core.start()
    own_half = half_sums(c)
    to_core.wait_recv()
    part[1] = (own_half + from_core[...].astype(f32)).astype(bf16)
    quarter = blocks // 2
    to_y = remote(
        part.at[1, pl.ds((1 - y) * quarter, quarter)], from_y, rs_send.at[1], rs_recv.at[1], y_peer
    )
    to_y.start()

    far = 2 - 2 * high
    far_copy = remote(four.at[pl.ds(far, 2)], from_far, rs_send.at[2], rs_recv.at[2], toward)
    near_copy = remote(four.at[1 + high], from_near, rs_send.at[3], rs_recv.at[3], toward)
    cross_copy = remote(four.at[pl.ds(far, 2)], from_cross, rs_send.at[4], rs_recv.at[4], across)
    out_copy = remote(cross_out, from_out, rs_send.at[5], rs_recv.at[5], outward)

    def stage_y():
        to_y.wait_recv()
        mine = part[1, pl.ds(y * quarter, quarter)].astype(f32)
        four[...] = (mine + from_y[...].astype(f32)).astype(bf16)

        @pl.when(inner == 0)
        def _():
            far_copy.start()
            near_copy.start()

    def stage_cross():
        @pl.when(inner == 1)
        def _():
            far_copy.wait_recv()
            both = four[pl.ds(far, 2)].astype(f32) + from_far[...].astype(f32)
            four[pl.ds(far, 2)] = both.astype(bf16)
            cross_copy.start()

    def stage_out():
        @pl.when(inner == 1)
        def _():
            near_copy.wait_recv()
            cross_copy.wait_recv()
            attn_ref[...] = (
                four[z].astype(f32) + from_near[...].astype(f32) + from_cross[1 - high].astype(f32)
            )
            out = four[3 * high].astype(f32) + from_cross[high].astype(f32)
            cross_out[...] = out.astype(bf16)
            out_copy.start()

    def stage_end():
        @pl.when(inner == 0)
        def _():
            out_copy.wait_recv()
            attn_ref[...] = four[z].astype(f32) + from_out[...].astype(f32)

    feed_ref[...] = jnp.zeros_like(feed_ref)

    def visit(p, carry):
        zz, yy, other = piece(p)
        pair = 4 * zz + 2 * yy

        @pl.when(p > 0)
        def _():
            shard_copy(0, p, pair + c, me).wait_recv()
            each_send(p, zz, yy, other, lambda copy: copy.start())

        shard_copy(0, p, pair + 1 - c, me).wait_recv()

        @pl.when(p < 7)
        def _():
            n_copy(p + 1).start()

        n_copy(p).wait()
        n_rows = n_buf[p % 2]
        g_rows = jnp.concatenate([shards[pair, :t, :], shards[pair + 1, :t, :]], axis=0)
        gu = dot_last(n_rows, w_ref[: 2 * f, :])
        gh = dot_last(g_rows, w_ref[2 * f :, :])
        act, slope = gelu_parts(gu[:, :f])
        up = gu[:, f:]
        dg = (gh * up * slope).astype(bf16)
        du = (gh * act).astype(bf16)
        hid = (act * up).astype(bf16)
        feed_ref[:f, :] += dot_rows(dg, n_rows)
        feed_ref[f : 2 * f, :] += dot_rows(du, n_rows)
        feed_ref[2 * f :, :] += dot_rows(hid, g_rows)
        pl.when(p == 3)(stage_y)
        pl.when(p == 4)(stage_cross)
        pl.when(p == 5)(stage_out)
        pl.when(p == 6)(stage_end)
        return carry

    lax.fori_loop(0, 8, visit, 0)

    def add_tiny(s, total):
        both = shards[s, t:, :].astype(f32)
        return total + both[:8] + both[8:]

    total_ref[...] = lax.fori_loop(0, 16, add_tiny, jnp.zeros(total_ref.shape, f32))

    def settle(p, carry):
        zz, yy, other = piece(p)
        each_send(p, zz, yy, other, lambda copy: copy.wait_send())
        return carry

    lax.fori_loop(0, 8, settle, 0)
    to_core.wait_send()
    to_y.wait_send()

    @pl.when(inner == 0)
    def _():
        far_copy.wait_send()
        near_copy.wait_send()

    @pl.when(inner == 1)
    def _():
        cross_copy.wait_send()
        out_copy.wait_send()


def tail(tiny, gf, lefts, n1, ga, w_own, n_all):
    t, d = gf.shape
    rows = w_own.shape[0]
    blocks = 8
    per = lefts.shape[1] // blocks
    vm = pl.BlockSpec(memory_space=pltpu.VMEM)
    return pl.pallas_call(
        tail_kernel,
        out_shape=(
            jax.ShapeDtypeStruct((rows, d), f32),
            jax.ShapeDtypeStruct((per, d), f32),
            jax.ShapeDtypeStruct(tiny.shape, f32),
        ),
        in_specs=[vm] * 6 + [pl.BlockSpec(memory_space=pl.ANY)],
        out_specs=(vm,) * 3,
        scratch_shapes=[
            pltpu.VMEM((16, t + 16, d), bf16),
            pltpu.VMEM((2, 2 * t, d), bf16),
            pltpu.VMEM((2, blocks, per, d), bf16),
            pltpu.VMEM((blocks, per, d), bf16),
            pltpu.VMEM((4, per, d), bf16),
            pltpu.VMEM((4, per, d), bf16),
            pltpu.VMEM((2, per, d), bf16),
            pltpu.VMEM((per, d), bf16),
            pltpu.VMEM((2, per, d), bf16),
            pltpu.VMEM((per, d), bf16),
            pltpu.VMEM((per, d), bf16),
            pltpu.SemaphoreType.DMA((4, 8)),
            pltpu.SemaphoreType.DMA((16,)),
            pltpu.SemaphoreType.DMA((6,)),
            pltpu.SemaphoreType.DMA((6,)),
            pltpu.SemaphoreType.DMA((2,)),
        ],
        compiler_params=pltpu.CompilerParams(
            vmem_limit_bytes=VMEM_BYTES, collective_id=0, has_side_effects=True
        ),
        cost_estimate=pl.CostEstimate(
            flops=2 * t * 16 * d * rows * 2, bytes_accessed=16 * t * d * 4, transcendentals=16 * t * rows
        ),
    )(tiny, gf, lefts, n1, ga, w_own, n_all)


def front_kernel(
    length, cnt_ref, order_ref, x_ref, g_attn_ref, g_feed_ref, g_final_ref,
    attn_own, feed_own, half_own,
    attn_all, feed_all, first_all, second_all,
    n1_ref, qkv_ref, mixed_ref, y1_ref, n2_ref, gu_ref, y2_ref, enc_ref, arrived_ref,
    w_attn, w_feed, place, wide_buf, first_own,
    send_sem, recv_sem, own_sem, load_sem, x_send, x_recv,
):
    section = lax.axis_index("section")
    me = lax.axis_index("rows")
    z, y, c = me // 4, (me // 2) % 2, me % 2
    core_peer, y_peer = me + 1 - 2 * c, me + 2 - 4 * y
    mesh_id = pl.DeviceIdType.MESH
    inner = mixed_ref.shape[1]
    f = feed_own.shape[0] // 3

    barrier = pltpu.get_barrier_semaphore()

    def greet(where):
        pl.semaphore_signal(barrier, inc=1, device_id=where, device_id_type=mesh_id)

    greet({"rows": core_peer})
    greet({"rows": y_peer})
    greet({"section": 1 - section})

    @pl.when(z > 0)
    def _():
        greet({"rows": me - 4})

    @pl.when(z < 3)
    def _():
        greet({"rows": me + 4})

    own_copies = [
        pltpu.make_async_copy(own, whole.at[me], own_sem.at[k])
        for k, (own, whole) in enumerate(
            [(attn_own, attn_all), (feed_own, feed_all), (half_own, second_all)]
        )
    ]
    own_copies[0].start()
    own_copies[1].start()

    @pl.when(section == 1)
    def _():
        own_copies[2].start()

    pl.semaphore_wait(barrier, 4 + (z + z // 2) % 2)

    def remote(src, dst, send, recv, where):
        return pltpu.make_async_remote_copy(
            src_ref=src, dst_ref=dst, send_sem=send, recv_sem=recv,
            device_id=where, device_id_type=mesh_id,
        )

    kinds = [pl.ds(k * f, f) for k in range(3)]
    parts = {
        "A": (0, attn_all, None, 2, attn_own),
        "G": (1, feed_all, kinds[0], 1, feed_own.at[kinds[0]]),
        "U": (2, feed_all, kinds[1], 1, feed_own.at[kinds[1]]),
        "O": (3, feed_all, kinds[2], 1, feed_own.at[kinds[2]]),
        "X": (4, first_all, None, 1, first_own),
        "Y": (5, second_all, None, 2, half_own),
    }

    def place_of(route, p):
        if route == 1:
            j, other = [(0, 0), (1, 0), (0, 1), (2, 0), (1, 1), (3, 0), (2, 1), (3, 1)][p]
        else:
            j, other = p // 2, p % 2
        zz = [z, z + 1 - 2 * (z % 2), 2 - z // 2, 3 - 3 * (z // 2)][j]
        yy = y + other - 2 * other * y
        return zz, yy, other

    def part_copy(name, kind, p, s, where):
        k, whole, rows, _, own = parts[name]
        dst = whole.at[s] if rows is None else whole.at[s, rows]
        return remote(own if p == 0 else dst, dst, send_sem.at[k, kind, p], recv_sem.at[k, s], where)

    def each_send(name, p, act, ways="zyc"):
        route = parts[name][3]
        zz, yy, other = place_of(route, p)
        s = 4 * zz + 2 * yy + c
        if "z" in ways and (route == 2 or other == 0):

            @pl.when((zz <= z) & (z < 3))
            def _():
                act(part_copy(name, 0, p, s, {"rows": me + 4}))

            @pl.when((zz >= z) & (z > 0))
            def _():
                act(part_copy(name, 1, p, s, {"rows": me - 4}))

        if "y" in ways and (p == 0 or (route == 1 and other == 0)):
            act(part_copy(name, 2, p, s, {"rows": y_peer}))
        if "c" in ways:
            act(part_copy(name, 3, p, s, {"rows": core_peer}))

    def begin(name, ways):
        each_send(name, 0, lambda copy: copy.start(), ways)

    def arrive(name, p):
        zz, yy, _ = place_of(parts[name][3], p)
        part_copy(name, 0, p, 4 * zz + 2 * yy + c, {"rows": me}).wait_recv()
        each_send(name, p, lambda copy: copy.start())

    def meet(name, p):
        zz, yy, _ = place_of(parts[name][3], p)
        part_copy(name, 0, p, 4 * zz + 2 * yy + 1 - c, {"rows": me}).wait_recv()

    def settle(name):
        for p in range(8):
            each_send(name, p, lambda copy: copy.wait_send())

    half_copy = remote(half_own, first_own, x_send.at[0], x_recv.at[0], {"section": 1 - section})
    enc_copy = remote(enc_ref, arrived_ref, x_send.at[1], x_recv.at[1], {"section": 1 - section})
    own_first = pltpu.make_async_copy(first_own, first_all.at[me], own_sem.at[3])

    def project():
        for p in range(8):
            meet("A", p)
        own_copies[0].wait()
        load = pltpu.make_async_copy(attn_all, w_attn, load_sem.at[0])
        load.start()
        load.wait()
        wide_buf[...] = dot_last(n1_ref[...], w_attn[...].reshape(4 * inner, -1)).astype(bf16)
        qkv_ref[...] = dot(wide_buf[...], place[:, : 3 * inner]).astype(bf16)

    def mix(s):
        low = low_half(length)
        allowed = allowed_twice(cnt_ref, s, length)
        rows = slice(s * length, (s + 1) * length)
        for h in range(inner // PAIR):
            cols = [slice(j * inner + h * PAIR, j * inner + (h + 1) * PAIR) for j in range(3)]
            q2 = stack_pair(qkv_ref[rows, cols[0]], low)
            p = soft_pair(q2, qkv_ref[rows, cols[1]], allowed).astype(bf16)
            wide = jnp.concatenate([p[:length], p[length:]], axis=1)
            mixed_ref[rows, cols[0]] = dot(wide, stack_pair(qkv_ref[rows, cols[2]], low)).astype(bf16)

    def mix_out():
        for s in range(x_ref.shape[0] // length // 2, x_ref.shape[0] // length):
            mix(s)
        wide_buf[...] = dot_last(mixed_ref[...], place[:, 3 * inner :]).astype(bf16)
        y1_ref[...] = x_ref[...].astype(f32) + dot(wide_buf[...], w_attn[...].reshape(4 * inner, -1))
        y2_ref[...] = y1_ref[...]
        n2_ref[...] = (unit_rows(y1_ref[...])[1] * g_feed_ref[...]).astype(bf16)

    def mix_first():
        for s in range(x_ref.shape[0] // length // 2):
            mix(s)

    def feed(p):
        if p == 0:
            own_copies[1].wait()
        for name in "GUO":
            meet(name, p)
        zz, yy, _ = place_of(1, p)
        pair = 4 * zz + 2 * yy

        @pl.when(section == 0)
        def _():
            blocks = pltpu.make_async_copy(feed_all.at[pl.ds(pair, 2)], w_feed, load_sem.at[1])
            blocks.start()
            blocks.wait()
            for k in range(2):
                gu = dot_last(n2_ref[...], w_feed[k, : 2 * f, :])
                gu_ref[pair + k] = gu
                hidden = (gelu_parts(gu[:, :f])[0] * gu[:, f:]).astype(bf16)
                y2_ref[...] += dot(hidden, w_feed[k, 2 * f :, :])

    begin("A", "zyc")

    @pl.when(section == 0)
    def _():
        half_copy.start()

    @pl.when(section == 1)
    def _():
        begin("Y", "yc")

    for name in "GUO":
        begin(name, "yc")
    begin("G", "z")

    @pl.when(section == 1)
    def _():
        begin("Y", "z")

    row = lax.broadcasted_iota(jnp.int32, place.shape, 0)
    place[...] = jnp.where(row == order_ref[...], 1.0, 0.0).astype(bf16)
    n1_ref[...] = (unit_rows(x_ref[...].astype(f32))[1] * g_attn_ref[...]).astype(bf16)

    tasks = {"c1": project, "c2": mix_first, "c3": mix_out}
    for step in FRONT_STEPS:
        if step in tasks:
            tasks[step]()
        elif step[0] == "f":
            feed(int(step[1]))
        elif step[0] == "o":
            begin(step[1], "z")
        elif step == "X0":

            @pl.when(section == 1)
            def _():
                half_copy.wait_recv()
                own_first.start()
                begin("X", "zyc")

        elif step[0] == "X":

            @pl.when(section == 1)
            def _(p=int(step[1])):
                arrive("X", p)
                arrive("Y", p)

        else:
            arrive(step[0], int(step[1]))

    @pl.when(section == 0)
    def _():
        enc_ref[...] = (unit_rows(y2_ref[...])[1] * g_final_ref[...]).astype(bf16)
        enc_copy.start()

    for name in "AGUO":
        settle(name)

    @pl.when(section == 1)
    def _():
        for name in "XY":
            for p in range(8):
                meet(name, p)
            settle(name)
        own_first.wait()
        own_copies[2].wait()
        enc_copy.wait_recv()

    @pl.when(section == 0)
    def _():
        half_copy.wait_send()
        enc_copy.wait_send()


FRONT_STEPS = (
    ("A1", "oU", "G1", "A2", "X0", "A3", "oO", "A4", "O1", "U1", "G2", "U2", "O2", "A5", "A6", "X1", "X2", "G3", "A7")
    + ("c1", "O3", "G4", "O4", "U3", "c2", "U4", "c3", "f0", "O5", "f1", "U5", "U6", "G5", "O6", "X3", "X4", "X5")
    + ("X6", "O7", "f2", "f3", "G6", "f4", "f5", "U7", "f6", "X7", "G7", "f7")
)


def front(counts, order, x, gain_attn, gain_feed, gain_final, attn_own, feed_own, half_own, length):
    t, d = x.shape
    attn_rows, feed_rows = attn_own.shape[0], feed_own.shape[0]
    inner = attn_rows * 4
    half_shape = (16,) + half_own.shape
    vm = pl.BlockSpec(memory_space=pltpu.VMEM)
    anywhere = pl.BlockSpec(memory_space=pl.ANY)
    return pl.pallas_call(
        functools.partial(front_kernel, length),
        out_shape=(
            jax.ShapeDtypeStruct((16, attn_rows, d), bf16),
            jax.ShapeDtypeStruct((16, feed_rows, d), bf16),
            jax.ShapeDtypeStruct(half_shape, bf16),
            jax.ShapeDtypeStruct(half_shape, bf16),
            jax.ShapeDtypeStruct((t, d), bf16),
            jax.ShapeDtypeStruct((t, 3 * inner), bf16),
            jax.ShapeDtypeStruct((t, inner), bf16),
            jax.ShapeDtypeStruct((t, d), f32),
            jax.ShapeDtypeStruct((t, d), bf16),
            jax.ShapeDtypeStruct((16, t, feed_rows // 3 * 2), f32),
            jax.ShapeDtypeStruct((t, d), f32),
            jax.ShapeDtypeStruct((t, d), bf16),
            jax.ShapeDtypeStruct((t, d), bf16),
        ),
        in_specs=[pl.BlockSpec(memory_space=pltpu.SMEM)] + [vm] * 5 + [anywhere] * 3,
        out_specs=(anywhere,) * 4 + (vm,) * 9,
        scratch_shapes=[
            pltpu.VMEM((16, attn_rows, d), bf16),
            pltpu.VMEM((2, feed_rows, d), bf16),
            pltpu.VMEM((4 * inner, 4 * inner), bf16),
            pltpu.VMEM((t, 4 * inner), bf16),
            pltpu.VMEM(half_own.shape, bf16),
            pltpu.SemaphoreType.DMA((6, 4, 8)),
            pltpu.SemaphoreType.DMA((6, 16)),
            pltpu.SemaphoreType.DMA((4,)),
            pltpu.SemaphoreType.DMA((2,)),
            pltpu.SemaphoreType.DMA((2,)),
            pltpu.SemaphoreType.DMA((2,)),
        ],
        compiler_params=pltpu.CompilerParams(
            vmem_limit_bytes=VMEM_BYTES, collective_id=1, has_side_effects=True
        ),
        cost_estimate=pl.CostEstimate(
            flops=2 * t * d * (feed_rows * 16 + 8 * inner),
            bytes_accessed=2 * 16 * (attn_rows + feed_rows) * d * 2,
            transcendentals=t * feed_rows * 6,
        ),
    )(counts, order, x, gain_attn, gain_feed, gain_final, attn_own, feed_own, half_own)


def adam_step(weight, first_moment, second_moment, gradient, step_rate, weight_decay):
    first_new = 0.9 * first_moment + 0.1 * gradient
    second_new = 0.999 * second_moment + 0.001 * gradient * gradient
    first_fix = 1.0 - 0.9**STEP
    second_fix = 1.0 - 0.999**STEP
    update = first_new / first_fix / (jnp.sqrt(second_new / second_fix) + 1e-08)
    return (first_new, second_new, weight - step_rate * (update + weight_decay * weight))


def kinds_first(gathered, n, kinds, per):
    d = gathered.shape[-1]
    return gathered.reshape(n, kinds, per, d).transpose(1, 0, 2, 3).reshape(kinds * n * per, d)


def owners_first(left, right, n):
    t, k, units = left.shape
    grad = jnp.einsum("tku,td->kud", left, right, preferred_element_type=f32)
    return grad.reshape(k, n, units // n, -1).transpose(1, 0, 2, 3)


def local(
    block_input,
    lengths,
    targets,
    attention_weight,
    attention_first,
    attention_second,
    feed_weight,
    feed_first,
    feed_second,
    norm_gain,
    gain_first,
    gain_second,
    cross_weight,
    cross_first,
    cross_second,
    head_weight,
    head_first,
    head_second,
    cross_gain,
    cross_gain_first,
    cross_gain_second,
):
    n = lax.axis_size("rows")
    is_encoder = lax.axis_index("section") == 0
    micro, length, d = block_input.shape[1:]
    t = micro * length
    per = attention_weight.shape[1]
    f = feed_weight.shape[1]
    inner = per * n

    attn_own = attention_weight[0].astype(bf16).transpose(1, 0, 2).reshape(4 * per, d)
    feed_own = feed_weight[0].astype(bf16).transpose(1, 0, 2)
    half_rows = jnp.concatenate(
        [cross_weight.astype(bf16).transpose(1, 0, 2), head_weight.astype(bf16)[None]], axis=0
    )

    gains = norm_gain[0]
    gain_attn, gain_feed, gain_final = gains[0:1], gains[1:2], gains[2:3]
    gain_cross = cross_gain[None]
    x = block_input[0].reshape(t, d)
    enc_counts = lengths[0, :, 0]
    dec_counts = lengths[1, :, 0]
    zero_one = jnp.zeros((1,), jnp.int32)
    self_counts = jnp.concatenate([jnp.where(is_encoder, 0, 1).astype(jnp.int32)[None], enc_counts])
    cross_counts = jnp.concatenate([zero_one, enc_counts])
    target_column = targets.reshape(t, 1)

    def blank(maker):
        return jax.tree.map(lambda a: jnp.zeros(a.shape, a.dtype), jax.eval_shape(maker))

    emit = n != BLOCKS
    if emit:
        attn_all = lax.all_gather(attn_own, "rows", axis=0, tiled=True)
        attn_w = kinds_first(attn_all, n, 4, per)
        feed_all = lax.all_gather(feed_own.reshape(3 * f, d), "rows", axis=0, tiled=True)
        feed_w = kinds_first(feed_all, n, 3, f).reshape(3, BLOCKS, -1, d)
        feed_w = feed_w.transpose(1, 0, 2, 3).reshape(BLOCKS, -1, d)
        other_half = lax.ppermute(half_rows, "section", [(0, 1)])
        extra_own = jnp.concatenate([other_half, half_rows], axis=-1).reshape(5 * per, d)
        extra_all = lax.all_gather(extra_own, "rows", axis=0, tiled=True)
        n1, qkv, mixed, y1 = attend_fwd(self_counts, x, gain_attn, attn_w, length)

        def enc_feed():
            return feed_fwd(y1, gain_feed, gain_final, feed_w)

        enc_state = lax.cond(is_encoder, enc_feed, lambda: blank(enc_feed))
        encoded = lax.ppermute(enc_state[3], "section", [(0, 1)])
    else:
        units = jnp.arange(4 * inner, dtype=jnp.int32).reshape(n, 4, per)
        order = units.transpose(1, 0, 2).reshape(1, 4 * inner)
        pad = -(5 * per) % 16
        half_own = jnp.pad(half_rows.reshape(5 * per, d // 2), ((0, pad), (0, 0)))
        outs = front(
            self_counts, order, x, gain_attn, gain_feed, gain_final,
            attn_own, feed_own.reshape(3 * f, d), half_own, length,
        )
        attn_all, feed_w, first_all, second_all, n1, qkv, mixed, y1 = outs[:8]
        enc_state, encoded = outs[8:12], outs[12]
        attn_w = kinds_first(attn_all, n, 4, per)
        extra_all = jnp.concatenate([first_all, second_all], axis=-1)[:, : 5 * per]
    extra_w = kinds_first(extra_all, n, 5, per)
    cross_w, head_w = extra_w[: 4 * inner], extra_w[4 * inner :]

    def dec_front():
        mc, cqkv, cmixed, z2 = attend_fwd(cross_counts, y1, gain_cross, cross_w, length, encoded)
        return feed_fwd(z2, gain_feed, gain_final, feed_w) + (mc, cqkv, cmixed, z2)

    def enc_pass():
        rest = jax.eval_shape(dec_front)[4:7]
        return tuple(enc_state) + tuple(jnp.zeros(a.shape, a.dtype) for a in rest) + (y1,)

    n2, gu, y2, final, mc, cqkv, cmixed, mid = lax.cond(is_encoder, enc_pass, dec_front)
    if not emit:
        n2_all = lax.all_gather(n2, "rows", axis=0, tiled=True)

    def dec_back():
        gl, up, loss = head_loss(dec_counts, final, head_w, target_column, length)
        feed_out = feed_bwd(up, mid, y2, gain_feed, gain_final, gu, feed_w, emit)
        ga_c, dqkv_c, gy1, gg_c, ge = attend_bwd(
            cross_counts, y1, gain_cross, feed_out[1], cqkv, cross_w, length, True
        )
        return (ge, gy1, feed_out[2], feed_out[0], *feed_out[3:], gl, ga_c, dqkv_c, gg_c, loss)

    back = lax.cond(is_encoder, lambda: blank(dec_back), dec_back)
    returned = lax.ppermute(back[0], "section", [(1, 0)])
    at = 6 if emit else 4
    gl, ga_c, dqkv_c, gg_c, loss = back[at:]

    def enc_back():
        feed_out = feed_bwd(returned, mid, y2, gain_feed, gain_final, gu, feed_w, emit)
        return (feed_out[1], feed_out[2], feed_out[0], *feed_out[3:])

    backs = lax.cond(is_encoder, enc_back, lambda: tuple(back[1:at]))
    gy1, gg_feed, gf = backs[:3]
    if not emit:
        gy1, n2_all = lax.optimization_barrier((gy1, n2_all))

    ga, dqkv, gx, gg_attn = attend_bwd(self_counts, x, gain_attn, gy1, qkv, attn_w, length)

    extra_part = jnp.concatenate(
        [
            owners_first(dqkv_c[:, None, :inner], mc, n),
            owners_first(dqkv_c[:, inner:].reshape(t, 2, inner), encoded, n),
            owners_first(cmixed[:, None], ga_c, n),
            owners_first(gl[:, None], final, n),
        ],
        axis=1,
    ).astype(bf16)
    if not emit:
        extra_part, gx = lax.optimization_barrier((extra_part, gx))
    extra_sum = lax.psum_scatter(
        extra_part.reshape(n * 5 * per, d), "rows", scatter_dimension=0, tiled=True
    )
    half = d // 2
    extra_first = lax.ppermute(extra_sum[:, :half], "section", [(1, 0)])
    extra_grad = jnp.where(is_encoder, extra_first, extra_sum[:, half:]).astype(f32)
    extra_grad = extra_grad.reshape(5, per, half)

    tiny = jnp.concatenate(
        [
            gg_attn,
            gg_feed,
            gg_c,
            jnp.broadcast_to(loss, (1, d)),
            jnp.zeros((3, d), f32),
        ],
        axis=0,
    )

    if emit:
        attn_part = jnp.concatenate(
            [
                owners_first(dqkv.reshape(t, 3, inner), n1, n),
                owners_first(mixed[:, None], ga, n),
            ],
            axis=1,
        ).astype(bf16)
        attn_sum = lax.psum_scatter(
            attn_part.reshape(n * 4 * per, d), "rows", scatter_dimension=0, tiled=True
        ).astype(f32)
        dgu, hid = backs[3], backs[4]
        nb, _, fb = hid.shape
        left = dgu.reshape(nb, t, 2, fb).transpose(1, 2, 0, 3).reshape(t, 2, nb * fb)
        hid = hid.transpose(1, 0, 2).reshape(t, 1, nb * fb)
        feed_part = jnp.concatenate(
            [owners_first(left, n2, n), owners_first(hid, gf, n)], axis=1
        ).astype(bf16)
        feed_grad = lax.psum_scatter(
            feed_part.reshape(n * 3 * f, d), "rows", scatter_dimension=0, tiled=True
        ).astype(f32)
        tiny_sum = jnp.sum(lax.all_gather(tiny, "rows", axis=0), axis=0)
    else:
        lefts = jnp.concatenate([dqkv, mixed], axis=1).reshape(t, 4, 4, 2, 2, per)
        lefts = lefts.transpose(4, 3, 2, 1, 5, 0).reshape(2, 8 * 4 * per, t)
        feed_grad, attn_sum, tiny_sum = tail(
            tiny, gf, lefts, n1, ga, feed_own.reshape(3 * f, d), n2_all
        )
    attn_grad = attn_sum.reshape(4, per, d).transpose(1, 0, 2)
    feed_grad = feed_grad.reshape(3, f, d).transpose(1, 0, 2)
    tiny_dec = lax.ppermute(tiny_sum[3:5], "section", [(1, 0)])
    tiny_dec = jnp.where(is_encoder, tiny_dec, tiny_sum[3:5])
    cross_gain_total = tiny_dec[0]
    loss_total = tiny_dec[1, 0]

    attention_new = adam_step(
        attention_weight, attention_first, attention_second, attn_grad[None], 0.05, 0.1
    )
    feed_new = adam_step(feed_weight, feed_first, feed_second, feed_grad[None], 0.05, 0.1)
    gain_new = adam_step(norm_gain, gain_first, gain_second, tiny_sum[None, 0:3], 0.5, 0.0)
    cross_new = adam_step(
        cross_weight, cross_first, cross_second, extra_grad[:4].transpose(1, 0, 2), 0.05, 0.1
    )
    head_new = adam_step(head_weight, head_first, head_second, extra_grad[4], 0.05, 0.1)
    cross_gain_new = adam_step(
        cross_gain, cross_gain_first, cross_gain_second, cross_gain_total, 0.5, 0.0
    )
    return (
        gx.reshape(1, micro, length, d),
        loss_total,
        *attention_new,
        *feed_new,
        *gain_new,
        *cross_new,
        *head_new,
        *cross_gain_new,
    )


def solution(mesh):
    by_row = P("section", "rows", None, None)
    gain = P("section", None, None)
    cross = P("rows", None, "section")
    head = P("rows", "section")
    weights = (by_row,) * 6 + (gain,) * 3 + (cross,) * 3 + (head,) * 3 + (P(),) * 3
    tokens = P("section", None, "rows", None)
    return jax.shard_map(
        local,
        mesh=mesh,
        in_specs=(tokens, P(None, None, "rows"), P(None, "rows")) + weights,
        out_specs=(tokens, P()) + weights,
        check_vma=False,
    )
```

```python
import functools

import jax
import jax.numpy as jnp
from jax import lax
from jax.experimental import pallas as pl
from jax.experimental.pallas import tpu as pltpu
from jax.sharding import PartitionSpec as P

HD = 64
STEP = 10
PAIR = 2 * HD
BLOCKS = 16
VMEM_BYTES = 52 * 1024 * 1024

bf16 = jnp.bfloat16
f32 = jnp.float32
masked_value = -1000000000.0
scale = HD ** (-0.5)


def dot(a, b):
    return lax.dot_general(a, b, (((1,), (0,)), ((), ())), preferred_element_type=f32)


def dot_last(a, b):
    return lax.dot_general(a, b, (((1,), (1,)), ((), ())), preferred_element_type=f32)


def dot_rows(a, b):
    return lax.dot_general(a, b, (((0,), (0,)), ((), ())), preferred_element_type=f32)


def unit_rows(v):
    r = lax.rsqrt(jnp.mean(v * v, axis=-1, keepdims=True) + 1e-06)
    return r, v * r


def norm_back(v, gain, up):
    r, n = unit_rows(v)
    g = up * gain
    back = r * (g - n * jnp.mean(g * n, axis=-1, keepdims=True))
    return back, jnp.sum(up * n, axis=0, keepdims=True)


def gelu_parts(x):
    c = 0.7978845608028654
    t = jnp.tanh(c * (x + 0.044715 * (x * x * x)))
    act = 0.5 * x * (1.0 + t)
    slope = 0.5 * (1.0 + t) + 0.5 * x * (1.0 - t * t) * (c * (1.0 + 3.0 * 0.044715 * (x * x)))
    return act, slope


def low_half(length):
    return lax.broadcasted_iota(jnp.int32, (length, PAIR), 1) < HD


def stack_pair(m, low):
    zero = jnp.zeros_like(m)
    return jnp.concatenate([jnp.where(low, m, zero), jnp.where(low, zero, m)], axis=0)


def allowed_twice(cnt_ref, s, length):
    row = lax.broadcasted_iota(jnp.int32, (length, length), 0)
    col = lax.broadcasted_iota(jnp.int32, (length, length), 1)
    limit = jnp.where(cnt_ref[0] == 1, row + 1, cnt_ref[1 + s])
    one = jnp.where(col < limit, 1, 0)
    return jnp.concatenate([one, one], axis=0) == 1


def soft_pair(q2, k, allowed):
    s = dot_last(q2, k) * scale
    s = jnp.where(allowed, s, masked_value)
    e = jnp.exp(s - jnp.max(s, axis=-1, keepdims=True))
    return e / jnp.sum(e, axis=-1, keepdims=True)


def head_columns(inner, h):
    return [slice(j * inner + h * PAIR, j * inner + (h + 1) * PAIR) for j in range(3)]


def heads_fwd(cnt_ref, qkv_ref, o_ref, length):
    t, inner = o_ref.shape
    low = low_half(length)
    for s in range(t // length):
        allowed = allowed_twice(cnt_ref, s, length)
        rows = slice(s * length, (s + 1) * length)
        for h in range(inner // PAIR):
            cols = head_columns(inner, h)
            q2 = stack_pair(qkv_ref[rows, cols[0]], low)
            p = soft_pair(q2, qkv_ref[rows, cols[1]], allowed).astype(bf16)
            wide = jnp.concatenate([p[:length], p[length:]], axis=1)
            o_ref[rows, cols[0]] = dot(wide, stack_pair(qkv_ref[rows, cols[2]], low)).astype(bf16)


def heads_bwd(cnt_ref, qkv_ref, do_ref, dqkv_ref, length):
    t, inner = do_ref.shape
    low = low_half(length)
    for s in range(t // length):
        allowed = allowed_twice(cnt_ref, s, length)
        rows = slice(s * length, (s + 1) * length)
        for h in range(inner // PAIR):
            cols = head_columns(inner, h)
            q2 = stack_pair(qkv_ref[rows, cols[0]], low)
            k = qkv_ref[rows, cols[1]]
            p = soft_pair(q2, k, allowed)
            do2 = stack_pair(do_ref[rows, cols[0]], low)
            dp = dot_last(do2, qkv_ref[rows, cols[2]])
            ds = p * (dp - jnp.sum(dp * p, axis=-1, keepdims=True))
            ds = jnp.where(allowed, ds, 0.0).astype(bf16)
            wide = jnp.concatenate([ds[:length], ds[length:]], axis=1)
            dqkv_ref[rows, cols[0]] = (dot(wide, stack_pair(k, low)) * scale).astype(bf16)
            dqkv_ref[rows, cols[1]] = (dot_rows(ds, q2) * scale).astype(bf16)
            dqkv_ref[rows, cols[2]] = dot_rows(p.astype(bf16), do2).astype(bf16)


def loss_back(cnt_ref, f_ref, w_ref, target_ref, gl_ref, length):
    logits = dot_last(f_ref[...], w_ref[...])
    top = jnp.max(logits, axis=-1, keepdims=True)
    log_total = top + jnp.log(jnp.sum(jnp.exp(logits - top), axis=-1, keepdims=True))
    hit = lax.broadcasted_iota(jnp.int32, logits.shape, 1) == target_ref[...]
    picked = jnp.sum(jnp.where(hit, logits, 0.0), axis=-1, keepdims=True)
    probs = jnp.exp(logits - log_total) - jnp.where(hit, 1.0, 0.0)
    total = jnp.zeros((1, 1), f32)
    for s in range(logits.shape[0] // length):
        rows = slice(s * length, (s + 1) * length)
        valid = lax.broadcasted_iota(jnp.int32, (length, 1), 0) < cnt_ref[s]
        total += jnp.sum(
            jnp.where(valid, log_total[rows] - picked[rows], 0.0), axis=0, keepdims=True
        )
        gl_ref[rows, :] = jnp.where(valid, probs[rows], 0.0).astype(bf16)
    return total


def attend_fwd_kernel(cross, length, cnt_ref, x_ref, gain_ref, *refs):
    if cross:
        src_ref, w_ref, n_ref, qkv_ref, o_ref, y_ref = refs
    else:
        w_ref, n_ref, qkv_ref, o_ref, y_ref = refs
    inner = w_ref.shape[0] // 4
    x = x_ref[...].astype(f32)
    n = (unit_rows(x)[1] * gain_ref[...]).astype(bf16)
    n_ref[...] = n
    if cross:
        qkv_ref[:, :inner] = dot_last(n, w_ref[:inner, :]).astype(bf16)
        qkv_ref[:, inner:] = dot_last(src_ref[...], w_ref[inner : 3 * inner, :]).astype(bf16)
    else:
        qkv_ref[...] = dot_last(n, w_ref[: 3 * inner, :]).astype(bf16)
    heads_fwd(cnt_ref, qkv_ref, o_ref, length)
    y_ref[...] = x + dot(o_ref[...], w_ref[3 * inner :, :])


def attend_fwd(counts, x, gain, w, length, source=None):
    t, d = x.shape
    inner = w.shape[0] // 4
    ins = [counts, x, gain] + ([] if source is None else [source]) + [w]
    vm = pl.BlockSpec(memory_space=pltpu.VMEM)
    return pl.pallas_call(
        functools.partial(attend_fwd_kernel, source is not None, length),
        out_shape=(
            jax.ShapeDtypeStruct((t, d), bf16),
            jax.ShapeDtypeStruct((t, 3 * inner), bf16),
            jax.ShapeDtypeStruct((t, inner), bf16),
            jax.ShapeDtypeStruct((t, d), f32),
        ),
        in_specs=[pl.BlockSpec(memory_space=pltpu.SMEM)] + [vm] * (len(ins) - 1),
        out_specs=(vm,) * 4,
        compiler_params=pltpu.CompilerParams(vmem_limit_bytes=VMEM_BYTES),
        cost_estimate=pl.CostEstimate(
            flops=2 * t * d * inner * 4 + 8 * t * length * inner,
            bytes_accessed=w.size * 2 + t * d * 10,
            transcendentals=t * length * 6,
        ),
    )(*ins)


def attend_bwd_kernel(cross, length, cnt_ref, x_ref, gain_ref, gy_ref, qkv_ref, w_ref, *refs):
    if cross:
        ga_ref, dqkv_ref, gx_ref, gg_ref, gs_ref, do_ref = refs
    else:
        ga_ref, dqkv_ref, gx_ref, gg_ref, do_ref = refs
    inner = w_ref.shape[0] // 4
    ga = gy_ref[...].astype(bf16)
    ga_ref[...] = ga
    do_ref[...] = dot_last(ga, w_ref[3 * inner :, :]).astype(bf16)
    heads_bwd(cnt_ref, qkv_ref, do_ref, dqkv_ref, length)
    if cross:
        up = dot(dqkv_ref[:, :inner], w_ref[:inner, :])
        gs_ref[...] = dot(dqkv_ref[:, inner:], w_ref[inner : 3 * inner, :]).astype(bf16)
    else:
        up = dot(dqkv_ref[...], w_ref[: 3 * inner, :])
    back, gg_ref[...] = norm_back(x_ref[...].astype(f32), gain_ref[...], up)
    gx_ref[...] = gy_ref[...] + back


def attend_bwd(counts, x, gain, gy, qkv, w, length, cross=False):
    t, d = x.shape
    inner = w.shape[0] // 4
    vm = pl.BlockSpec(memory_space=pltpu.VMEM)
    outs = [
        jax.ShapeDtypeStruct((t, d), bf16),
        jax.ShapeDtypeStruct((t, 3 * inner), bf16),
        jax.ShapeDtypeStruct((t, d), f32),
        jax.ShapeDtypeStruct((1, d), f32),
    ]
    if cross:
        outs.append(jax.ShapeDtypeStruct((t, d), bf16))
    return pl.pallas_call(
        functools.partial(attend_bwd_kernel, cross, length),
        out_shape=tuple(outs),
        in_specs=[pl.BlockSpec(memory_space=pltpu.SMEM)] + [vm] * 5,
        out_specs=(vm,) * len(outs),
        scratch_shapes=[pltpu.VMEM((t, inner), bf16)],
        compiler_params=pltpu.CompilerParams(vmem_limit_bytes=VMEM_BYTES),
        cost_estimate=pl.CostEstimate(
            flops=2 * t * d * inner * 4 + 20 * t * length * inner,
            bytes_accessed=w.size * 2 + t * d * 16,
            transcendentals=t * length * 6,
        ),
    )(counts, x, gain, gy, qkv, w)


def feed_fwd_kernel(y_ref, g_in_ref, g_out_ref, w_ref, n_ref, gu_ref, y2_ref, f_ref):
    i = pl.program_id(0)
    f = w_ref.shape[1] // 3

    @pl.when(i == 0)
    def _():
        y = y_ref[...]
        n_ref[...] = (unit_rows(y)[1] * g_in_ref[...]).astype(bf16)
        y2_ref[...] = y

    gu = dot_last(n_ref[...], w_ref[0, : 2 * f, :])
    gu_ref[0] = gu
    hidden = (gelu_parts(gu[:, :f])[0] * gu[:, f:]).astype(bf16)
    y2_ref[...] += dot(hidden, w_ref[0, 2 * f :, :])

    @pl.when(i == pl.num_programs(0) - 1)
    def _():
        f_ref[...] = (unit_rows(y2_ref[...])[1] * g_out_ref[...]).astype(bf16)


def feed_fwd(y, gain_in, gain_out, w):
    t, d = y.shape
    nb, rows, _ = w.shape
    f = rows // 3
    whole = lambda *shape: pl.BlockSpec(shape, lambda i: (0,) * len(shape))
    part = lambda *shape: pl.BlockSpec((1,) + shape, lambda i: (i, 0, 0))
    return pl.pallas_call(
        feed_fwd_kernel,
        grid=(nb,),
        out_shape=(
            jax.ShapeDtypeStruct((t, d), bf16),
            jax.ShapeDtypeStruct((nb, t, 2 * f), f32),
            jax.ShapeDtypeStruct((t, d), f32),
            jax.ShapeDtypeStruct((t, d), bf16),
        ),
        in_specs=[whole(t, d), whole(1, d), whole(1, d), part(rows, d)],
        out_specs=(whole(t, d), part(t, 2 * f), whole(t, d), whole(t, d)),
        compiler_params=pltpu.CompilerParams(vmem_limit_bytes=VMEM_BYTES),
        cost_estimate=pl.CostEstimate(
            flops=2 * t * d * rows * nb,
            bytes_accessed=w.size * 2 + t * d * 12 + nb * t * f * 8,
            transcendentals=nb * t * f,
        ),
    )(y, gain_in, gain_out, w)


def feed_bwd_kernel(emit, up_ref, y_ref, y2_ref, g_in_ref, g_out_ref, gu_ref, w_ref, *refs):
    if emit:
        gf_ref, gy_ref, gg_ref, dgu_ref, hid_ref, last_ref = refs
    else:
        gf_ref, gy_ref, gg_ref, last_ref = refs
    i = pl.program_id(0)
    f = w_ref.shape[1] // 3

    @pl.when(i == 0)
    def _():
        back, gain_grad = norm_back(y2_ref[...], g_out_ref[...], up_ref[...].astype(f32))
        gg_ref[1:2, :] = gain_grad
        last_ref[...] = back
        gf_ref[...] = back.astype(bf16)
        gy_ref[...] = jnp.zeros_like(gy_ref)

    gh = dot_last(gf_ref[...], w_ref[0, 2 * f :, :])
    act, slope = gelu_parts(gu_ref[0, :, :f])
    u = gu_ref[0, :, f:]
    dg = (gh * u * slope).astype(bf16)
    du = (gh * act).astype(bf16)
    if emit:
        dgu_ref[0, :, :f] = dg
        dgu_ref[0, :, f:] = du
        hid_ref[0] = (act * u).astype(bf16)
    gy_ref[...] += dot(dg, w_ref[0, :f, :]) + dot(du, w_ref[0, f : 2 * f, :])

    @pl.when(i == pl.num_programs(0) - 1)
    def _():
        back, gain_grad = norm_back(y_ref[...], g_in_ref[...], gy_ref[...])
        gg_ref[0:1, :] = gain_grad
        gy_ref[...] = last_ref[...] + back


def feed_bwd(up, y, y2, gain_in, gain_out, gu, w, emit):
    t, d = y.shape
    nb, rows, _ = w.shape
    f = rows // 3
    whole = lambda *shape: pl.BlockSpec(shape, lambda i: (0,) * len(shape))
    part = lambda *shape: pl.BlockSpec((1,) + shape, lambda i: (i, 0, 0))
    outs = [
        jax.ShapeDtypeStruct((t, d), bf16),
        jax.ShapeDtypeStruct((t, d), f32),
        jax.ShapeDtypeStruct((2, d), f32),
    ]
    specs = [whole(t, d), whole(t, d), whole(2, d)]
    if emit:
        outs += [
            jax.ShapeDtypeStruct((nb, t, 2 * f), bf16),
            jax.ShapeDtypeStruct((nb, t, f), bf16),
        ]
        specs += [part(t, 2 * f), part(t, f)]
    return pl.pallas_call(
        functools.partial(feed_bwd_kernel, emit),
        grid=(nb,),
        out_shape=tuple(outs),
        in_specs=[whole(t, d)] * 3 + [whole(1, d)] * 2 + [part(t, 2 * f), part(rows, d)],
        out_specs=tuple(specs),
        scratch_shapes=[pltpu.VMEM((t, d), f32)],
        compiler_params=pltpu.CompilerParams(vmem_limit_bytes=VMEM_BYTES),
        cost_estimate=pl.CostEstimate(
            flops=2 * t * d * rows * nb,
            bytes_accessed=w.size * 2 + t * d * 18 + nb * t * f * 8,
            transcendentals=nb * t * f,
        ),
    )(up, y, y2, gain_in, gain_out, gu, w)


def head_kernel(length, cnt_ref, f_ref, w_ref, target_ref, gl_ref, up_ref, loss_ref):
    loss_ref[...] = loss_back(cnt_ref, f_ref, w_ref, target_ref, gl_ref, length)
    up_ref[...] = dot(gl_ref[...], w_ref[...])


def head_loss(counts, final, w, target, length):
    t, d = final.shape
    v = w.shape[0]
    vm = pl.BlockSpec(memory_space=pltpu.VMEM)
    return pl.pallas_call(
        functools.partial(head_kernel, length),
        out_shape=(
            jax.ShapeDtypeStruct((t, v), bf16),
            jax.ShapeDtypeStruct((t, d), f32),
            jax.ShapeDtypeStruct((1, 1), f32),
        ),
        in_specs=[pl.BlockSpec(memory_space=pltpu.SMEM), vm, vm, vm],
        out_specs=(vm,) * 3,
        compiler_params=pltpu.CompilerParams(vmem_limit_bytes=VMEM_BYTES),
        cost_estimate=pl.CostEstimate(
            flops=4 * t * d * v, bytes_accessed=w.size * 2 + t * d * 6, transcendentals=t * v * 2
        ),
    )(counts, final, w, target)


def tail_kernel(
    tiny_ref, gf_ref, lefts_ref, n1_ref, ga_ref, w_ref, n_all_ref,
    feed_ref, attn_ref, total_ref,
    shards, n_buf, part, from_core, four, from_y, from_far, from_near, from_cross, from_out, cross_out,
    ag_send, ag_recv, rs_send, rs_recv, n_sem,
):
    me = lax.axis_index("rows")
    z, y, c = me // 4, (me // 2) % 2, me % 2
    high = z // 2
    inner = (z + high) % 2
    t = gf_ref.shape[0]
    f = w_ref.shape[0] // 3
    core_peer, y_peer = me + 1 - 2 * c, me + 2 - 4 * y
    toward = me + 4 - 8 * high
    across = me + 4 - 8 * high
    outward = me - 4 + 8 * high

    def remote(src, dst, send, recv, device):
        return pltpu.make_async_remote_copy(
            src_ref=src, dst_ref=dst, send_sem=send, recv_sem=recv,
            device_id={"rows": device}, device_id_type=pl.DeviceIdType.MESH,
        )

    barrier = pltpu.get_barrier_semaphore()

    def greet(device):
        pl.semaphore_signal(
            barrier, inc=1, device_id={"rows": device}, device_id_type=pl.DeviceIdType.MESH
        )

    greet(core_peer)
    greet(y_peer)
    greet(toward)

    @pl.when(inner == 1)
    def _():
        greet(outward)

    pl.semaphore_wait(barrier, 3 + inner)

    def piece(p):
        odd = p % 2
        j = jnp.where(p == 0, 0, jnp.where(p == 7, 3, jnp.where(odd == 1, (p + 1) // 2, p // 2 - 1)))
        other = jnp.where(p == 0, 0, jnp.where(p == 7, 1, 1 - odd))
        first, second, third = z + 1 - 2 * (z % 2), 2 - high, 3 - 3 * high
        zz = jnp.where(j == 0, z, jnp.where(j == 1, first, jnp.where(j == 2, second, third)))
        yy = y + other - 2 * other * y
        return zz, yy, other

    def shard_copy(kind, p, s, device):
        return remote(shards.at[s], shards.at[s], ag_send.at[kind, p], ag_recv.at[s], device)

    def each_send(p, zz, yy, other, act):
        s = 4 * zz + 2 * yy + c

        @pl.when((other == 0) & (zz <= z) & (z < 3))
        def _():
            act(shard_copy(0, p, s, me + 4))

        @pl.when((other == 0) & (zz >= z) & (z > 0))
        def _():
            act(shard_copy(1, p, s, me - 4))

        @pl.when(other == 0)
        def _():
            act(shard_copy(2, p, s, y_peer))

        act(shard_copy(3, p, s, core_peer))

    def n_copy(p):
        zz, yy, _ = piece(p)
        rows = pl.ds((2 * zz + yy) * (2 * t), 2 * t)
        slot = p % 2
        return pltpu.make_async_copy(n_all_ref.at[rows], n_buf.at[slot], n_sem.at[slot])

    n_copy(0).start()
    shards[me, :t, :] = gf_ref[...]
    tiny = tiny_ref[...]
    tiny_high = tiny.astype(bf16)
    tiny_low = (tiny - tiny_high.astype(f32)).astype(bf16)
    shards[me, t:, :] = jnp.concatenate([tiny_high, tiny_low], axis=0)
    each_send(0, z, y, 0, lambda copy: copy.start())

    blocks, per = part.shape[1:3]
    row = lax.broadcasted_iota(jnp.int32, (blocks * per, n1_ref.shape[1]), 0)
    from_mixed = row % per >= per // 4 * 3

    def half_sums(half):
        left = lefts_ref[half]
        both = jnp.where(from_mixed, dot(left, ga_ref[...]), dot(left, n1_ref[...]))
        return both.reshape(blocks, per, -1)

    part[0] = half_sums(1 - c).astype(bf16)
    to_core = remote(part.at[0], from_core, rs_send.at[0], rs_recv.at[0], core_peer)
    to_core.start()
    own_half = half_sums(c)
    to_core.wait_recv()
    part[1] = (own_half + from_core[...].astype(f32)).astype(bf16)
    quarter = blocks // 2
    to_y = remote(
        part.at[1, pl.ds((1 - y) * quarter, quarter)], from_y, rs_send.at[1], rs_recv.at[1], y_peer
    )
    to_y.start()

    far = 2 - 2 * high
    far_copy = remote(four.at[pl.ds(far, 2)], from_far, rs_send.at[2], rs_recv.at[2], toward)
    near_copy = remote(four.at[1 + high], from_near, rs_send.at[3], rs_recv.at[3], toward)
    cross_copy = remote(four.at[pl.ds(far, 2)], from_cross, rs_send.at[4], rs_recv.at[4], across)
    out_copy = remote(cross_out, from_out, rs_send.at[5], rs_recv.at[5], outward)

    def stage_y():
        to_y.wait_recv()
        mine = part[1, pl.ds(y * quarter, quarter)].astype(f32)
        four[...] = (mine + from_y[...].astype(f32)).astype(bf16)

        @pl.when(inner == 0)
        def _():
            far_copy.start()
            near_copy.start()

    def stage_cross():
        @pl.when(inner == 1)
        def _():
            far_copy.wait_recv()
            both = four[pl.ds(far, 2)].astype(f32) + from_far[...].astype(f32)
            four[pl.ds(far, 2)] = both.astype(bf16)
            cross_copy.start()

    def stage_out():
        @pl.when(inner == 1)
        def _():
            near_copy.wait_recv()
            cross_copy.wait_recv()
            attn_ref[...] = (
                four[z].astype(f32) + from_near[...].astype(f32) + from_cross[1 - high].astype(f32)
            )
            out = four[3 * high].astype(f32) + from_cross[high].astype(f32)
            cross_out[...] = out.astype(bf16)
            out_copy.start()

    def stage_end():
        @pl.when(inner == 0)
        def _():
            out_copy.wait_recv()
            attn_ref[...] = four[z].astype(f32) + from_out[...].astype(f32)

    feed_ref[...] = jnp.zeros_like(feed_ref)

    def visit(p, carry):
        zz, yy, other = piece(p)
        pair = 4 * zz + 2 * yy

        @pl.when(p > 0)
        def _():
            shard_copy(0, p, pair + c, me).wait_recv()
            each_send(p, zz, yy, other, lambda copy: copy.start())

        shard_copy(0, p, pair + 1 - c, me).wait_recv()

        @pl.when(p < 7)
        def _():
            n_copy(p + 1).start()

        n_copy(p).wait()
        n_rows = n_buf[p % 2]
        g_rows = jnp.concatenate([shards[pair, :t, :], shards[pair + 1, :t, :]], axis=0)
        gu = dot_last(n_rows, w_ref[: 2 * f, :])
        gh = dot_last(g_rows, w_ref[2 * f :, :])
        act, slope = gelu_parts(gu[:, :f])
        up = gu[:, f:]
        dg = (gh * up * slope).astype(bf16)
        du = (gh * act).astype(bf16)
        hid = (act * up).astype(bf16)
        feed_ref[:f, :] += dot_rows(dg, n_rows)
        feed_ref[f : 2 * f, :] += dot_rows(du, n_rows)
        feed_ref[2 * f :, :] += dot_rows(hid, g_rows)
        pl.when(p == 3)(stage_y)
        pl.when(p == 4)(stage_cross)
        pl.when(p == 5)(stage_out)
        pl.when(p == 6)(stage_end)
        return carry

    lax.fori_loop(0, 8, visit, 0)

    def add_tiny(s, total):
        both = shards[s, t:, :].astype(f32)
        return total + both[:8] + both[8:]

    total_ref[...] = lax.fori_loop(0, 16, add_tiny, jnp.zeros(total_ref.shape, f32))

    def settle(p, carry):
        zz, yy, other = piece(p)
        each_send(p, zz, yy, other, lambda copy: copy.wait_send())
        return carry

    lax.fori_loop(0, 8, settle, 0)
    to_core.wait_send()
    to_y.wait_send()

    @pl.when(inner == 0)
    def _():
        far_copy.wait_send()
        near_copy.wait_send()

    @pl.when(inner == 1)
    def _():
        cross_copy.wait_send()
        out_copy.wait_send()


def tail(tiny, gf, lefts, n1, ga, w_own, n_all):
    t, d = gf.shape
    rows = w_own.shape[0]
    blocks = 8
    per = lefts.shape[1] // blocks
    vm = pl.BlockSpec(memory_space=pltpu.VMEM)
    return pl.pallas_call(
        tail_kernel,
        out_shape=(
            jax.ShapeDtypeStruct((rows, d), f32),
            jax.ShapeDtypeStruct((per, d), f32),
            jax.ShapeDtypeStruct(tiny.shape, f32),
        ),
        in_specs=[vm] * 6 + [pl.BlockSpec(memory_space=pl.ANY)],
        out_specs=(vm,) * 3,
        scratch_shapes=[
            pltpu.VMEM((16, t + 16, d), bf16),
            pltpu.VMEM((2, 2 * t, d), bf16),
            pltpu.VMEM((2, blocks, per, d), bf16),
            pltpu.VMEM((blocks, per, d), bf16),
            pltpu.VMEM((4, per, d), bf16),
            pltpu.VMEM((4, per, d), bf16),
            pltpu.VMEM((2, per, d), bf16),
            pltpu.VMEM((per, d), bf16),
            pltpu.VMEM((2, per, d), bf16),
            pltpu.VMEM((per, d), bf16),
            pltpu.VMEM((per, d), bf16),
            pltpu.SemaphoreType.DMA((4, 8)),
            pltpu.SemaphoreType.DMA((16,)),
            pltpu.SemaphoreType.DMA((6,)),
            pltpu.SemaphoreType.DMA((6,)),
            pltpu.SemaphoreType.DMA((2,)),
        ],
        compiler_params=pltpu.CompilerParams(
            vmem_limit_bytes=VMEM_BYTES, collective_id=0, has_side_effects=True
        ),
        cost_estimate=pl.CostEstimate(
            flops=2 * t * 16 * d * rows * 2, bytes_accessed=16 * t * d * 4, transcendentals=16 * t * rows
        ),
    )(tiny, gf, lefts, n1, ga, w_own, n_all)


def front_kernel(
    length, cnt_ref, order_ref, x_ref, g_attn_ref, g_feed_ref, g_final_ref,
    attn_own, feed_own, half_own,
    attn_all, feed_all, first_all, second_all,
    n1_ref, qkv_ref, mixed_ref, y1_ref, n2_ref, gu_ref, y2_ref, enc_ref, arrived_ref,
    w_attn, w_feed, place, wide_buf, first_own,
    send_sem, recv_sem, own_sem, load_sem, x_send, x_recv,
):
    section = lax.axis_index("section")
    me = lax.axis_index("rows")
    z, y, c = me // 4, (me // 2) % 2, me % 2
    core_peer, y_peer = me + 1 - 2 * c, me + 2 - 4 * y
    mesh_id = pl.DeviceIdType.MESH
    inner = mixed_ref.shape[1]
    f = feed_own.shape[0] // 3

    barrier = pltpu.get_barrier_semaphore()

    def greet(where):
        pl.semaphore_signal(barrier, inc=1, device_id=where, device_id_type=mesh_id)

    greet({"rows": core_peer})
    greet({"rows": y_peer})
    greet({"section": 1 - section})

    @pl.when(z > 0)
    def _():
        greet({"rows": me - 4})

    @pl.when(z < 3)
    def _():
        greet({"rows": me + 4})

    own_copies = [
        pltpu.make_async_copy(own, whole.at[me], own_sem.at[k])
        for k, (own, whole) in enumerate(
            [(attn_own, attn_all), (feed_own, feed_all), (half_own, second_all)]
        )
    ]
    own_copies[0].start()
    own_copies[1].start()

    @pl.when(section == 1)
    def _():
        own_copies[2].start()

    pl.semaphore_wait(barrier, 4 + (z + z // 2) % 2)

    def remote(src, dst, send, recv, where):
        return pltpu.make_async_remote_copy(
            src_ref=src, dst_ref=dst, send_sem=send, recv_sem=recv,
            device_id=where, device_id_type=mesh_id,
        )

    kinds = [pl.ds(k * f, f) for k in range(3)]
    parts = {
        "A": (0, attn_all, None, 2, attn_own),
        "G": (1, feed_all, kinds[0], 1, feed_own.at[kinds[0]]),
        "U": (2, feed_all, kinds[1], 1, feed_own.at[kinds[1]]),
        "O": (3, feed_all, kinds[2], 1, feed_own.at[kinds[2]]),
        "X": (4, first_all, None, 1, first_own),
        "Y": (5, second_all, None, 2, half_own),
    }

    def place_of(route, p):
        if route == 1:
            j, other = [(0, 0), (1, 0), (0, 1), (2, 0), (1, 1), (3, 0), (2, 1), (3, 1)][p]
        else:
            j, other = p // 2, p % 2
        zz = [z, z + 1 - 2 * (z % 2), 2 - z // 2, 3 - 3 * (z // 2)][j]
        yy = y + other - 2 * other * y
        return zz, yy, other

    def part_copy(name, kind, p, s, where):
        k, whole, rows, _, own = parts[name]
        dst = whole.at[s] if rows is None else whole.at[s, rows]
        return remote(own if p == 0 else dst, dst, send_sem.at[k, kind, p], recv_sem.at[k, s], where)

    def each_send(name, p, act, ways="zyc"):
        route = parts[name][3]
        zz, yy, other = place_of(route, p)
        s = 4 * zz + 2 * yy + c
        if "z" in ways and (route == 2 or other == 0):

            @pl.when((zz <= z) & (z < 3))
            def _():
                act(part_copy(name, 0, p, s, {"rows": me + 4}))

            @pl.when((zz >= z) & (z > 0))
            def _():
                act(part_copy(name, 1, p, s, {"rows": me - 4}))

        if "y" in ways and (p == 0 or (route == 1 and other == 0)):
            act(part_copy(name, 2, p, s, {"rows": y_peer}))
        if "c" in ways:
            act(part_copy(name, 3, p, s, {"rows": core_peer}))

    def begin(name, ways):
        each_send(name, 0, lambda copy: copy.start(), ways)

    def arrive(name, p):
        zz, yy, _ = place_of(parts[name][3], p)
        part_copy(name, 0, p, 4 * zz + 2 * yy + c, {"rows": me}).wait_recv()
        each_send(name, p, lambda copy: copy.start())

    def meet(name, p):
        zz, yy, _ = place_of(parts[name][3], p)
        part_copy(name, 0, p, 4 * zz + 2 * yy + 1 - c, {"rows": me}).wait_recv()

    def settle(name):
        for p in range(8):
            each_send(name, p, lambda copy: copy.wait_send())

    half_copy = remote(half_own, first_own, x_send.at[0], x_recv.at[0], {"section": 1 - section})
    enc_copy = remote(enc_ref, arrived_ref, x_send.at[1], x_recv.at[1], {"section": 1 - section})
    own_first = pltpu.make_async_copy(first_own, first_all.at[me], own_sem.at[3])

    def project():
        for p in range(8):
            meet("A", p)
        own_copies[0].wait()
        load = pltpu.make_async_copy(attn_all, w_attn, load_sem.at[0])
        load.start()
        load.wait()
        wide_buf[...] = dot_last(n1_ref[...], w_attn[...].reshape(4 * inner, -1)).astype(bf16)
        qkv_ref[...] = dot(wide_buf[...], place[:, : 3 * inner]).astype(bf16)

    def mix(s):
        low = low_half(length)
        allowed = allowed_twice(cnt_ref, s, length)
        rows = slice(s * length, (s + 1) * length)
        for h in range(inner // PAIR):
            cols = [slice(j * inner + h * PAIR, j * inner + (h + 1) * PAIR) for j in range(3)]
            q2 = stack_pair(qkv_ref[rows, cols[0]], low)
            p = soft_pair(q2, qkv_ref[rows, cols[1]], allowed).astype(bf16)
            wide = jnp.concatenate([p[:length], p[length:]], axis=1)
            mixed_ref[rows, cols[0]] = dot(wide, stack_pair(qkv_ref[rows, cols[2]], low)).astype(bf16)

    def mix_out():
        for s in range(x_ref.shape[0] // length // 2, x_ref.shape[0] // length):
            mix(s)
        wide_buf[...] = dot_last(mixed_ref[...], place[:, 3 * inner :]).astype(bf16)
        y1_ref[...] = x_ref[...].astype(f32) + dot(wide_buf[...], w_attn[...].reshape(4 * inner, -1))
        y2_ref[...] = y1_ref[...]
        n2_ref[...] = (unit_rows(y1_ref[...])[1] * g_feed_ref[...]).astype(bf16)

    def mix_first():
        for s in range(x_ref.shape[0] // length // 2):
            mix(s)

    def feed(p):
        if p == 0:
            own_copies[1].wait()
        for name in "GUO":
            meet(name, p)
        zz, yy, _ = place_of(1, p)
        pair = 4 * zz + 2 * yy

        @pl.when(section == 0)
        def _():
            blocks = pltpu.make_async_copy(feed_all.at[pl.ds(pair, 2)], w_feed, load_sem.at[1])
            blocks.start()
            blocks.wait()
            for k in range(2):
                gu = dot_last(n2_ref[...], w_feed[k, : 2 * f, :])
                gu_ref[pair + k] = gu
                hidden = (gelu_parts(gu[:, :f])[0] * gu[:, f:]).astype(bf16)
                y2_ref[...] += dot(hidden, w_feed[k, 2 * f :, :])

    begin("A", "zyc")

    @pl.when(section == 0)
    def _():
        half_copy.start()

    @pl.when(section == 1)
    def _():
        begin("Y", "yc")

    for name in "GUO":
        begin(name, "yc")
    begin("G", "z")

    @pl.when(section == 1)
    def _():
        begin("Y", "z")

    row = lax.broadcasted_iota(jnp.int32, place.shape, 0)
    place[...] = jnp.where(row == order_ref[...], 1.0, 0.0).astype(bf16)
    n1_ref[...] = (unit_rows(x_ref[...].astype(f32))[1] * g_attn_ref[...]).astype(bf16)

    tasks = {"c1": project, "c2": mix_first, "c3": mix_out}
    for step in FRONT_STEPS:
        if step in tasks:
            tasks[step]()
        elif step[0] == "f":
            feed(int(step[1]))
        elif step[0] == "o":
            begin(step[1], "z")
        elif step == "X0":

            @pl.when(section == 1)
            def _():
                half_copy.wait_recv()
                own_first.start()
                begin("X", "zyc")

        elif step[0] == "X":

            @pl.when(section == 1)
            def _(p=int(step[1])):
                arrive("X", p)
                arrive("Y", p)

        else:
            arrive(step[0], int(step[1]))

    @pl.when(section == 0)
    def _():
        enc_ref[...] = (unit_rows(y2_ref[...])[1] * g_final_ref[...]).astype(bf16)
        enc_copy.start()

    for name in "AGUO":
        settle(name)

    @pl.when(section == 1)
    def _():
        for name in "XY":
            for p in range(8):
                meet(name, p)
            settle(name)
        own_first.wait()
        own_copies[2].wait()
        enc_copy.wait_recv()

    @pl.when(section == 0)
    def _():
        half_copy.wait_send()
        enc_copy.wait_send()


FRONT_STEPS = (
    ("A1", "oU", "G1", "A2", "X0", "A3", "oO", "A4", "O1", "U1", "G2", "U2", "O2", "A5", "A6", "X1", "X2", "G3", "A7")
    + ("c1", "O3", "G4", "O4", "U3", "c2", "U4", "c3", "f0", "O5", "f1", "U5", "U6", "G5", "O6", "X3", "X4", "X5")
    + ("X6", "O7", "f2", "f3", "G6", "f4", "f5", "U7", "f6", "X7", "G7", "f7")
)


def front(counts, order, x, gain_attn, gain_feed, gain_final, attn_own, feed_own, half_own, length):
    t, d = x.shape
    attn_rows, feed_rows = attn_own.shape[0], feed_own.shape[0]
    inner = attn_rows * 4
    half_shape = (16,) + half_own.shape
    vm = pl.BlockSpec(memory_space=pltpu.VMEM)
    anywhere = pl.BlockSpec(memory_space=pl.ANY)
    return pl.pallas_call(
        functools.partial(front_kernel, length),
        out_shape=(
            jax.ShapeDtypeStruct((16, attn_rows, d), bf16),
            jax.ShapeDtypeStruct((16, feed_rows, d), bf16),
            jax.ShapeDtypeStruct(half_shape, bf16),
            jax.ShapeDtypeStruct(half_shape, bf16),
            jax.ShapeDtypeStruct((t, d), bf16),
            jax.ShapeDtypeStruct((t, 3 * inner), bf16),
            jax.ShapeDtypeStruct((t, inner), bf16),
            jax.ShapeDtypeStruct((t, d), f32),
            jax.ShapeDtypeStruct((t, d), bf16),
            jax.ShapeDtypeStruct((16, t, feed_rows // 3 * 2), f32),
            jax.ShapeDtypeStruct((t, d), f32),
            jax.ShapeDtypeStruct((t, d), bf16),
            jax.ShapeDtypeStruct((t, d), bf16),
        ),
        in_specs=[pl.BlockSpec(memory_space=pltpu.SMEM)] + [vm] * 5 + [anywhere] * 3,
        out_specs=(anywhere,) * 4 + (vm,) * 9,
        scratch_shapes=[
            pltpu.VMEM((16, attn_rows, d), bf16),
            pltpu.VMEM((2, feed_rows, d), bf16),
            pltpu.VMEM((4 * inner, 4 * inner), bf16),
            pltpu.VMEM((t, 4 * inner), bf16),
            pltpu.VMEM(half_own.shape, bf16),
            pltpu.SemaphoreType.DMA((6, 4, 8)),
            pltpu.SemaphoreType.DMA((6, 16)),
            pltpu.SemaphoreType.DMA((4,)),
            pltpu.SemaphoreType.DMA((2,)),
            pltpu.SemaphoreType.DMA((2,)),
            pltpu.SemaphoreType.DMA((2,)),
        ],
        compiler_params=pltpu.CompilerParams(
            vmem_limit_bytes=VMEM_BYTES, collective_id=1, has_side_effects=True
        ),
        cost_estimate=pl.CostEstimate(
            flops=2 * t * d * (feed_rows * 16 + 8 * inner),
            bytes_accessed=2 * 16 * (attn_rows + feed_rows) * d * 2,
            transcendentals=t * feed_rows * 6,
        ),
    )(counts, order, x, gain_attn, gain_feed, gain_final, attn_own, feed_own, half_own)


def mid_kernel(
    length, cross_cnt, self_cnt, dec_cnt, x_ref, y1_ref, y2_in, n2_in, qkv_ref, encoded_ref, target_ref, gain_ref,
    gu_in, attn_w, cross_w, head_w, feed_w,
    n_all, gf_ref, ga_ref, dqkv_ref, gx_ref, sums_ref, mc_ref, dcqkv_ref, cmixed_ref, gac_ref, final_ref, gl_ref,
    slots, gu_buf, w_att, w_head, mid, y2, acc, last, n2, cqkv, do_buf, grad_enc, returned,
    send_sem, recv_sem, slot_sem, load_sem, own_sem, x_send, x_recv,
):
    section = lax.axis_index("section")
    me = lax.axis_index("rows")
    z, y, c = me // 4, (me // 2) % 2, me % 2
    core_peer, y_peer = me + 1 - 2 * c, me + 2 - 4 * y
    mesh_id = pl.DeviceIdType.MESH
    inner = w_att.shape[0] // 4
    f = feed_w.shape[1] // 3
    t = n2.shape[0]
    held = slots.shape[0]
    spare = BLOCKS - held
    is_enc, is_dec = section == 0, section == 1

    def load(b):
        k = b % held
        return pltpu.make_async_copy(feed_w.at[b], slots.at[k], slot_sem.at[k])

    load_attn = pltpu.make_async_copy(attn_w, w_att, load_sem.at[0])
    load_cross = pltpu.make_async_copy(cross_w, w_att, load_sem.at[1])
    load_head = pltpu.make_async_copy(head_w, w_head, load_sem.at[2])
    load_gu = pltpu.make_async_copy(gu_in, gu_buf, load_sem.at[3])

    def start_loads(first):
        def step(k, carry):
            load(first + k).start()
            return carry

        lax.fori_loop(0, held, step, 0)

    @pl.when(is_enc)
    def _():
        start_loads(spare)
        load_gu.start()
        load_attn.start()

    @pl.when(is_dec)
    def _():
        load_cross.start()
        start_loads(0)
        load_head.start()

    barrier = pltpu.get_barrier_semaphore()

    def greet(where):
        pl.semaphore_signal(barrier, inc=1, device_id=where, device_id_type=mesh_id)

    greet({"rows": core_peer})
    greet({"rows": y_peer})
    greet({"section": 1 - section})

    @pl.when(z > 0)
    def _():
        greet({"rows": me - 4})

    @pl.when(z < 3)
    def _():
        greet({"rows": me + 4})

    pl.semaphore_wait(barrier, 4 + (z + z // 2) % 2)

    def remote(src, dst, send, recv, where):
        return pltpu.make_async_remote_copy(
            src_ref=src, dst_ref=dst, send_sem=send, recv_sem=recv,
            device_id=where, device_id_type=mesh_id,
        )

    cut = t // 16 * 11 // 16 * 16 if t >= 256 else t // 2
    parts = {"S": (0, pl.ds(0, cut), 1), "Q": (1, pl.ds(cut, t - cut), 2)}

    def place_of(route, p):
        if route == 1:
            j, other = [(0, 0), (1, 0), (0, 1), (2, 0), (1, 1), (3, 0), (2, 1), (3, 1)][p]
        else:
            j, other = p // 2, p % 2
        zz = [z, z + 1 - 2 * (z % 2), 2 - z // 2, 3 - 3 * (z // 2)][j]
        yy = y + other - 2 * other * y
        return zz, yy, other

    def part_copy(name, kind, p, s, where):
        k, rows, _ = parts[name]
        dst = n_all.at[s, rows]
        src = n2.at[rows] if p == 0 else dst
        return remote(src, dst, send_sem.at[k, kind, p], recv_sem.at[k, s], where)

    def each_send(name, p, act):
        route = parts[name][2]
        zz, yy, other = place_of(route, p)
        s = 4 * zz + 2 * yy + c
        if route == 2 or other == 0:

            @pl.when((zz <= z) & (z < 3))
            def _():
                act(part_copy(name, 0, p, s, {"rows": me + 4}))

            @pl.when((zz >= z) & (z > 0))
            def _():
                act(part_copy(name, 1, p, s, {"rows": me - 4}))

        if p == 0 or (route == 1 and other == 0):
            act(part_copy(name, 2, p, s, {"rows": y_peer}))
        act(part_copy(name, 3, p, s, {"rows": core_peer}))

    own_copy = pltpu.make_async_copy(n2, n_all.at[me], own_sem.at[0])

    def begin():
        own_copy.start()
        for name in "QS":
            each_send(name, 0, lambda copy: copy.start())

    def arrive(*steps):
        for name, p in steps:
            zz, yy, _ = place_of(parts[name][2], p)
            part_copy(name, 0, p, 4 * zz + 2 * yy + c, {"rows": me}).wait_recv()
            each_send(name, p, lambda copy: copy.start())

    back_copy = remote(grad_enc, returned, x_send.at[0], x_recv.at[0], {"section": 1 - section})

    def feed_forward(first, count):
        def step(i, carry):
            for k in range(2):
                b = first + 2 * i + k
                load(b).wait()
                w = slots.at[b % held]
                gu = dot_last(n2[...], w[: 2 * f, :])
                gu_buf[b] = gu
                hidden = (gelu_parts(gu[:, :f])[0] * gu[:, f:]).astype(bf16)
                y2[...] += dot(hidden, w[2 * f :, :])

                @pl.when(b < spare)
                def _():
                    load(b + held).start()

            return carry

        lax.fori_loop(0, count // 2, step, 0)

    def feed_backward(first, count, fresh):
        def step(i, carry):
            for k in range(2):
                b = BLOCKS - 1 - first - 2 * i - k

                @pl.when((b < spare) | fresh)
                def _():
                    load(b).wait()

                w = slots.at[b % held]
                gh = dot_last(gf_ref[...], w[2 * f :, :])
                gu = gu_buf[b]
                act, slope = gelu_parts(gu[:, :f])
                dg = (gh * gu[:, f:] * slope).astype(bf16)
                du = (gh * act).astype(bf16)
                acc[...] += dot(dg, w[:f, :]) + dot(du, w[f : 2 * f, :])

                @pl.when(b >= held)
                def _():
                    load(b - held).start()

            return carry

        lax.fori_loop(0, count // 2, step, 0)

    def final_backward(up):
        back, sums_ref[2:3, :] = norm_back(y2[...], gain_ref[2:3, :], up)
        last[...] = back
        gf_ref[...] = back.astype(bf16)
        acc[...] = jnp.zeros_like(acc)

    def feed_end():
        back, sums_ref[1:2, :] = norm_back(mid[...], gain_ref[1:2, :], acc[...])
        acc[...] = last[...] + back

    sums_ref[...] = jnp.zeros_like(sums_ref)

    @pl.when(is_enc)
    def _():
        n2[...] = n2_in[...]
        begin()
        mid[...] = y1_ref[...]
        y2[...] = y2_in[...]
        arrive(("Q", 1), ("Q", 2), ("S", 1), ("S", 2), ("Q", 3), ("Q", 4), ("S", 4), ("S", 3), ("Q", 5), ("Q", 6))
        back_copy.wait_recv()
        final_backward(returned[...].astype(f32))
        load_gu.wait()
        arrive(("S", 6))
        feed_backward(0, 8, True)
        arrive(("S", 5))
        feed_backward(8, 8, True)
        feed_end()
        load_attn.wait()

    @pl.when(is_dec)
    def _():
        y1 = y1_ref[...]
        mc_ref[...] = (unit_rows(y1)[1] * gain_ref[3:4, :]).astype(bf16)
        load_cross.wait()
        cqkv[:, :inner] = dot_last(mc_ref[...], w_att[:inner, :]).astype(bf16)
        cqkv[:, inner:] = dot_last(encoded_ref[...], w_att[inner : 3 * inner, :]).astype(bf16)
        heads_fwd(cross_cnt, cqkv, cmixed_ref, length)
        mid[...] = y1_ref[...] + dot(cmixed_ref[...], w_att[3 * inner :, :])
        y2[...] = mid[...]
        n2[...] = (unit_rows(mid[...])[1] * gain_ref[1:2, :]).astype(bf16)
        begin()
        feed_forward(0, 12)
        arrive(("Q", 1), ("Q", 2))
        feed_forward(12, 4)
        final_ref[...] = (unit_rows(y2[...])[1] * gain_ref[2:3, :]).astype(bf16)
        load_head.wait()
        loss = loss_back(dec_cnt, final_ref, w_head, target_ref, gl_ref, length)
        sums_ref[4:5, :] = jnp.broadcast_to(loss, (1, sums_ref.shape[1]))
        final_backward(dot(gl_ref[...], w_head[...]))
        feed_backward(0, 8, False)
        arrive(("S", 1), ("S", 2))
        feed_backward(8, 8, False)
        feed_end()
        arrive(("Q", 3))
        gac_ref[...] = acc[...].astype(bf16)
        do_buf[...] = dot_last(gac_ref[...], w_att[3 * inner :, :]).astype(bf16)
        heads_bwd(cross_cnt, cqkv, do_buf, dcqkv_ref, length)
        grad_enc[...] = dot(dcqkv_ref[:, inner:], w_att[inner : 3 * inner, :]).astype(bf16)
        back_copy.start()
        up = dot(dcqkv_ref[:, :inner], w_att[:inner, :])
        load_attn.start()
        back, sums_ref[3:4, :] = norm_back(y1_ref[...], gain_ref[3:4, :], up)
        acc[...] += back
        arrive(("Q", 4), ("S", 4))
        load_attn.wait()

    ga_ref[...] = acc[...].astype(bf16)
    do_buf[...] = dot_last(ga_ref[...], w_att[3 * inner :, :]).astype(bf16)
    heads_bwd(self_cnt, qkv_ref, do_buf, dqkv_ref, length)
    up = dot(dqkv_ref[...], w_att[: 3 * inner, :])
    back, sums_ref[0:1, :] = norm_back(x_ref[...].astype(f32), gain_ref[0:1, :], up)
    gx_ref[...] = acc[...] + back

    @pl.when(is_dec)
    def _():
        arrive(("S", 3), ("Q", 5), ("Q", 6), ("S", 6), ("S", 5))

    arrive(("Q", 7), ("S", 7))
    for name in parts:
        for p in range(8):
            zz, yy, _ = place_of(parts[name][2], p)
            part_copy(name, 0, p, 4 * zz + 2 * yy + 1 - c, {"rows": me}).wait_recv()
            each_send(name, p, lambda copy: copy.wait_send())
    own_copy.wait()

    @pl.when(is_dec)
    def _():
        back_copy.wait_send()


def middle(cross_cnt, self_cnt, dec_cnt, x, y1, y2, n2, qkv, encoded, target, gains, gu, attn_w, cross_w, head_w, feed_w, length):
    t, d = x.shape
    inner = attn_w.shape[0] // 4
    held = 10
    vm = pl.BlockSpec(memory_space=pltpu.VMEM)
    sm = pl.BlockSpec(memory_space=pltpu.SMEM)
    anywhere = pl.BlockSpec(memory_space=pl.ANY)
    half = jax.ShapeDtypeStruct((t, d), bf16)
    wide = jax.ShapeDtypeStruct((t, 3 * inner), bf16)
    return pl.pallas_call(
        functools.partial(mid_kernel, length),
        out_shape=(
            jax.ShapeDtypeStruct((16, t, d), bf16),
            half, half, wide,
            jax.ShapeDtypeStruct((t, d), f32),
            jax.ShapeDtypeStruct((8, d), f32),
            half, wide,
            jax.ShapeDtypeStruct((t, inner), bf16),
            half, half,
            jax.ShapeDtypeStruct((t, head_w.shape[0]), bf16),
        ),
        in_specs=[sm] * 3 + [vm] * 8 + [anywhere] * 5,
        out_specs=(anywhere,) + (vm,) * 11,
        scratch_shapes=[
            pltpu.VMEM((held,) + feed_w.shape[1:], bf16),
            pltpu.VMEM(gu.shape, f32),
            pltpu.VMEM(attn_w.shape, bf16),
            pltpu.VMEM(head_w.shape, bf16),
            pltpu.VMEM((t, d), f32),
            pltpu.VMEM((t, d), f32),
            pltpu.VMEM((t, d), f32),
            pltpu.VMEM((t, d), f32),
            pltpu.VMEM((t, d), bf16),
            pltpu.VMEM((t, 3 * inner), bf16),
            pltpu.VMEM((t, inner), bf16),
            pltpu.VMEM((t, d), bf16),
            pltpu.VMEM((t, d), bf16),
            pltpu.SemaphoreType.DMA((2, 4, 8)),
            pltpu.SemaphoreType.DMA((2, 16)),
            pltpu.SemaphoreType.DMA((held,)),
            pltpu.SemaphoreType.DMA((4,)),
            pltpu.SemaphoreType.DMA((1,)),
            pltpu.SemaphoreType.DMA((1,)),
            pltpu.SemaphoreType.DMA((1,)),
        ],
        compiler_params=pltpu.CompilerParams(
            vmem_limit_bytes=62 * 1024 * 1024, collective_id=2, has_side_effects=True
        ),
        cost_estimate=pl.CostEstimate(
            flops=4 * t * feed_w.size, bytes_accessed=2 * feed_w.size + 8 * gu.size, transcendentals=2 * gu.size
        ),
    )(cross_cnt, self_cnt, dec_cnt, x, y1, y2, n2, qkv, encoded, target, gains, gu, attn_w, cross_w, head_w, feed_w)


def adam_step(weight, first_moment, second_moment, gradient, step_rate, weight_decay):
    first_new = 0.9 * first_moment + 0.1 * gradient
    second_new = 0.999 * second_moment + 0.001 * gradient * gradient
    first_fix = 1.0 - 0.9**STEP
    second_fix = 1.0 - 0.999**STEP
    update = first_new / first_fix / (jnp.sqrt(second_new / second_fix) + 1e-08)
    return (first_new, second_new, weight - step_rate * (update + weight_decay * weight))


def kinds_first(gathered, n, kinds, per):
    d = gathered.shape[-1]
    return gathered.reshape(n, kinds, per, d).transpose(1, 0, 2, 3).reshape(kinds * n * per, d)


def owners_first(left, right, n):
    t, k, units = left.shape
    grad = jnp.einsum("tku,td->kud", left, right, preferred_element_type=f32)
    return grad.reshape(k, n, units // n, -1).transpose(1, 0, 2, 3)


def local(
    block_input,
    lengths,
    targets,
    attention_weight,
    attention_first,
    attention_second,
    feed_weight,
    feed_first,
    feed_second,
    norm_gain,
    gain_first,
    gain_second,
    cross_weight,
    cross_first,
    cross_second,
    head_weight,
    head_first,
    head_second,
    cross_gain,
    cross_gain_first,
    cross_gain_second,
):
    n = lax.axis_size("rows")
    is_encoder = lax.axis_index("section") == 0
    micro, length, d = block_input.shape[1:]
    t = micro * length
    per = attention_weight.shape[1]
    f = feed_weight.shape[1]
    inner = per * n

    attn_own = attention_weight[0].astype(bf16).transpose(1, 0, 2).reshape(4 * per, d)
    feed_own = feed_weight[0].astype(bf16).transpose(1, 0, 2)
    half_rows = jnp.concatenate(
        [cross_weight.astype(bf16).transpose(1, 0, 2), head_weight.astype(bf16)[None]], axis=0
    )

    gains = norm_gain[0]
    gain_attn, gain_feed, gain_final = gains[0:1], gains[1:2], gains[2:3]
    gain_cross = cross_gain[None]
    x = block_input[0].reshape(t, d)
    enc_counts = lengths[0, :, 0]
    dec_counts = lengths[1, :, 0]
    zero_one = jnp.zeros((1,), jnp.int32)
    self_counts = jnp.concatenate([jnp.where(is_encoder, 0, 1).astype(jnp.int32)[None], enc_counts])
    cross_counts = jnp.concatenate([zero_one, enc_counts])
    target_column = targets.reshape(t, 1)

    def blank(maker):
        return jax.tree.map(lambda a: jnp.zeros(a.shape, a.dtype), jax.eval_shape(maker))

    emit = n != BLOCKS
    if emit:
        attn_all = lax.all_gather(attn_own, "rows", axis=0, tiled=True)
        attn_w = kinds_first(attn_all, n, 4, per)
        feed_all = lax.all_gather(feed_own.reshape(3 * f, d), "rows", axis=0, tiled=True)
        feed_w = kinds_first(feed_all, n, 3, f).reshape(3, BLOCKS, -1, d)
        feed_w = feed_w.transpose(1, 0, 2, 3).reshape(BLOCKS, -1, d)
        other_half = lax.ppermute(half_rows, "section", [(0, 1)])
        extra_own = jnp.concatenate([other_half, half_rows], axis=-1).reshape(5 * per, d)
        extra_all = lax.all_gather(extra_own, "rows", axis=0, tiled=True)
        n1, qkv, mixed, y1 = attend_fwd(self_counts, x, gain_attn, attn_w, length)

        def enc_feed():
            return feed_fwd(y1, gain_feed, gain_final, feed_w)

        enc_state = lax.cond(is_encoder, enc_feed, lambda: blank(enc_feed))
        encoded = lax.ppermute(enc_state[3], "section", [(0, 1)])
    else:
        units = jnp.arange(4 * inner, dtype=jnp.int32).reshape(n, 4, per)
        order = units.transpose(1, 0, 2).reshape(1, 4 * inner)
        pad = -(5 * per) % 16
        half_own = jnp.pad(half_rows.reshape(5 * per, d // 2), ((0, pad), (0, 0)))
        outs = front(
            self_counts, order, x, gain_attn, gain_feed, gain_final,
            attn_own, feed_own.reshape(3 * f, d), half_own, length,
        )
        attn_all, feed_w, first_all, second_all, n1, qkv, mixed, y1 = outs[:8]
        enc_state, encoded = outs[8:12], outs[12]
        attn_w = kinds_first(attn_all, n, 4, per)
        extra_all = jnp.concatenate([first_all, second_all], axis=-1)[:, : 5 * per]
    extra_w = kinds_first(extra_all, n, 5, per)
    cross_w, head_w = extra_w[: 4 * inner], extra_w[4 * inner :]

    if emit:
        def dec_front():
            mc, cqkv, cmixed, z2 = attend_fwd(cross_counts, y1, gain_cross, cross_w, length, encoded)
            return feed_fwd(z2, gain_feed, gain_final, feed_w) + (mc, cqkv, cmixed, z2)

        def enc_pass():
            rest = jax.eval_shape(dec_front)[4:7]
            return tuple(enc_state) + tuple(jnp.zeros(a.shape, a.dtype) for a in rest) + (y1,)

        n2, gu, y2, final, mc, cqkv, cmixed, mid = lax.cond(is_encoder, enc_pass, dec_front)
        def dec_back():
            gl, up, loss = head_loss(dec_counts, final, head_w, target_column, length)
            feed_out = feed_bwd(up, mid, y2, gain_feed, gain_final, gu, feed_w, emit)
            ga_c, dqkv_c, gy1, gg_c, ge = attend_bwd(
                cross_counts, y1, gain_cross, feed_out[1], cqkv, cross_w, length, True
            )
            return (ge, gy1, feed_out[2], feed_out[0], *feed_out[3:], gl, ga_c, dqkv_c, gg_c, loss)

        back = lax.cond(is_encoder, lambda: blank(dec_back), dec_back)
        returned = lax.ppermute(back[0], "section", [(1, 0)])
        at = 6 if emit else 4
        gl, ga_c, dqkv_c, gg_c, loss = back[at:]

        def enc_back():
            feed_out = feed_bwd(returned, mid, y2, gain_feed, gain_final, gu, feed_w, emit)
            return (feed_out[1], feed_out[2], feed_out[0], *feed_out[3:])

        backs = lax.cond(is_encoder, enc_back, lambda: tuple(back[1:at]))
        gy1, gg_feed, gf = backs[:3]

        ga, dqkv, gx, gg_attn = attend_bwd(self_counts, x, gain_attn, gy1, qkv, attn_w, length)
        tiny = jnp.concatenate(
            [gg_attn, gg_feed, gg_c, jnp.broadcast_to(loss, (1, d)), jnp.zeros((3, d), f32)], axis=0
        )
    else:
        gain_rows = jnp.concatenate([gains, gain_cross], axis=0)
        n2, gu, y2 = enc_state[:3]
        (
            n2_all, gf, ga, dqkv, gx, tiny, mc, dqkv_c, cmixed, ga_c, final, gl,
        ) = middle(
            cross_counts, self_counts, dec_counts, x, y1, y2, n2, qkv, encoded, target_column,
            gain_rows, gu, attn_w, cross_w, head_w, feed_w, length,
        )
        n2_all = n2_all.reshape(n * t, d)

    extra_part = jnp.concatenate(
        [
            owners_first(dqkv_c[:, None, :inner], mc, n),
            owners_first(dqkv_c[:, inner:].reshape(t, 2, inner), encoded, n),
            owners_first(cmixed[:, None], ga_c, n),
            owners_first(gl[:, None], final, n),
        ],
        axis=1,
    ).astype(bf16)
    if not emit:
        extra_part, gx = lax.optimization_barrier((extra_part, gx))
    extra_sum = lax.psum_scatter(
        extra_part.reshape(n * 5 * per, d), "rows", scatter_dimension=0, tiled=True
    )
    half = d // 2
    extra_first = lax.ppermute(extra_sum[:, :half], "section", [(1, 0)])
    extra_grad = jnp.where(is_encoder, extra_first, extra_sum[:, half:]).astype(f32)
    extra_grad = extra_grad.reshape(5, per, half)

    if emit:
        attn_part = jnp.concatenate(
            [
                owners_first(dqkv.reshape(t, 3, inner), n1, n),
                owners_first(mixed[:, None], ga, n),
            ],
            axis=1,
        ).astype(bf16)
        attn_sum = lax.psum_scatter(
            attn_part.reshape(n * 4 * per, d), "rows", scatter_dimension=0, tiled=True
        ).astype(f32)
        dgu, hid = backs[3], backs[4]
        nb, _, fb = hid.shape
        left = dgu.reshape(nb, t, 2, fb).transpose(1, 2, 0, 3).reshape(t, 2, nb * fb)
        hid = hid.transpose(1, 0, 2).reshape(t, 1, nb * fb)
        feed_part = jnp.concatenate(
            [owners_first(left, n2, n), owners_first(hid, gf, n)], axis=1
        ).astype(bf16)
        feed_grad = lax.psum_scatter(
            feed_part.reshape(n * 3 * f, d), "rows", scatter_dimension=0, tiled=True
        ).astype(f32)
        tiny_sum = jnp.sum(lax.all_gather(tiny, "rows", axis=0), axis=0)
    else:
        lefts = jnp.concatenate([dqkv, mixed], axis=1).reshape(t, 4, 4, 2, 2, per)
        lefts = lefts.transpose(4, 3, 2, 1, 5, 0).reshape(2, 8 * 4 * per, t)
        feed_grad, attn_sum, tiny_sum = tail(
            tiny, gf, lefts, n1, ga, feed_own.reshape(3 * f, d), n2_all
        )
    attn_grad = attn_sum.reshape(4, per, d).transpose(1, 0, 2)
    feed_grad = feed_grad.reshape(3, f, d).transpose(1, 0, 2)
    tiny_dec = lax.ppermute(tiny_sum[3:5], "section", [(1, 0)])
    tiny_dec = jnp.where(is_encoder, tiny_dec, tiny_sum[3:5])
    cross_gain_total = tiny_dec[0]
    loss_total = tiny_dec[1, 0]

    attention_new = adam_step(
        attention_weight, attention_first, attention_second, attn_grad[None], 0.05, 0.1
    )
    feed_new = adam_step(feed_weight, feed_first, feed_second, feed_grad[None], 0.05, 0.1)
    gain_new = adam_step(norm_gain, gain_first, gain_second, tiny_sum[None, 0:3], 0.5, 0.0)
    cross_new = adam_step(
        cross_weight, cross_first, cross_second, extra_grad[:4].transpose(1, 0, 2), 0.05, 0.1
    )
    head_new = adam_step(head_weight, head_first, head_second, extra_grad[4], 0.05, 0.1)
    cross_gain_new = adam_step(
        cross_gain, cross_gain_first, cross_gain_second, cross_gain_total, 0.5, 0.0
    )
    return (
        gx.reshape(1, micro, length, d),
        loss_total,
        *attention_new,
        *feed_new,
        *gain_new,
        *cross_new,
        *head_new,
        *cross_gain_new,
    )


def solution(mesh):
    by_row = P("section", "rows", None, None)
    gain = P("section", None, None)
    cross = P("rows", None, "section")
    head = P("rows", "section")
    weights = (by_row,) * 6 + (gain,) * 3 + (cross,) * 3 + (head,) * 3 + (P(),) * 3
    tokens = P("section", None, "rows", None)
    return jax.shard_map(
        local,
        mesh=mesh,
        in_specs=(tokens, P(None, None, "rows"), P(None, "rows")) + weights,
        out_specs=(tokens, P()) + weights,
        check_vma=False,
    )
```

```python
import functools

import jax
import jax.numpy as jnp
from jax import lax
from jax.experimental import pallas as pl
from jax.experimental.pallas import tpu as pltpu
from jax.sharding import PartitionSpec as P

HD = 64
STEP = 10
PAIR = 2 * HD
BLOCKS = 16
VMEM_BYTES = 52 * 1024 * 1024

bf16 = jnp.bfloat16
f32 = jnp.float32
masked_value = -1000000000.0
scale = HD ** (-0.5)


def dot(a, b):
    return lax.dot_general(a, b, (((1,), (0,)), ((), ())), preferred_element_type=f32)


def dot_last(a, b):
    return lax.dot_general(a, b, (((1,), (1,)), ((), ())), preferred_element_type=f32)


def dot_rows(a, b):
    return lax.dot_general(a, b, (((0,), (0,)), ((), ())), preferred_element_type=f32)


def unit_rows(v):
    r = lax.rsqrt(jnp.mean(v * v, axis=-1, keepdims=True) + 1e-06)
    return r, v * r


def norm_back(v, gain, up):
    r, n = unit_rows(v)
    g = up * gain
    back = r * (g - n * jnp.mean(g * n, axis=-1, keepdims=True))
    return back, jnp.sum(up * n, axis=0, keepdims=True)


def gelu_parts(x):
    c = 0.7978845608028654
    t = jnp.tanh(c * (x + 0.044715 * (x * x * x)))
    act = 0.5 * x * (1.0 + t)
    slope = 0.5 * (1.0 + t) + 0.5 * x * (1.0 - t * t) * (c * (1.0 + 3.0 * 0.044715 * (x * x)))
    return act, slope


def low_half(length):
    return lax.broadcasted_iota(jnp.int32, (length, PAIR), 1) < HD


def stack_pair(m, low):
    zero = jnp.zeros_like(m)
    return jnp.concatenate([jnp.where(low, m, zero), jnp.where(low, zero, m)], axis=0)


def allowed_twice(cnt_ref, s, length):
    row = lax.broadcasted_iota(jnp.int32, (length, length), 0)
    col = lax.broadcasted_iota(jnp.int32, (length, length), 1)
    limit = jnp.where(cnt_ref[0] == 1, row + 1, cnt_ref[1 + s])
    one = jnp.where(col < limit, 1, 0)
    return jnp.concatenate([one, one], axis=0) == 1


def soft_pair(q2, k, allowed):
    s = dot_last(q2, k) * scale
    s = jnp.where(allowed, s, masked_value)
    e = jnp.exp(s - jnp.max(s, axis=-1, keepdims=True))
    return e / jnp.sum(e, axis=-1, keepdims=True)


def head_columns(inner, h):
    return [slice(j * inner + h * PAIR, j * inner + (h + 1) * PAIR) for j in range(3)]


def heads_fwd(cnt_ref, qkv_ref, o_ref, length):
    t, inner = o_ref.shape
    low = low_half(length)
    for s in range(t // length):
        allowed = allowed_twice(cnt_ref, s, length)
        rows = slice(s * length, (s + 1) * length)
        for h in range(inner // PAIR):
            cols = head_columns(inner, h)
            q2 = stack_pair(qkv_ref[rows, cols[0]], low)
            p = soft_pair(q2, qkv_ref[rows, cols[1]], allowed).astype(bf16)
            wide = jnp.concatenate([p[:length], p[length:]], axis=1)
            o_ref[rows, cols[0]] = dot(wide, stack_pair(qkv_ref[rows, cols[2]], low)).astype(bf16)


def heads_bwd(cnt_ref, qkv_ref, do_ref, dqkv_ref, length):
    t, inner = do_ref.shape
    low = low_half(length)
    for s in range(t // length):
        allowed = allowed_twice(cnt_ref, s, length)
        rows = slice(s * length, (s + 1) * length)
        for h in range(inner // PAIR):
            cols = head_columns(inner, h)
            q2 = stack_pair(qkv_ref[rows, cols[0]], low)
            k = qkv_ref[rows, cols[1]]
            p = soft_pair(q2, k, allowed)
            do2 = stack_pair(do_ref[rows, cols[0]], low)
            dp = dot_last(do2, qkv_ref[rows, cols[2]])
            ds = p * (dp - jnp.sum(dp * p, axis=-1, keepdims=True))
            ds = jnp.where(allowed, ds, 0.0).astype(bf16)
            wide = jnp.concatenate([ds[:length], ds[length:]], axis=1)
            dqkv_ref[rows, cols[0]] = (dot(wide, stack_pair(k, low)) * scale).astype(bf16)
            dqkv_ref[rows, cols[1]] = (dot_rows(ds, q2) * scale).astype(bf16)
            dqkv_ref[rows, cols[2]] = dot_rows(p.astype(bf16), do2).astype(bf16)


def loss_back(cnt_ref, f_ref, w_ref, target_ref, gl_ref, length):
    logits = dot_last(f_ref[...], w_ref[...])
    top = jnp.max(logits, axis=-1, keepdims=True)
    log_total = top + jnp.log(jnp.sum(jnp.exp(logits - top), axis=-1, keepdims=True))
    hit = lax.broadcasted_iota(jnp.int32, logits.shape, 1) == target_ref[...]
    picked = jnp.sum(jnp.where(hit, logits, 0.0), axis=-1, keepdims=True)
    probs = jnp.exp(logits - log_total) - jnp.where(hit, 1.0, 0.0)
    total = jnp.zeros((1, 1), f32)
    for s in range(logits.shape[0] // length):
        rows = slice(s * length, (s + 1) * length)
        valid = lax.broadcasted_iota(jnp.int32, (length, 1), 0) < cnt_ref[s]
        total += jnp.sum(
            jnp.where(valid, log_total[rows] - picked[rows], 0.0), axis=0, keepdims=True
        )
        gl_ref[rows, :] = jnp.where(valid, probs[rows], 0.0).astype(bf16)
    return total


def attend_fwd_kernel(cross, length, cnt_ref, x_ref, gain_ref, *refs):
    if cross:
        src_ref, w_ref, n_ref, qkv_ref, o_ref, y_ref = refs
    else:
        w_ref, n_ref, qkv_ref, o_ref, y_ref = refs
    inner = w_ref.shape[0] // 4
    x = x_ref[...].astype(f32)
    n = (unit_rows(x)[1] * gain_ref[...]).astype(bf16)
    n_ref[...] = n
    if cross:
        qkv_ref[:, :inner] = dot_last(n, w_ref[:inner, :]).astype(bf16)
        qkv_ref[:, inner:] = dot_last(src_ref[...], w_ref[inner : 3 * inner, :]).astype(bf16)
    else:
        qkv_ref[...] = dot_last(n, w_ref[: 3 * inner, :]).astype(bf16)
    heads_fwd(cnt_ref, qkv_ref, o_ref, length)
    y_ref[...] = x + dot(o_ref[...], w_ref[3 * inner :, :])


def attend_fwd(counts, x, gain, w, length, source=None):
    t, d = x.shape
    inner = w.shape[0] // 4
    ins = [counts, x, gain] + ([] if source is None else [source]) + [w]
    vm = pl.BlockSpec(memory_space=pltpu.VMEM)
    return pl.pallas_call(
        functools.partial(attend_fwd_kernel, source is not None, length),
        out_shape=(
            jax.ShapeDtypeStruct((t, d), bf16),
            jax.ShapeDtypeStruct((t, 3 * inner), bf16),
            jax.ShapeDtypeStruct((t, inner), bf16),
            jax.ShapeDtypeStruct((t, d), f32),
        ),
        in_specs=[pl.BlockSpec(memory_space=pltpu.SMEM)] + [vm] * (len(ins) - 1),
        out_specs=(vm,) * 4,
        compiler_params=pltpu.CompilerParams(vmem_limit_bytes=VMEM_BYTES),
        cost_estimate=pl.CostEstimate(
            flops=2 * t * d * inner * 4 + 8 * t * length * inner,
            bytes_accessed=w.size * 2 + t * d * 10,
            transcendentals=t * length * 6,
        ),
    )(*ins)


def attend_bwd_kernel(cross, length, cnt_ref, x_ref, gain_ref, gy_ref, qkv_ref, w_ref, *refs):
    if cross:
        ga_ref, dqkv_ref, gx_ref, gg_ref, gs_ref, do_ref = refs
    else:
        ga_ref, dqkv_ref, gx_ref, gg_ref, do_ref = refs
    inner = w_ref.shape[0] // 4
    ga = gy_ref[...].astype(bf16)
    ga_ref[...] = ga
    do_ref[...] = dot_last(ga, w_ref[3 * inner :, :]).astype(bf16)
    heads_bwd(cnt_ref, qkv_ref, do_ref, dqkv_ref, length)
    if cross:
        up = dot(dqkv_ref[:, :inner], w_ref[:inner, :])
        gs_ref[...] = dot(dqkv_ref[:, inner:], w_ref[inner : 3 * inner, :]).astype(bf16)
    else:
        up = dot(dqkv_ref[...], w_ref[: 3 * inner, :])
    back, gg_ref[...] = norm_back(x_ref[...].astype(f32), gain_ref[...], up)
    gx_ref[...] = gy_ref[...] + back


def attend_bwd(counts, x, gain, gy, qkv, w, length, cross=False):
    t, d = x.shape
    inner = w.shape[0] // 4
    vm = pl.BlockSpec(memory_space=pltpu.VMEM)
    outs = [
        jax.ShapeDtypeStruct((t, d), bf16),
        jax.ShapeDtypeStruct((t, 3 * inner), bf16),
        jax.ShapeDtypeStruct((t, d), f32),
        jax.ShapeDtypeStruct((1, d), f32),
    ]
    if cross:
        outs.append(jax.ShapeDtypeStruct((t, d), bf16))
    return pl.pallas_call(
        functools.partial(attend_bwd_kernel, cross, length),
        out_shape=tuple(outs),
        in_specs=[pl.BlockSpec(memory_space=pltpu.SMEM)] + [vm] * 5,
        out_specs=(vm,) * len(outs),
        scratch_shapes=[pltpu.VMEM((t, inner), bf16)],
        compiler_params=pltpu.CompilerParams(vmem_limit_bytes=VMEM_BYTES),
        cost_estimate=pl.CostEstimate(
            flops=2 * t * d * inner * 4 + 20 * t * length * inner,
            bytes_accessed=w.size * 2 + t * d * 16,
            transcendentals=t * length * 6,
        ),
    )(counts, x, gain, gy, qkv, w)


def feed_fwd_kernel(y_ref, g_in_ref, g_out_ref, w_ref, n_ref, gu_ref, y2_ref, f_ref):
    i = pl.program_id(0)
    f = w_ref.shape[1] // 3

    @pl.when(i == 0)
    def _():
        y = y_ref[...]
        n_ref[...] = (unit_rows(y)[1] * g_in_ref[...]).astype(bf16)
        y2_ref[...] = y

    gu = dot_last(n_ref[...], w_ref[0, : 2 * f, :])
    gu_ref[0] = gu
    hidden = (gelu_parts(gu[:, :f])[0] * gu[:, f:]).astype(bf16)
    y2_ref[...] += dot(hidden, w_ref[0, 2 * f :, :])

    @pl.when(i == pl.num_programs(0) - 1)
    def _():
        f_ref[...] = (unit_rows(y2_ref[...])[1] * g_out_ref[...]).astype(bf16)


def feed_fwd(y, gain_in, gain_out, w):
    t, d = y.shape
    nb, rows, _ = w.shape
    f = rows // 3
    whole = lambda *shape: pl.BlockSpec(shape, lambda i: (0,) * len(shape))
    part = lambda *shape: pl.BlockSpec((1,) + shape, lambda i: (i, 0, 0))
    return pl.pallas_call(
        feed_fwd_kernel,
        grid=(nb,),
        out_shape=(
            jax.ShapeDtypeStruct((t, d), bf16),
            jax.ShapeDtypeStruct((nb, t, 2 * f), f32),
            jax.ShapeDtypeStruct((t, d), f32),
            jax.ShapeDtypeStruct((t, d), bf16),
        ),
        in_specs=[whole(t, d), whole(1, d), whole(1, d), part(rows, d)],
        out_specs=(whole(t, d), part(t, 2 * f), whole(t, d), whole(t, d)),
        compiler_params=pltpu.CompilerParams(vmem_limit_bytes=VMEM_BYTES),
        cost_estimate=pl.CostEstimate(
            flops=2 * t * d * rows * nb,
            bytes_accessed=w.size * 2 + t * d * 12 + nb * t * f * 8,
            transcendentals=nb * t * f,
        ),
    )(y, gain_in, gain_out, w)


def feed_bwd_kernel(emit, up_ref, y_ref, y2_ref, g_in_ref, g_out_ref, gu_ref, w_ref, *refs):
    if emit:
        gf_ref, gy_ref, gg_ref, dgu_ref, hid_ref, last_ref = refs
    else:
        gf_ref, gy_ref, gg_ref, last_ref = refs
    i = pl.program_id(0)
    f = w_ref.shape[1] // 3

    @pl.when(i == 0)
    def _():
        back, gain_grad = norm_back(y2_ref[...], g_out_ref[...], up_ref[...].astype(f32))
        gg_ref[1:2, :] = gain_grad
        last_ref[...] = back
        gf_ref[...] = back.astype(bf16)
        gy_ref[...] = jnp.zeros_like(gy_ref)

    gh = dot_last(gf_ref[...], w_ref[0, 2 * f :, :])
    act, slope = gelu_parts(gu_ref[0, :, :f])
    u = gu_ref[0, :, f:]
    dg = (gh * u * slope).astype(bf16)
    du = (gh * act).astype(bf16)
    if emit:
        dgu_ref[0, :, :f] = dg
        dgu_ref[0, :, f:] = du
        hid_ref[0] = (act * u).astype(bf16)
    gy_ref[...] += dot(dg, w_ref[0, :f, :]) + dot(du, w_ref[0, f : 2 * f, :])

    @pl.when(i == pl.num_programs(0) - 1)
    def _():
        back, gain_grad = norm_back(y_ref[...], g_in_ref[...], gy_ref[...])
        gg_ref[0:1, :] = gain_grad
        gy_ref[...] = last_ref[...] + back


def feed_bwd(up, y, y2, gain_in, gain_out, gu, w, emit):
    t, d = y.shape
    nb, rows, _ = w.shape
    f = rows // 3
    whole = lambda *shape: pl.BlockSpec(shape, lambda i: (0,) * len(shape))
    part = lambda *shape: pl.BlockSpec((1,) + shape, lambda i: (i, 0, 0))
    outs = [
        jax.ShapeDtypeStruct((t, d), bf16),
        jax.ShapeDtypeStruct((t, d), f32),
        jax.ShapeDtypeStruct((2, d), f32),
    ]
    specs = [whole(t, d), whole(t, d), whole(2, d)]
    if emit:
        outs += [
            jax.ShapeDtypeStruct((nb, t, 2 * f), bf16),
            jax.ShapeDtypeStruct((nb, t, f), bf16),
        ]
        specs += [part(t, 2 * f), part(t, f)]
    return pl.pallas_call(
        functools.partial(feed_bwd_kernel, emit),
        grid=(nb,),
        out_shape=tuple(outs),
        in_specs=[whole(t, d)] * 3 + [whole(1, d)] * 2 + [part(t, 2 * f), part(rows, d)],
        out_specs=tuple(specs),
        scratch_shapes=[pltpu.VMEM((t, d), f32)],
        compiler_params=pltpu.CompilerParams(vmem_limit_bytes=VMEM_BYTES),
        cost_estimate=pl.CostEstimate(
            flops=2 * t * d * rows * nb,
            bytes_accessed=w.size * 2 + t * d * 18 + nb * t * f * 8,
            transcendentals=nb * t * f,
        ),
    )(up, y, y2, gain_in, gain_out, gu, w)


def head_kernel(length, cnt_ref, f_ref, w_ref, target_ref, gl_ref, up_ref, loss_ref):
    loss_ref[...] = loss_back(cnt_ref, f_ref, w_ref, target_ref, gl_ref, length)
    up_ref[...] = dot(gl_ref[...], w_ref[...])


def head_loss(counts, final, w, target, length):
    t, d = final.shape
    v = w.shape[0]
    vm = pl.BlockSpec(memory_space=pltpu.VMEM)
    return pl.pallas_call(
        functools.partial(head_kernel, length),
        out_shape=(
            jax.ShapeDtypeStruct((t, v), bf16),
            jax.ShapeDtypeStruct((t, d), f32),
            jax.ShapeDtypeStruct((1, 1), f32),
        ),
        in_specs=[pl.BlockSpec(memory_space=pltpu.SMEM), vm, vm, vm],
        out_specs=(vm,) * 3,
        compiler_params=pltpu.CompilerParams(vmem_limit_bytes=VMEM_BYTES),
        cost_estimate=pl.CostEstimate(
            flops=4 * t * d * v, bytes_accessed=w.size * 2 + t * d * 6, transcendentals=t * v * 2
        ),
    )(counts, final, w, target)


def tail_kernel(
    tiny_ref, lefts_ref, n1_ref, ga_ref, w_ref, extra_lefts_ref, mc_ref, encoded_ref, gac_ref, final_ref, n_all, g_all,
    feed_ref, attn_ref, extra_ref, total_ref,
    tinies, from_dec, half_out, n_buf, g_buf, *rest,
):
    attn_bufs, extra_bufs = rest[:9], rest[9:18]
    tiny_send, tiny_recv, rs_send, rs_recv, pair_sem, x_send, x_recv = rest[18:]
    section = lax.axis_index("section")
    me = lax.axis_index("rows")
    z, y, c = me // 4, (me // 2) % 2, me % 2
    high = z // 2
    inner = (z + high) % 2
    is_enc, is_dec = section == 0, section == 1
    f = w_ref.shape[0] // 3
    d = w_ref.shape[1]
    core_peer, y_peer = me + 1 - 2 * c, me + 2 - 4 * y
    toward = me + 4 - 8 * high
    outward = me - 4 + 8 * high
    mesh_id = pl.DeviceIdType.MESH

    def remote(src, dst, send, recv, where):
        return pltpu.make_async_remote_copy(
            src_ref=src, dst_ref=dst, send_sem=send, recv_sem=recv,
            device_id=where, device_id_type=mesh_id,
        )

    def pair_copies(p):
        slot = p % 2
        return [
            pltpu.make_async_copy(whole.at[pl.ds(2 * p, 2)], buf.at[slot], pair_sem.at[k, slot])
            for k, (whole, buf) in enumerate([(n_all, n_buf), (g_all, g_buf)])
        ]

    for copy in pair_copies(0):
        copy.start()

    barrier = pltpu.get_barrier_semaphore()

    def greet(where):
        pl.semaphore_signal(barrier, inc=1, device_id=where, device_id_type=mesh_id)

    greet({"rows": core_peer})
    greet({"rows": y_peer})
    greet({"section": 1 - section})
    greet({"rows": toward})

    @pl.when(inner == 1)
    def _():
        greet({"rows": outward})

    pl.semaphore_wait(barrier, 4 + inner)

    def place_of(p):
        j, other = [(0, 0), (1, 0), (0, 1), (2, 0), (1, 1), (3, 0), (2, 1), (3, 1)][p]
        zz = [z, z + 1 - 2 * (z % 2), 2 - high, 3 - 3 * high][j]
        yy = y + other - 2 * other * y
        return zz, yy, other

    def tiny_copy(kind, p, s, where):
        src = tiny_ref if p == 0 else tinies.at[s]
        return remote(src, tinies.at[s], tiny_send.at[kind, p], tiny_recv.at[s], where)

    def each_tiny(p, act):
        zz, yy, other = place_of(p)
        s = 4 * zz + 2 * yy + c
        if other == 0:

            @pl.when((zz <= z) & (z < 3))
            def _():
                act(tiny_copy(0, p, s, {"rows": me + 4}))

            @pl.when((zz >= z) & (z > 0))
            def _():
                act(tiny_copy(1, p, s, {"rows": me - 4}))

            act(tiny_copy(2, p, s, {"rows": y_peer}))
        act(tiny_copy(3, p, s, {"rows": core_peer}))

    def tiny_arrive(p):
        zz, yy, _ = place_of(p)
        tiny_copy(0, p, 4 * zz + 2 * yy + c, {"rows": me}).wait_recv()
        each_tiny(p, lambda copy: copy.start())

    def blocks_of(pieces):
        return jnp.concatenate([piece.reshape(8, -1, d) for piece in pieces], axis=1)

    def attn_half(half):
        left = lefts_ref.at[half]
        k = lefts_ref.shape[1] // 4
        qkv = dot(left[: 3 * k, :], n1_ref[...])
        return blocks_of([qkv[:k], qkv[k : 2 * k], qkv[2 * k :], dot(left[3 * k :, :], ga_ref[...])])

    def extra_half(half):
        left = extra_lefts_ref.at[half]
        k = extra_lefts_ref.shape[1] // 5
        key_value = dot(left[k : 3 * k, :], encoded_ref[...])
        pad = extra_bufs[0].shape[2] - 5 * k // 8
        return blocks_of(
            [
                dot(left[:k, :], mc_ref[...]),
                key_value[:k],
                key_value[k:],
                dot(left[3 * k : 4 * k, :], gac_ref[...]),
                dot(left[4 * k :, :], final_ref[...]),
                jnp.zeros((8 * pad, d), f32),
            ]
        )

    far, home = 2 - 2 * high, 2 * high

    def summed(bufs, k, half_sums, result):
        part, from_core, four, from_y, from_far, from_near, from_cross, from_out, cross_out = bufs

        def hop(i, src, dst, where):
            return remote(src, dst, rs_send.at[k, i], rs_recv.at[k, i], {"rows": where})

        to_core = hop(0, part.at[0], from_core, core_peer)
        theirs = (1 - y) * 4
        y_far = hop(1, part.at[1, pl.ds(theirs + far, 2)], from_y.at[pl.ds(far, 2)], y_peer)
        y_home = hop(2, part.at[1, pl.ds(theirs + home, 2)], from_y.at[pl.ds(home, 2)], y_peer)
        far_copy = hop(3, four.at[pl.ds(far, 2)], from_far, toward)
        near_copy = hop(4, four.at[1 + high], from_near, toward)
        cross_copy = hop(5, four.at[pl.ds(far, 2)], from_cross, toward)
        out_copy = hop(6, cross_out, from_out, outward)

        def core_send():
            part[0] = half_sums(1 - c).astype(bf16)
            to_core.start()

        def core_add():
            own = half_sums(c)
            to_core.wait_recv()
            part[1] = (own + from_core[...].astype(f32)).astype(bf16)
            y_far.start()
            y_home.start()

        def add_y(copy, at):
            copy.wait_recv()
            mine = part[1, pl.ds(4 * y + at, 2)].astype(f32)
            four[pl.ds(at, 2)] = (mine + from_y[pl.ds(at, 2)].astype(f32)).astype(bf16)

        def stage_far():
            add_y(y_far, far)
            pl.when(inner == 0)(far_copy.start)

        def stage_home():
            add_y(y_home, home)
            pl.when(inner == 0)(near_copy.start)

        def stage_cross():
            @pl.when(inner == 1)
            def _():
                far_copy.wait_recv()
                both = four[pl.ds(far, 2)].astype(f32) + from_far[...].astype(f32)
                four[pl.ds(far, 2)] = both.astype(bf16)
                cross_copy.start()

        def stage_out():
            @pl.when(inner == 1)
            def _():
                near_copy.wait_recv()
                cross_copy.wait_recv()
                out = four[3 * high].astype(f32) + from_cross[high].astype(f32)
                cross_out[...] = out.astype(bf16)
                out_copy.start()
                result(
                    four[z].astype(f32)
                    + from_near[...].astype(f32)
                    + from_cross[1 - high].astype(f32)
                )

        def stage_end():
            @pl.when(inner == 0)
            def _():
                out_copy.wait_recv()
                result(four[z].astype(f32) + from_out[...].astype(f32))

        def settle():
            to_core.wait_send()
            y_far.wait_send()
            y_home.wait_send()

            @pl.when(inner == 0)
            def _():
                far_copy.wait_send()
                near_copy.wait_send()

            @pl.when(inner == 1)
            def _():
                cross_copy.wait_send()
                out_copy.wait_send()

        return core_send, core_add, stage_far, stage_home, stage_cross, stage_out, stage_end, settle

    def attn_result(value):
        attn_ref[...] = value

    half_copy = remote(half_out, extra_ref, x_send.at[0], x_recv.at[0], {"section": 1 - section})
    total_copy = remote(total_ref, from_dec, x_send.at[1], x_recv.at[1], {"section": 1 - section})

    def extra_result(value):
        half_out[...] = value[:, : d // 2]
        half_copy.start()
        extra_ref[...] = value[:, d // 2 :]

    attn = summed(attn_bufs, 0, attn_half, attn_result)
    extra = summed(extra_bufs, 1, extra_half, extra_result)

    def of_dec(stage):
        pl.when(is_dec)(stage)

    def wgrad(p):
        if p < 7:
            for copy in pair_copies(p + 1):
                copy.start()
        for copy in pair_copies(p):
            copy.wait()
        n_rows = n_buf[p % 2].reshape(-1, d)
        g_rows = g_buf[p % 2].reshape(-1, d)
        gu = dot_last(n_rows, w_ref[: 2 * f, :])
        gh = dot_last(g_rows, w_ref[2 * f :, :])
        act, slope = gelu_parts(gu[:, :f])
        up = gu[:, f:]
        dg = (gh * up * slope).astype(bf16)
        du = (gh * act).astype(bf16)
        hid = (act * up).astype(bf16)
        if p == 0:
            feed_ref[:f, :] = dot_rows(dg, n_rows)
            feed_ref[f : 2 * f, :] = dot_rows(du, n_rows)
            feed_ref[2 * f :, :] = dot_rows(hid, g_rows)
        else:
            feed_ref[:f, :] += dot_rows(dg, n_rows)
            feed_ref[f : 2 * f, :] += dot_rows(du, n_rows)
            feed_ref[2 * f :, :] += dot_rows(hid, g_rows)

    tinies[me] = tiny_ref[...]
    each_tiny(0, lambda copy: copy.start())
    attn[0]()
    of_dec(extra[0])
    attn[1]()
    of_dec(extra[1])
    tiny_arrive(1)
    tiny_arrive(2)
    wgrad(0)
    tiny_arrive(3)
    tiny_arrive(4)
    wgrad(1)
    attn[2]()
    tiny_arrive(5)
    tiny_arrive(6)
    wgrad(2)
    attn[3]()
    tiny_arrive(7)
    wgrad(3)
    attn[4]()
    wgrad(4)
    of_dec(extra[2])
    attn[5]()
    wgrad(5)
    of_dec(extra[3])
    attn[6]()
    for p in range(8):
        zz, yy, _ = place_of(p)
        tiny_copy(0, p, 4 * zz + 2 * yy + 1 - c, {"rows": me}).wait_recv()
    total = tinies[0]
    for s in range(1, 16):
        total += tinies[s]
    total_ref[...] = total
    of_dec(total_copy.start)
    wgrad(6)
    of_dec(extra[4])
    wgrad(7)
    of_dec(extra[5])
    of_dec(extra[6])

    for p in range(8):
        each_tiny(p, lambda copy: copy.wait_send())
    attn[7]()
    of_dec(extra[7])

    @pl.when(is_dec)
    def _():
        half_copy.wait_send()
        total_copy.wait_send()

    @pl.when(is_enc)
    def _():
        total_copy.wait_recv()
        total_ref[3:5, :] = from_dec[3:5, :]
        half_copy.wait_recv()


def tail(tiny, lefts, n1, ga, w_own, extra_lefts, mc, encoded, gac, final, n_all, g_all):
    t, d = n1.shape
    rows = w_own.shape[0]
    per, more = lefts.shape[1] // 8, -(-extra_lefts.shape[1] // 8 // 16) * 16

    def sums(r):
        return [
            pltpu.VMEM(shape + (r, d), bf16)
            for shape in [(2, 8), (8,), (4,), (4,), (2,), (), (2,), (), ()]
        ]

    vm = pl.BlockSpec(memory_space=pltpu.VMEM)
    anywhere = pl.BlockSpec(memory_space=pl.ANY)
    return pl.pallas_call(
        tail_kernel,
        out_shape=(
            jax.ShapeDtypeStruct((rows, d), f32),
            jax.ShapeDtypeStruct((per, d), f32),
            jax.ShapeDtypeStruct((more, d // 2), f32),
            jax.ShapeDtypeStruct(tiny.shape, f32),
        ),
        in_specs=[vm] * 10 + [anywhere] * 2,
        out_specs=(vm,) * 4,
        scratch_shapes=[
            pltpu.VMEM((16,) + tiny.shape, f32),
            pltpu.VMEM(tiny.shape, f32),
            pltpu.VMEM((more, d // 2), f32),
            pltpu.VMEM((2, 2, t, d), bf16),
            pltpu.VMEM((2, 2, t, d), bf16),
            *sums(per),
            *sums(more),
            pltpu.SemaphoreType.DMA((4, 8)),
            pltpu.SemaphoreType.DMA((16,)),
            pltpu.SemaphoreType.DMA((2, 7)),
            pltpu.SemaphoreType.DMA((2, 7)),
            pltpu.SemaphoreType.DMA((2, 2)),
            pltpu.SemaphoreType.DMA((2,)),
            pltpu.SemaphoreType.DMA((2,)),
        ],
        compiler_params=pltpu.CompilerParams(
            vmem_limit_bytes=60 * 1024 * 1024, collective_id=0, has_side_effects=True
        ),
        cost_estimate=pl.CostEstimate(
            flops=2 * t * 16 * d * rows * 2, bytes_accessed=16 * t * d * 4, transcendentals=16 * t * rows
        ),
    )(tiny, lefts, n1, ga, w_own, extra_lefts, mc, encoded, gac, final, n_all, g_all)


def front_kernel(
    length, cnt_ref, order_ref, x_ref, g_attn_ref, g_feed_ref, g_final_ref,
    attn_own, feed_own, half_own,
    attn_all, feed_all, first_all, second_all,
    n1_ref, qkv_ref, mixed_ref, y1_ref, n2_ref, gu_ref, y2_ref, enc_ref, arrived_ref,
    w_attn, w_feed, place, wide_buf, first_own,
    send_sem, recv_sem, own_sem, load_sem, x_send, x_recv,
):
    section = lax.axis_index("section")
    me = lax.axis_index("rows")
    z, y, c = me // 4, (me // 2) % 2, me % 2
    core_peer, y_peer = me + 1 - 2 * c, me + 2 - 4 * y
    mesh_id = pl.DeviceIdType.MESH
    inner = mixed_ref.shape[1]
    f = feed_own.shape[0] // 3

    barrier = pltpu.get_barrier_semaphore()

    def greet(where):
        pl.semaphore_signal(barrier, inc=1, device_id=where, device_id_type=mesh_id)

    greet({"rows": core_peer})
    greet({"rows": y_peer})
    greet({"section": 1 - section})

    @pl.when(z > 0)
    def _():
        greet({"rows": me - 4})

    @pl.when(z < 3)
    def _():
        greet({"rows": me + 4})

    own_copies = [
        pltpu.make_async_copy(own, whole.at[me], own_sem.at[k])
        for k, (own, whole) in enumerate(
            [(attn_own, attn_all), (feed_own, feed_all), (half_own, second_all)]
        )
    ]
    own_copies[0].start()
    own_copies[1].start()

    @pl.when(section == 1)
    def _():
        own_copies[2].start()

    pl.semaphore_wait(barrier, 4 + (z + z // 2) % 2)

    def remote(src, dst, send, recv, where):
        return pltpu.make_async_remote_copy(
            src_ref=src, dst_ref=dst, send_sem=send, recv_sem=recv,
            device_id=where, device_id_type=mesh_id,
        )

    kinds = [pl.ds(k * f, f) for k in range(3)]
    parts = {
        "A": (0, attn_all, None, 2, attn_own),
        "G": (1, feed_all, kinds[0], 1, feed_own.at[kinds[0]]),
        "U": (2, feed_all, kinds[1], 1, feed_own.at[kinds[1]]),
        "O": (3, feed_all, kinds[2], 1, feed_own.at[kinds[2]]),
        "X": (4, first_all, None, 1, first_own),
        "Y": (5, second_all, None, 2, half_own),
    }

    def place_of(route, p):
        if route == 1:
            j, other = [(0, 0), (1, 0), (0, 1), (2, 0), (1, 1), (3, 0), (2, 1), (3, 1)][p]
        else:
            j, other = p // 2, p % 2
        zz = [z, z + 1 - 2 * (z % 2), 2 - z // 2, 3 - 3 * (z // 2)][j]
        yy = y + other - 2 * other * y
        return zz, yy, other

    def part_copy(name, kind, p, s, where):
        k, whole, rows, _, own = parts[name]
        dst = whole.at[s] if rows is None else whole.at[s, rows]
        return remote(own if p == 0 else dst, dst, send_sem.at[k, kind, p], recv_sem.at[k, s], where)

    def each_send(name, p, act, ways="zyc"):
        route = parts[name][3]
        zz, yy, other = place_of(route, p)
        s = 4 * zz + 2 * yy + c
        if "z" in ways and (route == 2 or other == 0):

            @pl.when((zz <= z) & (z < 3))
            def _():
                act(part_copy(name, 0, p, s, {"rows": me + 4}))

            @pl.when((zz >= z) & (z > 0))
            def _():
                act(part_copy(name, 1, p, s, {"rows": me - 4}))

        if "y" in ways and (p == 0 or (route == 1 and other == 0)):
            act(part_copy(name, 2, p, s, {"rows": y_peer}))
        if "c" in ways:
            act(part_copy(name, 3, p, s, {"rows": core_peer}))

    def begin(name, ways):
        each_send(name, 0, lambda copy: copy.start(), ways)

    def arrive(name, p):
        zz, yy, _ = place_of(parts[name][3], p)
        part_copy(name, 0, p, 4 * zz + 2 * yy + c, {"rows": me}).wait_recv()
        each_send(name, p, lambda copy: copy.start())

    def meet(name, p):
        zz, yy, _ = place_of(parts[name][3], p)
        part_copy(name, 0, p, 4 * zz + 2 * yy + 1 - c, {"rows": me}).wait_recv()

    def settle(name):
        for p in range(8):
            each_send(name, p, lambda copy: copy.wait_send())

    half_copy = remote(half_own, first_own, x_send.at[0], x_recv.at[0], {"section": 1 - section})
    enc_copy = remote(enc_ref, arrived_ref, x_send.at[1], x_recv.at[1], {"section": 1 - section})
    own_first = pltpu.make_async_copy(first_own, first_all.at[me], own_sem.at[3])

    def project():
        for p in range(8):
            meet("A", p)
        own_copies[0].wait()
        load = pltpu.make_async_copy(attn_all, w_attn, load_sem.at[0])
        load.start()
        load.wait()
        wide_buf[...] = dot_last(n1_ref[...], w_attn[...].reshape(4 * inner, -1)).astype(bf16)
        qkv_ref[...] = dot(wide_buf[...], place[:, : 3 * inner]).astype(bf16)

    def mix(s):
        low = low_half(length)
        allowed = allowed_twice(cnt_ref, s, length)
        rows = slice(s * length, (s + 1) * length)
        for h in range(inner // PAIR):
            cols = [slice(j * inner + h * PAIR, j * inner + (h + 1) * PAIR) for j in range(3)]
            q2 = stack_pair(qkv_ref[rows, cols[0]], low)
            p = soft_pair(q2, qkv_ref[rows, cols[1]], allowed).astype(bf16)
            wide = jnp.concatenate([p[:length], p[length:]], axis=1)
            mixed_ref[rows, cols[0]] = dot(wide, stack_pair(qkv_ref[rows, cols[2]], low)).astype(bf16)

    def mix_out():
        for s in range(x_ref.shape[0] // length // 2, x_ref.shape[0] // length):
            mix(s)
        wide_buf[...] = dot_last(mixed_ref[...], place[:, 3 * inner :]).astype(bf16)
        y1_ref[...] = x_ref[...].astype(f32) + dot(wide_buf[...], w_attn[...].reshape(4 * inner, -1))
        y2_ref[...] = y1_ref[...]
        n2_ref[...] = (unit_rows(y1_ref[...])[1] * g_feed_ref[...]).astype(bf16)

    def mix_first():
        for s in range(x_ref.shape[0] // length // 2):
            mix(s)

    def feed(p):
        if p == 0:
            own_copies[1].wait()
        for name in "GUO":
            meet(name, p)
        zz, yy, _ = place_of(1, p)
        pair = 4 * zz + 2 * yy

        @pl.when(section == 0)
        def _():
            blocks = pltpu.make_async_copy(feed_all.at[pl.ds(pair, 2)], w_feed, load_sem.at[1])
            blocks.start()
            blocks.wait()
            for k in range(2):
                gu = dot_last(n2_ref[...], w_feed[k, : 2 * f, :])
                gu_ref[pair + k] = gu
                hidden = (gelu_parts(gu[:, :f])[0] * gu[:, f:]).astype(bf16)
                y2_ref[...] += dot(hidden, w_feed[k, 2 * f :, :])

    begin("A", "zyc")

    @pl.when(section == 0)
    def _():
        half_copy.start()

    @pl.when(section == 1)
    def _():
        begin("Y", "yc")

    for name in "GUO":
        begin(name, "yc")
    begin("G", "z")

    @pl.when(section == 1)
    def _():
        begin("Y", "z")

    row = lax.broadcasted_iota(jnp.int32, place.shape, 0)
    place[...] = jnp.where(row == order_ref[...], 1.0, 0.0).astype(bf16)
    n1_ref[...] = (unit_rows(x_ref[...].astype(f32))[1] * g_attn_ref[...]).astype(bf16)

    tasks = {"c1": project, "c2": mix_first, "c3": mix_out}
    for step in FRONT_STEPS:
        if step in tasks:
            tasks[step]()
        elif step[0] == "f":
            feed(int(step[1]))
        elif step[0] == "o":
            begin(step[1], "z")
        elif step == "X0":

            @pl.when(section == 1)
            def _():
                half_copy.wait_recv()
                own_first.start()
                begin("X", "zyc")

        elif step[0] == "X":

            @pl.when(section == 1)
            def _(p=int(step[1])):
                arrive("X", p)
                arrive("Y", p)

        else:
            arrive(step[0], int(step[1]))

    @pl.when(section == 0)
    def _():
        enc_ref[...] = (unit_rows(y2_ref[...])[1] * g_final_ref[...]).astype(bf16)
        enc_copy.start()

    for name in "AGUO":
        settle(name)

    @pl.when(section == 1)
    def _():
        for name in "XY":
            for p in range(8):
                meet(name, p)
            settle(name)
        own_first.wait()
        own_copies[2].wait()
        enc_copy.wait_recv()

    @pl.when(section == 0)
    def _():
        half_copy.wait_send()
        enc_copy.wait_send()


FRONT_STEPS = (
    ("A1", "oU", "G1", "A2", "X0", "A3", "oO", "A4", "O1", "U1", "G2", "U2", "O2", "A5", "A6", "X1", "X2", "G3", "A7")
    + ("c1", "O3", "G4", "O4", "U3", "c2", "U4", "c3", "f0", "O5", "f1", "U5", "U6", "G5", "O6", "X3", "X4", "X5")
    + ("X6", "O7", "f2", "f3", "G6", "f4", "f5", "U7", "f6", "X7", "G7", "f7")
)


def front(counts, order, x, gain_attn, gain_feed, gain_final, attn_own, feed_own, half_own, length):
    t, d = x.shape
    attn_rows, feed_rows = attn_own.shape[0], feed_own.shape[0]
    inner = attn_rows * 4
    half_shape = (16,) + half_own.shape
    vm = pl.BlockSpec(memory_space=pltpu.VMEM)
    anywhere = pl.BlockSpec(memory_space=pl.ANY)
    return pl.pallas_call(
        functools.partial(front_kernel, length),
        out_shape=(
            jax.ShapeDtypeStruct((16, attn_rows, d), bf16),
            jax.ShapeDtypeStruct((16, feed_rows, d), bf16),
            jax.ShapeDtypeStruct(half_shape, bf16),
            jax.ShapeDtypeStruct(half_shape, bf16),
            jax.ShapeDtypeStruct((t, d), bf16),
            jax.ShapeDtypeStruct((t, 3 * inner), bf16),
            jax.ShapeDtypeStruct((t, inner), bf16),
            jax.ShapeDtypeStruct((t, d), f32),
            jax.ShapeDtypeStruct((t, d), bf16),
            jax.ShapeDtypeStruct((16, t, feed_rows // 3 * 2), f32),
            jax.ShapeDtypeStruct((t, d), f32),
            jax.ShapeDtypeStruct((t, d), bf16),
            jax.ShapeDtypeStruct((t, d), bf16),
        ),
        in_specs=[pl.BlockSpec(memory_space=pltpu.SMEM)] + [vm] * 5 + [anywhere] * 3,
        out_specs=(anywhere,) * 4 + (vm,) * 9,
        scratch_shapes=[
            pltpu.VMEM((16, attn_rows, d), bf16),
            pltpu.VMEM((2, feed_rows, d), bf16),
            pltpu.VMEM((4 * inner, 4 * inner), bf16),
            pltpu.VMEM((t, 4 * inner), bf16),
            pltpu.VMEM(half_own.shape, bf16),
            pltpu.SemaphoreType.DMA((6, 4, 8)),
            pltpu.SemaphoreType.DMA((6, 16)),
            pltpu.SemaphoreType.DMA((4,)),
            pltpu.SemaphoreType.DMA((2,)),
            pltpu.SemaphoreType.DMA((2,)),
            pltpu.SemaphoreType.DMA((2,)),
        ],
        compiler_params=pltpu.CompilerParams(
            vmem_limit_bytes=VMEM_BYTES, collective_id=1, has_side_effects=True
        ),
        cost_estimate=pl.CostEstimate(
            flops=2 * t * d * (feed_rows * 16 + 8 * inner),
            bytes_accessed=2 * 16 * (attn_rows + feed_rows) * d * 2,
            transcendentals=t * feed_rows * 6,
        ),
    )(counts, order, x, gain_attn, gain_feed, gain_final, attn_own, feed_own, half_own)


def mid_kernel(
    length, cross_cnt, self_cnt, dec_cnt, x_ref, y1_ref, y2_in, n2_in, qkv_ref, encoded_ref, target_ref, gain_ref,
    gu_in, attn_w, cross_w, head_w, feed_w,
    n_all, g_all, gf_ref, ga_ref, dqkv_ref, gx_ref, sums_ref, mc_ref, dcqkv_ref, cmixed_ref, gac_ref, final_ref, gl_ref,
    slots, gu_buf, w_att, w_head, mid, y2, acc, last, n2, cqkv, do_buf, grad_enc, returned,
    send_sem, recv_sem, slot_sem, load_sem, own_sem, x_send, x_recv,
):
    section = lax.axis_index("section")
    me = lax.axis_index("rows")
    z, y, c = me // 4, (me // 2) % 2, me % 2
    core_peer, y_peer = me + 1 - 2 * c, me + 2 - 4 * y
    mesh_id = pl.DeviceIdType.MESH
    inner = w_att.shape[0] // 4
    f = feed_w.shape[1] // 3
    t = n2.shape[0]
    held = slots.shape[0]
    spare = BLOCKS - held
    is_enc, is_dec = section == 0, section == 1

    def load(b):
        k = b % held
        return pltpu.make_async_copy(feed_w.at[b], slots.at[k], slot_sem.at[k])

    load_attn = pltpu.make_async_copy(attn_w, w_att, load_sem.at[0])
    load_cross = pltpu.make_async_copy(cross_w, w_att, load_sem.at[1])
    load_head = pltpu.make_async_copy(head_w, w_head, load_sem.at[2])
    load_gu = pltpu.make_async_copy(gu_in, gu_buf, load_sem.at[3])

    def start_loads(first):
        def step(k, carry):
            load(first + k).start()
            return carry

        lax.fori_loop(0, held, step, 0)

    @pl.when(is_enc)
    def _():
        start_loads(spare)
        load_gu.start()
        load_attn.start()

    @pl.when(is_dec)
    def _():
        load_cross.start()
        start_loads(0)
        load_head.start()

    barrier = pltpu.get_barrier_semaphore()

    def greet(where):
        pl.semaphore_signal(barrier, inc=1, device_id=where, device_id_type=mesh_id)

    greet({"rows": core_peer})
    greet({"rows": y_peer})
    greet({"section": 1 - section})

    @pl.when(z > 0)
    def _():
        greet({"rows": me - 4})

    @pl.when(z < 3)
    def _():
        greet({"rows": me + 4})

    pl.semaphore_wait(barrier, 4 + (z + z // 2) % 2)

    def remote(src, dst, send, recv, where):
        return pltpu.make_async_remote_copy(
            src_ref=src, dst_ref=dst, send_sem=send, recv_sem=recv,
            device_id=where, device_id_type=mesh_id,
        )

    cut = t * 13 // 256 * 16
    upper, lower = pl.ds(0, cut), pl.ds(cut, t - cut)
    parts = {
        "S": (0, upper, 1, n2, n_all),
        "Q": (1, lower, 2, n2, n_all),
        "V": (2, upper, 1, gf_ref, g_all),
        "W": (3, lower, 2, gf_ref, g_all),
    }

    def place_of(route, p):
        if route == 1:
            j, other = [(0, 0), (1, 0), (0, 1), (2, 0), (1, 1), (3, 0), (2, 1), (3, 1)][p]
        else:
            j, other = p // 2, p % 2
        zz = [z, z + 1 - 2 * (z % 2), 2 - z // 2, 3 - 3 * (z // 2)][j]
        yy = y + other - 2 * other * y
        return zz, yy, other

    def part_copy(name, kind, p, s, where):
        k, rows, _, own, whole = parts[name]
        dst = whole.at[s, rows]
        src = own.at[rows] if p == 0 else dst
        return remote(src, dst, send_sem.at[k, kind, p], recv_sem.at[k, s], where)

    def each_send(name, p, act):
        route = parts[name][2]
        zz, yy, other = place_of(route, p)
        s = 4 * zz + 2 * yy + c
        if route == 2 or other == 0:

            @pl.when((zz <= z) & (z < 3))
            def _():
                act(part_copy(name, 0, p, s, {"rows": me + 4}))

            @pl.when((zz >= z) & (z > 0))
            def _():
                act(part_copy(name, 1, p, s, {"rows": me - 4}))

        if p == 0 or (route == 1 and other == 0):
            act(part_copy(name, 2, p, s, {"rows": y_peer}))
        act(part_copy(name, 3, p, s, {"rows": core_peer}))

    own_copies = {
        "S": pltpu.make_async_copy(n2, n_all.at[me], own_sem.at[0]),
        "V": pltpu.make_async_copy(gf_ref, g_all.at[me], own_sem.at[1]),
    }

    def begin(names):
        own_copies[names[1]].start()
        for name in names:
            each_send(name, 0, lambda copy: copy.start())

    def arrive(*steps):
        for step in steps:
            name, p = step[0], int(step[1])
            zz, yy, _ = place_of(parts[name][2], p)
            part_copy(name, 0, p, 4 * zz + 2 * yy + c, {"rows": me}).wait_recv()
            each_send(name, p, lambda copy: copy.start())

    back_copy = remote(grad_enc, returned, x_send.at[0], x_recv.at[0], {"section": 1 - section})

    def feed_forward(first, count):
        def step(i, carry):
            for k in range(2):
                b = first + 2 * i + k
                load(b).wait()
                w = slots.at[b % held]
                gu = dot_last(n2[...], w[: 2 * f, :])
                gu_buf[b] = gu
                hidden = (gelu_parts(gu[:, :f])[0] * gu[:, f:]).astype(bf16)
                y2[...] += dot(hidden, w[2 * f :, :])

                @pl.when(b < spare)
                def _():
                    load(b + held).start()

            return carry

        lax.fori_loop(0, count // 2, step, 0)

    def feed_backward(first, count, fresh):
        def step(i, carry):
            for k in range(2):
                b = BLOCKS - 1 - first - 2 * i - k

                @pl.when((b < spare) | fresh)
                def _():
                    load(b).wait()

                w = slots.at[b % held]
                gh = dot_last(gf_ref[...], w[2 * f :, :])
                gu = gu_buf[b]
                act, slope = gelu_parts(gu[:, :f])
                dg = (gh * gu[:, f:] * slope).astype(bf16)
                du = (gh * act).astype(bf16)
                acc[...] += dot(dg, w[:f, :]) + dot(du, w[f : 2 * f, :])

                @pl.when(b >= held)
                def _():
                    load(b - held).start()

            return carry

        lax.fori_loop(0, count // 2, step, 0)

    def final_backward(up):
        back, sums_ref[2:3, :] = norm_back(y2[...], gain_ref[2:3, :], up)
        last[...] = back
        gf_ref[...] = back.astype(bf16)
        begin("WV")
        acc[...] = jnp.zeros_like(acc)

    def feed_end():
        back, sums_ref[1:2, :] = norm_back(mid[...], gain_ref[1:2, :], acc[...])
        acc[...] = last[...] + back

    sums_ref[...] = jnp.zeros_like(sums_ref)

    @pl.when(is_enc)
    def _():
        n2[...] = n2_in[...]
        begin("QS")
        mid[...] = y1_ref[...]
        y2[...] = y2_in[...]
        arrive("Q1", "Q2", "S2", "S1", "Q3", "Q4", "S4", "S3", "Q5", "Q6")
        back_copy.wait_recv()
        final_backward(returned[...].astype(f32))
        load_gu.wait()
        arrive("S6")
        feed_backward(0, 8, True)
        arrive("S5", "Q7")
        feed_backward(8, 8, True)
        feed_end()
        arrive("W1", "W2")
        load_attn.wait()

    @pl.when(is_dec)
    def _():
        y1 = y1_ref[...]
        mc_ref[...] = (unit_rows(y1)[1] * gain_ref[3:4, :]).astype(bf16)
        load_cross.wait()
        cqkv[:, :inner] = dot_last(mc_ref[...], w_att[:inner, :]).astype(bf16)
        cqkv[:, inner:] = dot_last(encoded_ref[...], w_att[inner : 3 * inner, :]).astype(bf16)
        heads_fwd(cross_cnt, cqkv, cmixed_ref, length)
        mid[...] = y1_ref[...] + dot(cmixed_ref[...], w_att[3 * inner :, :])
        y2[...] = mid[...]
        n2[...] = (unit_rows(mid[...])[1] * gain_ref[1:2, :]).astype(bf16)
        begin("QS")
        feed_forward(0, 12)
        arrive("Q1", "Q2")
        feed_forward(12, 4)
        final_ref[...] = (unit_rows(y2[...])[1] * gain_ref[2:3, :]).astype(bf16)
        load_head.wait()
        loss = loss_back(dec_cnt, final_ref, w_head, target_ref, gl_ref, length)
        sums_ref[4:5, :] = jnp.broadcast_to(loss, (1, sums_ref.shape[1]))
        final_backward(dot(gl_ref[...], w_head[...]))
        feed_backward(0, 8, False)
        arrive("S2", "S1")
        feed_backward(8, 8, False)
        feed_end()
        arrive("W1", "Q3")
        gac_ref[...] = acc[...].astype(bf16)
        do_buf[...] = dot_last(gac_ref[...], w_att[3 * inner :, :]).astype(bf16)
        heads_bwd(cross_cnt, cqkv, do_buf, dcqkv_ref, length)
        grad_enc[...] = dot(dcqkv_ref[:, inner:], w_att[inner : 3 * inner, :]).astype(bf16)
        back_copy.start()
        up = dot(dcqkv_ref[:, :inner], w_att[:inner, :])
        load_attn.start()
        back, sums_ref[3:4, :] = norm_back(y1_ref[...], gain_ref[3:4, :], up)
        acc[...] += back
        arrive("Q4", "W2")
        load_attn.wait()

    ga_ref[...] = acc[...].astype(bf16)
    do_buf[...] = dot_last(ga_ref[...], w_att[3 * inner :, :]).astype(bf16)
    heads_bwd(self_cnt, qkv_ref, do_buf, dqkv_ref, length)
    up = dot(dqkv_ref[...], w_att[: 3 * inner, :])
    back, sums_ref[0:1, :] = norm_back(x_ref[...].astype(f32), gain_ref[0:1, :], up)
    gx_ref[...] = acc[...] + back

    @pl.when(is_enc)
    def _():
        arrive("V2", "V1", "W4", "W3", "S7", "V3", "W6", "V4", "W5", "V6", "V5", "W7", "V7")

    @pl.when(is_dec)
    def _():
        arrive("V2", "V1", "S4", "S3", "W3", "Q5", "V4", "Q6", "W4", "S6")
        arrive("V3", "S5", "V6", "W5", "Q7", "W6", "S7", "V5", "W7", "V7")

    for name in parts:
        for p in range(8):
            zz, yy, _ = place_of(parts[name][2], p)
            part_copy(name, 0, p, 4 * zz + 2 * yy + 1 - c, {"rows": me}).wait_recv()
            each_send(name, p, lambda copy: copy.wait_send())
    own_copies["S"].wait()
    own_copies["V"].wait()

    @pl.when(is_dec)
    def _():
        back_copy.wait_send()


def middle(cross_cnt, self_cnt, dec_cnt, x, y1, y2, n2, qkv, encoded, target, gains, gu, attn_w, cross_w, head_w, feed_w, length):
    t, d = x.shape
    inner = attn_w.shape[0] // 4
    held = 10
    vm = pl.BlockSpec(memory_space=pltpu.VMEM)
    sm = pl.BlockSpec(memory_space=pltpu.SMEM)
    anywhere = pl.BlockSpec(memory_space=pl.ANY)
    half = jax.ShapeDtypeStruct((t, d), bf16)
    wide = jax.ShapeDtypeStruct((t, 3 * inner), bf16)
    return pl.pallas_call(
        functools.partial(mid_kernel, length),
        out_shape=(
            jax.ShapeDtypeStruct((16, t, d), bf16),
            jax.ShapeDtypeStruct((16, t, d), bf16),
            half, half, wide,
            jax.ShapeDtypeStruct((t, d), f32),
            jax.ShapeDtypeStruct((8, d), f32),
            half, wide,
            jax.ShapeDtypeStruct((t, inner), bf16),
            half, half,
            jax.ShapeDtypeStruct((t, head_w.shape[0]), bf16),
        ),
        in_specs=[sm] * 3 + [vm] * 8 + [anywhere] * 5,
        out_specs=(anywhere,) * 2 + (vm,) * 11,
        scratch_shapes=[
            pltpu.VMEM((held,) + feed_w.shape[1:], bf16),
            pltpu.VMEM(gu.shape, f32),
            pltpu.VMEM(attn_w.shape, bf16),
            pltpu.VMEM(head_w.shape, bf16),
            pltpu.VMEM((t, d), f32),
            pltpu.VMEM((t, d), f32),
            pltpu.VMEM((t, d), f32),
            pltpu.VMEM((t, d), f32),
            pltpu.VMEM((t, d), bf16),
            pltpu.VMEM((t, 3 * inner), bf16),
            pltpu.VMEM((t, inner), bf16),
            pltpu.VMEM((t, d), bf16),
            pltpu.VMEM((t, d), bf16),
            pltpu.SemaphoreType.DMA((4, 4, 8)),
            pltpu.SemaphoreType.DMA((4, 16)),
            pltpu.SemaphoreType.DMA((held,)),
            pltpu.SemaphoreType.DMA((4,)),
            pltpu.SemaphoreType.DMA((2,)),
            pltpu.SemaphoreType.DMA((1,)),
            pltpu.SemaphoreType.DMA((1,)),
        ],
        compiler_params=pltpu.CompilerParams(
            vmem_limit_bytes=62 * 1024 * 1024, collective_id=2, has_side_effects=True
        ),
        cost_estimate=pl.CostEstimate(
            flops=4 * t * feed_w.size, bytes_accessed=2 * feed_w.size + 8 * gu.size, transcendentals=2 * gu.size
        ),
    )(cross_cnt, self_cnt, dec_cnt, x, y1, y2, n2, qkv, encoded, target, gains, gu, attn_w, cross_w, head_w, feed_w)


def adam_step(weight, first_moment, second_moment, gradient, step_rate, weight_decay):
    first_new = 0.9 * first_moment + 0.1 * gradient
    second_new = 0.999 * second_moment + 0.001 * gradient * gradient
    first_fix = 1.0 - 0.9**STEP
    second_fix = 1.0 - 0.999**STEP
    update = first_new / first_fix / (jnp.sqrt(second_new / second_fix) + 1e-08)
    return (first_new, second_new, weight - step_rate * (update + weight_decay * weight))


def kinds_first(gathered, n, kinds, per):
    d = gathered.shape[-1]
    return gathered.reshape(n, kinds, per, d).transpose(1, 0, 2, 3).reshape(kinds * n * per, d)


def owners_first(left, right, n):
    t, k, units = left.shape
    grad = jnp.einsum("tku,td->kud", left, right, preferred_element_type=f32)
    return grad.reshape(k, n, units // n, -1).transpose(1, 0, 2, 3)


def local(
    block_input,
    lengths,
    targets,
    attention_weight,
    attention_first,
    attention_second,
    feed_weight,
    feed_first,
    feed_second,
    norm_gain,
    gain_first,
    gain_second,
    cross_weight,
    cross_first,
    cross_second,
    head_weight,
    head_first,
    head_second,
    cross_gain,
    cross_gain_first,
    cross_gain_second,
):
    n = lax.axis_size("rows")
    is_encoder = lax.axis_index("section") == 0
    micro, length, d = block_input.shape[1:]
    t = micro * length
    per = attention_weight.shape[1]
    f = feed_weight.shape[1]
    inner = per * n

    attn_own = attention_weight[0].astype(bf16).transpose(1, 0, 2).reshape(4 * per, d)
    feed_own = feed_weight[0].astype(bf16).transpose(1, 0, 2)
    half_rows = jnp.concatenate(
        [cross_weight.astype(bf16).transpose(1, 0, 2), head_weight.astype(bf16)[None]], axis=0
    )

    gains = norm_gain[0]
    gain_attn, gain_feed, gain_final = gains[0:1], gains[1:2], gains[2:3]
    gain_cross = cross_gain[None]
    x = block_input[0].reshape(t, d)
    enc_counts = lengths[0, :, 0]
    dec_counts = lengths[1, :, 0]
    zero_one = jnp.zeros((1,), jnp.int32)
    self_counts = jnp.concatenate([jnp.where(is_encoder, 0, 1).astype(jnp.int32)[None], enc_counts])
    cross_counts = jnp.concatenate([zero_one, enc_counts])
    target_column = targets.reshape(t, 1)

    def blank(maker):
        return jax.tree.map(lambda a: jnp.zeros(a.shape, a.dtype), jax.eval_shape(maker))

    emit = n != BLOCKS
    if emit:
        attn_all = lax.all_gather(attn_own, "rows", axis=0, tiled=True)
        attn_w = kinds_first(attn_all, n, 4, per)
        feed_all = lax.all_gather(feed_own.reshape(3 * f, d), "rows", axis=0, tiled=True)
        feed_w = kinds_first(feed_all, n, 3, f).reshape(3, BLOCKS, -1, d)
        feed_w = feed_w.transpose(1, 0, 2, 3).reshape(BLOCKS, -1, d)
        other_half = lax.ppermute(half_rows, "section", [(0, 1)])
        extra_own = jnp.concatenate([other_half, half_rows], axis=-1).reshape(5 * per, d)
        extra_all = lax.all_gather(extra_own, "rows", axis=0, tiled=True)
        n1, qkv, mixed, y1 = attend_fwd(self_counts, x, gain_attn, attn_w, length)

        def enc_feed():
            return feed_fwd(y1, gain_feed, gain_final, feed_w)

        enc_state = lax.cond(is_encoder, enc_feed, lambda: blank(enc_feed))
        encoded = lax.ppermute(enc_state[3], "section", [(0, 1)])
    else:
        units = jnp.arange(4 * inner, dtype=jnp.int32).reshape(n, 4, per)
        order = units.transpose(1, 0, 2).reshape(1, 4 * inner)
        pad = -(5 * per) % 16
        half_own = jnp.pad(half_rows.reshape(5 * per, d // 2), ((0, pad), (0, 0)))
        outs = front(
            self_counts, order, x, gain_attn, gain_feed, gain_final,
            attn_own, feed_own.reshape(3 * f, d), half_own, length,
        )
        attn_all, feed_w, first_all, second_all, n1, qkv, mixed, y1 = outs[:8]
        enc_state, encoded = outs[8:12], outs[12]
        attn_w = kinds_first(attn_all, n, 4, per)
        extra_all = jnp.concatenate([first_all, second_all], axis=-1)[:, : 5 * per]
    extra_w = kinds_first(extra_all, n, 5, per)
    cross_w, head_w = extra_w[: 4 * inner], extra_w[4 * inner :]

    if emit:
        def dec_front():
            mc, cqkv, cmixed, z2 = attend_fwd(cross_counts, y1, gain_cross, cross_w, length, encoded)
            return feed_fwd(z2, gain_feed, gain_final, feed_w) + (mc, cqkv, cmixed, z2)

        def enc_pass():
            rest = jax.eval_shape(dec_front)[4:7]
            return tuple(enc_state) + tuple(jnp.zeros(a.shape, a.dtype) for a in rest) + (y1,)

        n2, gu, y2, final, mc, cqkv, cmixed, mid = lax.cond(is_encoder, enc_pass, dec_front)
        def dec_back():
            gl, up, loss = head_loss(dec_counts, final, head_w, target_column, length)
            feed_out = feed_bwd(up, mid, y2, gain_feed, gain_final, gu, feed_w, emit)
            ga_c, dqkv_c, gy1, gg_c, ge = attend_bwd(
                cross_counts, y1, gain_cross, feed_out[1], cqkv, cross_w, length, True
            )
            return (ge, gy1, feed_out[2], feed_out[0], *feed_out[3:], gl, ga_c, dqkv_c, gg_c, loss)

        back = lax.cond(is_encoder, lambda: blank(dec_back), dec_back)
        returned = lax.ppermute(back[0], "section", [(1, 0)])
        at = 6 if emit else 4
        gl, ga_c, dqkv_c, gg_c, loss = back[at:]

        def enc_back():
            feed_out = feed_bwd(returned, mid, y2, gain_feed, gain_final, gu, feed_w, emit)
            return (feed_out[1], feed_out[2], feed_out[0], *feed_out[3:])

        backs = lax.cond(is_encoder, enc_back, lambda: tuple(back[1:at]))
        gy1, gg_feed, gf = backs[:3]

        ga, dqkv, gx, gg_attn = attend_bwd(self_counts, x, gain_attn, gy1, qkv, attn_w, length)
        tiny = jnp.concatenate(
            [gg_attn, gg_feed, gg_c, jnp.broadcast_to(loss, (1, d)), jnp.zeros((3, d), f32)], axis=0
        )
    else:
        gain_rows = jnp.concatenate([gains, gain_cross], axis=0)
        n2, gu, y2 = enc_state[:3]
        (
            n2_all, gf_all, _, ga, dqkv, gx, tiny, mc, dqkv_c, cmixed, ga_c, final, gl,
        ) = middle(
            cross_counts, self_counts, dec_counts, x, y1, y2, n2, qkv, encoded, target_column,
            gain_rows, gu, attn_w, cross_w, head_w, feed_w, length,
        )

    half = d // 2
    if emit:
        extra_part = jnp.concatenate(
            [
                owners_first(dqkv_c[:, None, :inner], mc, n),
                owners_first(dqkv_c[:, inner:].reshape(t, 2, inner), encoded, n),
                owners_first(cmixed[:, None], ga_c, n),
                owners_first(gl[:, None], final, n),
            ],
            axis=1,
        ).astype(bf16)
        extra_sum = lax.psum_scatter(
            extra_part.reshape(n * 5 * per, d), "rows", scatter_dimension=0, tiled=True
        )
        extra_first = lax.ppermute(extra_sum[:, :half], "section", [(1, 0)])
        extra_grad = jnp.where(is_encoder, extra_first, extra_sum[:, half:]).astype(f32)
        extra_grad = extra_grad.reshape(5, per, half)

        attn_part = jnp.concatenate(
            [
                owners_first(dqkv.reshape(t, 3, inner), n1, n),
                owners_first(mixed[:, None], ga, n),
            ],
            axis=1,
        ).astype(bf16)
        attn_sum = lax.psum_scatter(
            attn_part.reshape(n * 4 * per, d), "rows", scatter_dimension=0, tiled=True
        ).astype(f32)
        dgu, hid = backs[3], backs[4]
        nb, _, fb = hid.shape
        left = dgu.reshape(nb, t, 2, fb).transpose(1, 2, 0, 3).reshape(t, 2, nb * fb)
        hid = hid.transpose(1, 0, 2).reshape(t, 1, nb * fb)
        feed_part = jnp.concatenate(
            [owners_first(left, n2, n), owners_first(hid, gf, n)], axis=1
        ).astype(bf16)
        feed_grad = lax.psum_scatter(
            feed_part.reshape(n * 3 * f, d), "rows", scatter_dimension=0, tiled=True
        ).astype(f32)
        tiny_sum = jnp.sum(lax.all_gather(tiny, "rows", axis=0), axis=0)
        tiny_dec = lax.ppermute(tiny_sum[3:5], "section", [(1, 0)])
        tiny_dec = jnp.where(is_encoder, tiny_dec, tiny_sum[3:5])
        tiny_sum = jnp.concatenate([tiny_sum[:3], tiny_dec], axis=0)
    else:
        def lefts(units):
            units = units.reshape(t, -1, 4, 2, 2, per).transpose(4, 1, 3, 2, 5, 0)
            return units.reshape(2, -1, t)

        feed_grad, attn_sum, extra_grad, tiny_sum = tail(
            tiny, lefts(jnp.concatenate([dqkv, mixed], axis=1)), n1, ga, feed_own.reshape(3 * f, d),
            lefts(jnp.concatenate([dqkv_c, cmixed, gl], axis=1)), mc, encoded, ga_c, final, n2_all, gf_all,
        )
        extra_grad = extra_grad[: 5 * per].reshape(5, per, half)
    attn_grad = attn_sum.reshape(4, per, d).transpose(1, 0, 2)
    feed_grad = feed_grad.reshape(3, f, d).transpose(1, 0, 2)
    cross_gain_total = tiny_sum[3]
    loss_total = tiny_sum[4, 0]

    attention_new = adam_step(
        attention_weight, attention_first, attention_second, attn_grad[None], 0.05, 0.1
    )
    feed_new = adam_step(feed_weight, feed_first, feed_second, feed_grad[None], 0.05, 0.1)
    gain_new = adam_step(norm_gain, gain_first, gain_second, tiny_sum[None, 0:3], 0.5, 0.0)
    cross_new = adam_step(
        cross_weight, cross_first, cross_second, extra_grad[:4].transpose(1, 0, 2), 0.05, 0.1
    )
    head_new = adam_step(head_weight, head_first, head_second, extra_grad[4], 0.05, 0.1)
    cross_gain_new = adam_step(
        cross_gain, cross_gain_first, cross_gain_second, cross_gain_total, 0.5, 0.0
    )
    return (
        gx.reshape(1, micro, length, d),
        loss_total,
        *attention_new,
        *feed_new,
        *gain_new,
        *cross_new,
        *head_new,
        *cross_gain_new,
    )


def solution(mesh):
    by_row = P("section", "rows", None, None)
    gain = P("section", None, None)
    cross = P("rows", None, "section")
    head = P("rows", "section")
    weights = (by_row,) * 6 + (gain,) * 3 + (cross,) * 3 + (head,) * 3 + (P(),) * 3
    tokens = P("section", None, "rows", None)
    return jax.shard_map(
        local,
        mesh=mesh,
        in_specs=(tokens, P(None, None, "rows"), P(None, "rows")) + weights,
        out_specs=(tokens, P()) + weights,
        check_vma=False,
    )
```

```python
import functools

import jax
import jax.numpy as jnp
from jax import lax
from jax.experimental import pallas as pl
from jax.experimental.pallas import tpu as pltpu
from jax.sharding import PartitionSpec as P

HD = 64
STEP = 10
PAIR = 2 * HD
BLOCKS = 16
VMEM_BYTES = 52 * 1024 * 1024

bf16 = jnp.bfloat16
f32 = jnp.float32
masked_value = -1000000000.0
scale = HD ** (-0.5)


def dot(a, b):
    return lax.dot_general(a, b, (((1,), (0,)), ((), ())), preferred_element_type=f32)


def dot_last(a, b):
    return lax.dot_general(a, b, (((1,), (1,)), ((), ())), preferred_element_type=f32)


def dot_rows(a, b):
    return lax.dot_general(a, b, (((0,), (0,)), ((), ())), preferred_element_type=f32)


def unit_rows(v):
    r = lax.rsqrt(jnp.mean(v * v, axis=-1, keepdims=True) + 1e-06)
    return r, v * r


def norm_back(v, gain, up):
    r, n = unit_rows(v)
    g = up * gain
    back = r * (g - n * jnp.mean(g * n, axis=-1, keepdims=True))
    return back, jnp.sum(up * n, axis=0, keepdims=True)


def gelu_parts(x):
    c = 0.7978845608028654
    t = jnp.tanh(c * (x + 0.044715 * (x * x * x)))
    act = 0.5 * x * (1.0 + t)
    slope = 0.5 * (1.0 + t) + 0.5 * x * (1.0 - t * t) * (c * (1.0 + 3.0 * 0.044715 * (x * x)))
    return act, slope


def low_half(length):
    return lax.broadcasted_iota(jnp.int32, (length, PAIR), 1) < HD


def stack_pair(m, low):
    zero = jnp.zeros_like(m)
    return jnp.concatenate([jnp.where(low, m, zero), jnp.where(low, zero, m)], axis=0)


def allowed_twice(cnt_ref, s, length):
    row = lax.broadcasted_iota(jnp.int32, (length, length), 0)
    col = lax.broadcasted_iota(jnp.int32, (length, length), 1)
    limit = jnp.where(cnt_ref[0] == 1, row + 1, cnt_ref[1 + s])
    one = jnp.where(col < limit, 1, 0)
    return jnp.concatenate([one, one], axis=0) == 1


def soft_pair(q2, k, allowed):
    s = dot_last(q2, k) * scale
    s = jnp.where(allowed, s, masked_value)
    e = jnp.exp(s - jnp.max(s, axis=-1, keepdims=True))
    return e / jnp.sum(e, axis=-1, keepdims=True)


def head_columns(inner, h):
    return [slice(j * inner + h * PAIR, j * inner + (h + 1) * PAIR) for j in range(3)]


def heads_fwd(cnt_ref, qkv_ref, o_ref, length):
    t, inner = o_ref.shape
    low = low_half(length)
    for s in range(t // length):
        allowed = allowed_twice(cnt_ref, s, length)
        rows = slice(s * length, (s + 1) * length)
        for h in range(inner // PAIR):
            cols = head_columns(inner, h)
            q2 = stack_pair(qkv_ref[rows, cols[0]], low)
            p = soft_pair(q2, qkv_ref[rows, cols[1]], allowed).astype(bf16)
            wide = jnp.concatenate([p[:length], p[length:]], axis=1)
            o_ref[rows, cols[0]] = dot(wide, stack_pair(qkv_ref[rows, cols[2]], low)).astype(bf16)


def heads_bwd(cnt_ref, qkv_ref, do_ref, dqkv_ref, length):
    t, inner = do_ref.shape
    low = low_half(length)
    for s in range(t // length):
        allowed = allowed_twice(cnt_ref, s, length)
        rows = slice(s * length, (s + 1) * length)
        for h in range(inner // PAIR):
            cols = head_columns(inner, h)
            q2 = stack_pair(qkv_ref[rows, cols[0]], low)
            k = qkv_ref[rows, cols[1]]
            p = soft_pair(q2, k, allowed)
            do2 = stack_pair(do_ref[rows, cols[0]], low)
            dp = dot_last(do2, qkv_ref[rows, cols[2]])
            ds = p * (dp - jnp.sum(dp * p, axis=-1, keepdims=True))
            ds = jnp.where(allowed, ds, 0.0).astype(bf16)
            wide = jnp.concatenate([ds[:length], ds[length:]], axis=1)
            dqkv_ref[rows, cols[0]] = (dot(wide, stack_pair(k, low)) * scale).astype(bf16)
            dqkv_ref[rows, cols[1]] = (dot_rows(ds, q2) * scale).astype(bf16)
            dqkv_ref[rows, cols[2]] = dot_rows(p.astype(bf16), do2).astype(bf16)


def loss_back(cnt_ref, f_ref, w_ref, target_ref, gl_ref, length):
    logits = dot_last(f_ref[...], w_ref[...])
    top = jnp.max(logits, axis=-1, keepdims=True)
    log_total = top + jnp.log(jnp.sum(jnp.exp(logits - top), axis=-1, keepdims=True))
    hit = lax.broadcasted_iota(jnp.int32, logits.shape, 1) == target_ref[...]
    picked = jnp.sum(jnp.where(hit, logits, 0.0), axis=-1, keepdims=True)
    probs = jnp.exp(logits - log_total) - jnp.where(hit, 1.0, 0.0)
    total = jnp.zeros((1, 1), f32)
    for s in range(logits.shape[0] // length):
        rows = slice(s * length, (s + 1) * length)
        valid = lax.broadcasted_iota(jnp.int32, (length, 1), 0) < cnt_ref[s]
        total += jnp.sum(
            jnp.where(valid, log_total[rows] - picked[rows], 0.0), axis=0, keepdims=True
        )
        gl_ref[rows, :] = jnp.where(valid, probs[rows], 0.0).astype(bf16)
    return total


def attend_fwd_kernel(cross, length, cnt_ref, x_ref, gain_ref, *refs):
    if cross:
        src_ref, w_ref, n_ref, qkv_ref, o_ref, y_ref = refs
    else:
        w_ref, n_ref, qkv_ref, o_ref, y_ref = refs
    inner = w_ref.shape[0] // 4
    x = x_ref[...].astype(f32)
    n = (unit_rows(x)[1] * gain_ref[...]).astype(bf16)
    n_ref[...] = n
    if cross:
        qkv_ref[:, :inner] = dot_last(n, w_ref[:inner, :]).astype(bf16)
        qkv_ref[:, inner:] = dot_last(src_ref[...], w_ref[inner : 3 * inner, :]).astype(bf16)
    else:
        qkv_ref[...] = dot_last(n, w_ref[: 3 * inner, :]).astype(bf16)
    heads_fwd(cnt_ref, qkv_ref, o_ref, length)
    y_ref[...] = x + dot(o_ref[...], w_ref[3 * inner :, :])


def attend_fwd(counts, x, gain, w, length, source=None):
    t, d = x.shape
    inner = w.shape[0] // 4
    ins = [counts, x, gain] + ([] if source is None else [source]) + [w]
    vm = pl.BlockSpec(memory_space=pltpu.VMEM)
    return pl.pallas_call(
        functools.partial(attend_fwd_kernel, source is not None, length),
        out_shape=(
            jax.ShapeDtypeStruct((t, d), bf16),
            jax.ShapeDtypeStruct((t, 3 * inner), bf16),
            jax.ShapeDtypeStruct((t, inner), bf16),
            jax.ShapeDtypeStruct((t, d), f32),
        ),
        in_specs=[pl.BlockSpec(memory_space=pltpu.SMEM)] + [vm] * (len(ins) - 1),
        out_specs=(vm,) * 4,
        compiler_params=pltpu.CompilerParams(vmem_limit_bytes=VMEM_BYTES),
        cost_estimate=pl.CostEstimate(
            flops=2 * t * d * inner * 4 + 8 * t * length * inner,
            bytes_accessed=w.size * 2 + t * d * 10,
            transcendentals=t * length * 6,
        ),
    )(*ins)


def attend_bwd_kernel(cross, length, cnt_ref, x_ref, gain_ref, gy_ref, qkv_ref, w_ref, *refs):
    if cross:
        ga_ref, dqkv_ref, gx_ref, gg_ref, gs_ref, do_ref = refs
    else:
        ga_ref, dqkv_ref, gx_ref, gg_ref, do_ref = refs
    inner = w_ref.shape[0] // 4
    ga = gy_ref[...].astype(bf16)
    ga_ref[...] = ga
    do_ref[...] = dot_last(ga, w_ref[3 * inner :, :]).astype(bf16)
    heads_bwd(cnt_ref, qkv_ref, do_ref, dqkv_ref, length)
    if cross:
        up = dot(dqkv_ref[:, :inner], w_ref[:inner, :])
        gs_ref[...] = dot(dqkv_ref[:, inner:], w_ref[inner : 3 * inner, :]).astype(bf16)
    else:
        up = dot(dqkv_ref[...], w_ref[: 3 * inner, :])
    back, gg_ref[...] = norm_back(x_ref[...].astype(f32), gain_ref[...], up)
    gx_ref[...] = gy_ref[...] + back


def attend_bwd(counts, x, gain, gy, qkv, w, length, cross=False):
    t, d = x.shape
    inner = w.shape[0] // 4
    vm = pl.BlockSpec(memory_space=pltpu.VMEM)
    outs = [
        jax.ShapeDtypeStruct((t, d), bf16),
        jax.ShapeDtypeStruct((t, 3 * inner), bf16),
        jax.ShapeDtypeStruct((t, d), f32),
        jax.ShapeDtypeStruct((1, d), f32),
    ]
    if cross:
        outs.append(jax.ShapeDtypeStruct((t, d), bf16))
    return pl.pallas_call(
        functools.partial(attend_bwd_kernel, cross, length),
        out_shape=tuple(outs),
        in_specs=[pl.BlockSpec(memory_space=pltpu.SMEM)] + [vm] * 5,
        out_specs=(vm,) * len(outs),
        scratch_shapes=[pltpu.VMEM((t, inner), bf16)],
        compiler_params=pltpu.CompilerParams(vmem_limit_bytes=VMEM_BYTES),
        cost_estimate=pl.CostEstimate(
            flops=2 * t * d * inner * 4 + 20 * t * length * inner,
            bytes_accessed=w.size * 2 + t * d * 16,
            transcendentals=t * length * 6,
        ),
    )(counts, x, gain, gy, qkv, w)


def feed_fwd_kernel(y_ref, g_in_ref, g_out_ref, w_ref, n_ref, gu_ref, y2_ref, f_ref):
    i = pl.program_id(0)
    f = w_ref.shape[1] // 3

    @pl.when(i == 0)
    def _():
        y = y_ref[...]
        n_ref[...] = (unit_rows(y)[1] * g_in_ref[...]).astype(bf16)
        y2_ref[...] = y

    gu = dot_last(n_ref[...], w_ref[0, : 2 * f, :])
    gu_ref[0] = gu
    hidden = (gelu_parts(gu[:, :f])[0] * gu[:, f:]).astype(bf16)
    y2_ref[...] += dot(hidden, w_ref[0, 2 * f :, :])

    @pl.when(i == pl.num_programs(0) - 1)
    def _():
        f_ref[...] = (unit_rows(y2_ref[...])[1] * g_out_ref[...]).astype(bf16)


def feed_fwd(y, gain_in, gain_out, w):
    t, d = y.shape
    nb, rows, _ = w.shape
    f = rows // 3
    whole = lambda *shape: pl.BlockSpec(shape, lambda i: (0,) * len(shape))
    part = lambda *shape: pl.BlockSpec((1,) + shape, lambda i: (i, 0, 0))
    return pl.pallas_call(
        feed_fwd_kernel,
        grid=(nb,),
        out_shape=(
            jax.ShapeDtypeStruct((t, d), bf16),
            jax.ShapeDtypeStruct((nb, t, 2 * f), f32),
            jax.ShapeDtypeStruct((t, d), f32),
            jax.ShapeDtypeStruct((t, d), bf16),
        ),
        in_specs=[whole(t, d), whole(1, d), whole(1, d), part(rows, d)],
        out_specs=(whole(t, d), part(t, 2 * f), whole(t, d), whole(t, d)),
        compiler_params=pltpu.CompilerParams(vmem_limit_bytes=VMEM_BYTES),
        cost_estimate=pl.CostEstimate(
            flops=2 * t * d * rows * nb,
            bytes_accessed=w.size * 2 + t * d * 12 + nb * t * f * 8,
            transcendentals=nb * t * f,
        ),
    )(y, gain_in, gain_out, w)


def feed_bwd_kernel(emit, up_ref, y_ref, y2_ref, g_in_ref, g_out_ref, gu_ref, w_ref, *refs):
    if emit:
        gf_ref, gy_ref, gg_ref, dgu_ref, hid_ref, last_ref = refs
    else:
        gf_ref, gy_ref, gg_ref, last_ref = refs
    i = pl.program_id(0)
    f = w_ref.shape[1] // 3

    @pl.when(i == 0)
    def _():
        back, gain_grad = norm_back(y2_ref[...], g_out_ref[...], up_ref[...].astype(f32))
        gg_ref[1:2, :] = gain_grad
        last_ref[...] = back
        gf_ref[...] = back.astype(bf16)
        gy_ref[...] = jnp.zeros_like(gy_ref)

    gh = dot_last(gf_ref[...], w_ref[0, 2 * f :, :])
    act, slope = gelu_parts(gu_ref[0, :, :f])
    u = gu_ref[0, :, f:]
    dg = (gh * u * slope).astype(bf16)
    du = (gh * act).astype(bf16)
    if emit:
        dgu_ref[0, :, :f] = dg
        dgu_ref[0, :, f:] = du
        hid_ref[0] = (act * u).astype(bf16)
    gy_ref[...] += dot(dg, w_ref[0, :f, :]) + dot(du, w_ref[0, f : 2 * f, :])

    @pl.when(i == pl.num_programs(0) - 1)
    def _():
        back, gain_grad = norm_back(y_ref[...], g_in_ref[...], gy_ref[...])
        gg_ref[0:1, :] = gain_grad
        gy_ref[...] = last_ref[...] + back


def feed_bwd(up, y, y2, gain_in, gain_out, gu, w, emit):
    t, d = y.shape
    nb, rows, _ = w.shape
    f = rows // 3
    whole = lambda *shape: pl.BlockSpec(shape, lambda i: (0,) * len(shape))
    part = lambda *shape: pl.BlockSpec((1,) + shape, lambda i: (i, 0, 0))
    outs = [
        jax.ShapeDtypeStruct((t, d), bf16),
        jax.ShapeDtypeStruct((t, d), f32),
        jax.ShapeDtypeStruct((2, d), f32),
    ]
    specs = [whole(t, d), whole(t, d), whole(2, d)]
    if emit:
        outs += [
            jax.ShapeDtypeStruct((nb, t, 2 * f), bf16),
            jax.ShapeDtypeStruct((nb, t, f), bf16),
        ]
        specs += [part(t, 2 * f), part(t, f)]
    return pl.pallas_call(
        functools.partial(feed_bwd_kernel, emit),
        grid=(nb,),
        out_shape=tuple(outs),
        in_specs=[whole(t, d)] * 3 + [whole(1, d)] * 2 + [part(t, 2 * f), part(rows, d)],
        out_specs=tuple(specs),
        scratch_shapes=[pltpu.VMEM((t, d), f32)],
        compiler_params=pltpu.CompilerParams(vmem_limit_bytes=VMEM_BYTES),
        cost_estimate=pl.CostEstimate(
            flops=2 * t * d * rows * nb,
            bytes_accessed=w.size * 2 + t * d * 18 + nb * t * f * 8,
            transcendentals=nb * t * f,
        ),
    )(up, y, y2, gain_in, gain_out, gu, w)


def head_kernel(length, cnt_ref, f_ref, w_ref, target_ref, gl_ref, up_ref, loss_ref):
    loss_ref[...] = loss_back(cnt_ref, f_ref, w_ref, target_ref, gl_ref, length)
    up_ref[...] = dot(gl_ref[...], w_ref[...])


def head_loss(counts, final, w, target, length):
    t, d = final.shape
    v = w.shape[0]
    vm = pl.BlockSpec(memory_space=pltpu.VMEM)
    return pl.pallas_call(
        functools.partial(head_kernel, length),
        out_shape=(
            jax.ShapeDtypeStruct((t, v), bf16),
            jax.ShapeDtypeStruct((t, d), f32),
            jax.ShapeDtypeStruct((1, 1), f32),
        ),
        in_specs=[pl.BlockSpec(memory_space=pltpu.SMEM), vm, vm, vm],
        out_specs=(vm,) * 3,
        compiler_params=pltpu.CompilerParams(vmem_limit_bytes=VMEM_BYTES),
        cost_estimate=pl.CostEstimate(
            flops=4 * t * d * v, bytes_accessed=w.size * 2 + t * d * 6, transcendentals=t * v * 2
        ),
    )(counts, final, w, target)


def tail_kernel(
    tiny_ref, lefts_ref, n1_ref, ga_ref, w_ref, extra_lefts_ref, mc_ref, encoded_ref, gac_ref, final_ref, n_all, g_all,
    feed_ref, attn_ref, extra_ref, total_ref,
    tinies, n_buf, g_buf, *rest,
):
    attn_bufs, extra_bufs = rest[:9], rest[9:18]
    tiny_send, tiny_recv, rs_send, rs_recv, pair_sem = rest[18:]
    section = lax.axis_index("section")
    me = lax.axis_index("rows")
    z, y, c = me // 4, (me // 2) % 2, me % 2
    high = z // 2
    inner = (z + high) % 2
    is_enc, is_dec = section == 0, section == 1
    f = w_ref.shape[0] // 3
    d = w_ref.shape[1]
    core_peer, y_peer = me + 1 - 2 * c, me + 2 - 4 * y
    toward = me + 4 - 8 * high
    outward = me - 4 + 8 * high
    mesh_id = pl.DeviceIdType.MESH

    def remote(src, dst, send, recv, where):
        return pltpu.make_async_remote_copy(
            src_ref=src, dst_ref=dst, send_sem=send, recv_sem=recv,
            device_id=where, device_id_type=mesh_id,
        )

    def pair_copies(p):
        slot = p % 2
        return [
            pltpu.make_async_copy(whole.at[pl.ds(2 * p, 2)], buf.at[slot], pair_sem.at[k, slot])
            for k, (whole, buf) in enumerate([(n_all, n_buf), (g_all, g_buf)])
        ]

    for copy in pair_copies(0):
        copy.start()

    barrier = pltpu.get_barrier_semaphore()

    def greet(where):
        pl.semaphore_signal(barrier, inc=1, device_id=where, device_id_type=mesh_id)

    greet({"rows": core_peer})
    greet({"rows": y_peer})
    greet({"rows": toward})

    @pl.when(inner == 1)
    def _():
        greet({"rows": outward})

    pl.semaphore_wait(barrier, 3 + inner)

    def place_of(p):
        j, other = [(0, 0), (1, 0), (0, 1), (2, 0), (1, 1), (3, 0), (2, 1), (3, 1)][p]
        zz = [z, z + 1 - 2 * (z % 2), 2 - high, 3 - 3 * high][j]
        yy = y + other - 2 * other * y
        return zz, yy, other

    def tiny_copy(kind, p, s, where):
        src = tiny_ref if p == 0 else tinies.at[s]
        return remote(src, tinies.at[s], tiny_send.at[kind, p], tiny_recv.at[s], where)

    def each_tiny(p, act):
        zz, yy, other = place_of(p)
        s = 4 * zz + 2 * yy + c
        if other == 0:

            @pl.when((zz <= z) & (z < 3))
            def _():
                act(tiny_copy(0, p, s, {"rows": me + 4}))

            @pl.when((zz >= z) & (z > 0))
            def _():
                act(tiny_copy(1, p, s, {"rows": me - 4}))

            act(tiny_copy(2, p, s, {"rows": y_peer}))
        act(tiny_copy(3, p, s, {"rows": core_peer}))

    def tiny_arrive(p):
        zz, yy, _ = place_of(p)
        tiny_copy(0, p, 4 * zz + 2 * yy + c, {"rows": me}).wait_recv()
        each_tiny(p, lambda copy: copy.start())

    def blocks_of(pieces):
        return jnp.concatenate([piece.reshape(8, -1, d) for piece in pieces], axis=1)

    def attn_half(half):
        left = lefts_ref.at[half]
        k = lefts_ref.shape[1] // 4
        qkv = dot(left[: 3 * k, :], n1_ref[...])
        return blocks_of([qkv[:k], qkv[k : 2 * k], qkv[2 * k :], dot(left[3 * k :, :], ga_ref[...])])

    def extra_half(half):
        left = extra_lefts_ref.at[half]
        k = extra_lefts_ref.shape[1] // 5
        key_value = dot(left[k : 3 * k, :], encoded_ref[...])
        pad = extra_bufs[0].shape[2] - 5 * k // 8
        return blocks_of(
            [
                dot(left[:k, :], mc_ref[...]),
                key_value[:k],
                key_value[k:],
                dot(left[3 * k : 4 * k, :], gac_ref[...]),
                dot(left[4 * k :, :], final_ref[...]),
                jnp.zeros((8 * pad, d), f32),
            ]
        )

    far_out, far_in = 3 - 3 * high, 2 - high
    beside = (1 - inner) * (1 + high) + inner * 3 * high

    def summed(bufs, k, half_sums, result):
        part, from_core, four, from_y, from_far, from_near, from_cross, from_out, cross_out = bufs

        def hop(i, src, dst, where):
            return remote(src, dst, rs_send.at[k, i], rs_recv.at[k, i], {"rows": where})

        to_core = hop(0, part.at[0], from_core, core_peer)
        ys = [
            hop(1 + i, part.at[1, (1 - y) * 4 + at], from_y.at[at], y_peer)
            for i, at in enumerate([far_out, far_in, beside, z])
        ]
        fars = [hop(5 + i, four.at[at], from_far.at[i], toward) for i, at in enumerate([far_out, far_in])]
        near = hop(7, four.at[beside], from_near, toward)
        crosses = [hop(8 + i, four.at[at], from_cross.at[i], toward) for i, at in enumerate([far_out, far_in])]
        out = hop(10, cross_out, from_out, outward)

        def core_send():
            part[0] = half_sums(1 - c).astype(bf16)
            to_core.start()

        def core_add():
            own = half_sums(c)
            to_core.wait_recv()
            part[1] = (own + from_core[...].astype(f32)).astype(bf16)
            ys[0].start()
            ys[1].start()

        def rest():
            ys[2].start()
            ys[3].start()

        def add_y(i, at):
            ys[i].wait_recv()
            four[at] = (part[1, 4 * y + at].astype(f32) + from_y[at].astype(f32)).astype(bf16)

        def far(i):
            def stage():
                add_y(i, [far_out, far_in][i])
                pl.when(inner == 0)(fars[i].start)

            return stage

        def cross(i):
            def stage():
                @pl.when(inner == 1)
                def _():
                    at = [far_out, far_in][i]
                    fars[i].wait_recv()
                    four[at] = (four[at].astype(f32) + from_far[i].astype(f32)).astype(bf16)
                    crosses[i].start()

            return stage

        def home():
            add_y(2, beside)
            pl.when(inner == 0)(near.start)

        def own():
            add_y(3, z)

        def leave():
            @pl.when(inner == 1)
            def _():
                crosses[0].wait_recv()
                cross_out[...] = (four[beside].astype(f32) + from_cross[0].astype(f32)).astype(bf16)
                out.start()

        def last_inner():
            @pl.when(inner == 1)
            def _():
                crosses[1].wait_recv()
                near.wait_recv()
                result(four[z].astype(f32) + from_cross[1].astype(f32) + from_near[...].astype(f32))

        def last_outer():
            @pl.when(inner == 0)
            def _():
                out.wait_recv()
                result(four[z].astype(f32) + from_out[...].astype(f32))

        def settle():
            for copy in [to_core, *ys]:
                copy.wait_send()

            @pl.when(inner == 0)
            def _():
                for copy in [*fars, near]:
                    copy.wait_send()

            @pl.when(inner == 1)
            def _():
                for copy in [*crosses, out]:
                    copy.wait_send()

        return {
            "send": core_send, "add": core_add, "rest": rest, "0": far(0), "1": far(1), "2": cross(0), "3": cross(1),
            "4": home, "5": own, "6": leave, "7": last_inner, "8": last_outer, "settle": settle,
        }

    def attn_result(value):
        attn_ref[...] = value

    def extra_result(value):
        extra_ref[...] = value

    attn = summed(attn_bufs, 0, attn_half, attn_result)
    extra = summed(extra_bufs, 1, extra_half, extra_result)

    def of_dec(stage):
        pl.when(is_dec)(stage)

    def wgrad(p):
        if p < 7:
            for copy in pair_copies(p + 1):
                copy.start()
        for copy in pair_copies(p):
            copy.wait()
        n_rows = n_buf[p % 2].reshape(-1, d)
        g_rows = g_buf[p % 2].reshape(-1, d)
        gu = dot_last(w_ref[: 2 * f, :], n_rows)
        gh = dot_last(w_ref[2 * f :, :], g_rows)
        act, slope = gelu_parts(gu[:f])
        up = gu[f:]
        dg = (gh * up * slope).astype(bf16)
        du = (gh * act).astype(bf16)
        hid = (act * up).astype(bf16)
        from_n = dot(jnp.concatenate([dg, du], axis=0), n_rows)
        from_g = dot(hid, g_rows)
        if p == 0:
            feed_ref[: 2 * f, :] = from_n
            feed_ref[2 * f :, :] = from_g
        else:
            feed_ref[: 2 * f, :] += from_n
            feed_ref[2 * f :, :] += from_g

    def add_tinies():
        for p in range(8):
            zz, yy, _ = place_of(p)
            tiny_copy(0, p, 4 * zz + 2 * yy + 1 - c, {"rows": me}).wait_recv()
        total = tinies[0]
        for s in range(1, 16):
            total += tinies[s]
        total_ref[...] = total

    tinies[me] = tiny_ref[...]
    each_tiny(0, lambda copy: copy.start())
    attn["send"]()
    of_dec(extra["send"])
    attn["add"]()
    pl.when(is_enc)(attn["rest"])

    @pl.when(is_dec)
    def _():
        extra["add"]()
        attn["rest"]()
        extra["rest"]()

    for step in TAIL_STEPS:
        if step[0] == "w":
            wgrad(int(step[1]))
        elif step[0] == "t":
            tiny_arrive(int(step[1]))
        elif step[0] == "a":
            attn[step[1]]()
        elif step[0] == "x":
            of_dec(extra[step[1]])
        else:
            add_tinies()

    for p in range(8):
        each_tiny(p, lambda copy: copy.wait_send())
    attn["settle"]()
    of_dec(extra["settle"])


TAIL_STEPS = (
    ("a0", "w0", "a1", "t1", "t2", "w1", "a2", "x0", "t3", "t4", "a3", "w2", "x1", "w3", "x2", "a4", "t5", "t6", "w4")
    + ("a5", "x3", "a6", "a7", "w5", "x4", "a8", "t7", "w6", "x5", "x6", "sum", "w7", "x7", "x8")
)


def tail(tiny, lefts, n1, ga, w_own, extra_lefts, mc, encoded, gac, final, n_all, g_all):
    t, d = n1.shape
    rows = w_own.shape[0]
    per, more = lefts.shape[1] // 8, -(-extra_lefts.shape[1] // 8 // 16) * 16

    def sums(r):
        return [
            pltpu.VMEM(shape + (r, d), bf16)
            for shape in [(2, 8), (8,), (4,), (4,), (2,), (), (2,), (), ()]
        ]

    vm = pl.BlockSpec(memory_space=pltpu.VMEM)
    anywhere = pl.BlockSpec(memory_space=pl.ANY)
    return pl.pallas_call(
        tail_kernel,
        out_shape=(
            jax.ShapeDtypeStruct((rows, d), f32),
            jax.ShapeDtypeStruct((per, d), f32),
            jax.ShapeDtypeStruct((more, d), f32),
            jax.ShapeDtypeStruct(tiny.shape, f32),
        ),
        in_specs=[vm] * 10 + [anywhere] * 2,
        out_specs=(vm,) * 4,
        scratch_shapes=[
            pltpu.VMEM((16,) + tiny.shape, f32),
            pltpu.VMEM((2, 2, t, d), bf16),
            pltpu.VMEM((2, 2, t, d), bf16),
            *sums(per),
            *sums(more),
            pltpu.SemaphoreType.DMA((4, 8)),
            pltpu.SemaphoreType.DMA((16,)),
            pltpu.SemaphoreType.DMA((2, 11)),
            pltpu.SemaphoreType.DMA((2, 11)),
            pltpu.SemaphoreType.DMA((2, 2)),
        ],
        compiler_params=pltpu.CompilerParams(
            vmem_limit_bytes=60 * 1024 * 1024, collective_id=0, has_side_effects=True
        ),
        cost_estimate=pl.CostEstimate(
            flops=2 * t * 16 * d * rows * 2, bytes_accessed=16 * t * d * 4, transcendentals=16 * t * rows
        ),
    )(tiny, lefts, n1, ga, w_own, extra_lefts, mc, encoded, gac, final, n_all, g_all)


def front_kernel(
    length, cnt_ref, order_ref, x_ref, g_attn_ref, g_feed_ref, g_final_ref,
    attn_own, feed_own, half_own,
    attn_all, feed_all, extra_all,
    n1_ref, qkv_ref, mixed_ref, y1_ref, n2_ref, gu_ref, y2_ref, enc_ref, arrived_ref, sorted_ref,
    w_attn, w_feed, place, wide_buf, first_own, second_own, extra_own,
    send_sem, recv_sem, own_sem, load_sem, x_send, x_recv,
):
    section = lax.axis_index("section")
    me = lax.axis_index("rows")
    z, y, c = me // 4, (me // 2) % 2, me % 2
    core_peer, y_peer = me + 1 - 2 * c, me + 2 - 4 * y
    mesh_id = pl.DeviceIdType.MESH
    inner = mixed_ref.shape[1]
    f = feed_own.shape[0] // 3

    barrier = pltpu.get_barrier_semaphore()

    def greet(where):
        pl.semaphore_signal(barrier, inc=1, device_id=where, device_id_type=mesh_id)

    greet({"rows": core_peer})
    greet({"rows": y_peer})
    greet({"section": 1 - section})

    @pl.when(z > 0)
    def _():
        greet({"rows": me - 4})

    @pl.when(z < 3)
    def _():
        greet({"rows": me + 4})

    own_copies = [
        pltpu.make_async_copy(own, whole.at[me], own_sem.at[k])
        for k, (own, whole) in enumerate(
            [(attn_own, attn_all), (feed_own, feed_all), (extra_own, extra_all)]
        )
    ]
    load_half = pltpu.make_async_copy(half_own, second_own, own_sem.at[3])
    own_copies[0].start()
    own_copies[1].start()

    @pl.when(section == 1)
    def _():
        load_half.start()

    pl.semaphore_wait(barrier, 4 + (z + z // 2) % 2)

    def remote(src, dst, send, recv, where):
        return pltpu.make_async_remote_copy(
            src_ref=src, dst_ref=dst, send_sem=send, recv_sem=recv,
            device_id=where, device_id_type=mesh_id,
        )

    kinds = [pl.ds(k * f, f) for k in range(3)]
    cuts = [pl.ds(k * (extra_own.shape[0] // 2), extra_own.shape[0] // 2) for k in range(2)]
    parts = {
        "A": (0, attn_all, None, 2, attn_own),
        "G": (1, feed_all, kinds[0], 1, feed_own.at[kinds[0]]),
        "U": (2, feed_all, kinds[1], 1, feed_own.at[kinds[1]]),
        "O": (3, feed_all, kinds[2], 1, feed_own.at[kinds[2]]),
        "X": (4, extra_all, cuts[0], 1, extra_own.at[cuts[0]]),
        "Y": (5, extra_all, cuts[1], 2, extra_own.at[cuts[1]]),
    }

    def place_of(route, p):
        if route == 1:
            j, other = [(0, 0), (1, 0), (0, 1), (2, 0), (1, 1), (3, 0), (2, 1), (3, 1)][p]
        else:
            j, other = p // 2, p % 2
        zz = [z, z + 1 - 2 * (z % 2), 2 - z // 2, 3 - 3 * (z // 2)][j]
        yy = y + other - 2 * other * y
        return zz, yy, other

    def part_copy(name, kind, p, s, where):
        k, whole, rows, _, own = parts[name]
        dst = whole.at[s] if rows is None else whole.at[s, rows]
        return remote(own if p == 0 else dst, dst, send_sem.at[k, kind, p], recv_sem.at[k, s], where)

    def each_send(name, p, act, ways="zyc"):
        route = parts[name][3]
        zz, yy, other = place_of(route, p)
        s = 4 * zz + 2 * yy + c
        if "z" in ways and (route == 2 or other == 0):

            @pl.when((zz <= z) & (z < 3))
            def _():
                act(part_copy(name, 0, p, s, {"rows": me + 4}))

            @pl.when((zz >= z) & (z > 0))
            def _():
                act(part_copy(name, 1, p, s, {"rows": me - 4}))

        if "y" in ways and (p == 0 or (route == 1 and other == 0)):
            act(part_copy(name, 2, p, s, {"rows": y_peer}))
        if "c" in ways:
            act(part_copy(name, 3, p, s, {"rows": core_peer}))

    def begin(name, ways):
        each_send(name, 0, lambda copy: copy.start(), ways)

    def arrive(name, p):
        zz, yy, _ = place_of(parts[name][3], p)
        part_copy(name, 0, p, 4 * zz + 2 * yy + c, {"rows": me}).wait_recv()
        each_send(name, p, lambda copy: copy.start())

    def meet(name, p):
        zz, yy, _ = place_of(parts[name][3], p)
        part_copy(name, 0, p, 4 * zz + 2 * yy + 1 - c, {"rows": me}).wait_recv()

    def settle(name):
        for p in range(8):
            each_send(name, p, lambda copy: copy.wait_send())

    half_copy = remote(half_own, first_own, x_send.at[0], x_recv.at[0], {"section": 1 - section})
    enc_copy = remote(enc_ref, arrived_ref, x_send.at[1], x_recv.at[1], {"section": 1 - section})

    def project():
        for p in range(8):
            meet("A", p)
        own_copies[0].wait()
        load = pltpu.make_async_copy(attn_all, w_attn, load_sem.at[0])
        load.start()
        load.wait()
        wide_buf[...] = dot_last(n1_ref[...], w_attn[...].reshape(4 * inner, -1)).astype(bf16)
        qkv_ref[...] = dot(wide_buf[...], place[:, : 3 * inner]).astype(bf16)

    def mix(s):
        low = low_half(length)
        allowed = allowed_twice(cnt_ref, s, length)
        rows = slice(s * length, (s + 1) * length)
        for h in range(inner // PAIR):
            cols = [slice(j * inner + h * PAIR, j * inner + (h + 1) * PAIR) for j in range(3)]
            q2 = stack_pair(qkv_ref[rows, cols[0]], low)
            p = soft_pair(q2, qkv_ref[rows, cols[1]], allowed).astype(bf16)
            wide = jnp.concatenate([p[:length], p[length:]], axis=1)
            mixed_ref[rows, cols[0]] = dot(wide, stack_pair(qkv_ref[rows, cols[2]], low)).astype(bf16)

    def mix_out():
        for s in range(x_ref.shape[0] // length // 2, x_ref.shape[0] // length):
            mix(s)
        wide_buf[...] = dot_last(mixed_ref[...], place[:, 3 * inner :]).astype(bf16)
        y1_ref[...] = x_ref[...].astype(f32) + dot(wide_buf[...], w_attn[...].reshape(4 * inner, -1))
        y2_ref[...] = y1_ref[...]
        n2_ref[...] = (unit_rows(y1_ref[...])[1] * g_feed_ref[...]).astype(bf16)

    def mix_first():
        for s in range(x_ref.shape[0] // length // 2):
            mix(s)

    def feed(p):
        if p == 0:
            own_copies[1].wait()
        for name in "GUO":
            meet(name, p)
        zz, yy, _ = place_of(1, p)
        pair = 4 * zz + 2 * yy

        @pl.when(section == 0)
        def _():
            blocks = pltpu.make_async_copy(feed_all.at[pl.ds(pair, 2)], w_feed, load_sem.at[1])
            blocks.start()
            blocks.wait()
            for k in range(2):
                gu = dot_last(n2_ref[...], w_feed[k, : 2 * f, :])
                gu_ref[pair + k] = gu
                hidden = (gelu_parts(gu[:, :f])[0] * gu[:, f:]).astype(bf16)
                y2_ref[...] += dot(hidden, w_feed[k, 2 * f :, :])

    begin("A", "zyc")

    @pl.when(section == 0)
    def _():
        half_copy.start()

    begin("G", "zyc")

    @pl.when(section == 1)
    def _():
        load_half.wait()
        half_copy.wait_recv()
        extra_own[...] = jnp.concatenate([first_own[...], second_own[...]], axis=1)
        own_copies[2].start()
        begin("Y", "zyc")
        begin("X", "zyc")

    begin("U", "yc")
    begin("O", "yc")

    row = lax.broadcasted_iota(jnp.int32, place.shape, 0)
    place[...] = jnp.where(row == order_ref[...], 1.0, 0.0).astype(bf16)
    n1_ref[...] = (unit_rows(x_ref[...].astype(f32))[1] * g_attn_ref[...]).astype(bf16)

    tasks = {"c1": project, "c2": mix_first, "c3": mix_out}
    for step in FRONT_STEPS:
        if step in tasks:
            tasks[step]()
        elif step[0] == "f":
            feed(int(step[1]))
        elif step[0] == "o":
            begin(step[1], "z")
        elif step[0] == "X":

            @pl.when(section == 1)
            def _(p=int(step[1])):
                arrive("X", p)
                arrive("Y", p)

        else:
            arrive(step[0], int(step[1]))

    @pl.when(section == 0)
    def _():
        enc_ref[...] = (unit_rows(y2_ref[...])[1] * g_final_ref[...]).astype(bf16)
        enc_copy.start()

    for k in range(4):
        columns = slice(k * inner, (k + 1) * inner)
        w = w_attn[...].reshape(4 * inner, -1)
        sorted_ref[columns, :] = dot_rows(place[:, columns], w).astype(bf16)

    for name in "AGUO":
        settle(name)

    @pl.when(section == 1)
    def _():
        for name in "XY":
            for p in range(8):
                meet(name, p)
            settle(name)
        own_copies[2].wait()
        enc_copy.wait_recv()

    @pl.when(section == 0)
    def _():
        half_copy.wait_send()
        enc_copy.wait_send()


FRONT_STEPS = (
    ("A1", "oU", "G1", "A2", "A3", "oO", "A4", "O1", "U1", "G2", "U2", "O2", "A5", "A6", "X1", "X2", "G3", "A7")
    + ("c1", "O3", "G4", "O4", "U3", "c2", "U4", "c3", "f0", "O5", "f1", "U5", "U6", "G5", "O6", "X3", "X4", "X5")
    + ("X6", "O7", "f2", "f3", "G6", "f4", "f5", "U7", "f6", "X7", "G7", "f7")
)


def front(counts, order, x, gain_attn, gain_feed, gain_final, attn_own, feed_own, half_own, length):
    t, d = x.shape
    attn_rows, feed_rows = attn_own.shape[0], feed_own.shape[0]
    inner = attn_rows * 4
    vm = pl.BlockSpec(memory_space=pltpu.VMEM)
    anywhere = pl.BlockSpec(memory_space=pl.ANY)
    return pl.pallas_call(
        functools.partial(front_kernel, length),
        out_shape=(
            jax.ShapeDtypeStruct((16, attn_rows, d), bf16),
            jax.ShapeDtypeStruct((16, feed_rows, d), bf16),
            jax.ShapeDtypeStruct((16, half_own.shape[0], d), bf16),
            jax.ShapeDtypeStruct((t, d), bf16),
            jax.ShapeDtypeStruct((t, 3 * inner), bf16),
            jax.ShapeDtypeStruct((t, inner), bf16),
            jax.ShapeDtypeStruct((t, d), f32),
            jax.ShapeDtypeStruct((t, d), bf16),
            jax.ShapeDtypeStruct((16, t, feed_rows // 3 * 2), f32),
            jax.ShapeDtypeStruct((t, d), f32),
            jax.ShapeDtypeStruct((t, d), bf16),
            jax.ShapeDtypeStruct((t, d), bf16),
            jax.ShapeDtypeStruct((4 * inner, d), bf16),
        ),
        in_specs=[pl.BlockSpec(memory_space=pltpu.SMEM)] + [vm] * 5 + [anywhere] * 3,
        out_specs=(anywhere,) * 3 + (vm,) * 10,
        scratch_shapes=[
            pltpu.VMEM((16, attn_rows, d), bf16),
            pltpu.VMEM((2, feed_rows, d), bf16),
            pltpu.VMEM((4 * inner, 4 * inner), bf16),
            pltpu.VMEM((t, 4 * inner), bf16),
            pltpu.VMEM(half_own.shape, bf16),
            pltpu.VMEM(half_own.shape, bf16),
            pltpu.VMEM((half_own.shape[0], d), bf16),
            pltpu.SemaphoreType.DMA((6, 4, 8)),
            pltpu.SemaphoreType.DMA((6, 16)),
            pltpu.SemaphoreType.DMA((4,)),
            pltpu.SemaphoreType.DMA((2,)),
            pltpu.SemaphoreType.DMA((2,)),
            pltpu.SemaphoreType.DMA((2,)),
        ],
        compiler_params=pltpu.CompilerParams(
            vmem_limit_bytes=VMEM_BYTES, collective_id=1, has_side_effects=True
        ),
        cost_estimate=pl.CostEstimate(
            flops=2 * t * d * (feed_rows * 16 + 8 * inner),
            bytes_accessed=2 * 16 * (attn_rows + feed_rows) * d * 2,
            transcendentals=t * feed_rows * 6,
        ),
    )(counts, order, x, gain_attn, gain_feed, gain_final, attn_own, feed_own, half_own)


def mid_kernel(
    length, cross_cnt, self_cnt, dec_cnt, x_ref, y1_ref, y2_in, n2_in, qkv_ref, mixed_ref, encoded_ref,
    target_ref, gain_ref, order_ref, gu_in, attn_w, extra_w, feed_w,
    n_all, g_all, gf_ref, ga_ref, gx_ref, sums_ref, mc_ref, gac_ref, final_ref, lefts_ref, extra_lefts_ref,
    slots, gu_buf, w_att, w_head, mid, y2, acc, n2, cqkv, do_buf, grad_enc,
    dqkv_ref, dcqkv_ref, cmixed_ref, gl_ref,
    send_sem, recv_sem, slot_sem, load_sem, own_sem, x_send, x_recv,
):
    section = lax.axis_index("section")
    me = lax.axis_index("rows")
    z, y, c = me // 4, (me // 2) % 2, me % 2
    core_peer, y_peer = me + 1 - 2 * c, me + 2 - 4 * y
    mesh_id = pl.DeviceIdType.MESH
    inner = w_att.shape[0] // 4
    f = feed_w.shape[1] // 3
    t = n2.shape[0]
    held = slots.shape[0]
    spare = BLOCKS - held
    is_enc, is_dec = section == 0, section == 1

    def load(b):
        k = b % held
        return pltpu.make_async_copy(feed_w.at[b], slots.at[k], slot_sem.at[k])

    load_attn = pltpu.make_async_copy(attn_w, w_att, load_sem.at[0])
    load_cross = pltpu.make_async_copy(extra_w.at[pl.ds(0, 4 * inner)], w_att, load_sem.at[1])
    load_head = pltpu.make_async_copy(extra_w.at[pl.ds(4 * inner, inner)], w_head, load_sem.at[2])
    load_gu = pltpu.make_async_copy(gu_in, gu_buf, load_sem.at[3])

    def start_loads(first):
        def step(k, carry):
            load(first + k).start()
            return carry

        lax.fori_loop(0, held, step, 0)

    @pl.when(is_enc)
    def _():
        start_loads(spare)
        load_gu.start()
        load_attn.start()

    @pl.when(is_dec)
    def _():
        load_cross.start()
        start_loads(0)
        load_head.start()

    barrier = pltpu.get_barrier_semaphore()

    def greet(where):
        pl.semaphore_signal(barrier, inc=1, device_id=where, device_id_type=mesh_id)

    greet({"rows": core_peer})
    greet({"rows": y_peer})
    greet({"section": 1 - section})

    @pl.when(z > 0)
    def _():
        greet({"rows": me - 4})

    @pl.when(z < 3)
    def _():
        greet({"rows": me + 4})

    pl.semaphore_wait(barrier, 4 + (z + z // 2) % 2)

    def remote(src, dst, send, recv, where):
        return pltpu.make_async_remote_copy(
            src_ref=src, dst_ref=dst, send_sem=send, recv_sem=recv,
            device_id=where, device_id_type=mesh_id,
        )

    cut = t * 13 // 256 * 16
    upper, lower = pl.ds(0, cut), pl.ds(cut, t - cut)
    parts = {
        "S": (0, upper, 1, n2, n_all),
        "Q": (1, lower, 2, n2, n_all),
        "V": (2, upper, 1, gf_ref, g_all),
        "W": (3, lower, 2, gf_ref, g_all),
    }

    def place_of(route, p):
        if route == 1:
            j, other = [(0, 0), (1, 0), (0, 1), (2, 0), (1, 1), (3, 0), (2, 1), (3, 1)][p]
        else:
            j, other = p // 2, p % 2
        zz = [z, z + 1 - 2 * (z % 2), 2 - z // 2, 3 - 3 * (z // 2)][j]
        yy = y + other - 2 * other * y
        return zz, yy, other

    def part_copy(name, kind, p, s, where):
        k, rows, _, own, whole = parts[name]
        dst = whole.at[s, rows]
        src = own.at[rows] if p == 0 else dst
        return remote(src, dst, send_sem.at[k, kind, p], recv_sem.at[k, s], where)

    def each_send(name, p, act):
        route = parts[name][2]
        zz, yy, other = place_of(route, p)
        s = 4 * zz + 2 * yy + c
        if route == 2 or other == 0:

            @pl.when((zz <= z) & (z < 3))
            def _():
                act(part_copy(name, 0, p, s, {"rows": me + 4}))

            @pl.when((zz >= z) & (z > 0))
            def _():
                act(part_copy(name, 1, p, s, {"rows": me - 4}))

        if p == 0 or (route == 1 and other == 0):
            act(part_copy(name, 2, p, s, {"rows": y_peer}))
        act(part_copy(name, 3, p, s, {"rows": core_peer}))

    own_copies = {
        "S": pltpu.make_async_copy(n2, n_all.at[me], own_sem.at[0]),
        "V": pltpu.make_async_copy(gf_ref, g_all.at[me], own_sem.at[1]),
    }

    def begin(names):
        own_copies[names[1]].start()
        for name in names:
            each_send(name, 0, lambda copy: copy.start())

    def arrive(*steps):
        for step in steps:
            name, p = step[0], int(step[1])
            zz, yy, _ = place_of(parts[name][2], p)
            part_copy(name, 0, p, 4 * zz + 2 * yy + c, {"rows": me}).wait_recv()
            each_send(name, p, lambda copy: copy.start())

    back_copy = remote(grad_enc, grad_enc, x_send.at[0], x_recv.at[0], {"section": 1 - section})

    group = 4

    def feed_forward(first, count):
        def step(i, carry):
            blocks = [first + group * i + k for k in range(group)]
            rows = [slots.at[b % held] for b in blocks]
            for b in blocks:
                load(b).wait()
            hidden = []
            for b, w in zip(blocks, rows):
                gu = dot_last(n2[...], w[: 2 * f, :])
                gu_buf[b] = gu
                hidden.append((gelu_parts(gu[:, :f])[0] * gu[:, f:]).astype(bf16))
            total = None
            for k in range(0, group, 2):
                left = jnp.concatenate(hidden[k : k + 2], axis=1)
                right = jnp.concatenate([w[2 * f :, :] for w in rows[k : k + 2]], axis=0)
                term = dot(left, right)
                total = term if total is None else total + term
            y2[...] += total
            for b in blocks:

                @pl.when(b < spare)
                def _(b=b):
                    load(b + held).start()

            return carry

        lax.fori_loop(0, count // group, step, 0)

    def feed_backward(first, count, fresh):
        def step(i, carry):
            blocks = [BLOCKS - 1 - first - group * i - k for k in range(group)]
            rows = [slots.at[b % held] for b in blocks]
            for b in blocks:

                @pl.when((b < spare) | fresh)
                def _(b=b):
                    load(b).wait()

            lefts = []
            for b, w in zip(blocks, rows):
                gh = dot_last(gf_ref[...], w[2 * f :, :])
                gu = gu_buf[b]
                act, slope = gelu_parts(gu[:, :f])
                dg = (gh * gu[:, f:] * slope).astype(bf16)
                lefts.append(jnp.concatenate([dg, (gh * act).astype(bf16)], axis=1))
            total = None
            for left, w in zip(lefts, rows):
                term = dot(left, w[: 2 * f, :])
                total = term if total is None else total + term
            acc[...] += total
            for b in blocks:

                @pl.when(b >= held)
                def _(b=b):
                    load(b - held).start()

            return carry

        lax.fori_loop(0, count // group, step, 0)

    def final_backward(up):
        back, sums_ref[2:3, :] = norm_back(y2[...], gain_ref[2:3, :], up)
        gx_ref[...] = back
        gf_ref[...] = back.astype(bf16)
        begin("WV")
        acc[...] = jnp.zeros_like(acc)

    def feed_end():
        back, sums_ref[1:2, :] = norm_back(mid[...], gain_ref[1:2, :], acc[...])
        acc[...] = gx_ref[...] + back

    sums_ref[...] = jnp.zeros_like(sums_ref)

    @pl.when(is_enc)
    def _():
        n2[...] = n2_in[...]
        begin("QS")
        mid[...] = y1_ref[...]
        y2[...] = y2_in[...]
        arrive("Q1", "Q2", "S2", "S1", "Q3", "Q4", "S4", "S3", "Q5", "Q6")
        back_copy.wait_recv()
        final_backward(grad_enc[...].astype(f32))
        load_gu.wait()
        arrive("S6")
        feed_backward(0, 8, True)
        arrive("S5", "Q7")
        feed_backward(8, 8, True)
        feed_end()
        arrive("W1", "W2")
        load_attn.wait()

    @pl.when(is_dec)
    def _():
        y1 = y1_ref[...]
        mc_ref[...] = (unit_rows(y1)[1] * gain_ref[3:4, :]).astype(bf16)
        load_cross.wait()
        cqkv[:, :inner] = dot_last(mc_ref[...], w_att[:inner, :]).astype(bf16)
        cqkv[:, inner:] = dot_last(encoded_ref[...], w_att[inner : 3 * inner, :]).astype(bf16)
        heads_fwd(cross_cnt, cqkv, cmixed_ref, length)
        mid[...] = y1_ref[...] + dot(cmixed_ref[...], w_att[3 * inner :, :])
        y2[...] = mid[...]
        n2[...] = (unit_rows(mid[...])[1] * gain_ref[1:2, :]).astype(bf16)
        begin("QS")
        feed_forward(0, 12)
        arrive("Q1", "Q2")
        feed_forward(12, 4)
        final_ref[...] = (unit_rows(y2[...])[1] * gain_ref[2:3, :]).astype(bf16)
        load_head.wait()
        loss = loss_back(dec_cnt, final_ref, w_head, target_ref, gl_ref, length)
        sums_ref[4:5, :] = jnp.broadcast_to(loss, (1, sums_ref.shape[1]))
        final_backward(dot(gl_ref[...], w_head[...]))
        feed_backward(0, 8, False)
        arrive("S2", "S1")
        feed_backward(8, 8, False)
        feed_end()
        arrive("W1", "Q3")
        gac_ref[...] = acc[...].astype(bf16)
        do_buf[...] = dot_last(gac_ref[...], w_att[3 * inner :, :]).astype(bf16)
        heads_bwd(cross_cnt, cqkv, do_buf, dcqkv_ref, length)
        grad_enc[...] = dot(dcqkv_ref[:, inner:], w_att[inner : 3 * inner, :]).astype(bf16)
        back_copy.start()
        up = dot(dcqkv_ref[:, :inner], w_att[:inner, :])
        load_attn.start()
        back, sums_ref[3:4, :] = norm_back(y1_ref[...], gain_ref[3:4, :], up)
        acc[...] += back
        arrive("Q4", "W2")
        load_attn.wait()

    ga_ref[...] = acc[...].astype(bf16)
    do_buf[...] = dot_last(ga_ref[...], w_att[3 * inner :, :]).astype(bf16)
    heads_bwd(self_cnt, qkv_ref, do_buf, dqkv_ref, length)
    up = dot(dqkv_ref[...], w_att[: 3 * inner, :])
    back, sums_ref[0:1, :] = norm_back(x_ref[...].astype(f32), gain_ref[0:1, :], up)
    gx_ref[...] = acc[...] + back

    def arrange(sources, out_ref, lo, hi):
        chunk = inner // 2
        for k in range(lo, hi):
            source, at = sources[k]
            col = lax.broadcasted_iota(jnp.int32, (inner, inner), 1)
            pick = jnp.where(order_ref[...] == col, 1.0, 0.0).astype(bf16)
            both = dot_last(pick, source[:, at * inner : (at + 1) * inner]).astype(bf16)
            for half in range(2):
                out_ref[half, k * chunk : (k + 1) * chunk, :] = both[half * chunk : (half + 1) * chunk]

    arrange([(dqkv_ref, 0), (dqkv_ref, 1), (dqkv_ref, 2), (mixed_ref, 0)], lefts_ref, 0, 4)

    @pl.when(is_dec)
    def _():
        arrive("V2", "V1", "S4")
        sources = [(dcqkv_ref, 0), (dcqkv_ref, 1), (dcqkv_ref, 2), (cmixed_ref, 0), (gl_ref, 0)]
        arrange(sources, extra_lefts_ref, 0, 5)

    @pl.when(is_enc)
    def _():
        arrive("V2", "V1", "W4", "W3", "S7", "V3", "W6", "V4", "W5", "V6", "V5", "W7", "V7")

    @pl.when(is_dec)
    def _():
        arrive("S3", "W3", "Q5", "V4", "Q6", "W4", "S6")
        arrive("V3", "S5", "V6", "W5", "Q7", "W6", "S7", "V5", "W7", "V7")

    for name in parts:
        for p in range(8):
            zz, yy, _ = place_of(parts[name][2], p)
            part_copy(name, 0, p, 4 * zz + 2 * yy + 1 - c, {"rows": me}).wait_recv()
            each_send(name, p, lambda copy: copy.wait_send())
    own_copies["S"].wait()
    own_copies["V"].wait()

    @pl.when(is_dec)
    def _():
        back_copy.wait_send()


def middle(cross_cnt, self_cnt, dec_cnt, x, y1, y2, n2, qkv, mixed, encoded, target, gains, order, gu, attn_w, extra_w, feed_w, length):
    t, d = x.shape
    inner = attn_w.shape[0] // 4
    held = 8
    vm = pl.BlockSpec(memory_space=pltpu.VMEM)
    sm = pl.BlockSpec(memory_space=pltpu.SMEM)
    anywhere = pl.BlockSpec(memory_space=pl.ANY)
    half = jax.ShapeDtypeStruct((t, d), bf16)
    return pl.pallas_call(
        functools.partial(mid_kernel, length),
        out_shape=(
            jax.ShapeDtypeStruct((16, t, d), bf16),
            jax.ShapeDtypeStruct((16, t, d), bf16),
            half, half,
            jax.ShapeDtypeStruct((t, d), f32),
            jax.ShapeDtypeStruct((8, d), f32),
            half, half, half,
            jax.ShapeDtypeStruct((2, 2 * inner, t), bf16),
            jax.ShapeDtypeStruct((2, 5 * inner // 2, t), bf16),
        ),
        in_specs=[sm] * 3 + [vm] * 10 + [anywhere] * 4,
        out_specs=(anywhere,) * 2 + (vm,) * 9,
        scratch_shapes=[
            pltpu.VMEM((held,) + feed_w.shape[1:], bf16),
            pltpu.VMEM(gu.shape, f32),
            pltpu.VMEM(attn_w.shape, bf16),
            pltpu.VMEM((inner, d), bf16),
            pltpu.VMEM((t, d), f32),
            pltpu.VMEM((t, d), f32),
            pltpu.VMEM((t, d), f32),
            pltpu.VMEM((t, d), bf16),
            pltpu.VMEM((t, 3 * inner), bf16),
            pltpu.VMEM((t, inner), bf16),
            pltpu.VMEM((t, d), bf16),
            pltpu.VMEM((t, 3 * inner), bf16),
            pltpu.VMEM((t, 3 * inner), bf16),
            pltpu.VMEM((t, inner), bf16),
            pltpu.VMEM((t, inner), bf16),
            pltpu.SemaphoreType.DMA((4, 4, 8)),
            pltpu.SemaphoreType.DMA((4, 16)),
            pltpu.SemaphoreType.DMA((held,)),
            pltpu.SemaphoreType.DMA((4,)),
            pltpu.SemaphoreType.DMA((2,)),
            pltpu.SemaphoreType.DMA((1,)),
            pltpu.SemaphoreType.DMA((1,)),
        ],
        compiler_params=pltpu.CompilerParams(
            vmem_limit_bytes=62 * 1024 * 1024, collective_id=2, has_side_effects=True
        ),
        cost_estimate=pl.CostEstimate(
            flops=4 * t * feed_w.size, bytes_accessed=2 * feed_w.size + 8 * gu.size, transcendentals=2 * gu.size
        ),
    )(cross_cnt, self_cnt, dec_cnt, x, y1, y2, n2, qkv, mixed, encoded, target, gains, order, gu, attn_w, extra_w, feed_w)


def adam_step(weight, first_moment, second_moment, gradient, step_rate, weight_decay):
    first_new = 0.9 * first_moment + 0.1 * gradient
    second_new = 0.999 * second_moment + 0.001 * gradient * gradient
    first_fix = 1.0 - 0.9**STEP
    second_fix = 1.0 - 0.999**STEP
    update = first_new / first_fix / (jnp.sqrt(second_new / second_fix) + 1e-08)
    return (first_new, second_new, weight - step_rate * (update + weight_decay * weight))


def kinds_first(gathered, n, kinds, per):
    d = gathered.shape[-1]
    return gathered.reshape(n, kinds, per, d).transpose(1, 0, 2, 3).reshape(kinds * n * per, d)


def owners_first(left, right, n):
    t, k, units = left.shape
    grad = jnp.einsum("tku,td->kud", left, right, preferred_element_type=f32)
    return grad.reshape(k, n, units // n, -1).transpose(1, 0, 2, 3)


def local(
    block_input,
    lengths,
    targets,
    attention_weight,
    attention_first,
    attention_second,
    feed_weight,
    feed_first,
    feed_second,
    norm_gain,
    gain_first,
    gain_second,
    cross_weight,
    cross_first,
    cross_second,
    head_weight,
    head_first,
    head_second,
    cross_gain,
    cross_gain_first,
    cross_gain_second,
):
    n = lax.axis_size("rows")
    is_encoder = lax.axis_index("section") == 0
    micro, length, d = block_input.shape[1:]
    t = micro * length
    per = attention_weight.shape[1]
    f = feed_weight.shape[1]
    inner = per * n

    attn_own = attention_weight[0].astype(bf16).transpose(1, 0, 2).reshape(4 * per, d)
    feed_own = feed_weight[0].astype(bf16).transpose(1, 0, 2)
    half_rows = jnp.concatenate(
        [cross_weight.astype(bf16).transpose(1, 0, 2), head_weight.astype(bf16)[None]], axis=0
    )

    gains = norm_gain[0]
    gain_attn, gain_feed, gain_final = gains[0:1], gains[1:2], gains[2:3]
    gain_cross = cross_gain[None]
    x = block_input[0].reshape(t, d)
    enc_counts = lengths[0, :, 0]
    dec_counts = lengths[1, :, 0]
    zero_one = jnp.zeros((1,), jnp.int32)
    self_counts = jnp.concatenate([jnp.where(is_encoder, 0, 1).astype(jnp.int32)[None], enc_counts])
    cross_counts = jnp.concatenate([zero_one, enc_counts])
    target_column = targets.reshape(t, 1)

    def blank(maker):
        return jax.tree.map(lambda a: jnp.zeros(a.shape, a.dtype), jax.eval_shape(maker))

    emit = n != BLOCKS
    if emit:
        attn_all = lax.all_gather(attn_own, "rows", axis=0, tiled=True)
        attn_w = kinds_first(attn_all, n, 4, per)
        feed_all = lax.all_gather(feed_own.reshape(3 * f, d), "rows", axis=0, tiled=True)
        feed_w = kinds_first(feed_all, n, 3, f).reshape(3, BLOCKS, -1, d)
        feed_w = feed_w.transpose(1, 0, 2, 3).reshape(BLOCKS, -1, d)
        other_half = lax.ppermute(half_rows, "section", [(0, 1)])
        extra_own = jnp.concatenate([other_half, half_rows], axis=-1).reshape(5 * per, d)
        extra_all = lax.all_gather(extra_own, "rows", axis=0, tiled=True)
        n1, qkv, mixed, y1 = attend_fwd(self_counts, x, gain_attn, attn_w, length)

        def enc_feed():
            return feed_fwd(y1, gain_feed, gain_final, feed_w)

        enc_state = lax.cond(is_encoder, enc_feed, lambda: blank(enc_feed))
        encoded = lax.ppermute(enc_state[3], "section", [(0, 1)])
    else:
        units = jnp.arange(4 * inner, dtype=jnp.int32).reshape(n, 4, per)
        order = units.transpose(1, 0, 2).reshape(1, 4 * inner)
        units = jnp.arange(inner, dtype=jnp.int32).reshape(4, 2, 2, per)
        travel = units.transpose(2, 1, 0, 3).reshape(inner, 1)
        pad = -(5 * per) % 16
        half_own = jnp.pad(half_rows.reshape(5 * per, d // 2), ((0, pad), (0, 0)))
        outs = front(
            self_counts, order, x, gain_attn, gain_feed, gain_final,
            attn_own, feed_own.reshape(3 * f, d), half_own, length,
        )
        _, feed_w, extra_all, n1, qkv, mixed, y1 = outs[:7]
        enc_state, encoded, attn_w = outs[7:11], outs[11], outs[12]
        extra_all = extra_all[:, : 5 * per]
    extra_w = kinds_first(extra_all, n, 5, per)
    cross_w, head_w = extra_w[: 4 * inner], extra_w[4 * inner :]

    if emit:
        def dec_front():
            mc, cqkv, cmixed, z2 = attend_fwd(cross_counts, y1, gain_cross, cross_w, length, encoded)
            return feed_fwd(z2, gain_feed, gain_final, feed_w) + (mc, cqkv, cmixed, z2)

        def enc_pass():
            rest = jax.eval_shape(dec_front)[4:7]
            return tuple(enc_state) + tuple(jnp.zeros(a.shape, a.dtype) for a in rest) + (y1,)

        n2, gu, y2, final, mc, cqkv, cmixed, mid = lax.cond(is_encoder, enc_pass, dec_front)
        def dec_back():
            gl, up, loss = head_loss(dec_counts, final, head_w, target_column, length)
            feed_out = feed_bwd(up, mid, y2, gain_feed, gain_final, gu, feed_w, emit)
            ga_c, dqkv_c, gy1, gg_c, ge = attend_bwd(
                cross_counts, y1, gain_cross, feed_out[1], cqkv, cross_w, length, True
            )
            return (ge, gy1, feed_out[2], feed_out[0], *feed_out[3:], gl, ga_c, dqkv_c, gg_c, loss)

        back = lax.cond(is_encoder, lambda: blank(dec_back), dec_back)
        returned = lax.ppermute(back[0], "section", [(1, 0)])
        at = 6 if emit else 4
        gl, ga_c, dqkv_c, gg_c, loss = back[at:]

        def enc_back():
            feed_out = feed_bwd(returned, mid, y2, gain_feed, gain_final, gu, feed_w, emit)
            return (feed_out[1], feed_out[2], feed_out[0], *feed_out[3:])

        backs = lax.cond(is_encoder, enc_back, lambda: tuple(back[1:at]))
        gy1, gg_feed, gf = backs[:3]

        ga, dqkv, gx, gg_attn = attend_bwd(self_counts, x, gain_attn, gy1, qkv, attn_w, length)
        tiny = jnp.concatenate(
            [gg_attn, gg_feed, gg_c, jnp.broadcast_to(loss, (1, d)), jnp.zeros((3, d), f32)], axis=0
        )
    else:
        gain_rows = jnp.concatenate([gains, gain_cross], axis=0)
        n2, gu, y2 = enc_state[:3]
        (
            n2_all, gf_all, _, ga, gx, tiny, mc, ga_c, final, lefts, extra_lefts,
        ) = middle(
            cross_counts, self_counts, dec_counts, x, y1, y2, n2, qkv, mixed, encoded, target_column,
            gain_rows, travel, gu, attn_w, extra_w, feed_w, length,
        )

    half = d // 2
    if emit:
        extra_part = jnp.concatenate(
            [
                owners_first(dqkv_c[:, None, :inner], mc, n),
                owners_first(dqkv_c[:, inner:].reshape(t, 2, inner), encoded, n),
                owners_first(cmixed[:, None], ga_c, n),
                owners_first(gl[:, None], final, n),
            ],
            axis=1,
        ).astype(bf16)
        extra_sum = lax.psum_scatter(
            extra_part.reshape(n * 5 * per, d), "rows", scatter_dimension=0, tiled=True
        )
        attn_part = jnp.concatenate(
            [
                owners_first(dqkv.reshape(t, 3, inner), n1, n),
                owners_first(mixed[:, None], ga, n),
            ],
            axis=1,
        ).astype(bf16)
        attn_sum = lax.psum_scatter(
            attn_part.reshape(n * 4 * per, d), "rows", scatter_dimension=0, tiled=True
        ).astype(f32)
        dgu, hid = backs[3], backs[4]
        nb, _, fb = hid.shape
        left = dgu.reshape(nb, t, 2, fb).transpose(1, 2, 0, 3).reshape(t, 2, nb * fb)
        hid = hid.transpose(1, 0, 2).reshape(t, 1, nb * fb)
        feed_part = jnp.concatenate(
            [owners_first(left, n2, n), owners_first(hid, gf, n)], axis=1
        ).astype(bf16)
        feed_grad = lax.psum_scatter(
            feed_part.reshape(n * 3 * f, d), "rows", scatter_dimension=0, tiled=True
        ).astype(f32)
        tiny_sum = jnp.sum(lax.all_gather(tiny, "rows", axis=0), axis=0)
    else:
        feed_grad, attn_sum, extra_sum, tiny_sum = tail(
            tiny, lefts, n1, ga, feed_own.reshape(3 * f, d), extra_lefts, mc, encoded, ga_c, final, n2_all, gf_all
        )
        extra_sum = extra_sum[: 5 * per]
    extra_first = lax.ppermute(extra_sum[:, :half].astype(bf16), "section", [(1, 0)])
    extra_grad = jnp.where(is_encoder, extra_first.astype(f32), extra_sum[:, half:].astype(f32))
    extra_grad = extra_grad.reshape(5, per, half)
    tiny_dec = lax.ppermute(tiny_sum[3:5], "section", [(1, 0)])
    tiny_dec = jnp.where(is_encoder, tiny_dec, tiny_sum[3:5])
    attn_grad = attn_sum.reshape(4, per, d).transpose(1, 0, 2)
    feed_grad = feed_grad.reshape(3, f, d).transpose(1, 0, 2)
    cross_gain_total = tiny_dec[0]
    loss_total = tiny_dec[1, 0]

    attention_new = adam_step(
        attention_weight, attention_first, attention_second, attn_grad[None], 0.05, 0.1
    )
    feed_new = adam_step(feed_weight, feed_first, feed_second, feed_grad[None], 0.05, 0.1)
    gain_new = adam_step(norm_gain, gain_first, gain_second, tiny_sum[None, 0:3], 0.5, 0.0)
    cross_new = adam_step(
        cross_weight, cross_first, cross_second, extra_grad[:4].transpose(1, 0, 2), 0.05, 0.1
    )
    head_new = adam_step(head_weight, head_first, head_second, extra_grad[4], 0.05, 0.1)
    cross_gain_new = adam_step(
        cross_gain, cross_gain_first, cross_gain_second, cross_gain_total, 0.5, 0.0
    )
    return (
        gx.reshape(1, micro, length, d),
        loss_total,
        *attention_new,
        *feed_new,
        *gain_new,
        *cross_new,
        *head_new,
        *cross_gain_new,
    )


def solution(mesh):
    by_row = P("section", "rows", None, None)
    gain = P("section", None, None)
    cross = P("rows", None, "section")
    head = P("rows", "section")
    weights = (by_row,) * 6 + (gain,) * 3 + (cross,) * 3 + (head,) * 3 + (P(),) * 3
    tokens = P("section", None, "rows", None)
    return jax.shard_map(
        local,
        mesh=mesh,
        in_specs=(tokens, P(None, None, "rows"), P(None, "rows")) + weights,
        out_specs=(tokens, P()) + weights,
        check_vma=False,
    )
```

```python
import functools

import jax
import jax.numpy as jnp
from jax import lax
from jax.experimental import pallas as pl
from jax.experimental.pallas import tpu as pltpu
from jax.sharding import PartitionSpec as P

HD = 64
STEP = 10
PAIR = 2 * HD
BLOCKS = 16
VMEM_BYTES = 52 * 1024 * 1024

bf16 = jnp.bfloat16
f32 = jnp.float32
masked_value = -1000000000.0
scale = HD ** (-0.5)


def dot(a, b):
    return lax.dot_general(a, b, (((1,), (0,)), ((), ())), preferred_element_type=f32)


def dot_last(a, b):
    return lax.dot_general(a, b, (((1,), (1,)), ((), ())), preferred_element_type=f32)


def dot_rows(a, b):
    return lax.dot_general(a, b, (((0,), (0,)), ((), ())), preferred_element_type=f32)


def unit_rows(v):
    r = lax.rsqrt(jnp.mean(v * v, axis=-1, keepdims=True) + 1e-06)
    return r, v * r


def norm_back(v, gain, up):
    r, n = unit_rows(v)
    g = up * gain
    back = r * (g - n * jnp.mean(g * n, axis=-1, keepdims=True))
    return back, jnp.sum(up * n, axis=0, keepdims=True)


def gelu_parts(x):
    c = 0.7978845608028654
    t = jnp.tanh(c * (x + 0.044715 * (x * x * x)))
    act = 0.5 * x * (1.0 + t)
    slope = 0.5 * (1.0 + t) + 0.5 * x * (1.0 - t * t) * (c * (1.0 + 3.0 * 0.044715 * (x * x)))
    return act, slope


def low_half(length):
    return lax.broadcasted_iota(jnp.int32, (length, PAIR), 1) < HD


def stack_pair(m, low):
    zero = jnp.zeros_like(m)
    return jnp.concatenate([jnp.where(low, m, zero), jnp.where(low, zero, m)], axis=0)


def allowed_twice(cnt_ref, s, length):
    row = lax.broadcasted_iota(jnp.int32, (length, length), 0)
    col = lax.broadcasted_iota(jnp.int32, (length, length), 1)
    limit = jnp.where(cnt_ref[0] == 1, row + 1, cnt_ref[1 + s])
    one = jnp.where(col < limit, 1, 0)
    return jnp.concatenate([one, one], axis=0) == 1


def soft_pair(q2, k, allowed):
    s = dot_last(q2, k) * scale
    s = jnp.where(allowed, s, masked_value)
    e = jnp.exp(s - jnp.max(s, axis=-1, keepdims=True))
    return e / jnp.sum(e, axis=-1, keepdims=True)


def head_columns(inner, h):
    return [slice(j * inner + h * PAIR, j * inner + (h + 1) * PAIR) for j in range(3)]


def heads_fwd(cnt_ref, qkv_ref, o_ref, length):
    t, inner = o_ref.shape
    low = low_half(length)
    for s in range(t // length):
        allowed = allowed_twice(cnt_ref, s, length)
        rows = slice(s * length, (s + 1) * length)
        for h in range(inner // PAIR):
            cols = head_columns(inner, h)
            q2 = stack_pair(qkv_ref[rows, cols[0]], low)
            p = soft_pair(q2, qkv_ref[rows, cols[1]], allowed).astype(bf16)
            wide = jnp.concatenate([p[:length], p[length:]], axis=1)
            o_ref[rows, cols[0]] = dot(wide, stack_pair(qkv_ref[rows, cols[2]], low)).astype(bf16)


def heads_bwd(cnt_ref, qkv_ref, do_ref, dqkv_ref, length):
    t, inner = do_ref.shape
    low = low_half(length)
    for s in range(t // length):
        allowed = allowed_twice(cnt_ref, s, length)
        rows = slice(s * length, (s + 1) * length)
        for h in range(inner // PAIR):
            cols = head_columns(inner, h)
            q2 = stack_pair(qkv_ref[rows, cols[0]], low)
            k = qkv_ref[rows, cols[1]]
            p = soft_pair(q2, k, allowed)
            do2 = stack_pair(do_ref[rows, cols[0]], low)
            dp = dot_last(do2, qkv_ref[rows, cols[2]])
            ds = p * (dp - jnp.sum(dp * p, axis=-1, keepdims=True))
            ds = jnp.where(allowed, ds, 0.0).astype(bf16)
            wide = jnp.concatenate([ds[:length], ds[length:]], axis=1)
            dqkv_ref[rows, cols[0]] = (dot(wide, stack_pair(k, low)) * scale).astype(bf16)
            dqkv_ref[rows, cols[1]] = (dot_rows(ds, q2) * scale).astype(bf16)
            dqkv_ref[rows, cols[2]] = dot_rows(p.astype(bf16), do2).astype(bf16)


def loss_back(cnt_ref, f_ref, w_ref, target_ref, gl_ref, length):
    logits = dot_last(f_ref[...], w_ref[...])
    top = jnp.max(logits, axis=-1, keepdims=True)
    log_total = top + jnp.log(jnp.sum(jnp.exp(logits - top), axis=-1, keepdims=True))
    hit = lax.broadcasted_iota(jnp.int32, logits.shape, 1) == target_ref[...]
    picked = jnp.sum(jnp.where(hit, logits, 0.0), axis=-1, keepdims=True)
    probs = jnp.exp(logits - log_total) - jnp.where(hit, 1.0, 0.0)
    total = jnp.zeros((1, 1), f32)
    for s in range(logits.shape[0] // length):
        rows = slice(s * length, (s + 1) * length)
        valid = lax.broadcasted_iota(jnp.int32, (length, 1), 0) < cnt_ref[s]
        total += jnp.sum(
            jnp.where(valid, log_total[rows] - picked[rows], 0.0), axis=0, keepdims=True
        )
        gl_ref[rows, :] = jnp.where(valid, probs[rows], 0.0).astype(bf16)
    return total


def attend_fwd_kernel(cross, length, cnt_ref, x_ref, gain_ref, *refs):
    if cross:
        src_ref, w_ref, n_ref, qkv_ref, o_ref, y_ref = refs
    else:
        w_ref, n_ref, qkv_ref, o_ref, y_ref = refs
    inner = w_ref.shape[0] // 4
    x = x_ref[...].astype(f32)
    n = (unit_rows(x)[1] * gain_ref[...]).astype(bf16)
    n_ref[...] = n
    if cross:
        qkv_ref[:, :inner] = dot_last(n, w_ref[:inner, :]).astype(bf16)
        qkv_ref[:, inner:] = dot_last(src_ref[...], w_ref[inner : 3 * inner, :]).astype(bf16)
    else:
        qkv_ref[...] = dot_last(n, w_ref[: 3 * inner, :]).astype(bf16)
    heads_fwd(cnt_ref, qkv_ref, o_ref, length)
    y_ref[...] = x + dot(o_ref[...], w_ref[3 * inner :, :])


def attend_fwd(counts, x, gain, w, length, source=None):
    t, d = x.shape
    inner = w.shape[0] // 4
    ins = [counts, x, gain] + ([] if source is None else [source]) + [w]
    vm = pl.BlockSpec(memory_space=pltpu.VMEM)
    return pl.pallas_call(
        functools.partial(attend_fwd_kernel, source is not None, length),
        out_shape=(
            jax.ShapeDtypeStruct((t, d), bf16),
            jax.ShapeDtypeStruct((t, 3 * inner), bf16),
            jax.ShapeDtypeStruct((t, inner), bf16),
            jax.ShapeDtypeStruct((t, d), f32),
        ),
        in_specs=[pl.BlockSpec(memory_space=pltpu.SMEM)] + [vm] * (len(ins) - 1),
        out_specs=(vm,) * 4,
        compiler_params=pltpu.CompilerParams(vmem_limit_bytes=VMEM_BYTES),
        cost_estimate=pl.CostEstimate(
            flops=2 * t * d * inner * 4 + 8 * t * length * inner,
            bytes_accessed=w.size * 2 + t * d * 10,
            transcendentals=t * length * 6,
        ),
    )(*ins)


def attend_bwd_kernel(cross, length, cnt_ref, x_ref, gain_ref, gy_ref, qkv_ref, w_ref, *refs):
    if cross:
        ga_ref, dqkv_ref, gx_ref, gg_ref, gs_ref, do_ref = refs
    else:
        ga_ref, dqkv_ref, gx_ref, gg_ref, do_ref = refs
    inner = w_ref.shape[0] // 4
    ga = gy_ref[...].astype(bf16)
    ga_ref[...] = ga
    do_ref[...] = dot_last(ga, w_ref[3 * inner :, :]).astype(bf16)
    heads_bwd(cnt_ref, qkv_ref, do_ref, dqkv_ref, length)
    if cross:
        up = dot(dqkv_ref[:, :inner], w_ref[:inner, :])
        gs_ref[...] = dot(dqkv_ref[:, inner:], w_ref[inner : 3 * inner, :]).astype(bf16)
    else:
        up = dot(dqkv_ref[...], w_ref[: 3 * inner, :])
    back, gg_ref[...] = norm_back(x_ref[...].astype(f32), gain_ref[...], up)
    gx_ref[...] = gy_ref[...] + back


def attend_bwd(counts, x, gain, gy, qkv, w, length, cross=False):
    t, d = x.shape
    inner = w.shape[0] // 4
    vm = pl.BlockSpec(memory_space=pltpu.VMEM)
    outs = [
        jax.ShapeDtypeStruct((t, d), bf16),
        jax.ShapeDtypeStruct((t, 3 * inner), bf16),
        jax.ShapeDtypeStruct((t, d), f32),
        jax.ShapeDtypeStruct((1, d), f32),
    ]
    if cross:
        outs.append(jax.ShapeDtypeStruct((t, d), bf16))
    return pl.pallas_call(
        functools.partial(attend_bwd_kernel, cross, length),
        out_shape=tuple(outs),
        in_specs=[pl.BlockSpec(memory_space=pltpu.SMEM)] + [vm] * 5,
        out_specs=(vm,) * len(outs),
        scratch_shapes=[pltpu.VMEM((t, inner), bf16)],
        compiler_params=pltpu.CompilerParams(vmem_limit_bytes=VMEM_BYTES),
        cost_estimate=pl.CostEstimate(
            flops=2 * t * d * inner * 4 + 20 * t * length * inner,
            bytes_accessed=w.size * 2 + t * d * 16,
            transcendentals=t * length * 6,
        ),
    )(counts, x, gain, gy, qkv, w)


def feed_fwd_kernel(y_ref, g_in_ref, g_out_ref, w_ref, n_ref, gu_ref, y2_ref, f_ref):
    i = pl.program_id(0)
    f = w_ref.shape[1] // 3

    @pl.when(i == 0)
    def _():
        y = y_ref[...]
        n_ref[...] = (unit_rows(y)[1] * g_in_ref[...]).astype(bf16)
        y2_ref[...] = y

    gu = dot_last(n_ref[...], w_ref[0, : 2 * f, :])
    gu_ref[0] = gu
    hidden = (gelu_parts(gu[:, :f])[0] * gu[:, f:]).astype(bf16)
    y2_ref[...] += dot(hidden, w_ref[0, 2 * f :, :])

    @pl.when(i == pl.num_programs(0) - 1)
    def _():
        f_ref[...] = (unit_rows(y2_ref[...])[1] * g_out_ref[...]).astype(bf16)


def feed_fwd(y, gain_in, gain_out, w):
    t, d = y.shape
    nb, rows, _ = w.shape
    f = rows // 3
    whole = lambda *shape: pl.BlockSpec(shape, lambda i: (0,) * len(shape))
    part = lambda *shape: pl.BlockSpec((1,) + shape, lambda i: (i, 0, 0))
    return pl.pallas_call(
        feed_fwd_kernel,
        grid=(nb,),
        out_shape=(
            jax.ShapeDtypeStruct((t, d), bf16),
            jax.ShapeDtypeStruct((nb, t, 2 * f), f32),
            jax.ShapeDtypeStruct((t, d), f32),
            jax.ShapeDtypeStruct((t, d), bf16),
        ),
        in_specs=[whole(t, d), whole(1, d), whole(1, d), part(rows, d)],
        out_specs=(whole(t, d), part(t, 2 * f), whole(t, d), whole(t, d)),
        compiler_params=pltpu.CompilerParams(vmem_limit_bytes=VMEM_BYTES),
        cost_estimate=pl.CostEstimate(
            flops=2 * t * d * rows * nb,
            bytes_accessed=w.size * 2 + t * d * 12 + nb * t * f * 8,
            transcendentals=nb * t * f,
        ),
    )(y, gain_in, gain_out, w)


def feed_bwd_kernel(emit, up_ref, y_ref, y2_ref, g_in_ref, g_out_ref, gu_ref, w_ref, *refs):
    if emit:
        gf_ref, gy_ref, gg_ref, dgu_ref, hid_ref, last_ref = refs
    else:
        gf_ref, gy_ref, gg_ref, last_ref = refs
    i = pl.program_id(0)
    f = w_ref.shape[1] // 3

    @pl.when(i == 0)
    def _():
        back, gain_grad = norm_back(y2_ref[...], g_out_ref[...], up_ref[...].astype(f32))
        gg_ref[1:2, :] = gain_grad
        last_ref[...] = back
        gf_ref[...] = back.astype(bf16)
        gy_ref[...] = jnp.zeros_like(gy_ref)

    gh = dot_last(gf_ref[...], w_ref[0, 2 * f :, :])
    act, slope = gelu_parts(gu_ref[0, :, :f])
    u = gu_ref[0, :, f:]
    dg = (gh * u * slope).astype(bf16)
    du = (gh * act).astype(bf16)
    if emit:
        dgu_ref[0, :, :f] = dg
        dgu_ref[0, :, f:] = du
        hid_ref[0] = (act * u).astype(bf16)
    gy_ref[...] += dot(dg, w_ref[0, :f, :]) + dot(du, w_ref[0, f : 2 * f, :])

    @pl.when(i == pl.num_programs(0) - 1)
    def _():
        back, gain_grad = norm_back(y_ref[...], g_in_ref[...], gy_ref[...])
        gg_ref[0:1, :] = gain_grad
        gy_ref[...] = last_ref[...] + back


def feed_bwd(up, y, y2, gain_in, gain_out, gu, w, emit):
    t, d = y.shape
    nb, rows, _ = w.shape
    f = rows // 3
    whole = lambda *shape: pl.BlockSpec(shape, lambda i: (0,) * len(shape))
    part = lambda *shape: pl.BlockSpec((1,) + shape, lambda i: (i, 0, 0))
    outs = [
        jax.ShapeDtypeStruct((t, d), bf16),
        jax.ShapeDtypeStruct((t, d), f32),
        jax.ShapeDtypeStruct((2, d), f32),
    ]
    specs = [whole(t, d), whole(t, d), whole(2, d)]
    if emit:
        outs += [
            jax.ShapeDtypeStruct((nb, t, 2 * f), bf16),
            jax.ShapeDtypeStruct((nb, t, f), bf16),
        ]
        specs += [part(t, 2 * f), part(t, f)]
    return pl.pallas_call(
        functools.partial(feed_bwd_kernel, emit),
        grid=(nb,),
        out_shape=tuple(outs),
        in_specs=[whole(t, d)] * 3 + [whole(1, d)] * 2 + [part(t, 2 * f), part(rows, d)],
        out_specs=tuple(specs),
        scratch_shapes=[pltpu.VMEM((t, d), f32)],
        compiler_params=pltpu.CompilerParams(vmem_limit_bytes=VMEM_BYTES),
        cost_estimate=pl.CostEstimate(
            flops=2 * t * d * rows * nb,
            bytes_accessed=w.size * 2 + t * d * 18 + nb * t * f * 8,
            transcendentals=nb * t * f,
        ),
    )(up, y, y2, gain_in, gain_out, gu, w)


def head_kernel(length, cnt_ref, f_ref, w_ref, target_ref, gl_ref, up_ref, loss_ref):
    loss_ref[...] = loss_back(cnt_ref, f_ref, w_ref, target_ref, gl_ref, length)
    up_ref[...] = dot(gl_ref[...], w_ref[...])


def head_loss(counts, final, w, target, length):
    t, d = final.shape
    v = w.shape[0]
    vm = pl.BlockSpec(memory_space=pltpu.VMEM)
    return pl.pallas_call(
        functools.partial(head_kernel, length),
        out_shape=(
            jax.ShapeDtypeStruct((t, v), bf16),
            jax.ShapeDtypeStruct((t, d), f32),
            jax.ShapeDtypeStruct((1, 1), f32),
        ),
        in_specs=[pl.BlockSpec(memory_space=pltpu.SMEM), vm, vm, vm],
        out_specs=(vm,) * 3,
        compiler_params=pltpu.CompilerParams(vmem_limit_bytes=VMEM_BYTES),
        cost_estimate=pl.CostEstimate(
            flops=4 * t * d * v, bytes_accessed=w.size * 2 + t * d * 6, transcendentals=t * v * 2
        ),
    )(counts, final, w, target)


def tail_kernel(
    tiny_ref, attn_terms, extra_terms, w_ref, n_all, g_all,
    feed_ref, attn_ref, extra_ref, total_ref,
    tinies, n_buf, g_buf, *rest,
):
    attn_bufs, extra_bufs = rest[:8], rest[8:16]
    tiny_send, tiny_recv, rs_send, rs_recv, pair_sem = rest[16:]
    me = lax.axis_index("rows")
    z, y, c = me // 4, (me // 2) % 2, me % 2
    high = z // 2
    inner = (z + high) % 2
    f = w_ref.shape[0] // 3
    d = w_ref.shape[1]
    core_peer, y_peer = me + 1 - 2 * c, me + 2 - 4 * y
    toward = me + 4 - 8 * high
    outward = me - 4 + 8 * high
    mesh_id = pl.DeviceIdType.MESH

    def remote(src, dst, send, recv, where):
        return pltpu.make_async_remote_copy(
            src_ref=src, dst_ref=dst, send_sem=send, recv_sem=recv,
            device_id=where, device_id_type=mesh_id,
        )

    def pair_copies(p):
        slot = p % 2
        return [
            pltpu.make_async_copy(whole.at[pl.ds(2 * p, 2)], buf.at[slot], pair_sem.at[k, slot])
            for k, (whole, buf) in enumerate([(n_all, n_buf), (g_all, g_buf)])
        ]

    for copy in pair_copies(0):
        copy.start()

    barrier = pltpu.get_barrier_semaphore()

    def greet(where):
        pl.semaphore_signal(barrier, inc=1, device_id=where, device_id_type=mesh_id)

    greet({"rows": core_peer})
    greet({"rows": y_peer})
    greet({"rows": toward})

    @pl.when(inner == 1)
    def _():
        greet({"rows": outward})

    pl.semaphore_wait(barrier, 3 + inner)

    def place_of(p):
        j, other = [(0, 0), (1, 0), (0, 1), (2, 0), (1, 1), (3, 0), (2, 1), (3, 1)][p]
        zz = [z, z + 1 - 2 * (z % 2), 2 - high, 3 - 3 * high][j]
        yy = y + other - 2 * other * y
        return zz, yy, other

    def tiny_copy(kind, p, s, where):
        src = tiny_ref if p == 0 else tinies.at[s]
        return remote(src, tinies.at[s], tiny_send.at[kind, p], tiny_recv.at[s], where)

    def each_tiny(p, act):
        zz, yy, other = place_of(p)
        s = 4 * zz + 2 * yy + c
        if other == 0:

            @pl.when((zz <= z) & (z < 3))
            def _():
                act(tiny_copy(0, p, s, {"rows": me + 4}))

            @pl.when((zz >= z) & (z > 0))
            def _():
                act(tiny_copy(1, p, s, {"rows": me - 4}))

            act(tiny_copy(2, p, s, {"rows": y_peer}))
        act(tiny_copy(3, p, s, {"rows": core_peer}))

    def tiny_arrive(p):
        zz, yy, _ = place_of(p)
        tiny_copy(0, p, 4 * zz + 2 * yy + c, {"rows": me}).wait_recv()
        each_tiny(p, lambda copy: copy.start())

    far_out, far_in = 3 - 3 * high, 2 - high
    beside = (1 - inner) * (1 + high) + inner * 3 * high

    def summed(bufs, k, terms, result):
        part, four, from_y, from_far, from_near, from_cross, from_out, cross_out = bufs

        def hop(i, src, dst, where):
            return remote(src, dst, rs_send.at[k, i], rs_recv.at[k, i], {"rows": where})

        ys = [
            hop(1 + i, part.at[(1 - y) * 4 + at], from_y.at[at], y_peer)
            for i, at in enumerate([far_out, far_in, beside, z])
        ]
        fars = [hop(5 + i, four.at[at], from_far.at[i], toward) for i, at in enumerate([far_out, far_in])]
        near = hop(7, four.at[beside], from_near, toward)
        crosses = [hop(8 + i, four.at[at], from_cross.at[i], toward) for i, at in enumerate([far_out, far_in])]
        out = hop(10, cross_out, from_out, outward)

        def start():
            total = terms[...]
            if total.ndim == 3:
                total = (total[0].astype(f32) + total[1].astype(f32)).astype(bf16)
            part[...] = total.reshape(part.shape)
            ys[0].start()
            ys[1].start()

        def rest():
            ys[2].start()
            ys[3].start()

        def add_y(i, at):
            ys[i].wait_recv()
            four[at] = (part[4 * y + at].astype(f32) + from_y[at].astype(f32)).astype(bf16)

        def far(i):
            def stage():
                add_y(i, [far_out, far_in][i])
                pl.when(inner == 0)(fars[i].start)

            return stage

        def cross(i):
            def stage():
                @pl.when(inner == 1)
                def _():
                    at = [far_out, far_in][i]
                    fars[i].wait_recv()
                    four[at] = (four[at].astype(f32) + from_far[i].astype(f32)).astype(bf16)
                    crosses[i].start()

            return stage

        def home():
            add_y(2, beside)
            pl.when(inner == 0)(near.start)

        def own():
            add_y(3, z)

        def leave():
            @pl.when(inner == 1)
            def _():
                crosses[0].wait_recv()
                cross_out[...] = (four[beside].astype(f32) + from_cross[0].astype(f32)).astype(bf16)
                out.start()

        def last_inner():
            @pl.when(inner == 1)
            def _():
                crosses[1].wait_recv()
                near.wait_recv()
                result(four[z].astype(f32) + from_cross[1].astype(f32) + from_near[...].astype(f32))

        def last_outer():
            @pl.when(inner == 0)
            def _():
                out.wait_recv()
                result(four[z].astype(f32) + from_out[...].astype(f32))

        def settle():
            for copy in ys:
                copy.wait_send()

            @pl.when(inner == 0)
            def _():
                for copy in [*fars, near]:
                    copy.wait_send()

            @pl.when(inner == 1)
            def _():
                for copy in [*crosses, out]:
                    copy.wait_send()

        return {
            "start": start, "rest": rest, "0": far(0), "1": far(1), "2": cross(0), "3": cross(1),
            "4": home, "5": own, "6": leave, "7": last_inner, "8": last_outer, "settle": settle,
        }

    def attn_result(value):
        attn_ref[...] = value

    def extra_result(value):
        extra_ref[...] = value

    attn = summed(attn_bufs, 0, attn_terms, attn_result)
    extra = summed(extra_bufs, 1, extra_terms, extra_result)

    def wgrad(p):
        if p < 7:
            for copy in pair_copies(p + 1):
                copy.start()
        for copy in pair_copies(p):
            copy.wait()
        n_rows = n_buf[p % 2].reshape(-1, d)
        g_rows = g_buf[p % 2].reshape(-1, d)
        gu = dot_last(w_ref[: 2 * f, :], n_rows)
        gh = dot_last(w_ref[2 * f :, :], g_rows)
        act, slope = gelu_parts(gu[:f])
        up = gu[f:]
        dg = (gh * up * slope).astype(bf16)
        du = (gh * act).astype(bf16)
        hid = (act * up).astype(bf16)
        from_n = dot(jnp.concatenate([dg, du], axis=0), n_rows)
        from_g = dot(hid, g_rows)
        if p == 0:
            feed_ref[: 2 * f, :] = from_n
            feed_ref[2 * f :, :] = from_g
        else:
            feed_ref[: 2 * f, :] += from_n
            feed_ref[2 * f :, :] += from_g

    def add_tinies():
        for p in range(8):
            zz, yy, _ = place_of(p)
            tiny_copy(0, p, 4 * zz + 2 * yy + 1 - c, {"rows": me}).wait_recv()
        total = tinies[0]
        for s in range(1, 16):
            total += tinies[s]
        total_ref[...] = total

    tinies[me] = tiny_ref[...]
    each_tiny(0, lambda copy: copy.start())
    attn["start"]()
    extra["start"]()
    attn["rest"]()
    extra["rest"]()

    for step in TAIL_STEPS:
        if step[0] == "w":
            wgrad(int(step[1]))
        elif step[0] == "t":
            tiny_arrive(int(step[1]))
        elif step[0] == "a":
            attn[step[1]]()
        elif step[0] == "x":
            extra[step[1]]()
        else:
            add_tinies()

    for p in range(8):
        each_tiny(p, lambda copy: copy.wait_send())
    attn["settle"]()
    extra["settle"]()


TAIL_STEPS = (
    ("a0", "w0", "a1", "t1", "t2", "w1", "a2", "x0", "t3", "t4", "a3", "w2", "x1", "w3", "x2", "a4", "t5", "t6", "w4")
    + ("a5", "x3", "a6", "a7", "w5", "x4", "a8", "t7", "w6", "x5", "x6", "sum", "w7", "x7", "x8")
)


def tail(tiny, attn_terms, extra_terms, w_own, n_all, g_all):
    t, d = n_all.shape[1:]
    rows = w_own.shape[0]
    per, more = attn_terms.shape[1] // 8, extra_terms.shape[0] // 8

    def sums(r, d):
        return [
            pltpu.VMEM(shape + (r, d), bf16)
            for shape in [(8,), (4,), (4,), (2,), (), (2,), (), ()]
        ]

    vm = pl.BlockSpec(memory_space=pltpu.VMEM)
    anywhere = pl.BlockSpec(memory_space=pl.ANY)
    return pl.pallas_call(
        tail_kernel,
        out_shape=(
            jax.ShapeDtypeStruct((rows, d), f32),
            jax.ShapeDtypeStruct((per, d), f32),
            jax.ShapeDtypeStruct((more, extra_terms.shape[1]), f32),
            jax.ShapeDtypeStruct(tiny.shape, f32),
        ),
        in_specs=[vm] * 4 + [anywhere] * 2,
        out_specs=(vm,) * 4,
        scratch_shapes=[
            pltpu.VMEM((16,) + tiny.shape, f32),
            pltpu.VMEM((2, 2, t, d), bf16),
            pltpu.VMEM((2, 2, t, d), bf16),
            *sums(per, d),
            *sums(more, extra_terms.shape[1]),
            pltpu.SemaphoreType.DMA((4, 8)),
            pltpu.SemaphoreType.DMA((16,)),
            pltpu.SemaphoreType.DMA((2, 11)),
            pltpu.SemaphoreType.DMA((2, 11)),
            pltpu.SemaphoreType.DMA((2, 2)),
        ],
        compiler_params=pltpu.CompilerParams(
            vmem_limit_bytes=60 * 1024 * 1024, collective_id=0, has_side_effects=True
        ),
        cost_estimate=pl.CostEstimate(
            flops=2 * t * 16 * d * rows * 2, bytes_accessed=16 * t * d * 4, transcendentals=16 * t * rows
        ),
    )(tiny, attn_terms, extra_terms, w_own, n_all, g_all)


def front_kernel(
    length, cnt_ref, order_ref, x_ref, g_attn_ref, g_feed_ref, g_final_ref,
    attn_own, feed_own, half_own,
    attn_all, feed_all, extra_all,
    n1_ref, qkv_ref, mixed_ref, y1_ref, n2_ref, gu_ref, y2_ref, enc_ref, arrived_ref, sorted_ref,
    w_attn, w_feed, place, wide_buf, first_own, second_own, extra_own,
    send_sem, recv_sem, own_sem, load_sem, x_send, x_recv,
):
    section = lax.axis_index("section")
    me = lax.axis_index("rows")
    z, y, c = me // 4, (me // 2) % 2, me % 2
    core_peer, y_peer = me + 1 - 2 * c, me + 2 - 4 * y
    mesh_id = pl.DeviceIdType.MESH
    inner = mixed_ref.shape[1]
    f = feed_own.shape[0] // 3

    barrier = pltpu.get_barrier_semaphore()

    def greet(where):
        pl.semaphore_signal(barrier, inc=1, device_id=where, device_id_type=mesh_id)

    greet({"rows": core_peer})
    greet({"rows": y_peer})
    greet({"section": 1 - section})

    @pl.when(z > 0)
    def _():
        greet({"rows": me - 4})

    @pl.when(z < 3)
    def _():
        greet({"rows": me + 4})

    own_copies = [
        pltpu.make_async_copy(own, whole.at[me], own_sem.at[k])
        for k, (own, whole) in enumerate(
            [(attn_own, attn_all), (feed_own, feed_all), (extra_own, extra_all)]
        )
    ]
    load_half = pltpu.make_async_copy(half_own, second_own, own_sem.at[3])
    own_copies[0].start()
    own_copies[1].start()

    @pl.when(section == 1)
    def _():
        load_half.start()

    pl.semaphore_wait(barrier, 4 + (z + z // 2) % 2)

    def remote(src, dst, send, recv, where):
        return pltpu.make_async_remote_copy(
            src_ref=src, dst_ref=dst, send_sem=send, recv_sem=recv,
            device_id=where, device_id_type=mesh_id,
        )

    kinds = [pl.ds(k * f, f) for k in range(3)]
    cuts = [pl.ds(k * (extra_own.shape[0] // 2), extra_own.shape[0] // 2) for k in range(2)]
    parts = {
        "A": (0, attn_all, None, 2, attn_own),
        "G": (1, feed_all, kinds[0], 1, feed_own.at[kinds[0]]),
        "U": (2, feed_all, kinds[1], 1, feed_own.at[kinds[1]]),
        "O": (3, feed_all, kinds[2], 1, feed_own.at[kinds[2]]),
        "X": (4, extra_all, cuts[0], 1, extra_own.at[cuts[0]]),
        "Y": (5, extra_all, cuts[1], 2, extra_own.at[cuts[1]]),
    }

    def place_of(route, p):
        if route == 1:
            j, other = [(0, 0), (1, 0), (0, 1), (2, 0), (1, 1), (3, 0), (2, 1), (3, 1)][p]
        else:
            j, other = p // 2, p % 2
        zz = [z, z + 1 - 2 * (z % 2), 2 - z // 2, 3 - 3 * (z // 2)][j]
        yy = y + other - 2 * other * y
        return zz, yy, other

    def part_copy(name, kind, p, s, where):
        k, whole, rows, _, own = parts[name]
        dst = whole.at[s] if rows is None else whole.at[s, rows]
        return remote(own if p == 0 else dst, dst, send_sem.at[k, kind, p], recv_sem.at[k, s], where)

    def each_send(name, p, act, ways="zyc"):
        route = parts[name][3]
        zz, yy, other = place_of(route, p)
        s = 4 * zz + 2 * yy + c
        if "z" in ways and (route == 2 or other == 0):

            @pl.when((zz <= z) & (z < 3))
            def _():
                act(part_copy(name, 0, p, s, {"rows": me + 4}))

            @pl.when((zz >= z) & (z > 0))
            def _():
                act(part_copy(name, 1, p, s, {"rows": me - 4}))

        if "y" in ways and (p == 0 or (route == 1 and other == 0)):
            act(part_copy(name, 2, p, s, {"rows": y_peer}))
        if "c" in ways:
            act(part_copy(name, 3, p, s, {"rows": core_peer}))

    def begin(name, ways):
        each_send(name, 0, lambda copy: copy.start(), ways)

    def arrive(name, p):
        zz, yy, _ = place_of(parts[name][3], p)
        part_copy(name, 0, p, 4 * zz + 2 * yy + c, {"rows": me}).wait_recv()
        each_send(name, p, lambda copy: copy.start())

    def meet(name, p):
        zz, yy, _ = place_of(parts[name][3], p)
        part_copy(name, 0, p, 4 * zz + 2 * yy + 1 - c, {"rows": me}).wait_recv()

    def settle(name):
        for p in range(8):
            each_send(name, p, lambda copy: copy.wait_send())

    half_copy = remote(half_own, first_own, x_send.at[0], x_recv.at[0], {"section": 1 - section})
    enc_copy = remote(enc_ref, arrived_ref, x_send.at[1], x_recv.at[1], {"section": 1 - section})

    def project():
        for p in range(8):
            meet("A", p)
        own_copies[0].wait()
        load = pltpu.make_async_copy(attn_all, w_attn, load_sem.at[0])
        load.start()
        load.wait()
        wide_buf[...] = dot_last(n1_ref[...], w_attn[...].reshape(4 * inner, -1)).astype(bf16)
        qkv_ref[...] = dot(wide_buf[...], place[:, : 3 * inner]).astype(bf16)

    def mix(s):
        low = low_half(length)
        allowed = allowed_twice(cnt_ref, s, length)
        rows = slice(s * length, (s + 1) * length)
        for h in range(inner // PAIR):
            cols = [slice(j * inner + h * PAIR, j * inner + (h + 1) * PAIR) for j in range(3)]
            q2 = stack_pair(qkv_ref[rows, cols[0]], low)
            p = soft_pair(q2, qkv_ref[rows, cols[1]], allowed).astype(bf16)
            wide = jnp.concatenate([p[:length], p[length:]], axis=1)
            mixed_ref[rows, cols[0]] = dot(wide, stack_pair(qkv_ref[rows, cols[2]], low)).astype(bf16)

    def mix_out():
        for s in range(x_ref.shape[0] // length // 2, x_ref.shape[0] // length):
            mix(s)
        wide_buf[...] = dot_last(mixed_ref[...], place[:, 3 * inner :]).astype(bf16)
        y1_ref[...] = x_ref[...].astype(f32) + dot(wide_buf[...], w_attn[...].reshape(4 * inner, -1))
        y2_ref[...] = y1_ref[...]
        n2_ref[...] = (unit_rows(y1_ref[...])[1] * g_feed_ref[...]).astype(bf16)

    def mix_first():
        for s in range(x_ref.shape[0] // length // 2):
            mix(s)

    def feed(p):
        if p == 0:
            own_copies[1].wait()
        for name in "GUO":
            meet(name, p)
        zz, yy, _ = place_of(1, p)
        pair = 4 * zz + 2 * yy

        @pl.when(section == 0)
        def _():
            blocks = pltpu.make_async_copy(feed_all.at[pl.ds(pair, 2)], w_feed, load_sem.at[1])
            blocks.start()
            blocks.wait()
            for k in range(2):
                gu = dot_last(n2_ref[...], w_feed[k, : 2 * f, :])
                gu_ref[pair + k] = gu
                hidden = (gelu_parts(gu[:, :f])[0] * gu[:, f:]).astype(bf16)
                y2_ref[...] += dot(hidden, w_feed[k, 2 * f :, :])

    begin("A", "zyc")

    @pl.when(section == 0)
    def _():
        half_copy.start()

    begin("G", "zyc")

    @pl.when(section == 1)
    def _():
        load_half.wait()
        half_copy.wait_recv()
        extra_own[...] = jnp.concatenate([first_own[...], second_own[...]], axis=1)
        own_copies[2].start()
        begin("Y", "zyc")
        begin("X", "zyc")

    begin("U", "yc")
    begin("O", "yc")

    row = lax.broadcasted_iota(jnp.int32, place.shape, 0)
    place[...] = jnp.where(row == order_ref[...], 1.0, 0.0).astype(bf16)
    n1_ref[...] = (unit_rows(x_ref[...].astype(f32))[1] * g_attn_ref[...]).astype(bf16)

    tasks = {"c1": project, "c2": mix_first, "c3": mix_out}
    for step in FRONT_STEPS:
        if step in tasks:
            tasks[step]()
        elif step[0] == "f":
            feed(int(step[1]))
        elif step[0] == "o":
            begin(step[1], "z")
        elif step[0] == "X":

            @pl.when(section == 1)
            def _(p=int(step[1])):
                arrive("X", p)
                arrive("Y", p)

        else:
            arrive(step[0], int(step[1]))

    @pl.when(section == 0)
    def _():
        enc_ref[...] = (unit_rows(y2_ref[...])[1] * g_final_ref[...]).astype(bf16)
        enc_copy.start()

    for k in range(4):
        columns = slice(k * inner, (k + 1) * inner)
        w = w_attn[...].reshape(4 * inner, -1)
        sorted_ref[columns, :] = dot_rows(place[:, columns], w).astype(bf16)

    for name in "AGUO":
        settle(name)

    @pl.when(section == 1)
    def _():
        for name in "XY":
            for p in range(8):
                meet(name, p)
            settle(name)
        own_copies[2].wait()
        enc_copy.wait_recv()

    @pl.when(section == 0)
    def _():
        half_copy.wait_send()
        enc_copy.wait_send()


FRONT_STEPS = (
    ("A1", "oU", "G1", "A2", "A3", "oO", "A4", "O1", "U1", "G2", "U2", "O2", "A5", "A6", "X1", "X2", "G3", "A7")
    + ("c1", "O3", "G4", "O4", "U3", "c2", "U4", "c3", "f0", "O5", "f1", "U5", "U6", "G5", "O6", "X3", "X4", "X5")
    + ("X6", "O7", "f2", "f3", "G6", "f4", "f5", "U7", "f6", "X7", "G7", "f7")
)


def front(counts, order, x, gain_attn, gain_feed, gain_final, attn_own, feed_own, half_own, length):
    t, d = x.shape
    attn_rows, feed_rows = attn_own.shape[0], feed_own.shape[0]
    inner = attn_rows * 4
    vm = pl.BlockSpec(memory_space=pltpu.VMEM)
    anywhere = pl.BlockSpec(memory_space=pl.ANY)
    return pl.pallas_call(
        functools.partial(front_kernel, length),
        out_shape=(
            jax.ShapeDtypeStruct((16, attn_rows, d), bf16),
            jax.ShapeDtypeStruct((16, feed_rows, d), bf16),
            jax.ShapeDtypeStruct((16, half_own.shape[0], d), bf16),
            jax.ShapeDtypeStruct((t, d), bf16),
            jax.ShapeDtypeStruct((t, 3 * inner), bf16),
            jax.ShapeDtypeStruct((t, inner), bf16),
            jax.ShapeDtypeStruct((t, d), f32),
            jax.ShapeDtypeStruct((t, d), bf16),
            jax.ShapeDtypeStruct((16, t, feed_rows // 3 * 2), f32),
            jax.ShapeDtypeStruct((t, d), f32),
            jax.ShapeDtypeStruct((t, d), bf16),
            jax.ShapeDtypeStruct((t, d), bf16),
            jax.ShapeDtypeStruct((4 * inner, d), bf16),
        ),
        in_specs=[pl.BlockSpec(memory_space=pltpu.SMEM)] + [vm] * 5 + [anywhere] * 3,
        out_specs=(anywhere,) * 3 + (vm,) * 10,
        scratch_shapes=[
            pltpu.VMEM((16, attn_rows, d), bf16),
            pltpu.VMEM((2, feed_rows, d), bf16),
            pltpu.VMEM((4 * inner, 4 * inner), bf16),
            pltpu.VMEM((t, 4 * inner), bf16),
            pltpu.VMEM(half_own.shape, bf16),
            pltpu.VMEM(half_own.shape, bf16),
            pltpu.VMEM((half_own.shape[0], d), bf16),
            pltpu.SemaphoreType.DMA((6, 4, 8)),
            pltpu.SemaphoreType.DMA((6, 16)),
            pltpu.SemaphoreType.DMA((4,)),
            pltpu.SemaphoreType.DMA((2,)),
            pltpu.SemaphoreType.DMA((2,)),
            pltpu.SemaphoreType.DMA((2,)),
        ],
        compiler_params=pltpu.CompilerParams(
            vmem_limit_bytes=VMEM_BYTES, collective_id=1, has_side_effects=True
        ),
        cost_estimate=pl.CostEstimate(
            flops=2 * t * d * (feed_rows * 16 + 8 * inner),
            bytes_accessed=2 * 16 * (attn_rows + feed_rows) * d * 2,
            transcendentals=t * feed_rows * 6,
        ),
    )(counts, order, x, gain_attn, gain_feed, gain_final, attn_own, feed_own, half_own)


def mid_kernel(
    length, cross_cnt, self_cnt, dec_cnt, x_ref, y1_ref, y2_in, n2_in, qkv_ref, mixed_ref, n1_ref,
    encoded_ref, target_ref, gain_ref, order_ref, gu_in, attn_w, extra_w, feed_w,
    n_all, g_all, gx_ref, sums_ref, attn_sums, extra_sums, extra_pair,
    slots, gu_buf, w_att, w_head, mid, y2, acc, n2, cqkv, do_buf, grad_enc,
    dqkv_ref, dcqkv_ref, cmixed_ref, gl_ref, gf_ref, ga_ref, mc_ref, gac_ref, final_ref, lefts_ref,
    send_sem, recv_sem, slot_sem, load_sem, own_sem, x_send, x_recv, core_send, core_recv, put_sem, cross_send, cross_recv,
):
    section = lax.axis_index("section")
    me = lax.axis_index("rows")
    z, y, c = me // 4, (me // 2) % 2, me % 2
    core_peer, y_peer = me + 1 - 2 * c, me + 2 - 4 * y
    mesh_id = pl.DeviceIdType.MESH
    inner = w_att.shape[0] // 4
    f = feed_w.shape[1] // 3
    t = n2.shape[0]
    held = slots.shape[0]
    spare = BLOCKS - held
    is_enc, is_dec = section == 0, section == 1

    def load(b):
        k = b % held
        return pltpu.make_async_copy(feed_w.at[b], slots.at[k], slot_sem.at[k])

    load_attn = pltpu.make_async_copy(attn_w, w_att, load_sem.at[0])
    load_cross = pltpu.make_async_copy(extra_w.at[pl.ds(0, 4 * inner)], w_att, load_sem.at[1])
    load_head = pltpu.make_async_copy(extra_w.at[pl.ds(4 * inner, inner)], w_head, load_sem.at[2])
    load_gu = pltpu.make_async_copy(gu_in, gu_buf, load_sem.at[3])

    def start_loads(first):
        def step(k, carry):
            load(first + k).start()
            return carry

        lax.fori_loop(0, held, step, 0)

    @pl.when(is_enc)
    def _():
        start_loads(spare)
        load_gu.start()
        load_attn.start()

    @pl.when(is_dec)
    def _():
        load_cross.start()
        start_loads(0)
        load_head.start()

    barrier = pltpu.get_barrier_semaphore()

    def greet(where):
        pl.semaphore_signal(barrier, inc=1, device_id=where, device_id_type=mesh_id)

    greet({"rows": core_peer})
    greet({"rows": y_peer})
    greet({"section": 1 - section})

    @pl.when(z > 0)
    def _():
        greet({"rows": me - 4})

    @pl.when(z < 3)
    def _():
        greet({"rows": me + 4})

    pl.semaphore_wait(barrier, 4 + (z + z // 2) % 2)

    def remote(src, dst, send, recv, where):
        return pltpu.make_async_remote_copy(
            src_ref=src, dst_ref=dst, send_sem=send, recv_sem=recv,
            device_id=where, device_id_type=mesh_id,
        )

    cut = t * 13 // 256 * 16
    upper, lower = pl.ds(0, cut), pl.ds(cut, t - cut)
    parts = {
        "S": (0, upper, 1, n2, n_all),
        "Q": (1, lower, 2, n2, n_all),
        "V": (2, upper, 1, gf_ref, g_all),
        "W": (3, lower, 2, gf_ref, g_all),
    }

    def place_of(route, p):
        if route == 1:
            j, other = [(0, 0), (1, 0), (0, 1), (2, 0), (1, 1), (3, 0), (2, 1), (3, 1)][p]
        else:
            j, other = p // 2, p % 2
        zz = [z, z + 1 - 2 * (z % 2), 2 - z // 2, 3 - 3 * (z // 2)][j]
        yy = y + other - 2 * other * y
        return zz, yy, other

    def part_copy(name, kind, p, s, where):
        k, rows, _, own, whole = parts[name]
        dst = whole.at[s, rows]
        src = own.at[rows] if p == 0 else dst
        return remote(src, dst, send_sem.at[k, kind, p], recv_sem.at[k, s], where)

    def each_send(name, p, act):
        route = parts[name][2]
        zz, yy, other = place_of(route, p)
        s = 4 * zz + 2 * yy + c
        if route == 2 or other == 0:

            @pl.when((zz <= z) & (z < 3))
            def _():
                act(part_copy(name, 0, p, s, {"rows": me + 4}))

            @pl.when((zz >= z) & (z > 0))
            def _():
                act(part_copy(name, 1, p, s, {"rows": me - 4}))

        if p == 0 or (route == 1 and other == 0):
            act(part_copy(name, 2, p, s, {"rows": y_peer}))
        act(part_copy(name, 3, p, s, {"rows": core_peer}))

    own_copies = {
        "S": pltpu.make_async_copy(n2, n_all.at[me], own_sem.at[0]),
        "V": pltpu.make_async_copy(gf_ref, g_all.at[me], own_sem.at[1]),
    }

    def begin(names):
        own_copies[names[1]].start()
        for name in names:
            each_send(name, 0, lambda copy: copy.start())

    def arrive(*steps):
        for step in steps:
            name, p = step[0], int(step[1])
            zz, yy, _ = place_of(parts[name][2], p)
            part_copy(name, 0, p, 4 * zz + 2 * yy + c, {"rows": me}).wait_recv()
            each_send(name, p, lambda copy: copy.start())

    back_copy = remote(grad_enc, grad_enc, x_send.at[0], x_recv.at[0], {"section": 1 - section})

    group = 4

    def feed_forward(first, count):
        def step(i, carry):
            blocks = [first + group * i + k for k in range(group)]
            rows = [slots.at[b % held] for b in blocks]
            for b in blocks:
                load(b).wait()
            hidden = []
            for b, w in zip(blocks, rows):
                gu = dot_last(n2[...], w[: 2 * f, :])
                gu_buf[b] = gu
                hidden.append((gelu_parts(gu[:, :f])[0] * gu[:, f:]).astype(bf16))
            total = None
            for k in range(0, group, 2):
                left = jnp.concatenate(hidden[k : k + 2], axis=1)
                right = jnp.concatenate([w[2 * f :, :] for w in rows[k : k + 2]], axis=0)
                term = dot(left, right)
                total = term if total is None else total + term
            y2[...] += total
            for b in blocks:

                @pl.when(b < spare)
                def _(b=b):
                    load(b + held).start()

            return carry

        lax.fori_loop(0, count // group, step, 0)

    def feed_backward(first, count, fresh):
        def step(i, carry):
            blocks = [BLOCKS - 1 - first - group * i - k for k in range(group)]
            rows = [slots.at[b % held] for b in blocks]
            for b in blocks:

                @pl.when((b < spare) | fresh)
                def _(b=b):
                    load(b).wait()

            lefts = []
            for b, w in zip(blocks, rows):
                gh = dot_last(gf_ref[...], w[2 * f :, :])
                gu = gu_buf[b]
                act, slope = gelu_parts(gu[:, :f])
                dg = (gh * gu[:, f:] * slope).astype(bf16)
                lefts.append(jnp.concatenate([dg, (gh * act).astype(bf16)], axis=1))
            total = None
            for left, w in zip(lefts, rows):
                term = dot(left, w[: 2 * f, :])
                total = term if total is None else total + term
            acc[...] += total
            for b in blocks:

                @pl.when(b >= held)
                def _(b=b):
                    load(b - held).start()

            return carry

        lax.fori_loop(0, count // group, step, 0)

    def final_backward(up):
        back, sums_ref[2:3, :] = norm_back(y2[...], gain_ref[2:3, :], up)
        gx_ref[...] = back
        gf_ref[...] = back.astype(bf16)
        begin("WV")
        acc[...] = jnp.zeros_like(acc)

    def feed_end():
        back, sums_ref[1:2, :] = norm_back(mid[...], gain_ref[1:2, :], acc[...])
        acc[...] = gx_ref[...] + back

    sums_ref[...] = jnp.zeros_like(sums_ref)

    @pl.when(is_enc)
    def _():
        n2[...] = n2_in[...]
        begin("QS")
        mid[...] = y1_ref[...]
        y2[...] = y2_in[...]
        arrive("Q1", "Q2", "S2", "S1", "Q3", "Q4", "S4", "S3", "Q5", "Q6")
        back_copy.wait_recv()
        final_backward(grad_enc[...].astype(f32))
        load_gu.wait()
        arrive("S6")
        feed_backward(0, 8, True)
        arrive("S5", "Q7")
        feed_backward(8, 8, True)
        feed_end()
        arrive("W1", "W2")
        load_attn.wait()

    @pl.when(is_dec)
    def _():
        y1 = y1_ref[...]
        mc_ref[...] = (unit_rows(y1)[1] * gain_ref[3:4, :]).astype(bf16)
        load_cross.wait()
        cqkv[:, :inner] = dot_last(mc_ref[...], w_att[:inner, :]).astype(bf16)
        cqkv[:, inner:] = dot_last(encoded_ref[...], w_att[inner : 3 * inner, :]).astype(bf16)
        heads_fwd(cross_cnt, cqkv, cmixed_ref, length)
        mid[...] = y1_ref[...] + dot(cmixed_ref[...], w_att[3 * inner :, :])
        y2[...] = mid[...]
        n2[...] = (unit_rows(mid[...])[1] * gain_ref[1:2, :]).astype(bf16)
        begin("QS")
        feed_forward(0, 12)
        arrive("Q1", "Q2")
        feed_forward(12, 4)
        final_ref[...] = (unit_rows(y2[...])[1] * gain_ref[2:3, :]).astype(bf16)
        load_head.wait()
        loss = loss_back(dec_cnt, final_ref, w_head, target_ref, gl_ref, length)
        sums_ref[4:5, :] = jnp.broadcast_to(loss, (1, sums_ref.shape[1]))
        final_backward(dot(gl_ref[...], w_head[...]))
        feed_backward(0, 8, False)
        arrive("S2", "S1")
        feed_backward(8, 8, False)
        feed_end()
        arrive("W1", "Q3")
        gac_ref[...] = acc[...].astype(bf16)
        do_buf[...] = dot_last(gac_ref[...], w_att[3 * inner :, :]).astype(bf16)
        heads_bwd(cross_cnt, cqkv, do_buf, dcqkv_ref, length)
        grad_enc[...] = dot(dcqkv_ref[:, inner:], w_att[inner : 3 * inner, :]).astype(bf16)
        back_copy.start()
        up = dot(dcqkv_ref[:, :inner], w_att[:inner, :])
        load_attn.start()
        back, sums_ref[3:4, :] = norm_back(y1_ref[...], gain_ref[3:4, :], up)
        acc[...] += back
        arrive("Q4", "W2")
        load_attn.wait()

    ga_ref[...] = acc[...].astype(bf16)
    do_buf[...] = dot_last(ga_ref[...], w_att[3 * inner :, :]).astype(bf16)
    heads_bwd(self_cnt, qkv_ref, do_buf, dqkv_ref, length)
    up = dot(dqkv_ref[...], w_att[: 3 * inner, :])
    back, sums_ref[0:1, :] = norm_back(x_ref[...].astype(f32), gain_ref[0:1, :], up)
    gx_ref[...] = acc[...] + back

    def core_copies(k, out, rows, first):
        size = 4 * rows
        theirs = [
            remote(slots.at[first + i, pl.ds(0, size)], out.at[1, pl.ds(i * size, size)],
                   core_send.at[k, i], core_recv.at[k, i], {"rows": core_peer})
            for i in range(2)
        ]
        mine = [
            pltpu.make_async_copy(
                slots.at[first + 2 + i, pl.ds(0, size)], out.at[0, pl.ds(i * size, size)], put_sem.at[k, i]
            )
            for i in range(2)
        ]
        return theirs, mine

    def terms(sources, rights, copies, rows, first):
        chunk = inner // 2
        for k, (source, at) in enumerate(sources):
            col = lax.broadcasted_iota(jnp.int32, (inner, inner), 1)
            pick = jnp.where(order_ref[...] == col, 1.0, 0.0).astype(bf16)
            both = dot_last(pick, source[:, at * inner : (at + 1) * inner]).astype(bf16)
            for half in range(2):
                lefts_ref[half, k * chunk : (k + 1) * chunk, :] = both[half * chunk : (half + 1) * chunk]
        d = rights[0].shape[1]
        for which in range(2):
            left = lefts_ref.at[(1 - c) if which == 0 else c]
            pieces = []
            for k, right in enumerate(rights):
                product = dot(left[k * chunk : (k + 1) * chunk, :], right[...])
                pieces.append(product.reshape(8, -1, d))
            if rows > len(rights) * chunk // 8:
                pieces.append(jnp.zeros((8, rows - len(rights) * chunk // 8, d), f32))
            blocks = jnp.concatenate(pieces, axis=1).astype(bf16)
            for i in range(2):
                half = blocks[4 * i : 4 * i + 4].reshape(4 * rows, d)
                slots[first + 2 * which + i, : 4 * rows, :] = half
                if which == 0 or len(copies) > 1:
                    copies[which][i].start()

    attn_rows, extra_rows = attn_sums.shape[1] // 8, extra_sums.shape[0] // 8
    attn_copies = core_copies(0, attn_sums, attn_rows, 0)
    extra_copies = core_copies(1, extra_pair, extra_rows, 4)

    size, wide = 4 * extra_rows, extra_sums.shape[1]
    spread = [
        remote(slots.at[i, pl.ds(0, size), pl.ds(0, wide)], extra_sums.at[pl.ds(i * size, size)],
               cross_send.at[i], cross_recv.at[i], {"section": 1 - section})
        for i in range(2)
    ]
    keep = [
        pltpu.make_async_copy(
            slots.at[2 + i, pl.ds(0, size), pl.ds(0, wide)], extra_sums.at[pl.ds(i * size, size)], put_sem.at[1, i]
        )
        for i in range(2)
    ]

    def split_features():
        for copy in extra_copies[0]:
            copy.wait()
        for copies in attn_copies:
            for copy in copies:
                copy.wait()
        half = n2.shape[1] // 2
        for i in range(2):
            fetch = pltpu.make_async_copy(
                extra_pair.at[1, pl.ds(i * size, size)], slots.at[4 + i, pl.ds(0, size)], load_sem.at[3]
            )
            fetch.start()
            fetch.wait()
            total = slots[6 + i, :size, :].astype(f32) + slots[4 + i, :size, :].astype(f32)
            slots[i, :size, :half] = total[:, :half].astype(bf16)
            spread[i].start()
            slots[2 + i, :size, :half] = total[:, half:].astype(bf16)
            keep[i].start()

    terms(
        [(dqkv_ref, 0), (dqkv_ref, 1), (dqkv_ref, 2), (mixed_ref, 0)],
        [n1_ref, n1_ref, n1_ref, ga_ref], attn_copies, attn_rows, 0,
    )

    @pl.when(is_dec)
    def _():
        arrive("V2", "V1", "S4")
        terms(
            [(dcqkv_ref, 0), (dcqkv_ref, 1), (dcqkv_ref, 2), (cmixed_ref, 0), (gl_ref, 0)],
            [mc_ref, encoded_ref, encoded_ref, gac_ref, final_ref], extra_copies[:1], extra_rows, 4,
        )
        arrive("S3", "W3")
        split_features()

    @pl.when(is_enc)
    def _():
        arrive("V2", "V1", "W4", "W3", "S7", "V3", "W6", "V4", "W5", "V6", "V5", "W7", "V7")

    @pl.when(is_dec)
    def _():
        arrive("Q5", "V4", "Q6", "W4", "S6")
        arrive("V3", "S5", "V6", "W5", "Q7", "W6", "S7", "V5", "W7", "V7")

    for name in parts:
        for p in range(8):
            zz, yy, _ = place_of(parts[name][2], p)
            part_copy(name, 0, p, 4 * zz + 2 * yy + 1 - c, {"rows": me}).wait_recv()
            each_send(name, p, lambda copy: copy.wait_send())
    own_copies["S"].wait()
    own_copies["V"].wait()

    @pl.when(is_enc)
    def _():
        for copies in attn_copies:
            for copy in copies:
                copy.wait()
        for copy in spread:
            copy.wait_recv()

    @pl.when(is_dec)
    def _():
        for i in range(2):
            spread[i].wait_send()
            keep[i].wait()

    @pl.when(is_dec)
    def _():
        back_copy.wait_send()


def middle(cross_cnt, self_cnt, dec_cnt, x, y1, y2, n2, qkv, mixed, n1, encoded, target, gains, order, gu, attn_w, extra_w, feed_w, length):
    t, d = x.shape
    inner = attn_w.shape[0] // 4
    held = 8
    vm = pl.BlockSpec(memory_space=pltpu.VMEM)
    sm = pl.BlockSpec(memory_space=pltpu.SMEM)
    anywhere = pl.BlockSpec(memory_space=pl.ANY)
    attn_rows = inner // 4
    extra_rows = -(-5 * inner // 16 // 16) * 16
    return pl.pallas_call(
        functools.partial(mid_kernel, length),
        out_shape=(
            jax.ShapeDtypeStruct((16, t, d), bf16),
            jax.ShapeDtypeStruct((16, t, d), bf16),
            jax.ShapeDtypeStruct((t, d), f32),
            jax.ShapeDtypeStruct((8, d), f32),
            jax.ShapeDtypeStruct((2, 8 * attn_rows, d), bf16),
            jax.ShapeDtypeStruct((8 * extra_rows, -(-d // 2 // 128) * 128), bf16),
            jax.ShapeDtypeStruct((2, 8 * extra_rows, d), bf16),
        ),
        in_specs=[sm] * 3 + [vm] * 11 + [anywhere] * 4,
        out_specs=(anywhere,) * 2 + (vm,) * 2 + (anywhere,) * 3,
        scratch_shapes=[
            pltpu.VMEM((held,) + feed_w.shape[1:], bf16),
            pltpu.VMEM(gu.shape, f32),
            pltpu.VMEM(attn_w.shape, bf16),
            pltpu.VMEM((inner, d), bf16),
            pltpu.VMEM((t, d), f32),
            pltpu.VMEM((t, d), f32),
            pltpu.VMEM((t, d), f32),
            pltpu.VMEM((t, d), bf16),
            pltpu.VMEM((t, 3 * inner), bf16),
            pltpu.VMEM((t, inner), bf16),
            pltpu.VMEM((t, d), bf16),
            pltpu.VMEM((t, 3 * inner), bf16),
            pltpu.VMEM((t, 3 * inner), bf16),
            pltpu.VMEM((t, inner), bf16),
            pltpu.VMEM((t, inner), bf16),
            pltpu.VMEM((t, d), bf16),
            pltpu.VMEM((t, d), bf16),
            pltpu.VMEM((t, d), bf16),
            pltpu.VMEM((t, d), bf16),
            pltpu.VMEM((t, d), bf16),
            pltpu.VMEM((2, 5 * inner // 2, t), bf16),
            pltpu.SemaphoreType.DMA((4, 4, 8)),
            pltpu.SemaphoreType.DMA((4, 16)),
            pltpu.SemaphoreType.DMA((held,)),
            pltpu.SemaphoreType.DMA((4,)),
            pltpu.SemaphoreType.DMA((2,)),
            pltpu.SemaphoreType.DMA((1,)),
            pltpu.SemaphoreType.DMA((1,)),
            pltpu.SemaphoreType.DMA((2, 2)),
            pltpu.SemaphoreType.DMA((2, 2)),
            pltpu.SemaphoreType.DMA((2, 2)),
            pltpu.SemaphoreType.DMA((2,)),
            pltpu.SemaphoreType.DMA((2,)),
        ],
        compiler_params=pltpu.CompilerParams(
            vmem_limit_bytes=62 * 1024 * 1024, collective_id=2, has_side_effects=True
        ),
        cost_estimate=pl.CostEstimate(
            flops=4 * t * feed_w.size, bytes_accessed=2 * feed_w.size + 8 * gu.size, transcendentals=2 * gu.size
        ),
    )(cross_cnt, self_cnt, dec_cnt, x, y1, y2, n2, qkv, mixed, n1, encoded, target, gains, order, gu, attn_w, extra_w, feed_w)


def adam_step(weight, first_moment, second_moment, gradient, step_rate, weight_decay):
    first_new = 0.9 * first_moment + 0.1 * gradient
    second_new = 0.999 * second_moment + 0.001 * gradient * gradient
    first_fix = 1.0 - 0.9**STEP
    second_fix = 1.0 - 0.999**STEP
    update = first_new / first_fix / (jnp.sqrt(second_new / second_fix) + 1e-08)
    return (first_new, second_new, weight - step_rate * (update + weight_decay * weight))


def kinds_first(gathered, n, kinds, per):
    d = gathered.shape[-1]
    return gathered.reshape(n, kinds, per, d).transpose(1, 0, 2, 3).reshape(kinds * n * per, d)


def owners_first(left, right, n):
    t, k, units = left.shape
    grad = jnp.einsum("tku,td->kud", left, right, preferred_element_type=f32)
    return grad.reshape(k, n, units // n, -1).transpose(1, 0, 2, 3)


def local(
    block_input,
    lengths,
    targets,
    attention_weight,
    attention_first,
    attention_second,
    feed_weight,
    feed_first,
    feed_second,
    norm_gain,
    gain_first,
    gain_second,
    cross_weight,
    cross_first,
    cross_second,
    head_weight,
    head_first,
    head_second,
    cross_gain,
    cross_gain_first,
    cross_gain_second,
):
    n = lax.axis_size("rows")
    is_encoder = lax.axis_index("section") == 0
    micro, length, d = block_input.shape[1:]
    t = micro * length
    per = attention_weight.shape[1]
    f = feed_weight.shape[1]
    inner = per * n

    attn_own = attention_weight[0].astype(bf16).transpose(1, 0, 2).reshape(4 * per, d)
    feed_own = feed_weight[0].astype(bf16).transpose(1, 0, 2)
    half_rows = jnp.concatenate(
        [cross_weight.astype(bf16).transpose(1, 0, 2), head_weight.astype(bf16)[None]], axis=0
    )

    gains = norm_gain[0]
    gain_attn, gain_feed, gain_final = gains[0:1], gains[1:2], gains[2:3]
    gain_cross = cross_gain[None]
    x = block_input[0].reshape(t, d)
    enc_counts = lengths[0, :, 0]
    dec_counts = lengths[1, :, 0]
    zero_one = jnp.zeros((1,), jnp.int32)
    self_counts = jnp.concatenate([jnp.where(is_encoder, 0, 1).astype(jnp.int32)[None], enc_counts])
    cross_counts = jnp.concatenate([zero_one, enc_counts])
    target_column = targets.reshape(t, 1)

    def blank(maker):
        return jax.tree.map(lambda a: jnp.zeros(a.shape, a.dtype), jax.eval_shape(maker))

    emit = n != BLOCKS
    if emit:
        attn_all = lax.all_gather(attn_own, "rows", axis=0, tiled=True)
        attn_w = kinds_first(attn_all, n, 4, per)
        feed_all = lax.all_gather(feed_own.reshape(3 * f, d), "rows", axis=0, tiled=True)
        feed_w = kinds_first(feed_all, n, 3, f).reshape(3, BLOCKS, -1, d)
        feed_w = feed_w.transpose(1, 0, 2, 3).reshape(BLOCKS, -1, d)
        other_half = lax.ppermute(half_rows, "section", [(0, 1)])
        extra_own = jnp.concatenate([other_half, half_rows], axis=-1).reshape(5 * per, d)
        extra_all = lax.all_gather(extra_own, "rows", axis=0, tiled=True)
        n1, qkv, mixed, y1 = attend_fwd(self_counts, x, gain_attn, attn_w, length)

        def enc_feed():
            return feed_fwd(y1, gain_feed, gain_final, feed_w)

        enc_state = lax.cond(is_encoder, enc_feed, lambda: blank(enc_feed))
        encoded = lax.ppermute(enc_state[3], "section", [(0, 1)])
    else:
        units = jnp.arange(4 * inner, dtype=jnp.int32).reshape(n, 4, per)
        order = units.transpose(1, 0, 2).reshape(1, 4 * inner)
        units = jnp.arange(inner, dtype=jnp.int32).reshape(4, 2, 2, per)
        travel = units.transpose(2, 1, 0, 3).reshape(inner, 1)
        pad = -(5 * per) % 16
        half_own = jnp.pad(half_rows.reshape(5 * per, d // 2), ((0, pad), (0, 0)))
        outs = front(
            self_counts, order, x, gain_attn, gain_feed, gain_final,
            attn_own, feed_own.reshape(3 * f, d), half_own, length,
        )
        _, feed_w, extra_all, n1, qkv, mixed, y1 = outs[:7]
        enc_state, encoded, attn_w = outs[7:11], outs[11], outs[12]
        extra_all = extra_all[:, : 5 * per]
    extra_w = kinds_first(extra_all, n, 5, per)
    cross_w, head_w = extra_w[: 4 * inner], extra_w[4 * inner :]

    if emit:
        def dec_front():
            mc, cqkv, cmixed, z2 = attend_fwd(cross_counts, y1, gain_cross, cross_w, length, encoded)
            return feed_fwd(z2, gain_feed, gain_final, feed_w) + (mc, cqkv, cmixed, z2)

        def enc_pass():
            rest = jax.eval_shape(dec_front)[4:7]
            return tuple(enc_state) + tuple(jnp.zeros(a.shape, a.dtype) for a in rest) + (y1,)

        n2, gu, y2, final, mc, cqkv, cmixed, mid = lax.cond(is_encoder, enc_pass, dec_front)
        def dec_back():
            gl, up, loss = head_loss(dec_counts, final, head_w, target_column, length)
            feed_out = feed_bwd(up, mid, y2, gain_feed, gain_final, gu, feed_w, emit)
            ga_c, dqkv_c, gy1, gg_c, ge = attend_bwd(
                cross_counts, y1, gain_cross, feed_out[1], cqkv, cross_w, length, True
            )
            return (ge, gy1, feed_out[2], feed_out[0], *feed_out[3:], gl, ga_c, dqkv_c, gg_c, loss)

        back = lax.cond(is_encoder, lambda: blank(dec_back), dec_back)
        returned = lax.ppermute(back[0], "section", [(1, 0)])
        at = 6 if emit else 4
        gl, ga_c, dqkv_c, gg_c, loss = back[at:]

        def enc_back():
            feed_out = feed_bwd(returned, mid, y2, gain_feed, gain_final, gu, feed_w, emit)
            return (feed_out[1], feed_out[2], feed_out[0], *feed_out[3:])

        backs = lax.cond(is_encoder, enc_back, lambda: tuple(back[1:at]))
        gy1, gg_feed, gf = backs[:3]

        ga, dqkv, gx, gg_attn = attend_bwd(self_counts, x, gain_attn, gy1, qkv, attn_w, length)
        tiny = jnp.concatenate(
            [gg_attn, gg_feed, gg_c, jnp.broadcast_to(loss, (1, d)), jnp.zeros((3, d), f32)], axis=0
        )
    else:
        gain_rows = jnp.concatenate([gains, gain_cross], axis=0)
        n2, gu, y2 = enc_state[:3]
        (
            n2_all, gf_all, gx, tiny, attn_terms, extra_terms, _,
        ) = middle(
            cross_counts, self_counts, dec_counts, x, y1, y2, n2, qkv, mixed, n1, encoded, target_column,
            gain_rows, travel, gu, attn_w, extra_w, feed_w, length,
        )

    half = d // 2
    if emit:
        extra_part = jnp.concatenate(
            [
                owners_first(dqkv_c[:, None, :inner], mc, n),
                owners_first(dqkv_c[:, inner:].reshape(t, 2, inner), encoded, n),
                owners_first(cmixed[:, None], ga_c, n),
                owners_first(gl[:, None], final, n),
            ],
            axis=1,
        ).astype(bf16)
        extra_sum = lax.psum_scatter(
            extra_part.reshape(n * 5 * per, d), "rows", scatter_dimension=0, tiled=True
        )
        extra_first = lax.ppermute(extra_sum[:, :half], "section", [(1, 0)])
        extra_grad = jnp.where(is_encoder, extra_first, extra_sum[:, half:]).astype(f32)
        extra_grad = extra_grad.reshape(5, per, half)

        attn_part = jnp.concatenate(
            [
                owners_first(dqkv.reshape(t, 3, inner), n1, n),
                owners_first(mixed[:, None], ga, n),
            ],
            axis=1,
        ).astype(bf16)
        attn_sum = lax.psum_scatter(
            attn_part.reshape(n * 4 * per, d), "rows", scatter_dimension=0, tiled=True
        ).astype(f32)
        dgu, hid = backs[3], backs[4]
        nb, _, fb = hid.shape
        left = dgu.reshape(nb, t, 2, fb).transpose(1, 2, 0, 3).reshape(t, 2, nb * fb)
        hid = hid.transpose(1, 0, 2).reshape(t, 1, nb * fb)
        feed_part = jnp.concatenate(
            [owners_first(left, n2, n), owners_first(hid, gf, n)], axis=1
        ).astype(bf16)
        feed_grad = lax.psum_scatter(
            feed_part.reshape(n * 3 * f, d), "rows", scatter_dimension=0, tiled=True
        ).astype(f32)
        tiny_sum = jnp.sum(lax.all_gather(tiny, "rows", axis=0), axis=0)
    else:
        feed_grad, attn_sum, extra_sum, tiny_sum = tail(
            tiny, attn_terms, extra_terms, feed_own.reshape(3 * f, d), n2_all, gf_all
        )
        extra_grad = extra_sum[: 5 * per, :half].reshape(5, per, half)
    tiny_dec = lax.ppermute(tiny_sum[3:5], "section", [(1, 0)])
    tiny_dec = jnp.where(is_encoder, tiny_dec, tiny_sum[3:5])
    attn_grad = attn_sum.reshape(4, per, d).transpose(1, 0, 2)
    feed_grad = feed_grad.reshape(3, f, d).transpose(1, 0, 2)
    cross_gain_total = tiny_dec[0]
    loss_total = tiny_dec[1, 0]

    attention_new = adam_step(
        attention_weight, attention_first, attention_second, attn_grad[None], 0.05, 0.1
    )
    feed_new = adam_step(feed_weight, feed_first, feed_second, feed_grad[None], 0.05, 0.1)
    gain_new = adam_step(norm_gain, gain_first, gain_second, tiny_sum[None, 0:3], 0.5, 0.0)
    cross_new = adam_step(
        cross_weight, cross_first, cross_second, extra_grad[:4].transpose(1, 0, 2), 0.05, 0.1
    )
    head_new = adam_step(head_weight, head_first, head_second, extra_grad[4], 0.05, 0.1)
    cross_gain_new = adam_step(
        cross_gain, cross_gain_first, cross_gain_second, cross_gain_total, 0.5, 0.0
    )
    return (
        gx.reshape(1, micro, length, d),
        loss_total,
        *attention_new,
        *feed_new,
        *gain_new,
        *cross_new,
        *head_new,
        *cross_gain_new,
    )


def solution(mesh):
    by_row = P("section", "rows", None, None)
    gain = P("section", None, None)
    cross = P("rows", None, "section")
    head = P("rows", "section")
    weights = (by_row,) * 6 + (gain,) * 3 + (cross,) * 3 + (head,) * 3 + (P(),) * 3
    tokens = P("section", None, "rows", None)
    return jax.shard_map(
        local,
        mesh=mesh,
        in_specs=(tokens, P(None, None, "rows"), P(None, "rows")) + weights,
        out_specs=(tokens, P()) + weights,
        check_vma=False,
    )
```

```python
import functools

import jax
import jax.numpy as jnp
from jax import lax
from jax.experimental import pallas as pl
from jax.experimental.pallas import tpu as pltpu
from jax.sharding import PartitionSpec as P

HD = 64
STEP = 10
PAIR = 2 * HD
BLOCKS = 16
VMEM_BYTES = 52 * 1024 * 1024

bf16 = jnp.bfloat16
f32 = jnp.float32
masked_value = -1000000000.0
scale = HD ** (-0.5)


def dot(a, b):
    return lax.dot_general(a, b, (((1,), (0,)), ((), ())), preferred_element_type=f32)


def dot_last(a, b):
    return lax.dot_general(a, b, (((1,), (1,)), ((), ())), preferred_element_type=f32)


def dot_rows(a, b):
    return lax.dot_general(a, b, (((0,), (0,)), ((), ())), preferred_element_type=f32)


def unit_rows(v):
    r = lax.rsqrt(jnp.mean(v * v, axis=-1, keepdims=True) + 1e-06)
    return r, v * r


def norm_back(v, gain, up):
    r, n = unit_rows(v)
    g = up * gain
    back = r * (g - n * jnp.mean(g * n, axis=-1, keepdims=True))
    return back, jnp.sum(up * n, axis=0, keepdims=True)


def gelu_parts(x):
    c = 0.7978845608028654
    t = jnp.tanh(c * (x + 0.044715 * (x * x * x)))
    act = 0.5 * x * (1.0 + t)
    slope = 0.5 * (1.0 + t) + 0.5 * x * (1.0 - t * t) * (c * (1.0 + 3.0 * 0.044715 * (x * x)))
    return act, slope


def low_half(length):
    return lax.broadcasted_iota(jnp.int32, (length, PAIR), 1) < HD


def stack_pair(m, low):
    zero = jnp.zeros_like(m)
    return jnp.concatenate([jnp.where(low, m, zero), jnp.where(low, zero, m)], axis=0)


def allowed_twice(cnt_ref, s, length):
    row = lax.broadcasted_iota(jnp.int32, (length, length), 0)
    col = lax.broadcasted_iota(jnp.int32, (length, length), 1)
    limit = jnp.where(cnt_ref[0] == 1, row + 1, cnt_ref[1 + s])
    one = jnp.where(col < limit, 1, 0)
    return jnp.concatenate([one, one], axis=0) == 1


def soft_pair(q2, k, allowed):
    s = dot_last(q2, k) * scale
    s = jnp.where(allowed, s, masked_value)
    e = jnp.exp(s - jnp.max(s, axis=-1, keepdims=True))
    return e / jnp.sum(e, axis=-1, keepdims=True)


def head_columns(inner, h):
    return [slice(j * inner + h * PAIR, j * inner + (h + 1) * PAIR) for j in range(3)]


def heads_fwd(cnt_ref, qkv_ref, o_ref, length):
    t, inner = o_ref.shape
    low = low_half(length)
    for s in range(t // length):
        allowed = allowed_twice(cnt_ref, s, length)
        rows = slice(s * length, (s + 1) * length)
        for h in range(inner // PAIR):
            cols = head_columns(inner, h)
            q2 = stack_pair(qkv_ref[rows, cols[0]], low)
            p = soft_pair(q2, qkv_ref[rows, cols[1]], allowed).astype(bf16)
            wide = jnp.concatenate([p[:length], p[length:]], axis=1)
            o_ref[rows, cols[0]] = dot(wide, stack_pair(qkv_ref[rows, cols[2]], low)).astype(bf16)


def heads_bwd(cnt_ref, qkv_ref, do_ref, dqkv_ref, length):
    t, inner = do_ref.shape
    low = low_half(length)
    for s in range(t // length):
        allowed = allowed_twice(cnt_ref, s, length)
        rows = slice(s * length, (s + 1) * length)
        for h in range(inner // PAIR):
            cols = head_columns(inner, h)
            q2 = stack_pair(qkv_ref[rows, cols[0]], low)
            k = qkv_ref[rows, cols[1]]
            p = soft_pair(q2, k, allowed)
            do2 = stack_pair(do_ref[rows, cols[0]], low)
            dp = dot_last(do2, qkv_ref[rows, cols[2]])
            ds = p * (dp - jnp.sum(dp * p, axis=-1, keepdims=True))
            ds = jnp.where(allowed, ds, 0.0).astype(bf16)
            wide = jnp.concatenate([ds[:length], ds[length:]], axis=1)
            dqkv_ref[rows, cols[0]] = (dot(wide, stack_pair(k, low)) * scale).astype(bf16)
            dqkv_ref[rows, cols[1]] = (dot_rows(ds, q2) * scale).astype(bf16)
            dqkv_ref[rows, cols[2]] = dot_rows(p.astype(bf16), do2).astype(bf16)


def loss_back(cnt_ref, f_ref, w_ref, target_ref, gl_ref, length):
    logits = dot_last(f_ref[...], w_ref[...])
    top = jnp.max(logits, axis=-1, keepdims=True)
    log_total = top + jnp.log(jnp.sum(jnp.exp(logits - top), axis=-1, keepdims=True))
    hit = lax.broadcasted_iota(jnp.int32, logits.shape, 1) == target_ref[...]
    picked = jnp.sum(jnp.where(hit, logits, 0.0), axis=-1, keepdims=True)
    probs = jnp.exp(logits - log_total) - jnp.where(hit, 1.0, 0.0)
    total = jnp.zeros((1, 1), f32)
    for s in range(logits.shape[0] // length):
        rows = slice(s * length, (s + 1) * length)
        valid = lax.broadcasted_iota(jnp.int32, (length, 1), 0) < cnt_ref[s]
        total += jnp.sum(
            jnp.where(valid, log_total[rows] - picked[rows], 0.0), axis=0, keepdims=True
        )
        gl_ref[rows, :] = jnp.where(valid, probs[rows], 0.0).astype(bf16)
    return total


def attend_fwd_kernel(cross, length, cnt_ref, x_ref, gain_ref, *refs):
    if cross:
        src_ref, w_ref, n_ref, qkv_ref, o_ref, y_ref = refs
    else:
        w_ref, n_ref, qkv_ref, o_ref, y_ref = refs
    inner = w_ref.shape[0] // 4
    x = x_ref[...].astype(f32)
    n = (unit_rows(x)[1] * gain_ref[...]).astype(bf16)
    n_ref[...] = n
    if cross:
        qkv_ref[:, :inner] = dot_last(n, w_ref[:inner, :]).astype(bf16)
        qkv_ref[:, inner:] = dot_last(src_ref[...], w_ref[inner : 3 * inner, :]).astype(bf16)
    else:
        qkv_ref[...] = dot_last(n, w_ref[: 3 * inner, :]).astype(bf16)
    heads_fwd(cnt_ref, qkv_ref, o_ref, length)
    y_ref[...] = x + dot(o_ref[...], w_ref[3 * inner :, :])


def attend_fwd(counts, x, gain, w, length, source=None):
    t, d = x.shape
    inner = w.shape[0] // 4
    ins = [counts, x, gain] + ([] if source is None else [source]) + [w]
    vm = pl.BlockSpec(memory_space=pltpu.VMEM)
    return pl.pallas_call(
        functools.partial(attend_fwd_kernel, source is not None, length),
        out_shape=(
            jax.ShapeDtypeStruct((t, d), bf16),
            jax.ShapeDtypeStruct((t, 3 * inner), bf16),
            jax.ShapeDtypeStruct((t, inner), bf16),
            jax.ShapeDtypeStruct((t, d), f32),
        ),
        in_specs=[pl.BlockSpec(memory_space=pltpu.SMEM)] + [vm] * (len(ins) - 1),
        out_specs=(vm,) * 4,
        compiler_params=pltpu.CompilerParams(vmem_limit_bytes=VMEM_BYTES),
        cost_estimate=pl.CostEstimate(
            flops=2 * t * d * inner * 4 + 8 * t * length * inner,
            bytes_accessed=w.size * 2 + t * d * 10,
            transcendentals=t * length * 6,
        ),
    )(*ins)


def attend_bwd_kernel(cross, length, cnt_ref, x_ref, gain_ref, gy_ref, qkv_ref, w_ref, *refs):
    if cross:
        ga_ref, dqkv_ref, gx_ref, gg_ref, gs_ref, do_ref = refs
    else:
        ga_ref, dqkv_ref, gx_ref, gg_ref, do_ref = refs
    inner = w_ref.shape[0] // 4
    ga = gy_ref[...].astype(bf16)
    ga_ref[...] = ga
    do_ref[...] = dot_last(ga, w_ref[3 * inner :, :]).astype(bf16)
    heads_bwd(cnt_ref, qkv_ref, do_ref, dqkv_ref, length)
    if cross:
        up = dot(dqkv_ref[:, :inner], w_ref[:inner, :])
        gs_ref[...] = dot(dqkv_ref[:, inner:], w_ref[inner : 3 * inner, :]).astype(bf16)
    else:
        up = dot(dqkv_ref[...], w_ref[: 3 * inner, :])
    back, gg_ref[...] = norm_back(x_ref[...].astype(f32), gain_ref[...], up)
    gx_ref[...] = gy_ref[...] + back


def attend_bwd(counts, x, gain, gy, qkv, w, length, cross=False):
    t, d = x.shape
    inner = w.shape[0] // 4
    vm = pl.BlockSpec(memory_space=pltpu.VMEM)
    outs = [
        jax.ShapeDtypeStruct((t, d), bf16),
        jax.ShapeDtypeStruct((t, 3 * inner), bf16),
        jax.ShapeDtypeStruct((t, d), f32),
        jax.ShapeDtypeStruct((1, d), f32),
    ]
    if cross:
        outs.append(jax.ShapeDtypeStruct((t, d), bf16))
    return pl.pallas_call(
        functools.partial(attend_bwd_kernel, cross, length),
        out_shape=tuple(outs),
        in_specs=[pl.BlockSpec(memory_space=pltpu.SMEM)] + [vm] * 5,
        out_specs=(vm,) * len(outs),
        scratch_shapes=[pltpu.VMEM((t, inner), bf16)],
        compiler_params=pltpu.CompilerParams(vmem_limit_bytes=VMEM_BYTES),
        cost_estimate=pl.CostEstimate(
            flops=2 * t * d * inner * 4 + 20 * t * length * inner,
            bytes_accessed=w.size * 2 + t * d * 16,
            transcendentals=t * length * 6,
        ),
    )(counts, x, gain, gy, qkv, w)


def feed_fwd_kernel(y_ref, g_in_ref, g_out_ref, w_ref, n_ref, gu_ref, y2_ref, f_ref):
    i = pl.program_id(0)
    f = w_ref.shape[1] // 3

    @pl.when(i == 0)
    def _():
        y = y_ref[...]
        n_ref[...] = (unit_rows(y)[1] * g_in_ref[...]).astype(bf16)
        y2_ref[...] = y

    gu = dot_last(n_ref[...], w_ref[0, : 2 * f, :])
    gu_ref[0] = gu
    hidden = (gelu_parts(gu[:, :f])[0] * gu[:, f:]).astype(bf16)
    y2_ref[...] += dot(hidden, w_ref[0, 2 * f :, :])

    @pl.when(i == pl.num_programs(0) - 1)
    def _():
        f_ref[...] = (unit_rows(y2_ref[...])[1] * g_out_ref[...]).astype(bf16)


def feed_fwd(y, gain_in, gain_out, w):
    t, d = y.shape
    nb, rows, _ = w.shape
    f = rows // 3
    whole = lambda *shape: pl.BlockSpec(shape, lambda i: (0,) * len(shape))
    part = lambda *shape: pl.BlockSpec((1,) + shape, lambda i: (i, 0, 0))
    return pl.pallas_call(
        feed_fwd_kernel,
        grid=(nb,),
        out_shape=(
            jax.ShapeDtypeStruct((t, d), bf16),
            jax.ShapeDtypeStruct((nb, t, 2 * f), f32),
            jax.ShapeDtypeStruct((t, d), f32),
            jax.ShapeDtypeStruct((t, d), bf16),
        ),
        in_specs=[whole(t, d), whole(1, d), whole(1, d), part(rows, d)],
        out_specs=(whole(t, d), part(t, 2 * f), whole(t, d), whole(t, d)),
        compiler_params=pltpu.CompilerParams(vmem_limit_bytes=VMEM_BYTES),
        cost_estimate=pl.CostEstimate(
            flops=2 * t * d * rows * nb,
            bytes_accessed=w.size * 2 + t * d * 12 + nb * t * f * 8,
            transcendentals=nb * t * f,
        ),
    )(y, gain_in, gain_out, w)


def feed_bwd_kernel(emit, up_ref, y_ref, y2_ref, g_in_ref, g_out_ref, gu_ref, w_ref, *refs):
    if emit:
        gf_ref, gy_ref, gg_ref, dgu_ref, hid_ref, last_ref = refs
    else:
        gf_ref, gy_ref, gg_ref, last_ref = refs
    i = pl.program_id(0)
    f = w_ref.shape[1] // 3

    @pl.when(i == 0)
    def _():
        back, gain_grad = norm_back(y2_ref[...], g_out_ref[...], up_ref[...].astype(f32))
        gg_ref[1:2, :] = gain_grad
        last_ref[...] = back
        gf_ref[...] = back.astype(bf16)
        gy_ref[...] = jnp.zeros_like(gy_ref)

    gh = dot_last(gf_ref[...], w_ref[0, 2 * f :, :])
    act, slope = gelu_parts(gu_ref[0, :, :f])
    u = gu_ref[0, :, f:]
    dg = (gh * u * slope).astype(bf16)
    du = (gh * act).astype(bf16)
    if emit:
        dgu_ref[0, :, :f] = dg
        dgu_ref[0, :, f:] = du
        hid_ref[0] = (act * u).astype(bf16)
    gy_ref[...] += dot(dg, w_ref[0, :f, :]) + dot(du, w_ref[0, f : 2 * f, :])

    @pl.when(i == pl.num_programs(0) - 1)
    def _():
        back, gain_grad = norm_back(y_ref[...], g_in_ref[...], gy_ref[...])
        gg_ref[0:1, :] = gain_grad
        gy_ref[...] = last_ref[...] + back


def feed_bwd(up, y, y2, gain_in, gain_out, gu, w, emit):
    t, d = y.shape
    nb, rows, _ = w.shape
    f = rows // 3
    whole = lambda *shape: pl.BlockSpec(shape, lambda i: (0,) * len(shape))
    part = lambda *shape: pl.BlockSpec((1,) + shape, lambda i: (i, 0, 0))
    outs = [
        jax.ShapeDtypeStruct((t, d), bf16),
        jax.ShapeDtypeStruct((t, d), f32),
        jax.ShapeDtypeStruct((2, d), f32),
    ]
    specs = [whole(t, d), whole(t, d), whole(2, d)]
    if emit:
        outs += [
            jax.ShapeDtypeStruct((nb, t, 2 * f), bf16),
            jax.ShapeDtypeStruct((nb, t, f), bf16),
        ]
        specs += [part(t, 2 * f), part(t, f)]
    return pl.pallas_call(
        functools.partial(feed_bwd_kernel, emit),
        grid=(nb,),
        out_shape=tuple(outs),
        in_specs=[whole(t, d)] * 3 + [whole(1, d)] * 2 + [part(t, 2 * f), part(rows, d)],
        out_specs=tuple(specs),
        scratch_shapes=[pltpu.VMEM((t, d), f32)],
        compiler_params=pltpu.CompilerParams(vmem_limit_bytes=VMEM_BYTES),
        cost_estimate=pl.CostEstimate(
            flops=2 * t * d * rows * nb,
            bytes_accessed=w.size * 2 + t * d * 18 + nb * t * f * 8,
            transcendentals=nb * t * f,
        ),
    )(up, y, y2, gain_in, gain_out, gu, w)


def head_kernel(length, cnt_ref, f_ref, w_ref, target_ref, gl_ref, up_ref, loss_ref):
    loss_ref[...] = loss_back(cnt_ref, f_ref, w_ref, target_ref, gl_ref, length)
    up_ref[...] = dot(gl_ref[...], w_ref[...])


def head_loss(counts, final, w, target, length):
    t, d = final.shape
    v = w.shape[0]
    vm = pl.BlockSpec(memory_space=pltpu.VMEM)
    return pl.pallas_call(
        functools.partial(head_kernel, length),
        out_shape=(
            jax.ShapeDtypeStruct((t, v), bf16),
            jax.ShapeDtypeStruct((t, d), f32),
            jax.ShapeDtypeStruct((1, 1), f32),
        ),
        in_specs=[pl.BlockSpec(memory_space=pltpu.SMEM), vm, vm, vm],
        out_specs=(vm,) * 3,
        compiler_params=pltpu.CompilerParams(vmem_limit_bytes=VMEM_BYTES),
        cost_estimate=pl.CostEstimate(
            flops=4 * t * d * v, bytes_accessed=w.size * 2 + t * d * 6, transcendentals=t * v * 2
        ),
    )(counts, final, w, target)


def tail_kernel(
    tiny_ref, attn_terms, extra_terms, w_ref, n_all, g_all,
    feed_ref, attn_ref, extra_ref, total_ref,
    tinies, n_buf, g_buf, *rest,
):
    attn_bufs, extra_bufs = rest[:8], rest[8:16]
    tiny_send, tiny_recv, rs_send, rs_recv, pair_sem = rest[16:]
    me = lax.axis_index("rows")
    z, y, c = me // 4, (me // 2) % 2, me % 2
    high = z // 2
    inner = (z + high) % 2
    f = w_ref.shape[0] // 3
    d = w_ref.shape[1]
    core_peer, y_peer = me + 1 - 2 * c, me + 2 - 4 * y
    toward = me + 4 - 8 * high
    outward = me - 4 + 8 * high
    mesh_id = pl.DeviceIdType.MESH

    def remote(src, dst, send, recv, where):
        return pltpu.make_async_remote_copy(
            src_ref=src, dst_ref=dst, send_sem=send, recv_sem=recv,
            device_id=where, device_id_type=mesh_id,
        )

    def pair_copies(p):
        slot = p % 2
        return [
            pltpu.make_async_copy(whole.at[pl.ds(2 * p, 2)], buf.at[slot], pair_sem.at[k, slot])
            for k, (whole, buf) in enumerate([(n_all, n_buf), (g_all, g_buf)])
        ]

    for copy in pair_copies(0):
        copy.start()

    barrier = pltpu.get_barrier_semaphore()

    def greet(where):
        pl.semaphore_signal(barrier, inc=1, device_id=where, device_id_type=mesh_id)

    greet({"rows": core_peer})
    greet({"rows": y_peer})
    greet({"rows": toward})

    @pl.when(inner == 1)
    def _():
        greet({"rows": outward})

    pl.semaphore_wait(barrier, 3 + inner)

    def place_of(p):
        j, other = [(0, 0), (1, 0), (0, 1), (2, 0), (1, 1), (3, 0), (2, 1), (3, 1)][p]
        zz = [z, z + 1 - 2 * (z % 2), 2 - high, 3 - 3 * high][j]
        yy = y + other - 2 * other * y
        return zz, yy, other

    def tiny_copy(kind, p, s, where):
        src = tiny_ref if p == 0 else tinies.at[s]
        return remote(src, tinies.at[s], tiny_send.at[kind, p], tiny_recv.at[s], where)

    def each_tiny(p, act):
        zz, yy, other = place_of(p)
        s = 4 * zz + 2 * yy + c
        if other == 0:

            @pl.when((zz <= z) & (z < 3))
            def _():
                act(tiny_copy(0, p, s, {"rows": me + 4}))

            @pl.when((zz >= z) & (z > 0))
            def _():
                act(tiny_copy(1, p, s, {"rows": me - 4}))

            act(tiny_copy(2, p, s, {"rows": y_peer}))
        act(tiny_copy(3, p, s, {"rows": core_peer}))

    def tiny_arrive(p):
        zz, yy, _ = place_of(p)
        tiny_copy(0, p, 4 * zz + 2 * yy + c, {"rows": me}).wait_recv()
        each_tiny(p, lambda copy: copy.start())

    far_out, far_in = 3 - 3 * high, 2 - high
    beside = (1 - inner) * (1 + high) + inner * 3 * high

    def summed(bufs, k, terms, result):
        part, four, from_y, from_far, from_near, from_cross, from_out, cross_out = bufs

        def hop(i, src, dst, where):
            return remote(src, dst, rs_send.at[k, i], rs_recv.at[k, i], {"rows": where})

        ys = [
            hop(1 + i, part.at[(1 - y) * 4 + at], from_y.at[at], y_peer)
            for i, at in enumerate([far_out, far_in, beside, z])
        ]
        fars = [hop(5 + i, four.at[at], from_far.at[i], toward) for i, at in enumerate([far_out, far_in])]
        near = hop(7, four.at[beside], from_near, toward)
        crosses = [hop(8 + i, four.at[at], from_cross.at[i], toward) for i, at in enumerate([far_out, far_in])]
        out = hop(10, cross_out, from_out, outward)

        def start():
            total = terms[...]
            if total.ndim == 3:
                total = (total[0].astype(f32) + total[1].astype(f32)).astype(bf16)
            part[...] = total.reshape(part.shape)
            ys[0].start()
            ys[1].start()

        def rest():
            ys[2].start()
            ys[3].start()

        def add_y(i, at):
            ys[i].wait_recv()
            four[at] = (part[4 * y + at].astype(f32) + from_y[at].astype(f32)).astype(bf16)

        def far(i):
            def stage():
                add_y(i, [far_out, far_in][i])
                pl.when(inner == 0)(fars[i].start)

            return stage

        def cross(i):
            def stage():
                @pl.when(inner == 1)
                def _():
                    at = [far_out, far_in][i]
                    fars[i].wait_recv()
                    four[at] = (four[at].astype(f32) + from_far[i].astype(f32)).astype(bf16)
                    crosses[i].start()

            return stage

        def home():
            add_y(2, beside)
            pl.when(inner == 0)(near.start)

        def own():
            add_y(3, z)

        def leave():
            @pl.when(inner == 1)
            def _():
                crosses[0].wait_recv()
                cross_out[...] = (four[beside].astype(f32) + from_cross[0].astype(f32)).astype(bf16)
                out.start()

        def last_inner():
            @pl.when(inner == 1)
            def _():
                crosses[1].wait_recv()
                near.wait_recv()
                result(four[z].astype(f32) + from_cross[1].astype(f32) + from_near[...].astype(f32))

        def last_outer():
            @pl.when(inner == 0)
            def _():
                out.wait_recv()
                result(four[z].astype(f32) + from_out[...].astype(f32))

        def settle():
            for copy in ys:
                copy.wait_send()

            @pl.when(inner == 0)
            def _():
                for copy in [*fars, near]:
                    copy.wait_send()

            @pl.when(inner == 1)
            def _():
                for copy in [*crosses, out]:
                    copy.wait_send()

        return {
            "start": start, "rest": rest, "0": far(0), "1": far(1), "2": cross(0), "3": cross(1),
            "4": home, "5": own, "6": leave, "7": last_inner, "8": last_outer, "settle": settle,
        }

    def attn_result(value):
        attn_ref[...] = value

    def extra_result(value):
        extra_ref[...] = value

    attn = summed(attn_bufs, 0, attn_terms, attn_result)
    extra = summed(extra_bufs, 1, extra_terms, extra_result)

    def wgrad(p):
        if p < 7:
            for copy in pair_copies(p + 1):
                copy.start()
        for copy in pair_copies(p):
            copy.wait()
        n_rows = n_buf[p % 2].reshape(-1, d)
        g_rows = g_buf[p % 2].reshape(-1, d)
        gu = dot_last(w_ref[: 2 * f, :], n_rows)
        gh = dot_last(w_ref[2 * f :, :], g_rows)
        act, slope = gelu_parts(gu[:f])
        up = gu[f:]
        dg = (gh * up * slope).astype(bf16)
        du = (gh * act).astype(bf16)
        hid = (act * up).astype(bf16)
        from_n = dot(jnp.concatenate([dg, du], axis=0), n_rows)
        from_g = dot(hid, g_rows)
        if p == 0:
            feed_ref[: 2 * f, :] = from_n
            feed_ref[2 * f :, :] = from_g
        else:
            feed_ref[: 2 * f, :] += from_n
            feed_ref[2 * f :, :] += from_g

    def add_tinies():
        for p in range(8):
            zz, yy, _ = place_of(p)
            tiny_copy(0, p, 4 * zz + 2 * yy + 1 - c, {"rows": me}).wait_recv()
        total = tinies[0]
        for s in range(1, 16):
            total += tinies[s]
        total_ref[...] = total

    tinies[me] = tiny_ref[...]
    each_tiny(0, lambda copy: copy.start())
    attn["start"]()
    extra["start"]()
    attn["rest"]()
    extra["rest"]()

    for step in TAIL_STEPS:
        if step[0] == "w":
            wgrad(int(step[1]))
        elif step[0] == "t":
            tiny_arrive(int(step[1]))
        elif step[0] == "a":
            attn[step[1]]()
        elif step[0] == "x":
            extra[step[1]]()
        else:
            add_tinies()

    for p in range(8):
        each_tiny(p, lambda copy: copy.wait_send())
    attn["settle"]()
    extra["settle"]()


TAIL_STEPS = (
    ("a0", "w0", "a1", "t1", "t2", "w1", "a2", "x0", "t3", "t4", "a3", "w2", "x1", "w3", "x2", "a4", "t5", "t6", "w4")
    + ("a5", "x3", "a6", "a7", "w5", "x4", "a8", "t7", "w6", "x5", "x6", "sum", "w7", "x7", "x8")
)


def tail(tiny, attn_terms, extra_terms, w_own, n_all, g_all):
    t, d = n_all.shape[1:]
    rows = w_own.shape[0]
    per, more = attn_terms.shape[1] // 8, extra_terms.shape[0] // 8

    def sums(r, d):
        return [
            pltpu.VMEM(shape + (r, d), bf16)
            for shape in [(8,), (4,), (4,), (2,), (), (2,), (), ()]
        ]

    vm = pl.BlockSpec(memory_space=pltpu.VMEM)
    anywhere = pl.BlockSpec(memory_space=pl.ANY)
    return pl.pallas_call(
        tail_kernel,
        out_shape=(
            jax.ShapeDtypeStruct((rows, d), f32),
            jax.ShapeDtypeStruct((per, d), f32),
            jax.ShapeDtypeStruct((more, extra_terms.shape[1]), f32),
            jax.ShapeDtypeStruct(tiny.shape, f32),
        ),
        in_specs=[vm] * 4 + [anywhere] * 2,
        out_specs=(vm,) * 4,
        scratch_shapes=[
            pltpu.VMEM((16,) + tiny.shape, f32),
            pltpu.VMEM((2, 2, t, d), bf16),
            pltpu.VMEM((2, 2, t, d), bf16),
            *sums(per, d),
            *sums(more, extra_terms.shape[1]),
            pltpu.SemaphoreType.DMA((4, 8)),
            pltpu.SemaphoreType.DMA((16,)),
            pltpu.SemaphoreType.DMA((2, 11)),
            pltpu.SemaphoreType.DMA((2, 11)),
            pltpu.SemaphoreType.DMA((2, 2)),
        ],
        compiler_params=pltpu.CompilerParams(
            vmem_limit_bytes=60 * 1024 * 1024, collective_id=0, has_side_effects=True
        ),
        cost_estimate=pl.CostEstimate(
            flops=2 * t * 16 * d * rows * 2, bytes_accessed=16 * t * d * 4, transcendentals=16 * t * rows
        ),
    )(tiny, attn_terms, extra_terms, w_own, n_all, g_all)


def front_kernel(
    length, cnt_ref, order_ref, x_ref, g_attn_ref, g_feed_ref, g_final_ref,
    attn_own, feed_own, half_own,
    attn_all, feed_all, extra_all,
    n1_ref, qkv_ref, mixed_ref, y1_ref, n2_ref, gu_ref, y2_ref, enc_ref, arrived_ref, sorted_ref,
    w_attn, w_feed, place, wide_buf, first_own, second_own, extra_own,
    send_sem, recv_sem, own_sem, load_sem, x_send, x_recv,
):
    section = lax.axis_index("section")
    me = lax.axis_index("rows")
    z, y, c = me // 4, (me // 2) % 2, me % 2
    core_peer, y_peer = me + 1 - 2 * c, me + 2 - 4 * y
    mesh_id = pl.DeviceIdType.MESH
    inner = mixed_ref.shape[1]
    f = feed_own.shape[0] // 3

    barrier = pltpu.get_barrier_semaphore()

    def greet(where):
        pl.semaphore_signal(barrier, inc=1, device_id=where, device_id_type=mesh_id)

    greet({"rows": core_peer})
    greet({"rows": y_peer})
    greet({"section": 1 - section})

    @pl.when(z > 0)
    def _():
        greet({"rows": me - 4})

    @pl.when(z < 3)
    def _():
        greet({"rows": me + 4})

    own_copies = [
        pltpu.make_async_copy(own, whole.at[me], own_sem.at[k])
        for k, (own, whole) in enumerate(
            [(attn_own, attn_all), (feed_own, feed_all), (extra_own, extra_all)]
        )
    ]
    load_half = pltpu.make_async_copy(half_own, second_own, own_sem.at[3])
    own_copies[0].start()
    own_copies[1].start()

    @pl.when(section == 1)
    def _():
        load_half.start()

    pl.semaphore_wait(barrier, 4 + (z + z // 2) % 2)

    def remote(src, dst, send, recv, where):
        return pltpu.make_async_remote_copy(
            src_ref=src, dst_ref=dst, send_sem=send, recv_sem=recv,
            device_id=where, device_id_type=mesh_id,
        )

    kinds = [pl.ds(k * f, f) for k in range(3)]
    cuts = [pl.ds(k * (extra_own.shape[0] // 2), extra_own.shape[0] // 2) for k in range(2)]
    parts = {
        "A": (0, attn_all, None, 2, attn_own),
        "G": (1, feed_all, kinds[0], 1, feed_own.at[kinds[0]]),
        "U": (2, feed_all, kinds[1], 1, feed_own.at[kinds[1]]),
        "O": (3, feed_all, kinds[2], 1, feed_own.at[kinds[2]]),
        "X": (4, extra_all, cuts[0], 1, extra_own.at[cuts[0]]),
        "Y": (5, extra_all, cuts[1], 2, extra_own.at[cuts[1]]),
    }

    def place_of(route, p):
        if route == 1:
            j, other = [(0, 0), (1, 0), (0, 1), (2, 0), (1, 1), (3, 0), (2, 1), (3, 1)][p]
        else:
            j, other = p // 2, p % 2
        zz = [z, z + 1 - 2 * (z % 2), 2 - z // 2, 3 - 3 * (z // 2)][j]
        yy = y + other - 2 * other * y
        return zz, yy, other

    def part_copy(name, kind, p, s, where):
        k, whole, rows, _, own = parts[name]
        dst = whole.at[s] if rows is None else whole.at[s, rows]
        return remote(own if p == 0 else dst, dst, send_sem.at[k, kind, p], recv_sem.at[k, s], where)

    def each_send(name, p, act, ways="zyc"):
        route = parts[name][3]
        zz, yy, other = place_of(route, p)
        s = 4 * zz + 2 * yy + c
        if "z" in ways and (route == 2 or other == 0):

            @pl.when((zz <= z) & (z < 3))
            def _():
                act(part_copy(name, 0, p, s, {"rows": me + 4}))

            @pl.when((zz >= z) & (z > 0))
            def _():
                act(part_copy(name, 1, p, s, {"rows": me - 4}))

        if "y" in ways and (p == 0 or (route == 1 and other == 0)):
            act(part_copy(name, 2, p, s, {"rows": y_peer}))
        if "c" in ways:
            act(part_copy(name, 3, p, s, {"rows": core_peer}))

    def begin(name, ways):
        each_send(name, 0, lambda copy: copy.start(), ways)

    def arrive(name, p):
        zz, yy, _ = place_of(parts[name][3], p)
        part_copy(name, 0, p, 4 * zz + 2 * yy + c, {"rows": me}).wait_recv()
        each_send(name, p, lambda copy: copy.start())

    def meet(name, p):
        zz, yy, _ = place_of(parts[name][3], p)
        part_copy(name, 0, p, 4 * zz + 2 * yy + 1 - c, {"rows": me}).wait_recv()

    def settle(name):
        for p in range(8):
            each_send(name, p, lambda copy: copy.wait_send())

    half_copy = remote(half_own, first_own, x_send.at[0], x_recv.at[0], {"section": 1 - section})
    enc_copy = remote(enc_ref, arrived_ref, x_send.at[1], x_recv.at[1], {"section": 1 - section})

    def project():
        for p in range(8):
            meet("A", p)
        own_copies[0].wait()
        load = pltpu.make_async_copy(attn_all, w_attn, load_sem.at[0])
        load.start()
        load.wait()
        wide_buf[...] = dot_last(n1_ref[...], w_attn[...].reshape(4 * inner, -1)).astype(bf16)
        qkv_ref[...] = dot(wide_buf[...], place[:, : 3 * inner]).astype(bf16)

    def mix(s):
        low = low_half(length)
        allowed = allowed_twice(cnt_ref, s, length)
        rows = slice(s * length, (s + 1) * length)
        for h in range(inner // PAIR):
            cols = [slice(j * inner + h * PAIR, j * inner + (h + 1) * PAIR) for j in range(3)]
            q2 = stack_pair(qkv_ref[rows, cols[0]], low)
            p = soft_pair(q2, qkv_ref[rows, cols[1]], allowed).astype(bf16)
            wide = jnp.concatenate([p[:length], p[length:]], axis=1)
            mixed_ref[rows, cols[0]] = dot(wide, stack_pair(qkv_ref[rows, cols[2]], low)).astype(bf16)

    def mix_out():
        for s in range(x_ref.shape[0] // length // 2, x_ref.shape[0] // length):
            mix(s)
        wide_buf[...] = dot_last(mixed_ref[...], place[:, 3 * inner :]).astype(bf16)
        y1_ref[...] = x_ref[...].astype(f32) + dot(wide_buf[...], w_attn[...].reshape(4 * inner, -1))
        y2_ref[...] = y1_ref[...]
        n2_ref[...] = (unit_rows(y1_ref[...])[1] * g_feed_ref[...]).astype(bf16)

    def mix_first():
        for s in range(x_ref.shape[0] // length // 2):
            mix(s)

    def sort_rows():
        for k in range(4):
            columns = slice(k * inner, (k + 1) * inner)
            w = w_attn[...].reshape(4 * inner, -1)
            sorted_ref[columns, :] = dot_rows(place[:, columns], w).astype(bf16)

    def blocks_copy(p):
        zz, yy, _ = place_of(1, p)
        pair = 4 * zz + 2 * yy
        return pair, pltpu.make_async_copy(feed_all.at[pl.ds(pair, 2)], w_feed.at[p % 2], load_sem.at[1 + p % 2])

    def fetch(p):
        if p == 0:
            own_copies[1].wait()
        for name in "GUO":
            meet(name, p)

        @pl.when(section == 0)
        def _():
            blocks_copy(p)[1].start()

    def feed(p):
        @pl.when(section == 0)
        def _():
            pair, copy = blocks_copy(p)
            copy.wait()
            w = w_feed.at[p % 2]
            hidden = []
            for k in range(2):
                gu = dot_last(n2_ref[...], w[k, : 2 * f, :])
                gu_ref[pair + k] = gu
                hidden.append((gelu_parts(gu[:, :f])[0] * gu[:, f:]).astype(bf16))
            right = jnp.concatenate([w[k, 2 * f :, :] for k in range(2)], axis=0)
            y2_ref[...] += dot(jnp.concatenate(hidden, axis=1), right)

    begin("A", "zyc")

    @pl.when(section == 0)
    def _():
        half_copy.start()

    begin("G", "zyc")

    @pl.when(section == 1)
    def _():
        load_half.wait()
        half_copy.wait_recv()
        extra_own[...] = jnp.concatenate([first_own[...], second_own[...]], axis=1)
        own_copies[2].start()
        begin("Y", "zyc")
        begin("X", "zyc")

    begin("U", "yc")
    begin("O", "yc")

    row = lax.broadcasted_iota(jnp.int32, place.shape, 0)
    place[...] = jnp.where(row == order_ref[...], 1.0, 0.0).astype(bf16)
    n1_ref[...] = (unit_rows(x_ref[...].astype(f32))[1] * g_attn_ref[...]).astype(bf16)

    tasks = {"c1": project, "c2": mix_first, "c3": mix_out, "c4": lambda: pl.when(section == 1)(sort_rows)}
    for step in FRONT_STEPS:
        if step in tasks:
            tasks[step]()
        elif step[0] == "f":
            feed(int(step[1]))
        elif step[0] == "l":
            fetch(int(step[1]))
        elif step[0] == "o":
            begin(step[1], "z")
        elif step[0] == "X":

            @pl.when(section == 1)
            def _(p=int(step[1])):
                arrive("X", p)
                arrive("Y", p)

        else:
            arrive(step[0], int(step[1]))

    @pl.when(section == 0)
    def _():
        enc_ref[...] = (unit_rows(y2_ref[...])[1] * g_final_ref[...]).astype(bf16)
        enc_copy.start()

    pl.when(section == 0)(sort_rows)

    for name in "AGUO":
        settle(name)

    @pl.when(section == 1)
    def _():
        for name in "XY":
            for p in range(8):
                meet(name, p)
            settle(name)
        own_copies[2].wait()
        enc_copy.wait_recv()

    @pl.when(section == 0)
    def _():
        half_copy.wait_send()
        enc_copy.wait_send()


FRONT_STEPS = (
    ("A1", "oU", "G1", "A2", "A3", "oO", "A4", "O1", "U1", "G2", "U2", "O2", "A5", "A6", "X1", "X2", "G3", "A7")
    + ("c1", "O3", "G4", "O4", "U3", "c2", "U4", "l0", "c3", "l1", "f0", "O5", "l2", "f1", "c4", "U5", "U6", "G5", "O6", "X3")
    + ("X4", "X5", "X6", "O7", "l3", "f2", "l4", "f3", "G6", "l5", "f4", "l6", "f5", "U7", "f6", "X7", "G7", "l7", "f7")
)


def front(counts, order, x, gain_attn, gain_feed, gain_final, attn_own, feed_own, half_own, length):
    t, d = x.shape
    attn_rows, feed_rows = attn_own.shape[0], feed_own.shape[0]
    inner = attn_rows * 4
    vm = pl.BlockSpec(memory_space=pltpu.VMEM)
    anywhere = pl.BlockSpec(memory_space=pl.ANY)
    return pl.pallas_call(
        functools.partial(front_kernel, length),
        out_shape=(
            jax.ShapeDtypeStruct((16, attn_rows, d), bf16),
            jax.ShapeDtypeStruct((16, feed_rows, d), bf16),
            jax.ShapeDtypeStruct((16, half_own.shape[0], d), bf16),
            jax.ShapeDtypeStruct((t, d), bf16),
            jax.ShapeDtypeStruct((t, 3 * inner), bf16),
            jax.ShapeDtypeStruct((t, inner), bf16),
            jax.ShapeDtypeStruct((t, d), f32),
            jax.ShapeDtypeStruct((t, d), bf16),
            jax.ShapeDtypeStruct((16, t, feed_rows // 3 * 2), f32),
            jax.ShapeDtypeStruct((t, d), f32),
            jax.ShapeDtypeStruct((t, d), bf16),
            jax.ShapeDtypeStruct((t, d), bf16),
            jax.ShapeDtypeStruct((4 * inner, d), bf16),
        ),
        in_specs=[pl.BlockSpec(memory_space=pltpu.SMEM)] + [vm] * 5 + [anywhere] * 3,
        out_specs=(anywhere,) * 3 + (vm,) * 10,
        scratch_shapes=[
            pltpu.VMEM((16, attn_rows, d), bf16),
            pltpu.VMEM((2, 2, feed_rows, d), bf16),
            pltpu.VMEM((4 * inner, 4 * inner), bf16),
            pltpu.VMEM((t, 4 * inner), bf16),
            pltpu.VMEM(half_own.shape, bf16),
            pltpu.VMEM(half_own.shape, bf16),
            pltpu.VMEM((half_own.shape[0], d), bf16),
            pltpu.SemaphoreType.DMA((6, 4, 8)),
            pltpu.SemaphoreType.DMA((6, 16)),
            pltpu.SemaphoreType.DMA((4,)),
            pltpu.SemaphoreType.DMA((3,)),
            pltpu.SemaphoreType.DMA((2,)),
            pltpu.SemaphoreType.DMA((2,)),
        ],
        compiler_params=pltpu.CompilerParams(
            vmem_limit_bytes=60 * 1024 * 1024, collective_id=1, has_side_effects=True
        ),
        cost_estimate=pl.CostEstimate(
            flops=2 * t * d * (feed_rows * 16 + 8 * inner),
            bytes_accessed=2 * 16 * (attn_rows + feed_rows) * d * 2,
            transcendentals=t * feed_rows * 6,
        ),
    )(counts, order, x, gain_attn, gain_feed, gain_final, attn_own, feed_own, half_own)


def mid_kernel(
    length, cross_cnt, self_cnt, dec_cnt, x_ref, y1_ref, y2_in, n2_in, qkv_ref, mixed_ref, n1_ref,
    encoded_ref, target_ref, gain_ref, order_ref, gu_in, attn_w, extra_w, feed_w,
    n_all, g_all, gx_ref, sums_ref, attn_sums, extra_sums, extra_pair,
    slots, gu_buf, w_att, w_head, mid, y2, acc, n2, cqkv, do_buf, grad_enc,
    dqkv_ref, dcqkv_ref, cmixed_ref, gl_ref, gf_ref, ga_ref, mc_ref, gac_ref, final_ref, lefts_ref,
    send_sem, recv_sem, slot_sem, load_sem, own_sem, x_send, x_recv, core_send, core_recv, put_sem, cross_send, cross_recv,
):
    section = lax.axis_index("section")
    me = lax.axis_index("rows")
    z, y, c = me // 4, (me // 2) % 2, me % 2
    core_peer, y_peer = me + 1 - 2 * c, me + 2 - 4 * y
    mesh_id = pl.DeviceIdType.MESH
    inner = w_att.shape[0] // 4
    f = feed_w.shape[1] // 3
    t = n2.shape[0]
    held = slots.shape[0]
    spare = BLOCKS - held
    is_enc, is_dec = section == 0, section == 1

    def load(b):
        k = b % held
        return pltpu.make_async_copy(feed_w.at[b], slots.at[k], slot_sem.at[k])

    load_attn = pltpu.make_async_copy(attn_w, w_att, load_sem.at[0])
    load_cross = pltpu.make_async_copy(extra_w.at[pl.ds(0, 4 * inner)], w_att, load_sem.at[1])
    load_head = pltpu.make_async_copy(extra_w.at[pl.ds(4 * inner, inner)], w_head, load_sem.at[2])
    load_gu = pltpu.make_async_copy(gu_in, gu_buf, load_sem.at[3])

    def start_loads(first):
        def step(k, carry):
            load(first + k).start()
            return carry

        lax.fori_loop(0, held, step, 0)

    @pl.when(is_enc)
    def _():
        start_loads(spare)
        load_gu.start()
        load_attn.start()

    @pl.when(is_dec)
    def _():
        load_cross.start()

    barrier = pltpu.get_barrier_semaphore()

    def greet(where):
        pl.semaphore_signal(barrier, inc=1, device_id=where, device_id_type=mesh_id)

    greet({"rows": core_peer})
    greet({"rows": y_peer})
    greet({"section": 1 - section})

    @pl.when(z > 0)
    def _():
        greet({"rows": me - 4})

    @pl.when(z < 3)
    def _():
        greet({"rows": me + 4})

    pl.semaphore_wait(barrier, 4 + (z + z // 2) % 2)

    def remote(src, dst, send, recv, where):
        return pltpu.make_async_remote_copy(
            src_ref=src, dst_ref=dst, send_sem=send, recv_sem=recv,
            device_id=where, device_id_type=mesh_id,
        )

    cuts = [0, t * 7 // 256 * 16, t * 13 // 256 * 16, t]
    thirds = [pl.ds(lo, hi - lo) for lo, hi in zip(cuts, cuts[1:])]
    parts = {
        "S": (0, thirds[0], 1, n2, n_all),
        "T": (1, thirds[1], 1, n2, n_all),
        "Q": (2, thirds[2], 2, n2, n_all),
        "V": (3, thirds[0], 1, gf_ref, g_all),
        "U": (4, thirds[1], 1, gf_ref, g_all),
        "W": (5, thirds[2], 2, gf_ref, g_all),
    }

    def place_of(route, p):
        if route == 1:
            j, other = [(0, 0), (1, 0), (0, 1), (2, 0), (1, 1), (3, 0), (2, 1), (3, 1)][p]
        else:
            j, other = p // 2, p % 2
        zz = [z, z + 1 - 2 * (z % 2), 2 - z // 2, 3 - 3 * (z // 2)][j]
        yy = y + other - 2 * other * y
        return zz, yy, other

    def part_copy(name, kind, p, s, where):
        k, rows, _, own, whole = parts[name]
        dst = whole.at[s, rows]
        src = own.at[rows] if p == 0 else dst
        return remote(src, dst, send_sem.at[k, kind, p], recv_sem.at[k, s], where)

    def each_send(name, p, act):
        route = parts[name][2]
        zz, yy, other = place_of(route, p)
        s = 4 * zz + 2 * yy + c
        if route == 2 or other == 0:

            @pl.when((zz <= z) & (z < 3))
            def _():
                act(part_copy(name, 0, p, s, {"rows": me + 4}))

            @pl.when((zz >= z) & (z > 0))
            def _():
                act(part_copy(name, 1, p, s, {"rows": me - 4}))

        if p == 0 or (route == 1 and other == 0):
            act(part_copy(name, 2, p, s, {"rows": y_peer}))
        act(part_copy(name, 3, p, s, {"rows": core_peer}))

    own_copies = {
        "S": pltpu.make_async_copy(n2, n_all.at[me], own_sem.at[0]),
        "V": pltpu.make_async_copy(gf_ref, g_all.at[me], own_sem.at[1]),
    }

    def begin(names):
        own_copies[names[0]].start()
        for name in names:
            each_send(name, 0, lambda copy: copy.start())

    def arrive(*steps):
        for step in steps:
            name, p = step[0], int(step[1])
            zz, yy, _ = place_of(parts[name][2], p)
            part_copy(name, 0, p, 4 * zz + 2 * yy + c, {"rows": me}).wait_recv()
            each_send(name, p, lambda copy: copy.start())

    back_copy = remote(grad_enc, grad_enc, x_send.at[0], x_recv.at[0], {"section": 1 - section})

    group = 4

    def feed_forward(first, count):
        def step(i, carry):
            blocks = [first + group * i + k for k in range(group)]
            rows = [slots.at[b % held] for b in blocks]
            for b in blocks:
                load(b).wait()
            hidden = []
            for b, w in zip(blocks, rows):
                gu = dot_last(n2[...], w[: 2 * f, :])
                gu_buf[b] = gu
                hidden.append((gelu_parts(gu[:, :f])[0] * gu[:, f:]).astype(bf16))
            total = None
            for k in range(0, group, 2):
                left = jnp.concatenate(hidden[k : k + 2], axis=1)
                right = jnp.concatenate([w[2 * f :, :] for w in rows[k : k + 2]], axis=0)
                term = dot(left, right)
                total = term if total is None else total + term
            y2[...] += total
            for b in blocks:

                @pl.when(b < spare)
                def _(b=b):
                    load(b + held).start()

            return carry

        lax.fori_loop(0, count // group, step, 0)

    def feed_backward(first, count, fresh):
        def step(i, carry):
            blocks = [BLOCKS - 1 - first - group * i - k for k in range(group)]
            rows = [slots.at[b % held] for b in blocks]
            for b in blocks:

                @pl.when((b < spare) | fresh)
                def _(b=b):
                    load(b).wait()

            lefts = []
            for b, w in zip(blocks, rows):
                gh = dot_last(gf_ref[...], w[2 * f :, :])
                gu = gu_buf[b]
                act, slope = gelu_parts(gu[:, :f])
                dg = (gh * gu[:, f:] * slope).astype(bf16)
                lefts.append(jnp.concatenate([dg, (gh * act).astype(bf16)], axis=1))
            total = None
            for left, w in zip(lefts, rows):
                term = dot(left, w[: 2 * f, :])
                total = term if total is None else total + term
            acc[...] += total
            for b in blocks:

                @pl.when(b >= held)
                def _(b=b):
                    load(b - held).start()

            return carry

        lax.fori_loop(0, count // group, step, 0)

    def final_backward(up):
        back, sums_ref[2:3, :] = norm_back(y2[...], gain_ref[2:3, :], up)
        gx_ref[...] = back
        gf_ref[...] = back.astype(bf16)
        begin("VUW")
        acc[...] = jnp.zeros_like(acc)

    def feed_end():
        back, sums_ref[1:2, :] = norm_back(mid[...], gain_ref[1:2, :], acc[...])
        acc[...] = gx_ref[...] + back

    sums_ref[...] = jnp.zeros_like(sums_ref)

    @pl.when(is_enc)
    def _():
        n2[...] = n2_in[...]
        begin("STQ")
        mid[...] = y1_ref[...]
        y2[...] = y2_in[...]
        arrive("S2", "S1", "T2", "T1", "Q1", "Q2", "S4", "S3", "T4", "T3", "Q3", "Q4", "S6", "T6", "S5", "T5")
        arrive("S7", "Q5", "Q6", "T7", "Q7")
        back_copy.wait_recv()
        final_backward(grad_enc[...].astype(f32))
        load_gu.wait()
        feed_backward(0, 8, True)
        arrive("V2", "V1")
        feed_backward(8, 8, True)
        feed_end()
        arrive("U2", "U1", "W1", "W2")
        load_attn.wait()

    @pl.when(is_dec)
    def _():
        y1 = y1_ref[...]
        mc_ref[...] = (unit_rows(y1)[1] * gain_ref[3:4, :]).astype(bf16)
        load_cross.wait()
        start_loads(0)
        load_head.start()
        cqkv[:, :inner] = dot_last(mc_ref[...], w_att[:inner, :]).astype(bf16)
        cqkv[:, inner:] = dot_last(encoded_ref[...], w_att[inner : 3 * inner, :]).astype(bf16)
        heads_fwd(cross_cnt, cqkv, cmixed_ref, length)
        mid[...] = y1_ref[...] + dot(cmixed_ref[...], w_att[3 * inner :, :])
        y2[...] = mid[...]
        n2[...] = (unit_rows(mid[...])[1] * gain_ref[1:2, :]).astype(bf16)
        begin("STQ")
        feed_forward(0, 12)
        arrive("S2", "S1")
        feed_forward(12, 4)
        final_ref[...] = (unit_rows(y2[...])[1] * gain_ref[2:3, :]).astype(bf16)
        load_head.wait()
        loss = loss_back(dec_cnt, final_ref, w_head, target_ref, gl_ref, length)
        sums_ref[4:5, :] = jnp.broadcast_to(loss, (1, sums_ref.shape[1]))
        final_backward(dot(gl_ref[...], w_head[...]))
        feed_backward(0, 8, False)
        arrive("T2", "T1")
        feed_backward(8, 8, False)
        feed_end()
        arrive("Q1", "Q2")
        gac_ref[...] = acc[...].astype(bf16)
        do_buf[...] = dot_last(gac_ref[...], w_att[3 * inner :, :]).astype(bf16)
        heads_bwd(cross_cnt, cqkv, do_buf, dcqkv_ref, length)
        grad_enc[...] = dot(dcqkv_ref[:, inner:], w_att[inner : 3 * inner, :]).astype(bf16)
        back_copy.start()
        up = dot(dcqkv_ref[:, :inner], w_att[:inner, :])
        load_attn.start()
        back, sums_ref[3:4, :] = norm_back(y1_ref[...], gain_ref[3:4, :], up)
        acc[...] += back
        arrive("S4", "S3", "V2", "V1", "T4", "T3", "Q3", "Q4")
        load_attn.wait()

    ga_ref[...] = acc[...].astype(bf16)
    do_buf[...] = dot_last(ga_ref[...], w_att[3 * inner :, :]).astype(bf16)
    heads_bwd(self_cnt, qkv_ref, do_buf, dqkv_ref, length)
    up = dot(dqkv_ref[...], w_att[: 3 * inner, :])
    back, sums_ref[0:1, :] = norm_back(x_ref[...].astype(f32), gain_ref[0:1, :], up)
    gx_ref[...] = acc[...] + back

    def core_copies(k, out, rows, first):
        size = 4 * rows
        theirs = [
            remote(slots.at[first + i, pl.ds(0, size)], out.at[1, pl.ds(i * size, size)],
                   core_send.at[k, i], core_recv.at[k, i], {"rows": core_peer})
            for i in range(2)
        ]
        mine = [
            pltpu.make_async_copy(
                slots.at[first + 2 + i, pl.ds(0, size)], out.at[0, pl.ds(i * size, size)], put_sem.at[k, i]
            )
            for i in range(2)
        ]
        return theirs, mine

    def terms(sources, rights, copies, rows, first):
        chunk = inner // 2
        for k, (source, at) in enumerate(sources):
            col = lax.broadcasted_iota(jnp.int32, (inner, inner), 1)
            pick = jnp.where(order_ref[...] == col, 1.0, 0.0).astype(bf16)
            both = dot_last(pick, source[:, at * inner : (at + 1) * inner]).astype(bf16)
            for half in range(2):
                lefts_ref[half, k * chunk : (k + 1) * chunk, :] = both[half * chunk : (half + 1) * chunk]
        d = rights[0].shape[1]
        for which in range(2):
            left = lefts_ref.at[(1 - c) if which == 0 else c]
            pieces = []
            for k, right in enumerate(rights):
                product = dot(left[k * chunk : (k + 1) * chunk, :], right[...])
                pieces.append(product.reshape(8, -1, d))
            if rows > len(rights) * chunk // 8:
                pieces.append(jnp.zeros((8, rows - len(rights) * chunk // 8, d), f32))
            blocks = jnp.concatenate(pieces, axis=1).astype(bf16)
            for i in range(2):
                half = blocks[4 * i : 4 * i + 4].reshape(4 * rows, d)
                slots[first + 2 * which + i, : 4 * rows, :] = half
                if which == 0 or len(copies) > 1:
                    copies[which][i].start()

    attn_rows, extra_rows = attn_sums.shape[1] // 8, extra_sums.shape[0] // 8
    attn_copies = core_copies(0, attn_sums, attn_rows, 0)
    extra_copies = core_copies(1, extra_pair, extra_rows, 4)

    size, wide = 4 * extra_rows, extra_sums.shape[1]
    spread = [
        remote(slots.at[i, pl.ds(0, size), pl.ds(0, wide)], extra_sums.at[pl.ds(i * size, size)],
               cross_send.at[i], cross_recv.at[i], {"section": 1 - section})
        for i in range(2)
    ]
    keep = [
        pltpu.make_async_copy(
            slots.at[2 + i, pl.ds(0, size), pl.ds(0, wide)], extra_sums.at[pl.ds(i * size, size)], put_sem.at[1, i]
        )
        for i in range(2)
    ]

    def split_features():
        for copy in extra_copies[0]:
            copy.wait()
        for copies in attn_copies:
            for copy in copies:
                copy.wait()
        half = n2.shape[1] // 2
        for i in range(2):
            fetch = pltpu.make_async_copy(
                extra_pair.at[1, pl.ds(i * size, size)], slots.at[4 + i, pl.ds(0, size)], load_sem.at[3]
            )
            fetch.start()
            fetch.wait()
            total = slots[6 + i, :size, :].astype(f32) + slots[4 + i, :size, :].astype(f32)
            slots[i, :size, :half] = total[:, :half].astype(bf16)
            spread[i].start()
            slots[2 + i, :size, :half] = total[:, half:].astype(bf16)
            keep[i].start()

    @pl.when(is_enc)
    def _():
        arrive("V4", "V3")

    terms(
        [(dqkv_ref, 0), (dqkv_ref, 1), (dqkv_ref, 2), (mixed_ref, 0)],
        [n1_ref, n1_ref, n1_ref, ga_ref], attn_copies, attn_rows, 0,
    )

    @pl.when(is_dec)
    def _():
        arrive("U2", "W1", "U1", "W2", "S6", "S5", "V4")
        terms(
            [(dcqkv_ref, 0), (dcqkv_ref, 1), (dcqkv_ref, 2), (cmixed_ref, 0), (gl_ref, 0)],
            [mc_ref, encoded_ref, encoded_ref, gac_ref, final_ref], extra_copies[:1], extra_rows, 4,
        )
        arrive("T6", "V3")
        split_features()

    @pl.when(is_enc)
    def _():
        arrive("U4", "U3", "W3", "W4", "V6", "U6", "V5", "U5", "V7", "W5", "W6", "U7", "W7")

    @pl.when(is_dec)
    def _():
        arrive("U4", "T5", "Q5", "Q6", "S7", "U3", "V6", "W4", "W3", "T7", "V5", "U6", "Q7", "V7", "U5", "W6")
        arrive("W7", "U7", "W5")

    for name in parts:
        for p in range(8):
            zz, yy, _ = place_of(parts[name][2], p)
            part_copy(name, 0, p, 4 * zz + 2 * yy + 1 - c, {"rows": me}).wait_recv()
            each_send(name, p, lambda copy: copy.wait_send())
    own_copies["S"].wait()
    own_copies["V"].wait()

    @pl.when(is_enc)
    def _():
        for copies in attn_copies:
            for copy in copies:
                copy.wait()
        for copy in spread:
            copy.wait_recv()

    @pl.when(is_dec)
    def _():
        for i in range(2):
            spread[i].wait_send()
            keep[i].wait()

    @pl.when(is_dec)
    def _():
        back_copy.wait_send()


def middle(cross_cnt, self_cnt, dec_cnt, x, y1, y2, n2, qkv, mixed, n1, encoded, target, gains, order, gu, attn_w, extra_w, feed_w, length):
    t, d = x.shape
    inner = attn_w.shape[0] // 4
    held = 8
    vm = pl.BlockSpec(memory_space=pltpu.VMEM)
    sm = pl.BlockSpec(memory_space=pltpu.SMEM)
    anywhere = pl.BlockSpec(memory_space=pl.ANY)
    attn_rows = inner // 4
    extra_rows = -(-5 * inner // 16 // 16) * 16
    return pl.pallas_call(
        functools.partial(mid_kernel, length),
        out_shape=(
            jax.ShapeDtypeStruct((16, t, d), bf16),
            jax.ShapeDtypeStruct((16, t, d), bf16),
            jax.ShapeDtypeStruct((t, d), f32),
            jax.ShapeDtypeStruct((8, d), f32),
            jax.ShapeDtypeStruct((2, 8 * attn_rows, d), bf16),
            jax.ShapeDtypeStruct((8 * extra_rows, -(-d // 2 // 128) * 128), bf16),
            jax.ShapeDtypeStruct((2, 8 * extra_rows, d), bf16),
        ),
        in_specs=[sm] * 3 + [vm] * 11 + [anywhere] * 4,
        out_specs=(anywhere,) * 2 + (vm,) * 2 + (anywhere,) * 3,
        scratch_shapes=[
            pltpu.VMEM((held,) + feed_w.shape[1:], bf16),
            pltpu.VMEM(gu.shape, f32),
            pltpu.VMEM(attn_w.shape, bf16),
            pltpu.VMEM((inner, d), bf16),
            pltpu.VMEM((t, d), f32),
            pltpu.VMEM((t, d), f32),
            pltpu.VMEM((t, d), f32),
            pltpu.VMEM((t, d), bf16),
            pltpu.VMEM((t, 3 * inner), bf16),
            pltpu.VMEM((t, inner), bf16),
            pltpu.VMEM((t, d), bf16),
            pltpu.VMEM((t, 3 * inner), bf16),
            pltpu.VMEM((t, 3 * inner), bf16),
            pltpu.VMEM((t, inner), bf16),
            pltpu.VMEM((t, inner), bf16),
            pltpu.VMEM((t, d), bf16),
            pltpu.VMEM((t, d), bf16),
            pltpu.VMEM((t, d), bf16),
            pltpu.VMEM((t, d), bf16),
            pltpu.VMEM((t, d), bf16),
            pltpu.VMEM((2, 5 * inner // 2, t), bf16),
            pltpu.SemaphoreType.DMA((6, 4, 8)),
            pltpu.SemaphoreType.DMA((6, 16)),
            pltpu.SemaphoreType.DMA((held,)),
            pltpu.SemaphoreType.DMA((4,)),
            pltpu.SemaphoreType.DMA((2,)),
            pltpu.SemaphoreType.DMA((1,)),
            pltpu.SemaphoreType.DMA((1,)),
            pltpu.SemaphoreType.DMA((2, 2)),
            pltpu.SemaphoreType.DMA((2, 2)),
            pltpu.SemaphoreType.DMA((2, 2)),
            pltpu.SemaphoreType.DMA((2,)),
            pltpu.SemaphoreType.DMA((2,)),
        ],
        compiler_params=pltpu.CompilerParams(
            vmem_limit_bytes=62 * 1024 * 1024, collective_id=2, has_side_effects=True
        ),
        cost_estimate=pl.CostEstimate(
            flops=4 * t * feed_w.size, bytes_accessed=2 * feed_w.size + 8 * gu.size, transcendentals=2 * gu.size
        ),
    )(cross_cnt, self_cnt, dec_cnt, x, y1, y2, n2, qkv, mixed, n1, encoded, target, gains, order, gu, attn_w, extra_w, feed_w)


def adam_step(weight, first_moment, second_moment, gradient, step_rate, weight_decay):
    first_new = 0.9 * first_moment + 0.1 * gradient
    second_new = 0.999 * second_moment + 0.001 * gradient * gradient
    first_fix = 1.0 - 0.9**STEP
    second_fix = 1.0 - 0.999**STEP
    update = first_new / first_fix / (jnp.sqrt(second_new / second_fix) + 1e-08)
    return (first_new, second_new, weight - step_rate * (update + weight_decay * weight))


def kinds_first(gathered, n, kinds, per):
    d = gathered.shape[-1]
    return gathered.reshape(n, kinds, per, d).transpose(1, 0, 2, 3).reshape(kinds * n * per, d)


def owners_first(left, right, n):
    t, k, units = left.shape
    grad = jnp.einsum("tku,td->kud", left, right, preferred_element_type=f32)
    return grad.reshape(k, n, units // n, -1).transpose(1, 0, 2, 3)


def local(
    block_input,
    lengths,
    targets,
    attention_weight,
    attention_first,
    attention_second,
    feed_weight,
    feed_first,
    feed_second,
    norm_gain,
    gain_first,
    gain_second,
    cross_weight,
    cross_first,
    cross_second,
    head_weight,
    head_first,
    head_second,
    cross_gain,
    cross_gain_first,
    cross_gain_second,
):
    n = lax.axis_size("rows")
    is_encoder = lax.axis_index("section") == 0
    micro, length, d = block_input.shape[1:]
    t = micro * length
    per = attention_weight.shape[1]
    f = feed_weight.shape[1]
    inner = per * n

    attn_own = attention_weight[0].astype(bf16).transpose(1, 0, 2).reshape(4 * per, d)
    feed_own = feed_weight[0].astype(bf16).transpose(1, 0, 2)
    half_rows = jnp.concatenate(
        [cross_weight.astype(bf16).transpose(1, 0, 2), head_weight.astype(bf16)[None]], axis=0
    )

    gains = norm_gain[0]
    gain_attn, gain_feed, gain_final = gains[0:1], gains[1:2], gains[2:3]
    gain_cross = cross_gain[None]
    x = block_input[0].reshape(t, d)
    enc_counts = lengths[0, :, 0]
    dec_counts = lengths[1, :, 0]
    zero_one = jnp.zeros((1,), jnp.int32)
    self_counts = jnp.concatenate([jnp.where(is_encoder, 0, 1).astype(jnp.int32)[None], enc_counts])
    cross_counts = jnp.concatenate([zero_one, enc_counts])
    target_column = targets.reshape(t, 1)

    def blank(maker):
        return jax.tree.map(lambda a: jnp.zeros(a.shape, a.dtype), jax.eval_shape(maker))

    emit = n != BLOCKS
    if emit:
        attn_all = lax.all_gather(attn_own, "rows", axis=0, tiled=True)
        attn_w = kinds_first(attn_all, n, 4, per)
        feed_all = lax.all_gather(feed_own.reshape(3 * f, d), "rows", axis=0, tiled=True)
        feed_w = kinds_first(feed_all, n, 3, f).reshape(3, BLOCKS, -1, d)
        feed_w = feed_w.transpose(1, 0, 2, 3).reshape(BLOCKS, -1, d)
        other_half = lax.ppermute(half_rows, "section", [(0, 1)])
        extra_own = jnp.concatenate([other_half, half_rows], axis=-1).reshape(5 * per, d)
        extra_all = lax.all_gather(extra_own, "rows", axis=0, tiled=True)
        n1, qkv, mixed, y1 = attend_fwd(self_counts, x, gain_attn, attn_w, length)

        def enc_feed():
            return feed_fwd(y1, gain_feed, gain_final, feed_w)

        enc_state = lax.cond(is_encoder, enc_feed, lambda: blank(enc_feed))
        encoded = lax.ppermute(enc_state[3], "section", [(0, 1)])
    else:
        units = jnp.arange(4 * inner, dtype=jnp.int32).reshape(n, 4, per)
        order = units.transpose(1, 0, 2).reshape(1, 4 * inner)
        units = jnp.arange(inner, dtype=jnp.int32).reshape(4, 2, 2, per)
        travel = units.transpose(2, 1, 0, 3).reshape(inner, 1)
        pad = -(5 * per) % 16
        half_own = jnp.pad(half_rows.reshape(5 * per, d // 2), ((0, pad), (0, 0)))
        outs = front(
            self_counts, order, x, gain_attn, gain_feed, gain_final,
            attn_own, feed_own.reshape(3 * f, d), half_own, length,
        )
        _, feed_w, extra_all, n1, qkv, mixed, y1 = outs[:7]
        enc_state, encoded, attn_w = outs[7:11], outs[11], outs[12]
        extra_all = extra_all[:, : 5 * per]
    extra_w = kinds_first(extra_all, n, 5, per)
    cross_w, head_w = extra_w[: 4 * inner], extra_w[4 * inner :]

    if emit:
        def dec_front():
            mc, cqkv, cmixed, z2 = attend_fwd(cross_counts, y1, gain_cross, cross_w, length, encoded)
            return feed_fwd(z2, gain_feed, gain_final, feed_w) + (mc, cqkv, cmixed, z2)

        def enc_pass():
            rest = jax.eval_shape(dec_front)[4:7]
            return tuple(enc_state) + tuple(jnp.zeros(a.shape, a.dtype) for a in rest) + (y1,)

        n2, gu, y2, final, mc, cqkv, cmixed, mid = lax.cond(is_encoder, enc_pass, dec_front)
        def dec_back():
            gl, up, loss = head_loss(dec_counts, final, head_w, target_column, length)
            feed_out = feed_bwd(up, mid, y2, gain_feed, gain_final, gu, feed_w, emit)
            ga_c, dqkv_c, gy1, gg_c, ge = attend_bwd(
                cross_counts, y1, gain_cross, feed_out[1], cqkv, cross_w, length, True
            )
            return (ge, gy1, feed_out[2], feed_out[0], *feed_out[3:], gl, ga_c, dqkv_c, gg_c, loss)

        back = lax.cond(is_encoder, lambda: blank(dec_back), dec_back)
        returned = lax.ppermute(back[0], "section", [(1, 0)])
        at = 6 if emit else 4
        gl, ga_c, dqkv_c, gg_c, loss = back[at:]

        def enc_back():
            feed_out = feed_bwd(returned, mid, y2, gain_feed, gain_final, gu, feed_w, emit)
            return (feed_out[1], feed_out[2], feed_out[0], *feed_out[3:])

        backs = lax.cond(is_encoder, enc_back, lambda: tuple(back[1:at]))
        gy1, gg_feed, gf = backs[:3]

        ga, dqkv, gx, gg_attn = attend_bwd(self_counts, x, gain_attn, gy1, qkv, attn_w, length)
        tiny = jnp.concatenate(
            [gg_attn, gg_feed, gg_c, jnp.broadcast_to(loss, (1, d)), jnp.zeros((3, d), f32)], axis=0
        )
    else:
        gain_rows = jnp.concatenate([gains, gain_cross], axis=0)
        n2, gu, y2 = enc_state[:3]
        (
            n2_all, gf_all, gx, tiny, attn_terms, extra_terms, _,
        ) = middle(
            cross_counts, self_counts, dec_counts, x, y1, y2, n2, qkv, mixed, n1, encoded, target_column,
            gain_rows, travel, gu, attn_w, extra_w, feed_w, length,
        )

    half = d // 2
    if emit:
        extra_part = jnp.concatenate(
            [
                owners_first(dqkv_c[:, None, :inner], mc, n),
                owners_first(dqkv_c[:, inner:].reshape(t, 2, inner), encoded, n),
                owners_first(cmixed[:, None], ga_c, n),
                owners_first(gl[:, None], final, n),
            ],
            axis=1,
        ).astype(bf16)
        extra_sum = lax.psum_scatter(
            extra_part.reshape(n * 5 * per, d), "rows", scatter_dimension=0, tiled=True
        )
        extra_first = lax.ppermute(extra_sum[:, :half], "section", [(1, 0)])
        extra_grad = jnp.where(is_encoder, extra_first, extra_sum[:, half:]).astype(f32)
        extra_grad = extra_grad.reshape(5, per, half)

        attn_part = jnp.concatenate(
            [
                owners_first(dqkv.reshape(t, 3, inner), n1, n),
                owners_first(mixed[:, None], ga, n),
            ],
            axis=1,
        ).astype(bf16)
        attn_sum = lax.psum_scatter(
            attn_part.reshape(n * 4 * per, d), "rows", scatter_dimension=0, tiled=True
        ).astype(f32)
        dgu, hid = backs[3], backs[4]
        nb, _, fb = hid.shape
        left = dgu.reshape(nb, t, 2, fb).transpose(1, 2, 0, 3).reshape(t, 2, nb * fb)
        hid = hid.transpose(1, 0, 2).reshape(t, 1, nb * fb)
        feed_part = jnp.concatenate(
            [owners_first(left, n2, n), owners_first(hid, gf, n)], axis=1
        ).astype(bf16)
        feed_grad = lax.psum_scatter(
            feed_part.reshape(n * 3 * f, d), "rows", scatter_dimension=0, tiled=True
        ).astype(f32)
        tiny_sum = jnp.sum(lax.all_gather(tiny, "rows", axis=0), axis=0)
    else:
        feed_grad, attn_sum, extra_sum, tiny_sum = tail(
            tiny, attn_terms, extra_terms, feed_own.reshape(3 * f, d), n2_all, gf_all
        )
        extra_grad = extra_sum[: 5 * per, :half].reshape(5, per, half)
    tiny_dec = lax.ppermute(tiny_sum[3:5], "section", [(1, 0)])
    tiny_dec = jnp.where(is_encoder, tiny_dec, tiny_sum[3:5])
    attn_grad = attn_sum.reshape(4, per, d).transpose(1, 0, 2)
    feed_grad = feed_grad.reshape(3, f, d).transpose(1, 0, 2)
    cross_gain_total = tiny_dec[0]
    loss_total = tiny_dec[1, 0]

    attention_new = adam_step(
        attention_weight, attention_first, attention_second, attn_grad[None], 0.05, 0.1
    )
    feed_new = adam_step(feed_weight, feed_first, feed_second, feed_grad[None], 0.05, 0.1)
    gain_new = adam_step(norm_gain, gain_first, gain_second, tiny_sum[None, 0:3], 0.5, 0.0)
    cross_new = adam_step(
        cross_weight, cross_first, cross_second, extra_grad[:4].transpose(1, 0, 2), 0.05, 0.1
    )
    head_new = adam_step(head_weight, head_first, head_second, extra_grad[4], 0.05, 0.1)
    cross_gain_new = adam_step(
        cross_gain, cross_gain_first, cross_gain_second, cross_gain_total, 0.5, 0.0
    )
    return (
        gx.reshape(1, micro, length, d),
        loss_total,
        *attention_new,
        *feed_new,
        *gain_new,
        *cross_new,
        *head_new,
        *cross_gain_new,
    )


def solution(mesh):
    by_row = P("section", "rows", None, None)
    gain = P("section", None, None)
    cross = P("rows", None, "section")
    head = P("rows", "section")
    weights = (by_row,) * 6 + (gain,) * 3 + (cross,) * 3 + (head,) * 3 + (P(),) * 3
    tokens = P("section", None, "rows", None)
    return jax.shard_map(
        local,
        mesh=mesh,
        in_specs=(tokens, P(None, None, "rows"), P(None, "rows")) + weights,
        out_specs=(tokens, P()) + weights,
        check_vma=False,
    )
```

```python
import functools

import jax
import jax.numpy as jnp
from jax import lax
from jax.experimental import pallas as pl
from jax.experimental.pallas import tpu as pltpu
from jax.sharding import PartitionSpec as P

HD = 64
STEP = 10
PAIR = 2 * HD
BLOCKS = 16
VMEM_BYTES = 52 * 1024 * 1024

bf16 = jnp.bfloat16
f32 = jnp.float32
masked_value = -1000000000.0
scale = HD ** (-0.5)


def dot(a, b):
    return lax.dot_general(a, b, (((1,), (0,)), ((), ())), preferred_element_type=f32)


def dot_last(a, b):
    return lax.dot_general(a, b, (((1,), (1,)), ((), ())), preferred_element_type=f32)


def dot_rows(a, b):
    return lax.dot_general(a, b, (((0,), (0,)), ((), ())), preferred_element_type=f32)


def unit_rows(v):
    r = lax.rsqrt(jnp.mean(v * v, axis=-1, keepdims=True) + 1e-06)
    return r, v * r


def norm_back(v, gain, up):
    r, n = unit_rows(v)
    g = up * gain
    back = r * (g - n * jnp.mean(g * n, axis=-1, keepdims=True))
    return back, jnp.sum(up * n, axis=0, keepdims=True)


def gelu_parts(x):
    c = 0.7978845608028654
    t = jnp.tanh(c * (x + 0.044715 * (x * x * x)))
    act = 0.5 * x * (1.0 + t)
    slope = 0.5 * (1.0 + t) + 0.5 * x * (1.0 - t * t) * (c * (1.0 + 3.0 * 0.044715 * (x * x)))
    return act, slope


def low_half(length):
    return lax.broadcasted_iota(jnp.int32, (length, PAIR), 1) < HD


def stack_pair(m, low):
    zero = jnp.zeros_like(m)
    return jnp.concatenate([jnp.where(low, m, zero), jnp.where(low, zero, m)], axis=0)


def allowed_twice(cnt_ref, s, length):
    row = lax.broadcasted_iota(jnp.int32, (length, length), 0)
    col = lax.broadcasted_iota(jnp.int32, (length, length), 1)
    limit = jnp.where(cnt_ref[0] == 1, row + 1, cnt_ref[1 + s])
    one = jnp.where(col < limit, 1, 0)
    return jnp.concatenate([one, one], axis=0) == 1


def soft_pair(q2, k, allowed):
    s = dot_last(q2, k) * scale
    s = jnp.where(allowed, s, masked_value)
    e = jnp.exp(s - jnp.max(s, axis=-1, keepdims=True))
    return e / jnp.sum(e, axis=-1, keepdims=True)


def head_columns(inner, h):
    return [slice(j * inner + h * PAIR, j * inner + (h + 1) * PAIR) for j in range(3)]


def heads_fwd(cnt_ref, qkv_ref, o_ref, length):
    t, inner = o_ref.shape
    low = low_half(length)
    for s in range(t // length):
        allowed = allowed_twice(cnt_ref, s, length)
        rows = slice(s * length, (s + 1) * length)
        for h in range(inner // PAIR):
            cols = head_columns(inner, h)
            q2 = stack_pair(qkv_ref[rows, cols[0]], low)
            p = soft_pair(q2, qkv_ref[rows, cols[1]], allowed).astype(bf16)
            wide = jnp.concatenate([p[:length], p[length:]], axis=1)
            o_ref[rows, cols[0]] = dot(wide, stack_pair(qkv_ref[rows, cols[2]], low)).astype(bf16)


def heads_bwd(cnt_ref, qkv_ref, do_ref, dqkv_ref, length):
    t, inner = do_ref.shape
    low = low_half(length)
    for s in range(t // length):
        allowed = allowed_twice(cnt_ref, s, length)
        rows = slice(s * length, (s + 1) * length)
        for h in range(inner // PAIR):
            cols = head_columns(inner, h)
            q2 = stack_pair(qkv_ref[rows, cols[0]], low)
            k = qkv_ref[rows, cols[1]]
            p = soft_pair(q2, k, allowed)
            do2 = stack_pair(do_ref[rows, cols[0]], low)
            dp = dot_last(do2, qkv_ref[rows, cols[2]])
            ds = p * (dp - jnp.sum(dp * p, axis=-1, keepdims=True))
            ds = jnp.where(allowed, ds, 0.0).astype(bf16)
            wide = jnp.concatenate([ds[:length], ds[length:]], axis=1)
            dqkv_ref[rows, cols[0]] = (dot(wide, stack_pair(k, low)) * scale).astype(bf16)
            dqkv_ref[rows, cols[1]] = (dot_rows(ds, q2) * scale).astype(bf16)
            dqkv_ref[rows, cols[2]] = dot_rows(p.astype(bf16), do2).astype(bf16)


def loss_back(cnt_ref, f_ref, w_ref, target_ref, gl_ref, length):
    logits = dot_last(f_ref[...], w_ref[...])
    top = jnp.max(logits, axis=-1, keepdims=True)
    log_total = top + jnp.log(jnp.sum(jnp.exp(logits - top), axis=-1, keepdims=True))
    hit = lax.broadcasted_iota(jnp.int32, logits.shape, 1) == target_ref[...]
    picked = jnp.sum(jnp.where(hit, logits, 0.0), axis=-1, keepdims=True)
    probs = jnp.exp(logits - log_total) - jnp.where(hit, 1.0, 0.0)
    total = jnp.zeros((1, 1), f32)
    for s in range(logits.shape[0] // length):
        rows = slice(s * length, (s + 1) * length)
        valid = lax.broadcasted_iota(jnp.int32, (length, 1), 0) < cnt_ref[s]
        total += jnp.sum(
            jnp.where(valid, log_total[rows] - picked[rows], 0.0), axis=0, keepdims=True
        )
        gl_ref[rows, :] = jnp.where(valid, probs[rows], 0.0).astype(bf16)
    return total


def attend_fwd_kernel(cross, length, cnt_ref, x_ref, gain_ref, *refs):
    if cross:
        src_ref, w_ref, n_ref, qkv_ref, o_ref, y_ref = refs
    else:
        w_ref, n_ref, qkv_ref, o_ref, y_ref = refs
    inner = w_ref.shape[0] // 4
    x = x_ref[...].astype(f32)
    n = (unit_rows(x)[1] * gain_ref[...]).astype(bf16)
    n_ref[...] = n
    if cross:
        qkv_ref[:, :inner] = dot_last(n, w_ref[:inner, :]).astype(bf16)
        qkv_ref[:, inner:] = dot_last(src_ref[...], w_ref[inner : 3 * inner, :]).astype(bf16)
    else:
        qkv_ref[...] = dot_last(n, w_ref[: 3 * inner, :]).astype(bf16)
    heads_fwd(cnt_ref, qkv_ref, o_ref, length)
    y_ref[...] = x + dot(o_ref[...], w_ref[3 * inner :, :])


def attend_fwd(counts, x, gain, w, length, source=None):
    t, d = x.shape
    inner = w.shape[0] // 4
    ins = [counts, x, gain] + ([] if source is None else [source]) + [w]
    vm = pl.BlockSpec(memory_space=pltpu.VMEM)
    return pl.pallas_call(
        functools.partial(attend_fwd_kernel, source is not None, length),
        out_shape=(
            jax.ShapeDtypeStruct((t, d), bf16),
            jax.ShapeDtypeStruct((t, 3 * inner), bf16),
            jax.ShapeDtypeStruct((t, inner), bf16),
            jax.ShapeDtypeStruct((t, d), f32),
        ),
        in_specs=[pl.BlockSpec(memory_space=pltpu.SMEM)] + [vm] * (len(ins) - 1),
        out_specs=(vm,) * 4,
        compiler_params=pltpu.CompilerParams(vmem_limit_bytes=VMEM_BYTES),
        cost_estimate=pl.CostEstimate(
            flops=2 * t * d * inner * 4 + 8 * t * length * inner,
            bytes_accessed=w.size * 2 + t * d * 10,
            transcendentals=t * length * 6,
        ),
    )(*ins)


def attend_bwd_kernel(cross, length, cnt_ref, x_ref, gain_ref, gy_ref, qkv_ref, w_ref, *refs):
    if cross:
        ga_ref, dqkv_ref, gx_ref, gg_ref, gs_ref, do_ref = refs
    else:
        ga_ref, dqkv_ref, gx_ref, gg_ref, do_ref = refs
    inner = w_ref.shape[0] // 4
    ga = gy_ref[...].astype(bf16)
    ga_ref[...] = ga
    do_ref[...] = dot_last(ga, w_ref[3 * inner :, :]).astype(bf16)
    heads_bwd(cnt_ref, qkv_ref, do_ref, dqkv_ref, length)
    if cross:
        up = dot(dqkv_ref[:, :inner], w_ref[:inner, :])
        gs_ref[...] = dot(dqkv_ref[:, inner:], w_ref[inner : 3 * inner, :]).astype(bf16)
    else:
        up = dot(dqkv_ref[...], w_ref[: 3 * inner, :])
    back, gg_ref[...] = norm_back(x_ref[...].astype(f32), gain_ref[...], up)
    gx_ref[...] = gy_ref[...] + back


def attend_bwd(counts, x, gain, gy, qkv, w, length, cross=False):
    t, d = x.shape
    inner = w.shape[0] // 4
    vm = pl.BlockSpec(memory_space=pltpu.VMEM)
    outs = [
        jax.ShapeDtypeStruct((t, d), bf16),
        jax.ShapeDtypeStruct((t, 3 * inner), bf16),
        jax.ShapeDtypeStruct((t, d), f32),
        jax.ShapeDtypeStruct((1, d), f32),
    ]
    if cross:
        outs.append(jax.ShapeDtypeStruct((t, d), bf16))
    return pl.pallas_call(
        functools.partial(attend_bwd_kernel, cross, length),
        out_shape=tuple(outs),
        in_specs=[pl.BlockSpec(memory_space=pltpu.SMEM)] + [vm] * 5,
        out_specs=(vm,) * len(outs),
        scratch_shapes=[pltpu.VMEM((t, inner), bf16)],
        compiler_params=pltpu.CompilerParams(vmem_limit_bytes=VMEM_BYTES),
        cost_estimate=pl.CostEstimate(
            flops=2 * t * d * inner * 4 + 20 * t * length * inner,
            bytes_accessed=w.size * 2 + t * d * 16,
            transcendentals=t * length * 6,
        ),
    )(counts, x, gain, gy, qkv, w)


def feed_fwd_kernel(y_ref, g_in_ref, g_out_ref, w_ref, n_ref, gu_ref, y2_ref, f_ref):
    i = pl.program_id(0)
    f = w_ref.shape[1] // 3

    @pl.when(i == 0)
    def _():
        y = y_ref[...]
        n_ref[...] = (unit_rows(y)[1] * g_in_ref[...]).astype(bf16)
        y2_ref[...] = y

    gu = dot_last(n_ref[...], w_ref[0, : 2 * f, :])
    gu_ref[0] = gu
    hidden = (gelu_parts(gu[:, :f])[0] * gu[:, f:]).astype(bf16)
    y2_ref[...] += dot(hidden, w_ref[0, 2 * f :, :])

    @pl.when(i == pl.num_programs(0) - 1)
    def _():
        f_ref[...] = (unit_rows(y2_ref[...])[1] * g_out_ref[...]).astype(bf16)


def feed_fwd(y, gain_in, gain_out, w):
    t, d = y.shape
    nb, rows, _ = w.shape
    f = rows // 3
    whole = lambda *shape: pl.BlockSpec(shape, lambda i: (0,) * len(shape))
    part = lambda *shape: pl.BlockSpec((1,) + shape, lambda i: (i, 0, 0))
    return pl.pallas_call(
        feed_fwd_kernel,
        grid=(nb,),
        out_shape=(
            jax.ShapeDtypeStruct((t, d), bf16),
            jax.ShapeDtypeStruct((nb, t, 2 * f), f32),
            jax.ShapeDtypeStruct((t, d), f32),
            jax.ShapeDtypeStruct((t, d), bf16),
        ),
        in_specs=[whole(t, d), whole(1, d), whole(1, d), part(rows, d)],
        out_specs=(whole(t, d), part(t, 2 * f), whole(t, d), whole(t, d)),
        compiler_params=pltpu.CompilerParams(vmem_limit_bytes=VMEM_BYTES),
        cost_estimate=pl.CostEstimate(
            flops=2 * t * d * rows * nb,
            bytes_accessed=w.size * 2 + t * d * 12 + nb * t * f * 8,
            transcendentals=nb * t * f,
        ),
    )(y, gain_in, gain_out, w)


def feed_bwd_kernel(emit, up_ref, y_ref, y2_ref, g_in_ref, g_out_ref, gu_ref, w_ref, *refs):
    if emit:
        gf_ref, gy_ref, gg_ref, dgu_ref, hid_ref, last_ref = refs
    else:
        gf_ref, gy_ref, gg_ref, last_ref = refs
    i = pl.program_id(0)
    f = w_ref.shape[1] // 3

    @pl.when(i == 0)
    def _():
        back, gain_grad = norm_back(y2_ref[...], g_out_ref[...], up_ref[...].astype(f32))
        gg_ref[1:2, :] = gain_grad
        last_ref[...] = back
        gf_ref[...] = back.astype(bf16)
        gy_ref[...] = jnp.zeros_like(gy_ref)

    gh = dot_last(gf_ref[...], w_ref[0, 2 * f :, :])
    act, slope = gelu_parts(gu_ref[0, :, :f])
    u = gu_ref[0, :, f:]
    dg = (gh * u * slope).astype(bf16)
    du = (gh * act).astype(bf16)
    if emit:
        dgu_ref[0, :, :f] = dg
        dgu_ref[0, :, f:] = du
        hid_ref[0] = (act * u).astype(bf16)
    gy_ref[...] += dot(dg, w_ref[0, :f, :]) + dot(du, w_ref[0, f : 2 * f, :])

    @pl.when(i == pl.num_programs(0) - 1)
    def _():
        back, gain_grad = norm_back(y_ref[...], g_in_ref[...], gy_ref[...])
        gg_ref[0:1, :] = gain_grad
        gy_ref[...] = last_ref[...] + back


def feed_bwd(up, y, y2, gain_in, gain_out, gu, w, emit):
    t, d = y.shape
    nb, rows, _ = w.shape
    f = rows // 3
    whole = lambda *shape: pl.BlockSpec(shape, lambda i: (0,) * len(shape))
    part = lambda *shape: pl.BlockSpec((1,) + shape, lambda i: (i, 0, 0))
    outs = [
        jax.ShapeDtypeStruct((t, d), bf16),
        jax.ShapeDtypeStruct((t, d), f32),
        jax.ShapeDtypeStruct((2, d), f32),
    ]
    specs = [whole(t, d), whole(t, d), whole(2, d)]
    if emit:
        outs += [
            jax.ShapeDtypeStruct((nb, t, 2 * f), bf16),
            jax.ShapeDtypeStruct((nb, t, f), bf16),
        ]
        specs += [part(t, 2 * f), part(t, f)]
    return pl.pallas_call(
        functools.partial(feed_bwd_kernel, emit),
        grid=(nb,),
        out_shape=tuple(outs),
        in_specs=[whole(t, d)] * 3 + [whole(1, d)] * 2 + [part(t, 2 * f), part(rows, d)],
        out_specs=tuple(specs),
        scratch_shapes=[pltpu.VMEM((t, d), f32)],
        compiler_params=pltpu.CompilerParams(vmem_limit_bytes=VMEM_BYTES),
        cost_estimate=pl.CostEstimate(
            flops=2 * t * d * rows * nb,
            bytes_accessed=w.size * 2 + t * d * 18 + nb * t * f * 8,
            transcendentals=nb * t * f,
        ),
    )(up, y, y2, gain_in, gain_out, gu, w)


def head_kernel(length, cnt_ref, f_ref, w_ref, target_ref, gl_ref, up_ref, loss_ref):
    loss_ref[...] = loss_back(cnt_ref, f_ref, w_ref, target_ref, gl_ref, length)
    up_ref[...] = dot(gl_ref[...], w_ref[...])


def head_loss(counts, final, w, target, length):
    t, d = final.shape
    v = w.shape[0]
    vm = pl.BlockSpec(memory_space=pltpu.VMEM)
    return pl.pallas_call(
        functools.partial(head_kernel, length),
        out_shape=(
            jax.ShapeDtypeStruct((t, v), bf16),
            jax.ShapeDtypeStruct((t, d), f32),
            jax.ShapeDtypeStruct((1, 1), f32),
        ),
        in_specs=[pl.BlockSpec(memory_space=pltpu.SMEM), vm, vm, vm],
        out_specs=(vm,) * 3,
        compiler_params=pltpu.CompilerParams(vmem_limit_bytes=VMEM_BYTES),
        cost_estimate=pl.CostEstimate(
            flops=4 * t * d * v, bytes_accessed=w.size * 2 + t * d * 6, transcendentals=t * v * 2
        ),
    )(counts, final, w, target)


def tail_kernel(
    tiny_ref, attn_terms, extra_terms, w_ref, n_all, g_all,
    feed_ref, attn_ref, extra_ref, total_ref,
    tinies, n_buf, g_buf, *rest,
):
    attn_bufs, extra_bufs = rest[:8], rest[8:16]
    tiny_send, tiny_recv, rs_send, rs_recv, pair_sem = rest[16:]
    me = lax.axis_index("rows")
    z, y, c = me // 4, (me // 2) % 2, me % 2
    high = z // 2
    inner = (z + high) % 2
    f = w_ref.shape[0] // 3
    d = w_ref.shape[1]
    core_peer, y_peer = me + 1 - 2 * c, me + 2 - 4 * y
    toward = me + 4 - 8 * high
    outward = me - 4 + 8 * high
    mesh_id = pl.DeviceIdType.MESH

    def remote(src, dst, send, recv, where):
        return pltpu.make_async_remote_copy(
            src_ref=src, dst_ref=dst, send_sem=send, recv_sem=recv,
            device_id=where, device_id_type=mesh_id,
        )

    def pair_copies(p):
        slot = p % 2
        return [
            pltpu.make_async_copy(whole.at[pl.ds(2 * p, 2)], buf.at[slot], pair_sem.at[k, slot])
            for k, (whole, buf) in enumerate([(n_all, n_buf), (g_all, g_buf)])
        ]

    for copy in pair_copies(0):
        copy.start()

    barrier = pltpu.get_barrier_semaphore()

    def greet(where):
        pl.semaphore_signal(barrier, inc=1, device_id=where, device_id_type=mesh_id)

    greet({"rows": core_peer})
    greet({"rows": y_peer})
    greet({"rows": toward})

    @pl.when(inner == 1)
    def _():
        greet({"rows": outward})

    pl.semaphore_wait(barrier, 3 + inner)

    def place_of(p):
        j, other = p // 2, p % 2
        zz = [z, z + 1 - 2 * (z % 2), 2 - high, 3 - 3 * high][j]
        yy = y + other - 2 * other * y
        return zz, yy, other

    def tiny_copy(kind, p, s, where):
        src = tiny_ref if p == 0 else tinies.at[s]
        return remote(src, tinies.at[s], tiny_send.at[kind, p], tiny_recv.at[s], where)

    def each_tiny(p, act):
        zz, yy, other = place_of(p)
        s = 4 * zz + 2 * yy + c
        if p == 0:
            act(tiny_copy(2, p, s, {"rows": y_peer}))

        @pl.when((zz <= z) & (z < 3))
        def _():
            act(tiny_copy(0, p, s, {"rows": me + 4}))

        @pl.when((zz >= z) & (z > 0))
        def _():
            act(tiny_copy(1, p, s, {"rows": me - 4}))

        act(tiny_copy(3, p, s, {"rows": core_peer}))

    def tiny_arrive(p):
        zz, yy, _ = place_of(p)
        tiny_copy(0, p, 4 * zz + 2 * yy + c, {"rows": me}).wait_recv()
        each_tiny(p, lambda copy: copy.start())

    far_out, far_in = 3 - 3 * high, 2 - high
    beside = (1 - inner) * (1 + high) + inner * 3 * high

    def summed(bufs, k, terms, result):
        part, four, from_y, from_far, from_near, from_cross, from_out, cross_out = bufs

        def hop(i, src, dst, where):
            return remote(src, dst, rs_send.at[k, i], rs_recv.at[k, i], {"rows": where})

        ys = [
            hop(1 + i, part.at[(1 - y) * 4 + at], from_y.at[at], y_peer)
            for i, at in enumerate([far_out, far_in, beside, z])
        ]
        fars = [hop(5 + i, four.at[at], from_far.at[i], toward) for i, at in enumerate([far_out, far_in])]
        near = hop(7, four.at[beside], from_near, toward)
        crosses = [hop(8 + i, four.at[at], from_cross.at[i], toward) for i, at in enumerate([far_out, far_in])]
        out = hop(10, cross_out, from_out, outward)

        def start():
            total = terms[...]
            if total.ndim == 3:
                total = (total[0].astype(f32) + total[1].astype(f32)).astype(bf16)
            part[...] = total.reshape(part.shape)
            ys[0].start()
            ys[1].start()

        def rest():
            ys[2].start()
            ys[3].start()

        def add_y(i, at):
            ys[i].wait_recv()
            four[at] = (part[4 * y + at].astype(f32) + from_y[at].astype(f32)).astype(bf16)

        def far(i):
            def stage():
                add_y(i, [far_out, far_in][i])
                pl.when(inner == 0)(fars[i].start)

            return stage

        def cross(i):
            def stage():
                @pl.when(inner == 1)
                def _():
                    at = [far_out, far_in][i]
                    fars[i].wait_recv()
                    four[at] = (four[at].astype(f32) + from_far[i].astype(f32)).astype(bf16)
                    crosses[i].start()

            return stage

        def home():
            add_y(2, beside)
            pl.when(inner == 0)(near.start)

        def own():
            add_y(3, z)

        def leave():
            @pl.when(inner == 1)
            def _():
                crosses[0].wait_recv()
                cross_out[...] = (four[beside].astype(f32) + from_cross[0].astype(f32)).astype(bf16)
                out.start()

        def last_inner():
            @pl.when(inner == 1)
            def _():
                crosses[1].wait_recv()
                near.wait_recv()
                result(four[z].astype(f32) + from_cross[1].astype(f32) + from_near[...].astype(f32))

        def last_outer():
            @pl.when(inner == 0)
            def _():
                out.wait_recv()
                result(four[z].astype(f32) + from_out[...].astype(f32))

        def settle():
            for copy in ys:
                copy.wait_send()

            @pl.when(inner == 0)
            def _():
                for copy in [*fars, near]:
                    copy.wait_send()

            @pl.when(inner == 1)
            def _():
                for copy in [*crosses, out]:
                    copy.wait_send()

        return {
            "start": start, "rest": rest, "0": far(0), "1": far(1), "2": cross(0), "3": cross(1),
            "4": home, "5": own, "6": leave, "7": last_inner, "8": last_outer, "settle": settle,
        }

    def attn_result(value):
        attn_ref[...] = value

    def extra_result(value):
        extra_ref[...] = value

    attn = summed(attn_bufs, 0, attn_terms, attn_result)
    extra = summed(extra_bufs, 1, extra_terms, extra_result)

    def wgrad(p):
        if p < 7:
            for copy in pair_copies(p + 1):
                copy.start()
        for copy in pair_copies(p):
            copy.wait()
        n_rows = n_buf[p % 2].reshape(-1, d)
        g_rows = g_buf[p % 2].reshape(-1, d)
        gu = dot_last(w_ref[: 2 * f, :], n_rows)
        gh = dot_last(w_ref[2 * f :, :], g_rows)
        act, slope = gelu_parts(gu[:f])
        up = gu[f:]
        dg = (gh * up * slope).astype(bf16)
        du = (gh * act).astype(bf16)
        hid = (act * up).astype(bf16)
        from_n = dot(jnp.concatenate([dg, du], axis=0), n_rows)
        from_g = dot(hid, g_rows)
        if p == 0:
            feed_ref[: 2 * f, :] = from_n
            feed_ref[2 * f :, :] = from_g
        else:
            feed_ref[: 2 * f, :] += from_n
            feed_ref[2 * f :, :] += from_g

    def add_tinies():
        for p in range(8):
            zz, yy, _ = place_of(p)
            tiny_copy(0, p, 4 * zz + 2 * yy + 1 - c, {"rows": me}).wait_recv()
        total = tinies[0]
        for s in range(1, 16):
            total += tinies[s]
        total_ref[...] = total

    tinies[me] = tiny_ref[...]
    each_tiny(0, lambda copy: copy.start())
    attn["start"]()
    extra["start"]()
    attn["rest"]()
    extra["rest"]()

    for step in TAIL_STEPS:
        if step[0] == "w":
            wgrad(int(step[1]))
        elif step[0] == "t":
            tiny_arrive(int(step[1]))
        elif step[0] == "a":
            attn[step[1]]()
        elif step[0] == "x":
            extra[step[1]]()
        else:
            add_tinies()

    for p in range(8):
        each_tiny(p, lambda copy: copy.wait_send())
    attn["settle"]()
    extra["settle"]()


TAIL_STEPS = (
    ("w0", "t1", "t2", "t3", "t4", "t5", "t6", "t7", "a0", "w1", "a1", "a2", "w2", "x0", "x1", "a3", "w3", "x2", "a4")
    + ("x3", "a6", "w4", "a5", "a7", "w5", "x4", "x6", "a8", "w6", "x5", "w7", "x7", "x8", "sum")
)


def tail(tiny, attn_terms, extra_terms, w_own, n_all, g_all):
    t, d = n_all.shape[1:]
    rows = w_own.shape[0]
    per, more = attn_terms.shape[1] // 8, extra_terms.shape[0] // 8

    def sums(r, d):
        return [
            pltpu.VMEM(shape + (r, d), bf16)
            for shape in [(8,), (4,), (4,), (2,), (), (2,), (), ()]
        ]

    vm = pl.BlockSpec(memory_space=pltpu.VMEM)
    anywhere = pl.BlockSpec(memory_space=pl.ANY)
    return pl.pallas_call(
        tail_kernel,
        out_shape=(
            jax.ShapeDtypeStruct((rows, d), f32),
            jax.ShapeDtypeStruct((per, d), f32),
            jax.ShapeDtypeStruct((more, extra_terms.shape[1]), f32),
            jax.ShapeDtypeStruct(tiny.shape, f32),
        ),
        in_specs=[vm] * 4 + [anywhere] * 2,
        out_specs=(vm,) * 4,
        scratch_shapes=[
            pltpu.VMEM((16,) + tiny.shape, f32),
            pltpu.VMEM((2, 2, t, d), bf16),
            pltpu.VMEM((2, 2, t, d), bf16),
            *sums(per, d),
            *sums(more, extra_terms.shape[1]),
            pltpu.SemaphoreType.DMA((4, 8)),
            pltpu.SemaphoreType.DMA((16,)),
            pltpu.SemaphoreType.DMA((2, 11)),
            pltpu.SemaphoreType.DMA((2, 11)),
            pltpu.SemaphoreType.DMA((2, 2)),
        ],
        compiler_params=pltpu.CompilerParams(
            vmem_limit_bytes=60 * 1024 * 1024, collective_id=0, has_side_effects=True
        ),
        cost_estimate=pl.CostEstimate(
            flops=2 * t * 16 * d * rows * 2, bytes_accessed=16 * t * d * 4, transcendentals=16 * t * rows
        ),
    )(tiny, attn_terms, extra_terms, w_own, n_all, g_all)


def front_kernel(
    length, cnt_ref, order_ref, x_ref, g_attn_ref, g_feed_ref, g_final_ref,
    attn_own, feed_own, half_own,
    attn_all, feed_all, extra_all,
    n1_ref, qkv_ref, mixed_ref, y1_ref, n2_ref, gu_ref, y2_ref, enc_ref, arrived_ref, sorted_ref,
    w_attn, w_feed, place, wide_buf, first_own, second_own, extra_own,
    send_sem, recv_sem, own_sem, load_sem, x_send, x_recv,
):
    section = lax.axis_index("section")
    me = lax.axis_index("rows")
    z, y, c = me // 4, (me // 2) % 2, me % 2
    core_peer, y_peer = me + 1 - 2 * c, me + 2 - 4 * y
    mesh_id = pl.DeviceIdType.MESH
    inner = mixed_ref.shape[1]
    f = feed_own.shape[0] // 3

    barrier = pltpu.get_barrier_semaphore()

    def greet(where):
        pl.semaphore_signal(barrier, inc=1, device_id=where, device_id_type=mesh_id)

    greet({"rows": core_peer})
    greet({"rows": y_peer})
    greet({"section": 1 - section})

    @pl.when(z > 0)
    def _():
        greet({"rows": me - 4})

    @pl.when(z < 3)
    def _():
        greet({"rows": me + 4})

    own_copies = [
        pltpu.make_async_copy(own, whole.at[me], own_sem.at[k])
        for k, (own, whole) in enumerate(
            [(attn_own, attn_all), (feed_own, feed_all), (extra_own, extra_all)]
        )
    ]
    load_half = pltpu.make_async_copy(half_own, second_own, own_sem.at[3])
    own_copies[0].start()
    own_copies[1].start()

    @pl.when(section == 1)
    def _():
        load_half.start()

    pl.semaphore_wait(barrier, 4 + (z + z // 2) % 2)

    def remote(src, dst, send, recv, where):
        return pltpu.make_async_remote_copy(
            src_ref=src, dst_ref=dst, send_sem=send, recv_sem=recv,
            device_id=where, device_id_type=mesh_id,
        )

    kinds = [pl.ds(k * f, f) for k in range(3)]
    cuts = [pl.ds(k * (extra_own.shape[0] // 2), extra_own.shape[0] // 2) for k in range(2)]
    parts = {
        "A": (0, attn_all, None, 2, attn_own),
        "G": (1, feed_all, kinds[0], 1, feed_own.at[kinds[0]]),
        "U": (2, feed_all, kinds[1], 1, feed_own.at[kinds[1]]),
        "O": (3, feed_all, kinds[2], 1, feed_own.at[kinds[2]]),
        "X": (4, extra_all, cuts[0], 1, extra_own.at[cuts[0]]),
        "Y": (5, extra_all, cuts[1], 2, extra_own.at[cuts[1]]),
    }

    def place_of(route, p):
        if route == 1:
            j, other = [(0, 0), (1, 0), (0, 1), (2, 0), (1, 1), (3, 0), (2, 1), (3, 1)][p]
        else:
            j, other = p // 2, p % 2
        zz = [z, z + 1 - 2 * (z % 2), 2 - z // 2, 3 - 3 * (z // 2)][j]
        yy = y + other - 2 * other * y
        return zz, yy, other

    def part_copy(name, kind, p, s, where):
        k, whole, rows, _, own = parts[name]
        dst = whole.at[s] if rows is None else whole.at[s, rows]
        return remote(own if p == 0 else dst, dst, send_sem.at[k, kind, p], recv_sem.at[k, s], where)

    def each_send(name, p, act, ways="zyc"):
        route = parts[name][3]
        zz, yy, other = place_of(route, p)
        s = 4 * zz + 2 * yy + c
        if "z" in ways and (route == 2 or other == 0):

            @pl.when((zz <= z) & (z < 3))
            def _():
                act(part_copy(name, 0, p, s, {"rows": me + 4}))

            @pl.when((zz >= z) & (z > 0))
            def _():
                act(part_copy(name, 1, p, s, {"rows": me - 4}))

        if "y" in ways and (p == 0 or (route == 1 and other == 0)):
            act(part_copy(name, 2, p, s, {"rows": y_peer}))
        if "c" in ways:
            act(part_copy(name, 3, p, s, {"rows": core_peer}))

    def begin(name, ways):
        each_send(name, 0, lambda copy: copy.start(), ways)

    def arrive(name, p):
        zz, yy, _ = place_of(parts[name][3], p)
        part_copy(name, 0, p, 4 * zz + 2 * yy + c, {"rows": me}).wait_recv()
        each_send(name, p, lambda copy: copy.start())

    def meet(name, p):
        zz, yy, _ = place_of(parts[name][3], p)
        part_copy(name, 0, p, 4 * zz + 2 * yy + 1 - c, {"rows": me}).wait_recv()

    def settle(name):
        for p in range(8):
            each_send(name, p, lambda copy: copy.wait_send())

    half_copy = remote(half_own, first_own, x_send.at[0], x_recv.at[0], {"section": 1 - section})
    enc_copy = remote(enc_ref, arrived_ref, x_send.at[1], x_recv.at[1], {"section": 1 - section})

    def project():
        for p in range(8):
            meet("A", p)
        own_copies[0].wait()
        load = pltpu.make_async_copy(attn_all, w_attn, load_sem.at[0])
        load.start()
        load.wait()
        wide_buf[...] = dot_last(n1_ref[...], w_attn[...].reshape(4 * inner, -1)).astype(bf16)
        qkv_ref[...] = dot(wide_buf[...], place[:, : 3 * inner]).astype(bf16)

    def mix(s):
        low = low_half(length)
        allowed = allowed_twice(cnt_ref, s, length)
        rows = slice(s * length, (s + 1) * length)
        for h in range(inner // PAIR):
            cols = [slice(j * inner + h * PAIR, j * inner + (h + 1) * PAIR) for j in range(3)]
            q2 = stack_pair(qkv_ref[rows, cols[0]], low)
            p = soft_pair(q2, qkv_ref[rows, cols[1]], allowed).astype(bf16)
            wide = jnp.concatenate([p[:length], p[length:]], axis=1)
            mixed_ref[rows, cols[0]] = dot(wide, stack_pair(qkv_ref[rows, cols[2]], low)).astype(bf16)

    def mix_out():
        for s in range(x_ref.shape[0] // length // 2, x_ref.shape[0] // length):
            mix(s)
        wide_buf[...] = dot_last(mixed_ref[...], place[:, 3 * inner :]).astype(bf16)
        y1_ref[...] = x_ref[...].astype(f32) + dot(wide_buf[...], w_attn[...].reshape(4 * inner, -1))
        y2_ref[...] = y1_ref[...]
        n2_ref[...] = (unit_rows(y1_ref[...])[1] * g_feed_ref[...]).astype(bf16)

    def mix_first():
        for s in range(x_ref.shape[0] // length // 2):
            mix(s)

    def sort_rows():
        for k in range(4):
            columns = slice(k * inner, (k + 1) * inner)
            w = w_attn[...].reshape(4 * inner, -1)
            sorted_ref[columns, :] = dot_rows(place[:, columns], w).astype(bf16)

    def blocks_copy(p):
        zz, yy, _ = place_of(1, p)
        pair = 4 * zz + 2 * yy
        return pair, pltpu.make_async_copy(feed_all.at[pl.ds(pair, 2)], w_feed.at[p % 2], load_sem.at[1 + p % 2])

    def fetch(p):
        if p == 0:
            own_copies[1].wait()
        for name in "GUO":
            meet(name, p)

        @pl.when(section == 0)
        def _():
            blocks_copy(p)[1].start()

    def feed(p):
        @pl.when(section == 0)
        def _():
            pair, copy = blocks_copy(p)
            copy.wait()
            w = w_feed.at[p % 2]
            hidden = []
            for k in range(2):
                gu = dot_last(n2_ref[...], w[k, : 2 * f, :])
                gu_ref[pair + k] = gu
                hidden.append((gelu_parts(gu[:, :f])[0] * gu[:, f:]).astype(bf16))
            right = jnp.concatenate([w[k, 2 * f :, :] for k in range(2)], axis=0)
            y2_ref[...] += dot(jnp.concatenate(hidden, axis=1), right)

    begin("A", "zyc")

    @pl.when(section == 0)
    def _():
        half_copy.start()

    begin("G", "zyc")

    @pl.when(section == 1)
    def _():
        load_half.wait()
        half_copy.wait_recv()
        extra_own[...] = jnp.concatenate([first_own[...], second_own[...]], axis=1)
        own_copies[2].start()
        begin("Y", "zyc")
        begin("X", "zyc")

    begin("U", "yc")
    begin("O", "yc")

    row = lax.broadcasted_iota(jnp.int32, place.shape, 0)
    place[...] = jnp.where(row == order_ref[...], 1.0, 0.0).astype(bf16)
    n1_ref[...] = (unit_rows(x_ref[...].astype(f32))[1] * g_attn_ref[...]).astype(bf16)

    tasks = {"c1": project, "c2": mix_first, "c3": mix_out, "c4": lambda: pl.when(section == 1)(sort_rows)}
    for step in FRONT_STEPS:
        if step in tasks:
            tasks[step]()
        elif step[0] == "f":
            feed(int(step[1]))
        elif step[0] == "l":
            fetch(int(step[1]))
        elif step[0] == "o":
            begin(step[1], "z")
        elif step[0] == "X":

            @pl.when(section == 1)
            def _(p=int(step[1])):
                arrive("X", p)
                arrive("Y", p)

        else:
            arrive(step[0], int(step[1]))

    @pl.when(section == 0)
    def _():
        enc_ref[...] = (unit_rows(y2_ref[...])[1] * g_final_ref[...]).astype(bf16)
        enc_copy.start()

    pl.when(section == 0)(sort_rows)

    for name in "AGUO":
        settle(name)

    @pl.when(section == 1)
    def _():
        for name in "XY":
            for p in range(8):
                meet(name, p)
            settle(name)
        own_copies[2].wait()
        enc_copy.wait_recv()

    @pl.when(section == 0)
    def _():
        half_copy.wait_send()
        enc_copy.wait_send()


FRONT_STEPS = (
    ("A1", "oU", "G1", "A2", "A3", "oO", "A4", "O1", "U1", "G2", "U2", "O2", "A5", "A6", "X1", "X2", "G3", "A7")
    + ("c1", "O3", "G4", "O4", "U3", "c2", "U4", "l0", "c3", "l1", "f0", "O5", "l2", "f1", "c4", "U5", "U6", "G5", "O6", "X3")
    + ("X4", "X5", "X6", "O7", "l3", "f2", "l4", "f3", "G6", "l5", "f4", "l6", "f5", "U7", "f6", "X7", "G7", "l7", "f7")
)


def front(counts, order, x, gain_attn, gain_feed, gain_final, attn_own, feed_own, half_own, length):
    t, d = x.shape
    attn_rows, feed_rows = attn_own.shape[0], feed_own.shape[0]
    inner = attn_rows * 4
    vm = pl.BlockSpec(memory_space=pltpu.VMEM)
    anywhere = pl.BlockSpec(memory_space=pl.ANY)
    return pl.pallas_call(
        functools.partial(front_kernel, length),
        out_shape=(
            jax.ShapeDtypeStruct((16, attn_rows, d), bf16),
            jax.ShapeDtypeStruct((16, feed_rows, d), bf16),
            jax.ShapeDtypeStruct((16, half_own.shape[0], d), bf16),
            jax.ShapeDtypeStruct((t, d), bf16),
            jax.ShapeDtypeStruct((t, 3 * inner), bf16),
            jax.ShapeDtypeStruct((t, inner), bf16),
            jax.ShapeDtypeStruct((t, d), f32),
            jax.ShapeDtypeStruct((t, d), bf16),
            jax.ShapeDtypeStruct((16, t, feed_rows // 3 * 2), f32),
            jax.ShapeDtypeStruct((t, d), f32),
            jax.ShapeDtypeStruct((t, d), bf16),
            jax.ShapeDtypeStruct((t, d), bf16),
            jax.ShapeDtypeStruct((4 * inner, d), bf16),
        ),
        in_specs=[pl.BlockSpec(memory_space=pltpu.SMEM)] + [vm] * 5 + [anywhere] * 3,
        out_specs=(anywhere,) * 3 + (vm,) * 10,
        scratch_shapes=[
            pltpu.VMEM((16, attn_rows, d), bf16),
            pltpu.VMEM((2, 2, feed_rows, d), bf16),
            pltpu.VMEM((4 * inner, 4 * inner), bf16),
            pltpu.VMEM((t, 4 * inner), bf16),
            pltpu.VMEM(half_own.shape, bf16),
            pltpu.VMEM(half_own.shape, bf16),
            pltpu.VMEM((half_own.shape[0], d), bf16),
            pltpu.SemaphoreType.DMA((6, 4, 8)),
            pltpu.SemaphoreType.DMA((6, 16)),
            pltpu.SemaphoreType.DMA((4,)),
            pltpu.SemaphoreType.DMA((3,)),
            pltpu.SemaphoreType.DMA((2,)),
            pltpu.SemaphoreType.DMA((2,)),
        ],
        compiler_params=pltpu.CompilerParams(
            vmem_limit_bytes=60 * 1024 * 1024, collective_id=1, has_side_effects=True
        ),
        cost_estimate=pl.CostEstimate(
            flops=2 * t * d * (feed_rows * 16 + 8 * inner),
            bytes_accessed=2 * 16 * (attn_rows + feed_rows) * d * 2,
            transcendentals=t * feed_rows * 6,
        ),
    )(counts, order, x, gain_attn, gain_feed, gain_final, attn_own, feed_own, half_own)


def mid_kernel(
    length, cross_cnt, self_cnt, dec_cnt, x_ref, y1_ref, y2_in, n2_in, qkv_ref, mixed_ref, n1_ref,
    encoded_ref, target_ref, gain_ref, order_ref, gu_in, attn_w, extra_w, feed_w,
    n_all, g_all, gx_ref, sums_ref, attn_sums, extra_sums, extra_pair,
    slots, gu_buf, w_att, w_head, mid, y2, acc, n2, cqkv, do_buf, grad_enc,
    dqkv_ref, dcqkv_ref, cmixed_ref, gl_ref, gf_ref, ga_ref, mc_ref, gac_ref, final_ref, lefts_ref,
    send_sem, recv_sem, slot_sem, load_sem, own_sem, x_send, x_recv, core_send, core_recv, put_sem, cross_send, cross_recv,
):
    section = lax.axis_index("section")
    me = lax.axis_index("rows")
    z, y, c = me // 4, (me // 2) % 2, me % 2
    core_peer, y_peer = me + 1 - 2 * c, me + 2 - 4 * y
    mesh_id = pl.DeviceIdType.MESH
    inner = w_att.shape[0] // 4
    f = feed_w.shape[1] // 3
    t = n2.shape[0]
    held = slots.shape[0]
    spare = BLOCKS - held
    is_enc, is_dec = section == 0, section == 1

    def load(b):
        k = b % held
        return pltpu.make_async_copy(feed_w.at[b], slots.at[k], slot_sem.at[k])

    load_attn = pltpu.make_async_copy(attn_w, w_att, load_sem.at[0])
    load_cross = pltpu.make_async_copy(extra_w.at[pl.ds(0, 4 * inner)], w_att, load_sem.at[1])
    load_head = pltpu.make_async_copy(extra_w.at[pl.ds(4 * inner, inner)], w_head, load_sem.at[2])
    load_gu = pltpu.make_async_copy(gu_in, gu_buf, load_sem.at[3])

    def start_loads(first):
        def step(k, carry):
            load(first + k).start()
            return carry

        lax.fori_loop(0, held, step, 0)

    @pl.when(is_enc)
    def _():
        start_loads(spare)
        load_gu.start()
        load_attn.start()

    @pl.when(is_dec)
    def _():
        load_cross.start()

    barrier = pltpu.get_barrier_semaphore()

    def greet(where):
        pl.semaphore_signal(barrier, inc=1, device_id=where, device_id_type=mesh_id)

    greet({"rows": core_peer})
    greet({"rows": y_peer})
    greet({"section": 1 - section})

    @pl.when(z > 0)
    def _():
        greet({"rows": me - 4})

    @pl.when(z < 3)
    def _():
        greet({"rows": me + 4})

    pl.semaphore_wait(barrier, 4 + (z + z // 2) % 2)

    def remote(src, dst, send, recv, where):
        return pltpu.make_async_remote_copy(
            src_ref=src, dst_ref=dst, send_sem=send, recv_sem=recv,
            device_id=where, device_id_type=mesh_id,
        )

    cuts = [0, t * 7 // 256 * 16, t * 13 // 256 * 16, t]
    thirds = [pl.ds(lo, hi - lo) for lo, hi in zip(cuts, cuts[1:])]
    parts = {
        "S": (0, thirds[0], 1, n2, n_all),
        "T": (1, thirds[1], 1, n2, n_all),
        "Q": (2, thirds[2], 2, n2, n_all),
        "V": (3, thirds[0], 1, gf_ref, g_all),
        "U": (4, thirds[1], 1, gf_ref, g_all),
        "W": (5, thirds[2], 2, gf_ref, g_all),
    }

    def place_of(route, p):
        if route == 1:
            j, other = [(0, 0), (1, 0), (0, 1), (2, 0), (1, 1), (3, 0), (2, 1), (3, 1)][p]
        else:
            j, other = p // 2, p % 2
        zz = [z, z + 1 - 2 * (z % 2), 2 - z // 2, 3 - 3 * (z // 2)][j]
        yy = y + other - 2 * other * y
        return zz, yy, other

    def part_copy(name, kind, p, s, where):
        k, rows, _, own, whole = parts[name]
        dst = whole.at[s, rows]
        src = own.at[rows] if p == 0 else dst
        return remote(src, dst, send_sem.at[k, kind, p], recv_sem.at[k, s], where)

    def each_send(name, p, act):
        route = parts[name][2]
        zz, yy, other = place_of(route, p)
        s = 4 * zz + 2 * yy + c
        if route == 2 or other == 0:

            @pl.when((zz <= z) & (z < 3))
            def _():
                act(part_copy(name, 0, p, s, {"rows": me + 4}))

            @pl.when((zz >= z) & (z > 0))
            def _():
                act(part_copy(name, 1, p, s, {"rows": me - 4}))

        if p == 0 or (route == 1 and other == 0):
            act(part_copy(name, 2, p, s, {"rows": y_peer}))
        act(part_copy(name, 3, p, s, {"rows": core_peer}))

    own_copies = {
        "S": pltpu.make_async_copy(n2, n_all.at[me], own_sem.at[0]),
        "V": pltpu.make_async_copy(gf_ref, g_all.at[me], own_sem.at[1]),
    }

    def begin(names):
        own_copies[names[0]].start()
        for name in names:
            each_send(name, 0, lambda copy: copy.start())

    def arrive(*steps):
        for step in steps:
            name, p = step[0], int(step[1])
            zz, yy, _ = place_of(parts[name][2], p)
            part_copy(name, 0, p, 4 * zz + 2 * yy + c, {"rows": me}).wait_recv()
            each_send(name, p, lambda copy: copy.start())

    back_copy = remote(grad_enc, grad_enc, x_send.at[0], x_recv.at[0], {"section": 1 - section})

    group = 4

    def feed_forward(first, count):
        def step(i, carry):
            blocks = [first + group * i + k for k in range(group)]
            rows = [slots.at[b % held] for b in blocks]
            for b in blocks:
                load(b).wait()
            hidden = []
            for b, w in zip(blocks, rows):
                gu = dot_last(n2[...], w[: 2 * f, :])
                gu_buf[b] = gu
                hidden.append((gelu_parts(gu[:, :f])[0] * gu[:, f:]).astype(bf16))
            total = None
            for k in range(0, group, 2):
                left = jnp.concatenate(hidden[k : k + 2], axis=1)
                right = jnp.concatenate([w[2 * f :, :] for w in rows[k : k + 2]], axis=0)
                term = dot(left, right)
                total = term if total is None else total + term
            y2[...] += total
            for b in blocks:

                @pl.when(b < spare)
                def _(b=b):
                    load(b + held).start()

            return carry

        lax.fori_loop(0, count // group, step, 0)

    def feed_backward(first, count, fresh):
        def step(i, carry):
            blocks = [BLOCKS - 1 - first - group * i - k for k in range(group)]
            rows = [slots.at[b % held] for b in blocks]
            for b in blocks:

                @pl.when((b < spare) | fresh)
                def _(b=b):
                    load(b).wait()

            lefts = []
            for b, w in zip(blocks, rows):
                gh = dot_last(gf_ref[...], w[2 * f :, :])
                gu = gu_buf[b]
                act, slope = gelu_parts(gu[:, :f])
                dg = (gh * gu[:, f:] * slope).astype(bf16)
                lefts.append(jnp.concatenate([dg, (gh * act).astype(bf16)], axis=1))
            total = None
            for left, w in zip(lefts, rows):
                term = dot(left, w[: 2 * f, :])
                total = term if total is None else total + term
            acc[...] += total
            for b in blocks:

                @pl.when(b >= held)
                def _(b=b):
                    load(b - held).start()

            return carry

        lax.fori_loop(0, count // group, step, 0)

    def final_backward(up):
        back, sums_ref[2:3, :] = norm_back(y2[...], gain_ref[2:3, :], up)
        gx_ref[...] = back
        gf_ref[...] = back.astype(bf16)
        begin("VUW")
        acc[...] = jnp.zeros_like(acc)

    def feed_end():
        back, sums_ref[1:2, :] = norm_back(mid[...], gain_ref[1:2, :], acc[...])
        acc[...] = gx_ref[...] + back

    sums_ref[...] = jnp.zeros_like(sums_ref)

    @pl.when(is_enc)
    def _():
        n2[...] = n2_in[...]
        begin("STQ")
        mid[...] = y1_ref[...]
        y2[...] = y2_in[...]
        arrive("S2", "S1", "T2", "T1", "Q1", "Q2", "S4", "S3", "T4", "T3", "Q3", "Q4", "S6", "T6", "S5", "T5")
        arrive("S7", "Q5", "Q6", "T7", "Q7")
        back_copy.wait_recv()
        final_backward(grad_enc[...].astype(f32))
        load_gu.wait()
        feed_backward(0, 8, True)
        arrive("V2", "V1")
        feed_backward(8, 8, True)
        feed_end()
        arrive("U2", "U1", "W1", "W2")
        load_attn.wait()

    @pl.when(is_dec)
    def _():
        y1 = y1_ref[...]
        mc_ref[...] = (unit_rows(y1)[1] * gain_ref[3:4, :]).astype(bf16)
        load_cross.wait()
        start_loads(0)
        load_head.start()
        cqkv[:, :inner] = dot_last(mc_ref[...], w_att[:inner, :]).astype(bf16)
        cqkv[:, inner:] = dot_last(encoded_ref[...], w_att[inner : 3 * inner, :]).astype(bf16)
        heads_fwd(cross_cnt, cqkv, cmixed_ref, length)
        mid[...] = y1_ref[...] + dot(cmixed_ref[...], w_att[3 * inner :, :])
        y2[...] = mid[...]
        n2[...] = (unit_rows(mid[...])[1] * gain_ref[1:2, :]).astype(bf16)
        begin("STQ")
        feed_forward(0, 12)
        arrive("S2", "S1")
        feed_forward(12, 4)
        final_ref[...] = (unit_rows(y2[...])[1] * gain_ref[2:3, :]).astype(bf16)
        load_head.wait()
        loss = loss_back(dec_cnt, final_ref, w_head, target_ref, gl_ref, length)
        sums_ref[4:5, :] = jnp.broadcast_to(loss, (1, sums_ref.shape[1]))
        final_backward(dot(gl_ref[...], w_head[...]))
        feed_backward(0, 8, False)
        arrive("T2", "T1")
        feed_backward(8, 8, False)
        feed_end()
        arrive("Q1", "Q2")
        gac_ref[...] = acc[...].astype(bf16)
        do_buf[...] = dot_last(gac_ref[...], w_att[3 * inner :, :]).astype(bf16)
        heads_bwd(cross_cnt, cqkv, do_buf, dcqkv_ref, length)
        grad_enc[...] = dot(dcqkv_ref[:, inner:], w_att[inner : 3 * inner, :]).astype(bf16)
        back_copy.start()
        up = dot(dcqkv_ref[:, :inner], w_att[:inner, :])
        load_attn.start()
        back, sums_ref[3:4, :] = norm_back(y1_ref[...], gain_ref[3:4, :], up)
        acc[...] += back
        arrive("S4", "S3", "V2", "V1", "T4", "T3", "Q3", "Q4")
        load_attn.wait()

    ga_ref[...] = acc[...].astype(bf16)
    do_buf[...] = dot_last(ga_ref[...], w_att[3 * inner :, :]).astype(bf16)
    heads_bwd(self_cnt, qkv_ref, do_buf, dqkv_ref, length)
    up = dot(dqkv_ref[...], w_att[: 3 * inner, :])
    back, sums_ref[0:1, :] = norm_back(x_ref[...].astype(f32), gain_ref[0:1, :], up)
    gx_ref[...] = acc[...] + back

    def core_copies(k, out, rows, first):
        size = 4 * rows
        theirs = [
            remote(slots.at[first + i, pl.ds(0, size)], out.at[1, pl.ds(i * size, size)],
                   core_send.at[k, i], core_recv.at[k, i], {"rows": core_peer})
            for i in range(2)
        ]
        mine = [
            pltpu.make_async_copy(
                slots.at[first + 2 + i, pl.ds(0, size)], out.at[0, pl.ds(i * size, size)], put_sem.at[k, i]
            )
            for i in range(2)
        ]
        return theirs, mine

    def terms(sources, rights, copies, rows, first):
        chunk = inner // 2
        for k, (source, at) in enumerate(sources):
            col = lax.broadcasted_iota(jnp.int32, (inner, inner), 1)
            pick = jnp.where(order_ref[...] == col, 1.0, 0.0).astype(bf16)
            both = dot_last(pick, source[:, at * inner : (at + 1) * inner]).astype(bf16)
            for half in range(2):
                lefts_ref[half, k * chunk : (k + 1) * chunk, :] = both[half * chunk : (half + 1) * chunk]
        d = rights[0].shape[1]
        for which in range(2):
            left = lefts_ref.at[(1 - c) if which == 0 else c]
            pieces = []
            for k, right in enumerate(rights):
                product = dot(left[k * chunk : (k + 1) * chunk, :], right[...])
                pieces.append(product.reshape(8, -1, d))
            if rows > len(rights) * chunk // 8:
                pieces.append(jnp.zeros((8, rows - len(rights) * chunk // 8, d), f32))
            blocks = jnp.concatenate(pieces, axis=1).astype(bf16)
            for i in range(2):
                half = blocks[4 * i : 4 * i + 4].reshape(4 * rows, d)
                slots[first + 2 * which + i, : 4 * rows, :] = half
                if which == 0 or len(copies) > 1:
                    copies[which][i].start()

    attn_rows, extra_rows = attn_sums.shape[1] // 8, extra_sums.shape[0] // 8
    attn_copies = core_copies(0, attn_sums, attn_rows, 0)
    extra_copies = core_copies(1, extra_pair, extra_rows, 4)

    size, wide = 4 * extra_rows, extra_sums.shape[1]
    spread = [
        remote(slots.at[i, pl.ds(0, size), pl.ds(0, wide)], extra_sums.at[pl.ds(i * size, size)],
               cross_send.at[i], cross_recv.at[i], {"section": 1 - section})
        for i in range(2)
    ]
    keep = [
        pltpu.make_async_copy(
            slots.at[2 + i, pl.ds(0, size), pl.ds(0, wide)], extra_sums.at[pl.ds(i * size, size)], put_sem.at[1, i]
        )
        for i in range(2)
    ]

    def split_features():
        for copy in extra_copies[0]:
            copy.wait()
        for copies in attn_copies:
            for copy in copies:
                copy.wait()
        half = n2.shape[1] // 2
        for i in range(2):
            fetch = pltpu.make_async_copy(
                extra_pair.at[1, pl.ds(i * size, size)], slots.at[4 + i, pl.ds(0, size)], load_sem.at[3]
            )
            fetch.start()
            fetch.wait()
            total = slots[6 + i, :size, :].astype(f32) + slots[4 + i, :size, :].astype(f32)
            slots[i, :size, :half] = total[:, :half].astype(bf16)
            spread[i].start()
            slots[2 + i, :size, :half] = total[:, half:].astype(bf16)
            keep[i].start()

    @pl.when(is_enc)
    def _():
        arrive("V4", "V3")

    terms(
        [(dqkv_ref, 0), (dqkv_ref, 1), (dqkv_ref, 2), (mixed_ref, 0)],
        [n1_ref, n1_ref, n1_ref, ga_ref], attn_copies, attn_rows, 0,
    )

    @pl.when(is_dec)
    def _():
        arrive("U2", "W1", "U1", "W2", "S6", "S5", "V4")
        terms(
            [(dcqkv_ref, 0), (dcqkv_ref, 1), (dcqkv_ref, 2), (cmixed_ref, 0), (gl_ref, 0)],
            [mc_ref, encoded_ref, encoded_ref, gac_ref, final_ref], extra_copies[:1], extra_rows, 4,
        )
        arrive("T6", "V3")
        split_features()

    @pl.when(is_enc)
    def _():
        arrive("U4", "U3", "W3", "W4", "V6", "U6", "V5", "U5", "V7", "W5", "W6", "U7", "W7")

    @pl.when(is_dec)
    def _():
        arrive("U4", "T5", "Q5", "Q6", "S7", "U3", "V6", "W4", "W3", "T7", "V5", "U6", "Q7", "V7", "U5", "W6")
        arrive("W7", "U7", "W5")

    for name in parts:
        for p in range(8):
            zz, yy, _ = place_of(parts[name][2], p)
            part_copy(name, 0, p, 4 * zz + 2 * yy + 1 - c, {"rows": me}).wait_recv()
            each_send(name, p, lambda copy: copy.wait_send())
    own_copies["S"].wait()
    own_copies["V"].wait()

    @pl.when(is_enc)
    def _():
        for copies in attn_copies:
            for copy in copies:
                copy.wait()
        for copy in spread:
            copy.wait_recv()

    @pl.when(is_dec)
    def _():
        for i in range(2):
            spread[i].wait_send()
            keep[i].wait()

    @pl.when(is_dec)
    def _():
        back_copy.wait_send()


def middle(cross_cnt, self_cnt, dec_cnt, x, y1, y2, n2, qkv, mixed, n1, encoded, target, gains, order, gu, attn_w, extra_w, feed_w, length):
    t, d = x.shape
    inner = attn_w.shape[0] // 4
    held = 8
    vm = pl.BlockSpec(memory_space=pltpu.VMEM)
    sm = pl.BlockSpec(memory_space=pltpu.SMEM)
    anywhere = pl.BlockSpec(memory_space=pl.ANY)
    attn_rows = inner // 4
    extra_rows = -(-5 * inner // 16 // 16) * 16
    return pl.pallas_call(
        functools.partial(mid_kernel, length),
        out_shape=(
            jax.ShapeDtypeStruct((16, t, d), bf16),
            jax.ShapeDtypeStruct((16, t, d), bf16),
            jax.ShapeDtypeStruct((t, d), f32),
            jax.ShapeDtypeStruct((8, d), f32),
            jax.ShapeDtypeStruct((2, 8 * attn_rows, d), bf16),
            jax.ShapeDtypeStruct((8 * extra_rows, -(-d // 2 // 128) * 128), bf16),
            jax.ShapeDtypeStruct((2, 8 * extra_rows, d), bf16),
        ),
        in_specs=[sm] * 3 + [vm] * 11 + [anywhere] * 4,
        out_specs=(anywhere,) * 2 + (vm,) * 2 + (anywhere,) * 3,
        scratch_shapes=[
            pltpu.VMEM((held,) + feed_w.shape[1:], bf16),
            pltpu.VMEM(gu.shape, f32),
            pltpu.VMEM(attn_w.shape, bf16),
            pltpu.VMEM((inner, d), bf16),
            pltpu.VMEM((t, d), f32),
            pltpu.VMEM((t, d), f32),
            pltpu.VMEM((t, d), f32),
            pltpu.VMEM((t, d), bf16),
            pltpu.VMEM((t, 3 * inner), bf16),
            pltpu.VMEM((t, inner), bf16),
            pltpu.VMEM((t, d), bf16),
            pltpu.VMEM((t, 3 * inner), bf16),
            pltpu.VMEM((t, 3 * inner), bf16),
            pltpu.VMEM((t, inner), bf16),
            pltpu.VMEM((t, inner), bf16),
            pltpu.VMEM((t, d), bf16),
            pltpu.VMEM((t, d), bf16),
            pltpu.VMEM((t, d), bf16),
            pltpu.VMEM((t, d), bf16),
            pltpu.VMEM((t, d), bf16),
            pltpu.VMEM((2, 5 * inner // 2, t), bf16),
            pltpu.SemaphoreType.DMA((6, 4, 8)),
            pltpu.SemaphoreType.DMA((6, 16)),
            pltpu.SemaphoreType.DMA((held,)),
            pltpu.SemaphoreType.DMA((4,)),
            pltpu.SemaphoreType.DMA((2,)),
            pltpu.SemaphoreType.DMA((1,)),
            pltpu.SemaphoreType.DMA((1,)),
            pltpu.SemaphoreType.DMA((2, 2)),
            pltpu.SemaphoreType.DMA((2, 2)),
            pltpu.SemaphoreType.DMA((2, 2)),
            pltpu.SemaphoreType.DMA((2,)),
            pltpu.SemaphoreType.DMA((2,)),
        ],
        compiler_params=pltpu.CompilerParams(
            vmem_limit_bytes=62 * 1024 * 1024, collective_id=2, has_side_effects=True
        ),
        cost_estimate=pl.CostEstimate(
            flops=4 * t * feed_w.size, bytes_accessed=2 * feed_w.size + 8 * gu.size, transcendentals=2 * gu.size
        ),
    )(cross_cnt, self_cnt, dec_cnt, x, y1, y2, n2, qkv, mixed, n1, encoded, target, gains, order, gu, attn_w, extra_w, feed_w)


def adam_step(weight, first_moment, second_moment, gradient, step_rate, weight_decay):
    first_new = 0.9 * first_moment + 0.1 * gradient
    second_new = 0.999 * second_moment + 0.001 * gradient * gradient
    first_fix = 1.0 - 0.9**STEP
    second_fix = 1.0 - 0.999**STEP
    update = first_new / first_fix / (jnp.sqrt(second_new / second_fix) + 1e-08)
    return (first_new, second_new, weight - step_rate * (update + weight_decay * weight))


def kinds_first(gathered, n, kinds, per):
    d = gathered.shape[-1]
    return gathered.reshape(n, kinds, per, d).transpose(1, 0, 2, 3).reshape(kinds * n * per, d)


def owners_first(left, right, n):
    t, k, units = left.shape
    grad = jnp.einsum("tku,td->kud", left, right, preferred_element_type=f32)
    return grad.reshape(k, n, units // n, -1).transpose(1, 0, 2, 3)


def local(
    block_input,
    lengths,
    targets,
    attention_weight,
    attention_first,
    attention_second,
    feed_weight,
    feed_first,
    feed_second,
    norm_gain,
    gain_first,
    gain_second,
    cross_weight,
    cross_first,
    cross_second,
    head_weight,
    head_first,
    head_second,
    cross_gain,
    cross_gain_first,
    cross_gain_second,
):
    n = lax.axis_size("rows")
    is_encoder = lax.axis_index("section") == 0
    micro, length, d = block_input.shape[1:]
    t = micro * length
    per = attention_weight.shape[1]
    f = feed_weight.shape[1]
    inner = per * n

    attn_own = attention_weight[0].astype(bf16).transpose(1, 0, 2).reshape(4 * per, d)
    feed_own = feed_weight[0].astype(bf16).transpose(1, 0, 2)
    half_rows = jnp.concatenate(
        [cross_weight.astype(bf16).transpose(1, 0, 2), head_weight.astype(bf16)[None]], axis=0
    )

    gains = norm_gain[0]
    gain_attn, gain_feed, gain_final = gains[0:1], gains[1:2], gains[2:3]
    gain_cross = cross_gain[None]
    x = block_input[0].reshape(t, d)
    enc_counts = lengths[0, :, 0]
    dec_counts = lengths[1, :, 0]
    zero_one = jnp.zeros((1,), jnp.int32)
    self_counts = jnp.concatenate([jnp.where(is_encoder, 0, 1).astype(jnp.int32)[None], enc_counts])
    cross_counts = jnp.concatenate([zero_one, enc_counts])
    target_column = targets.reshape(t, 1)

    def blank(maker):
        return jax.tree.map(lambda a: jnp.zeros(a.shape, a.dtype), jax.eval_shape(maker))

    emit = n != BLOCKS
    if emit:
        attn_all = lax.all_gather(attn_own, "rows", axis=0, tiled=True)
        attn_w = kinds_first(attn_all, n, 4, per)
        feed_all = lax.all_gather(feed_own.reshape(3 * f, d), "rows", axis=0, tiled=True)
        feed_w = kinds_first(feed_all, n, 3, f).reshape(3, BLOCKS, -1, d)
        feed_w = feed_w.transpose(1, 0, 2, 3).reshape(BLOCKS, -1, d)
        other_half = lax.ppermute(half_rows, "section", [(0, 1)])
        extra_own = jnp.concatenate([other_half, half_rows], axis=-1).reshape(5 * per, d)
        extra_all = lax.all_gather(extra_own, "rows", axis=0, tiled=True)
        n1, qkv, mixed, y1 = attend_fwd(self_counts, x, gain_attn, attn_w, length)

        def enc_feed():
            return feed_fwd(y1, gain_feed, gain_final, feed_w)

        enc_state = lax.cond(is_encoder, enc_feed, lambda: blank(enc_feed))
        encoded = lax.ppermute(enc_state[3], "section", [(0, 1)])
    else:
        units = jnp.arange(4 * inner, dtype=jnp.int32).reshape(n, 4, per)
        order = units.transpose(1, 0, 2).reshape(1, 4 * inner)
        units = jnp.arange(inner, dtype=jnp.int32).reshape(4, 2, 2, per)
        travel = units.transpose(2, 1, 0, 3).reshape(inner, 1)
        pad = -(5 * per) % 16
        half_own = jnp.pad(half_rows.reshape(5 * per, d // 2), ((0, pad), (0, 0)))
        outs = front(
            self_counts, order, x, gain_attn, gain_feed, gain_final,
            attn_own, feed_own.reshape(3 * f, d), half_own, length,
        )
        _, feed_w, extra_all, n1, qkv, mixed, y1 = outs[:7]
        enc_state, encoded, attn_w = outs[7:11], outs[11], outs[12]
        extra_all = extra_all[:, : 5 * per]
    extra_w = kinds_first(extra_all, n, 5, per)
    cross_w, head_w = extra_w[: 4 * inner], extra_w[4 * inner :]

    if emit:
        def dec_front():
            mc, cqkv, cmixed, z2 = attend_fwd(cross_counts, y1, gain_cross, cross_w, length, encoded)
            return feed_fwd(z2, gain_feed, gain_final, feed_w) + (mc, cqkv, cmixed, z2)

        def enc_pass():
            rest = jax.eval_shape(dec_front)[4:7]
            return tuple(enc_state) + tuple(jnp.zeros(a.shape, a.dtype) for a in rest) + (y1,)

        n2, gu, y2, final, mc, cqkv, cmixed, mid = lax.cond(is_encoder, enc_pass, dec_front)
        def dec_back():
            gl, up, loss = head_loss(dec_counts, final, head_w, target_column, length)
            feed_out = feed_bwd(up, mid, y2, gain_feed, gain_final, gu, feed_w, emit)
            ga_c, dqkv_c, gy1, gg_c, ge = attend_bwd(
                cross_counts, y1, gain_cross, feed_out[1], cqkv, cross_w, length, True
            )
            return (ge, gy1, feed_out[2], feed_out[0], *feed_out[3:], gl, ga_c, dqkv_c, gg_c, loss)

        back = lax.cond(is_encoder, lambda: blank(dec_back), dec_back)
        returned = lax.ppermute(back[0], "section", [(1, 0)])
        at = 6 if emit else 4
        gl, ga_c, dqkv_c, gg_c, loss = back[at:]

        def enc_back():
            feed_out = feed_bwd(returned, mid, y2, gain_feed, gain_final, gu, feed_w, emit)
            return (feed_out[1], feed_out[2], feed_out[0], *feed_out[3:])

        backs = lax.cond(is_encoder, enc_back, lambda: tuple(back[1:at]))
        gy1, gg_feed, gf = backs[:3]

        ga, dqkv, gx, gg_attn = attend_bwd(self_counts, x, gain_attn, gy1, qkv, attn_w, length)
        tiny = jnp.concatenate(
            [gg_attn, gg_feed, gg_c, jnp.broadcast_to(loss, (1, d)), jnp.zeros((3, d), f32)], axis=0
        )
    else:
        gain_rows = jnp.concatenate([gains, gain_cross], axis=0)
        n2, gu, y2 = enc_state[:3]
        (
            n2_all, gf_all, gx, tiny, attn_terms, extra_terms, _,
        ) = middle(
            cross_counts, self_counts, dec_counts, x, y1, y2, n2, qkv, mixed, n1, encoded, target_column,
            gain_rows, travel, gu, attn_w, extra_w, feed_w, length,
        )

    half = d // 2
    if emit:
        extra_part = jnp.concatenate(
            [
                owners_first(dqkv_c[:, None, :inner], mc, n),
                owners_first(dqkv_c[:, inner:].reshape(t, 2, inner), encoded, n),
                owners_first(cmixed[:, None], ga_c, n),
                owners_first(gl[:, None], final, n),
            ],
            axis=1,
        ).astype(bf16)
        extra_sum = lax.psum_scatter(
            extra_part.reshape(n * 5 * per, d), "rows", scatter_dimension=0, tiled=True
        )
        extra_first = lax.ppermute(extra_sum[:, :half], "section", [(1, 0)])
        extra_grad = jnp.where(is_encoder, extra_first, extra_sum[:, half:]).astype(f32)
        extra_grad = extra_grad.reshape(5, per, half)

        attn_part = jnp.concatenate(
            [
                owners_first(dqkv.reshape(t, 3, inner), n1, n),
                owners_first(mixed[:, None], ga, n),
            ],
            axis=1,
        ).astype(bf16)
        attn_sum = lax.psum_scatter(
            attn_part.reshape(n * 4 * per, d), "rows", scatter_dimension=0, tiled=True
        ).astype(f32)
        dgu, hid = backs[3], backs[4]
        nb, _, fb = hid.shape
        left = dgu.reshape(nb, t, 2, fb).transpose(1, 2, 0, 3).reshape(t, 2, nb * fb)
        hid = hid.transpose(1, 0, 2).reshape(t, 1, nb * fb)
        feed_part = jnp.concatenate(
            [owners_first(left, n2, n), owners_first(hid, gf, n)], axis=1
        ).astype(bf16)
        feed_grad = lax.psum_scatter(
            feed_part.reshape(n * 3 * f, d), "rows", scatter_dimension=0, tiled=True
        ).astype(f32)
        tiny_sum = jnp.sum(lax.all_gather(tiny, "rows", axis=0), axis=0)
    else:
        feed_grad, attn_sum, extra_sum, tiny_sum = tail(
            tiny, attn_terms, extra_terms, feed_own.reshape(3 * f, d), n2_all, gf_all
        )
        extra_grad = extra_sum[: 5 * per, :half].reshape(5, per, half)
    tiny_dec = lax.ppermute(tiny_sum[3:5], "section", [(1, 0)])
    tiny_dec = jnp.where(is_encoder, tiny_dec, tiny_sum[3:5])
    attn_grad = attn_sum.reshape(4, per, d).transpose(1, 0, 2)
    feed_grad = feed_grad.reshape(3, f, d).transpose(1, 0, 2)
    cross_gain_total = tiny_dec[0]
    loss_total = tiny_dec[1, 0]

    attention_new = adam_step(
        attention_weight, attention_first, attention_second, attn_grad[None], 0.05, 0.1
    )
    feed_new = adam_step(feed_weight, feed_first, feed_second, feed_grad[None], 0.05, 0.1)
    gain_new = adam_step(norm_gain, gain_first, gain_second, tiny_sum[None, 0:3], 0.5, 0.0)
    cross_new = adam_step(
        cross_weight, cross_first, cross_second, extra_grad[:4].transpose(1, 0, 2), 0.05, 0.1
    )
    head_new = adam_step(head_weight, head_first, head_second, extra_grad[4], 0.05, 0.1)
    cross_gain_new = adam_step(
        cross_gain, cross_gain_first, cross_gain_second, cross_gain_total, 0.5, 0.0
    )
    return (
        gx.reshape(1, micro, length, d),
        loss_total,
        *attention_new,
        *feed_new,
        *gain_new,
        *cross_new,
        *head_new,
        *cross_gain_new,
    )


def solution(mesh):
    by_row = P("section", "rows", None, None)
    gain = P("section", None, None)
    cross = P("rows", None, "section")
    head = P("rows", "section")
    weights = (by_row,) * 6 + (gain,) * 3 + (cross,) * 3 + (head,) * 3 + (P(),) * 3
    tokens = P("section", None, "rows", None)
    return jax.shard_map(
        local,
        mesh=mesh,
        in_specs=(tokens, P(None, None, "rows"), P(None, "rows")) + weights,
        out_specs=(tokens, P()) + weights,
        check_vma=False,
    )
```
